32 devices in a mesh: groups: 2 (over y), tensor: 4 (over z), dp: 4 (over x, core).
Axes of the slice: x: 2, y: 2, z: 4, core: 2. Of those that a mesh axis runs over, the one named last changes fastest.
Arguments:
- layer_input: bfloat16 [4096, 4096], P(('groups', 'dp'), 'tensor'), parts along dimension 0, may hold values from -6 to 6
- gate_act: bfloat16 [4096, 14336], P(('groups', 'dp'), 'tensor'), parts along dimension 0, may hold values from -6 to 6
- up_act: bfloat16 [4096, 14336], P(('groups', 'dp'), 'tensor'), parts along dimension 0, may hold values from -6 to 6
- out_grad: bfloat16 [4096, 4096], P(('groups', 'dp'), 'tensor'), parts along dimension 0, may hold values from -6 to 6
- w_gate: bfloat16 [4096, 14336], P('dp', 'tensor'), may hold values from -0.09375 to 0.09375
- w_up: bfloat16 [4096, 14336], P('dp', 'tensor'), may hold values from -0.09375 to 0.09375
- w_down: bfloat16 [14336, 4096], P('tensor'), may hold values from -0.046875 to 0.046875
- proj_x: bfloat16 [4096, 64], P('tensor'), may hold values from -0.09375 to 0.09375
- proj_u: bfloat16 [14336, 64], P('tensor'), may hold values from -0.046875 to 0.046875
- proj_h: bfloat16 [14336, 64], P('tensor'), may hold values from -0.046875 to 0.046875
- proj_g: bfloat16 [4096, 64], P('tensor'), may hold values from -0.09375 to 0.09375
- doc_lengths: int32 [8, 8], P(('groups', 'dp')), parts along dimension 0, may hold values from 1 to 256, 512 in all within a row
Outputs:
- input_grad: bfloat16 [4096, 4096], P(('groups', 'dp'), 'tensor'), parts along dimension 0
- doc_logs: float32 [64, 2, 4096], P(('groups', 'dp'), None, 'tensor'), parts along dimension 0
The draws below stay inside these ranges and needn't reach their ends.
There are 2 independent parts, one for each index of `groups`. The reference program is written for one: setup_inputs(seed, part) draws one part's arguments, and reference() takes and returns one part's arrays. A program takes and returns all parts, laid end to end along the dimension named above; an argument that names none is the same for every part. Nothing has to cross between parts.
Inputs may be any that keep to these rules, and one draw needn't show every extreme that they name: `doc_lengths`: each row sums to 512, and its largest entry is 256.
All inputs are finite; a program needn't handle non-finite values.
Results may differ from the reference program's by a relative error of at most 0.0059.
Values may be sent and summed in bfloat16 or wider, within the bound.
No kernel may reach another device: no remote copies, remote signals or barrier semaphores. Data moves between devices by JAX's collectives and lax.ppermute only.
A program may use at most 256 MiB of HBM per device.

```python
import math
import jax
import jax.numpy as jnp
import numpy as np
from jax import lax

D = 4096
FF = 14336
RANK = 64
TOK_DEV = 512
DOC_DEV = 8
MOST = 256
TOKENS = 2048
NDOC = 32
N_DP = 4


def steps_of(key, shape, pieces, least, top_value):
    def one(axis_at, parts):
        draws = jax.random.uniform(jax.random.fold_in(jax.random.fold_in(key, 6), axis_at), (parts,), jnp.float32, least / len(pieces), top_value / len(pieces))
        return jnp.repeat(jnp.exp(draws), shape[axis_at] // parts).reshape((-1,) + (1,) * (len(shape) - axis_at - 1))

    gain = one(*pieces[0])
    for cut in pieces[1:]:
        gain = gain * one(*cut)
    return gain


def length_profile(amount, total, reach, skew):
    loads = [(1 << 20) // math.isqrt(rank ** skew) + 1 for rank in range(2, amount + 1)]
    spare, counts = total - reach - (amount - 1), [1] * (amount - 1)
    while spare > 0:
        movable = [i for i in range(amount - 1) if counts[i] < reach]
        whole, remaining = sum([loads[i] for i in movable]), spare
        for i in movable:
            extra = min(reach - counts[i], max(1, remaining * loads[i] // whole), spare)
            counts[i] = counts[i] + extra
            spare = spare - extra
    return np.array([reach] + counts)


def uneven(rng, count, total, most, slope):
    if count == 2:
        one = jax.random.randint(rng, (), max(1, total - most), min(most, total - 1) + 1)
        return jnp.stack([one, total - one])
    lengths = jnp.asarray(length_profile(count, total, most, slope), jnp.int32)
    couples = (count - 1) // 2
    giver, receiver = lengths[1:1 + 2 * couples:2], lengths[2:2 + 2 * couples:2]
    slack = jnp.minimum(giver - 1, most - receiver)
    shifted = jax.random.randint(jax.random.fold_in(rng, 1), (couples,), 0, 1 << 20) % (slack + 1)
    lengths = lengths.at[1:1 + 2 * couples:2].set(giver - shifted).at[2:2 + 2 * couples:2].set(receiver + shifted)
    return lengths[jax.random.permutation(jax.random.fold_in(rng, 2), count)]


def scatter_about(own_key, extent, spread, limit, shards=(), kind=jnp.bfloat16):
    values = jax.random.normal(own_key, extent, jnp.float32) * spread
    if len(shards) > 0:
        values = steps_of(own_key, extent, shards, -0.22, 0.18) * values
    return jnp.clip(values, min=-limit, max=limit).astype(kind)


def setup_inputs(seed: int = 0, part: int = 0) -> dict:
    key_list = jax.random.split(jax.random.key(seed), 13)
    part_splits = jax.random.split(jax.random.fold_in(key_list[12], part), 13)
    return {
        "layer_input": scatter_about(part_splits[0], (TOKENS, D), 1.0, 6.0, ((0, 4), (1, 4))),
        "gate_act": scatter_about(part_splits[1], (TOKENS, FF), 1.0, 6.0, ((0, 4), (1, 4))),
        "up_act": scatter_about(part_splits[2], (TOKENS, FF), 1.0, 6.0, ((0, 4), (1, 4))),
        "out_grad": scatter_about(part_splits[3], (TOKENS, D), 1.0, 6.0, ((0, 4), (1, 4))),
        "w_gate": scatter_about(key_list[4], (D, FF), D ** -0.5, 0.09375, ((0, 4), (1, 4))),
        "w_up": scatter_about(key_list[5], (D, FF), D ** -0.5, 0.09375, ((0, 4), (1, 4))),
        "w_down": scatter_about(key_list[6], (FF, D), FF ** -0.5, 0.046875, ((0, 4),)),
        "proj_x": scatter_about(key_list[7], (D, RANK), D ** -0.5, 0.09375, ((0, 4),)),
        "proj_u": scatter_about(key_list[8], (FF, RANK), FF ** -0.5, 0.046875, ((0, 4),)),
        "proj_h": scatter_about(key_list[9], (FF, RANK), FF ** -0.5, 0.046875, ((0, 4),)),
        "proj_g": scatter_about(key_list[10], (D, RANK), D ** -0.5, 0.09375, ((0, 4),)),
        "doc_lengths": jax.vmap(lambda own: uneven(own, DOC_DEV, TOK_DEV, MOST, 2))(jax.random.split(part_splits[11], N_DP)).reshape((N_DP, DOC_DEV)).astype(jnp.int32),
    }


def members(doc_lengths):
    ends = jnp.cumsum(doc_lengths, axis=1)
    starts = ends - doc_lengths
    position = jnp.arange(TOK_DEV, dtype=jnp.int32)[None, :, None]
    inside = (position >= starts[:, None, :]) & (position < ends[:, None, :])
    return inside.astype(jnp.float32)


def doc_table(member, grads, inputs):
    grads_wide = grads.astype(jnp.float32).reshape(N_DP, TOK_DEV, RANK)
    inputs_wide = inputs.astype(jnp.float32).reshape(N_DP, TOK_DEV, RANK)
    table = jnp.einsum('ptk,pti,ptj->pkij', member, grads_wide, inputs_wide)
    return table.reshape(NDOC, RANK * RANK)


def reference(layer_input, gate_act, up_act, out_grad, w_gate, w_up, w_down, proj_x, proj_u, proj_h, proj_g, doc_lengths):
    member = members(doc_lengths)
    gate_wide = gate_act.astype(jnp.float32)
    up_wide = up_act.astype(jnp.float32)
    sigma = jax.nn.sigmoid(gate_wide)
    swish = gate_wide * sigma
    hidden = (swish * up_wide).astype(jnp.bfloat16)
    hidden_grad = lax.dot_general(out_grad, w_down, (((1,), (1,)), ((), ())), preferred_element_type=jnp.float32)
    up_grad = (hidden_grad * swish).astype(jnp.bfloat16)
    gate_grad = (hidden_grad * up_wide * sigma * (1.0 + gate_wide * (1.0 - sigma))).astype(jnp.bfloat16)
    summed = lax.dot_general(gate_grad, w_gate, (((1,), (1,)), ((), ())), preferred_element_type=jnp.float32)
    summed = summed + lax.dot_general(up_grad, w_up, (((1,), (1,)), ((), ())), preferred_element_type=jnp.float32)
    input_grad = summed.astype(jnp.bfloat16)
    in_up = jnp.dot(layer_input, proj_x, preferred_element_type=jnp.float32).astype(jnp.bfloat16)
    up_out = jnp.dot(up_grad, proj_u, preferred_element_type=jnp.float32).astype(jnp.bfloat16)
    in_down = jnp.dot(hidden, proj_h, preferred_element_type=jnp.float32).astype(jnp.bfloat16)
    out_down = jnp.dot(out_grad, proj_g, preferred_element_type=jnp.float32).astype(jnp.bfloat16)
    up_log = doc_table(member, up_out, in_up)
    down_log = doc_table(member, out_down, in_down)
    doc_logs = jnp.stack([up_log, down_log], axis=1)
    return input_grad, doc_logs
```

```python
import jax
import jax.numpy as jnp
from jax import lax
from jax.sharding import PartitionSpec as P

CORES = 2
CHUNKS = 4


def contract_right(left, right):
    return lax.dot_general(
        left, right, (((1,), (1,)), ((), ())), preferred_element_type=jnp.float32
    )


def project(proj, rows):
    return lax.dot_general(
        proj, rows, (((0,), (1,)), ((), ())), preferred_element_type=jnp.float32
    )


def pack_table(doc_lengths, count):
    lengths = doc_lengths[0]
    ends = jnp.cumsum(lengths)
    starts = ends - lengths
    position = jnp.arange(count, dtype=jnp.int32)[None, :]
    inside = (position >= starts[:, None]) & (position < ends[:, None])
    return inside.astype(jnp.bfloat16)


def doc_outer(member, grad_rows, inputs):
    count = member.shape[1]
    weighted = (member[:, None, :] * grad_rows[None, :, :]).reshape(-1, count)
    table = contract_right(weighted, inputs)
    return table.reshape(member.shape[0], grad_rows.shape[0] * inputs.shape[0])


def swap_cores(value):
    size = lax.axis_size("dp")
    return lax.ppermute(value, "dp", [(i, i ^ 1) for i in range(size)])


def from_chip(value, shift):
    size = lax.axis_size("dp")
    step = shift * CORES
    return lax.ppermute(value, "dp", [((i + step) % size, i) for i in range(size)])


def from_group(value, shift):
    size = lax.axis_size("groups")
    return lax.ppermute(value, "groups", [((i + shift) % size, i) for i in range(size)])


def to_rank(value, shift):
    size = lax.axis_size("tensor")
    return lax.ppermute(value, "tensor", [(i, (i + shift) % size) for i in range(size)])


def per_device(
    layer_input,
    gate_act,
    up_act,
    out_grad,
    w_gate,
    w_up,
    w_down,
    proj_x,
    proj_u,
    proj_h,
    proj_g,
    doc_lengths,
):
    groups, ranks = lax.axis_size("groups"), lax.axis_size("tensor")
    blocks = lax.axis_size("dp")
    chips = blocks // CORES
    group, rank = lax.axis_index("groups"), lax.axis_index("tensor")
    place = lax.axis_index("dp")
    chip, core = place // CORES, place % CORES
    rows = w_gate.shape[0]
    part = rows // groups
    piece = part // CHUNKS
    units = blocks * groups
    per_rank = units // ranks

    def share(k):
        first = group * part + k * piece
        return jnp.concatenate(
            [
                lax.dynamic_slice_in_dim(w_gate, first, piece, 0),
                lax.dynamic_slice_in_dim(w_up, first, piece, 0),
            ],
            axis=1,
        )

    partner_gate, partner_up = swap_cores(w_gate), swap_cores(w_up)
    fetched = {}
    for k in range(CHUNKS):
        mine = share(k)
        for s in range(1, chips):
            first_hand = from_chip(mine, s)
            for r in range(groups):
                got = first_hand if r == 0 else from_group(first_hand, r)
                fetched[k, s, 0, r] = got
                fetched[k, s, 1, r] = swap_cores(got)

    full_grad = lax.all_gather(out_grad, "tensor", axis=1, tiled=True)
    gate_wide = gate_act.astype(jnp.float32)
    up_wide = up_act.astype(jnp.float32)
    sigma = jax.nn.sigmoid(gate_wide)
    swish = gate_wide * sigma
    hidden = (swish * up_wide).astype(jnp.bfloat16)
    hidden_grad = contract_right(full_grad, w_down)
    up_grad = (hidden_grad * swish).astype(jnp.bfloat16)
    gate_grad = (hidden_grad * up_wide * sigma * (1.0 + gate_wide * (1.0 - sigma))).astype(
        jnp.bfloat16
    )
    grads = jnp.concatenate([gate_grad, up_grad], axis=1)

    in_up_part = project(proj_x, layer_input)
    up_out_part = project(proj_u, up_grad)
    in_down_part = project(proj_h, hidden)
    out_down_part = project(proj_g, out_grad)
    slot = up_out_part.shape[0] // ranks

    def factors_for(other):
        return jnp.concatenate(
            [
                in_up_part,
                in_down_part,
                lax.dynamic_slice_in_dim(out_down_part, other * slot, slot, 0),
                lax.dynamic_slice_in_dim(up_out_part, other * slot, slot, 0),
            ],
            axis=0,
        )

    factors = factors_for(rank)
    for t in range(1, ranks):
        factors = factors + to_rank(factors_for((rank + t) % ranks), t)
    factors = factors.astype(jnp.bfloat16)
    width = in_up_part.shape[0]
    in_up, in_down = factors[:width], factors[width : 2 * width]
    out_down, up_out = factors[2 * width : 2 * width + slot], factors[2 * width + slot :]
    member = pack_table(doc_lengths, layer_input.shape[0])
    doc_logs = jnp.stack(
        [doc_outer(member, up_out, in_up), doc_outer(member, out_down, in_down)], axis=1
    )

    def by_unit(table):
        table = table.astype(jnp.bfloat16).reshape(table.shape[0], groups, CHUNKS, piece)
        return jnp.roll(table, -group, axis=1)

    near = [
        by_unit(contract_right(gate_grad, w_gate) + contract_right(up_grad, w_up)),
        by_unit(contract_right(gate_grad, partner_gate) + contract_right(up_grad, partner_up)),
    ]

    def position(unit):
        block, at = unit // groups, unit % groups
        away = (block // CORES - chip) % chips
        return (away * CORES + (block % CORES) ^ core) * groups + (at - group) % groups

    results = []
    for k in range(CHUNKS):
        terms = []
        for s in range(chips):
            for c in range(CORES):
                for r in range(groups):
                    if s == 0:
                        terms.append(near[c][:, r, k])
                    else:
                        terms.append(
                            contract_right(grads, fetched[k, s, c, r]).astype(jnp.bfloat16)
                        )
        terms = jnp.stack(terms)

        def terms_for(other):
            return jnp.stack(
                [
                    lax.dynamic_index_in_dim(
                        terms, position(other * per_rank + j), 0, keepdims=False
                    )
                    for j in range(per_rank)
                ]
            )

        total = terms_for(rank).astype(jnp.float32)
        for t in range(1, ranks):
            total = total + to_rank(terms_for((rank + t) % ranks), t).astype(jnp.float32)
        results.append(total.astype(jnp.bfloat16))
    input_grad = jnp.stack(results).transpose(2, 1, 0, 3).reshape(layer_input.shape[0], -1)
    return (input_grad, doc_logs)


def solution(mesh):
    placed = (
        P(("groups", "dp"), "tensor"),
        P(("groups", "dp"), "tensor"),
        P(("groups", "dp"), "tensor"),
        P(("groups", "dp"), "tensor"),
        P("dp", "tensor"),
        P("dp", "tensor"),
        P("tensor", None),
        P("tensor", None),
        P("tensor", None),
        P("tensor", None),
        P("tensor", None),
        P(("groups", "dp"), None),
    )
    return jax.shard_map(
        per_device,
        mesh=mesh,
        in_specs=placed,
        out_specs=(P(("groups", "dp"), "tensor"), P(("groups", "dp"), None, "tensor")),
        check_vma=False,
    )
```

```python
import functools

import jax
import jax.numpy as jnp
import numpy as np
from jax import lax
from jax.experimental import pallas as pl
from jax.experimental.pallas import tpu as pltpu
from jax.sharding import PartitionSpec as P

CORES = 2
CHUNKS = 8
VMEM_BYTES = 60 * 1024 * 1024
LIGHT = pl.CostEstimate(flops=1, bytes_accessed=1, transcendentals=0)
ANYWHERE = pl.BlockSpec(memory_space=pl.ANY)


def contract_right(left, right):
    return lax.dot_general(
        left, right, (((1,), (1,)), ((), ())), preferred_element_type=jnp.float32
    )


def project(proj, rows):
    return lax.dot_general(
        proj, rows, (((0,), (1,)), ((), ())), preferred_element_type=jnp.float32
    )


def pack_table(doc_lengths, count):
    lengths = doc_lengths[0]
    ends = jnp.cumsum(lengths)
    starts = ends - lengths
    position = jnp.arange(count, dtype=jnp.int32)[None, :]
    inside = (position >= starts[:, None]) & (position < ends[:, None])
    return inside.astype(jnp.bfloat16)


def doc_outer(member, grad_rows, inputs):
    count = member.shape[1]
    weighted = (member[:, None, :] * grad_rows[None, :, :]).reshape(-1, count)
    table = contract_right(weighted, inputs)
    return table.reshape(member.shape[0], grad_rows.shape[0] * inputs.shape[0])


def swap_cores(value):
    size = lax.axis_size("dp")
    return lax.ppermute(value, "dp", [(i, i ^ 1) for i in range(size)])


def from_chip(value, shift):
    size = lax.axis_size("dp")
    step = shift * CORES
    return lax.ppermute(value, "dp", [((i + step) % size, i) for i in range(size)])


def from_group(value, shift):
    size = lax.axis_size("groups")
    return lax.ppermute(value, "groups", [((i + shift) % size, i) for i in range(size)])


def widest(size, options):
    return next((w for w in options if size % w == 0), size)


def share_rows(w_gate, w_up, group, places, piece, part, carried, after):
    width = w_gate.shape[1]
    kept, waits = len(carried), len(after)

    def kernel(group_ref, gate_ref, up_ref, *refs):
        outs = refs[kept + waits + kept : kept + waits + kept + len(places)]
        sems = refs[-1] if places else None
        copies = []
        for at, k in enumerate(places):
            first = pl.multiple_of(group_ref[0] * part + k * piece, piece)
            for half, source in enumerate((gate_ref, up_ref)):
                copies.append(
                    pltpu.make_async_copy(
                        source.at[pl.ds(first, piece), :],
                        outs[at].at[:, pl.ds(half * width, width)],
                        sems.at[2 * at + half],
                    )
                )
        for copy in copies:
            copy.start()
        for copy in copies:
            copy.wait()

    results = pl.pallas_call(
        kernel,
        out_shape=[jax.ShapeDtypeStruct(a.shape, a.dtype) for a in carried]
        + [jax.ShapeDtypeStruct((piece, 2 * width), w_gate.dtype) for _ in places],
        in_specs=[pl.BlockSpec(memory_space=pltpu.SMEM)] + [ANYWHERE] * (2 + kept + waits),
        out_specs=[ANYWHERE] * (kept + len(places)),
        scratch_shapes=[pltpu.SemaphoreType.DMA((2 * len(places),))] if places else [],
        input_output_aliases={3 + i: i for i in range(kept)},
        compiler_params=pltpu.CompilerParams(vmem_limit_bytes=VMEM_BYTES),
        cost_estimate=LIGHT,
        name="share_rows",
    )(group, w_gate, w_up, *carried, *after)
    return list(results[:kept]), list(results[kept:])


def spread_ranks(value):
    ranks = lax.axis_size("tensor")
    below, above = [value], [value]
    for _ in range(1, ranks):
        below.append(lax.ppermute(below[-1], "tensor", [(i, i + 1) for i in range(ranks - 1)]))
        above.append(lax.ppermute(above[-1], "tensor", [(i + 1, i) for i in range(ranks - 1)]))
    return below, above[1:]


def hidden_grads(rank, below, above, w_down, gate_act, up_act, proj_u, after):
    ranks = len(below)
    count, features = below[0].shape
    hidden, depth = w_down.shape
    tile = widest(hidden, (512, 256, 128))
    step = min(tile, 256)
    narrow = proj_u.shape[1]

    def kernel(rank_ref, down_ref, gate_ref, up_ref, proj_ref, *refs):
        both_ref, out_ref, grad_ref, sem = refs[-4:]

        def gather(at, wait):
            block = lax.rem(rank_ref[0] + ranks - at, ranks)
            cols = pl.ds(pl.multiple_of(block * features, features), features)
            for source, valid in (
                (refs[at], rank_ref[0] >= at),
                (refs[ranks + ranks - at - 1] if at else None, rank_ref[0] < at),
            ):
                if source is not None:

                    @pl.when(valid)
                    def _():
                        copy = pltpu.make_async_copy(source, grad_ref.at[:, cols], sem.at[at])
                        copy.wait() if wait else copy.start()

        @pl.when(pl.program_id(0) == 0)
        def _():
            out_ref[...] = jnp.zeros_like(out_ref)
            for at in range(ranks):
                gather(at, False)
            for at in range(ranks):
                gather(at, True)

        for first in range(0, tile, step):
            cols = slice(first, first + step)
            wide = contract_right(grad_ref[...], down_ref[cols, :])
            gate = gate_ref[:, cols].astype(jnp.float32)
            up = up_ref[:, cols].astype(jnp.float32)
            sigma = jax.nn.sigmoid(gate)
            up_grad = (wide * (gate * sigma)).astype(jnp.bfloat16)
            slope = sigma * (1.0 + gate * (1.0 - sigma))
            both_ref[0, :, cols] = (wide * up * slope).astype(jnp.bfloat16)
            both_ref[1, :, cols] = up_grad
            out_ref[...] += jnp.dot(
                up_grad, proj_ref[cols, :], preferred_element_type=jnp.float32
            )

    return pl.pallas_call(
        kernel,
        grid=(hidden // tile,),
        out_shape=[
            jax.ShapeDtypeStruct((2, count, hidden), jnp.bfloat16),
            jax.ShapeDtypeStruct((count, narrow), jnp.float32),
        ],
        in_specs=[
            pl.BlockSpec(memory_space=pltpu.SMEM),
            pl.BlockSpec((tile, depth), lambda i: (i, 0)),
            pl.BlockSpec((count, tile), lambda i: (0, i)),
            pl.BlockSpec((count, tile), lambda i: (0, i)),
            pl.BlockSpec((tile, narrow), lambda i: (i, 0)),
        ]
        + [ANYWHERE] * (2 * ranks - 1 + len(after)),
        out_specs=[
            pl.BlockSpec((2, count, tile), lambda i: (0, 0, i)),
            pl.BlockSpec((count, narrow), lambda i: (0, 0)),
        ],
        scratch_shapes=[
            pltpu.VMEM((count, depth), jnp.bfloat16),
            pltpu.SemaphoreType.DMA((ranks,)),
        ],
        compiler_params=pltpu.CompilerParams(vmem_limit_bytes=VMEM_BYTES),
        cost_estimate=LIGHT,
        name="hidden_grads",
    )(rank, w_down, gate_act, up_act, proj_u, *below, *above, *after)


def weigh(units, grads, after):
    hidden = grads[0].shape[2]
    tile = widest(hidden, (512, 256, 128))
    steps = hidden // tile
    counts = [g.shape[1] for g in grads]
    heights = [u[0].shape[0] for u in units]
    rows, count = sum(heights), sum(counts)

    def kernel(*refs):
        weights = refs[: 2 * len(units)]
        both = refs[2 * len(units) : 2 * len(units) + len(grads)]
        out_ref, total = refs[-2:]
        at = pl.program_id(0)

        @pl.when(at == 0)
        def _():
            total[...] = jnp.zeros_like(total)

        gate = jnp.concatenate([w[...] for w in weights[0::2]], axis=0)
        up = jnp.concatenate([w[...] for w in weights[1::2]], axis=0)
        first = 0
        for ref in both:
            span = slice(first, first + ref.shape[1])
            total[:, span] += contract_right(gate, ref[0]) + contract_right(up, ref[1])
            first += ref.shape[1]

        @pl.when(at == steps - 1)
        def _():
            out_ref[...] = total[...].astype(jnp.bfloat16)

    specs, operands = [], []
    for gate, up, up_at in units:
        specs.append(pl.BlockSpec((gate.shape[0], tile), lambda i: (0, i)))
        specs.append(
            pl.BlockSpec((up.shape[0], tile), functools.partial(lambda o, i: (0, o + i), up_at // tile))
        )
        operands += [gate, up]
    for g in grads:
        specs.append(pl.BlockSpec((2, g.shape[1], tile), lambda i: (0, 0, i)))
        operands.append(g)
    return pl.pallas_call(
        kernel,
        grid=(steps,),
        out_shape=jax.ShapeDtypeStruct((rows, count), jnp.bfloat16),
        in_specs=specs + [ANYWHERE] * len(after),
        out_specs=pl.BlockSpec((rows, count), lambda i: (0, 0)),
        scratch_shapes=[pltpu.VMEM((rows, count), jnp.float32)],
        compiler_params=pltpu.CompilerParams(vmem_limit_bytes=VMEM_BYTES),
        cost_estimate=LIGHT,
        name="weigh_rows",
    )(*operands, *after)


def reduce_to(value, owner):
    groups, ranks, blocks = (lax.axis_size(a) for a in ("groups", "tensor", "dp"))
    bit = 1
    while bit < ranks:
        pairs = []
        for g in range(groups):
            for p in range(blocks):
                target = owner[g, p]
                for z in range(ranks):
                    if z % bit == target % bit and (z ^ target) & bit:
                        pairs.append(((g * ranks + z) * blocks + p, (g * ranks + (z ^ bit)) * blocks + p))
        got = lax.ppermute(value, ("groups", "tensor", "dp"), pairs)
        value = (value.astype(jnp.float32) + got.astype(jnp.float32)).astype(jnp.bfloat16)
        bit *= 2
    return value


def per_device(
    layer_input,
    gate_act,
    up_act,
    out_grad,
    w_gate,
    w_up,
    w_down,
    proj_x,
    proj_u,
    proj_h,
    proj_g,
    doc_lengths,
):
    groups, ranks = lax.axis_size("groups"), lax.axis_size("tensor")
    blocks = lax.axis_size("dp")
    chips = blocks // CORES
    group, rank = lax.axis_index("groups"), lax.axis_index("tensor")
    place = lax.axis_index("dp")
    chip, core = place // CORES, place % CORES
    rows, hidden_width = w_gate.shape
    count = layer_input.shape[0]
    features = out_grad.shape[1]
    part = rows // groups
    piece = part // CHUNKS
    split = max(1, ranks // blocks)
    group_word = jnp.full((1,), group, jnp.int32)
    rank_word = jnp.full((1,), rank, jnp.int32)

    below, above = spread_ranks(out_grad)
    gate_wide = gate_act.astype(jnp.float32)
    hidden = (gate_wide * jax.nn.sigmoid(gate_wide) * up_act.astype(jnp.float32)).astype(jnp.bfloat16)
    early_part = jnp.concatenate(
        [project(proj_x, layer_input), project(proj_h, hidden), project(proj_g, out_grad)], axis=0
    )
    early = lax.all_gather(early_part, "tensor", axis=0, tiled=False)

    _, shares = share_rows(w_gate, w_up, group_word, [0, 1], piece, part, [], [])
    fetched, arriving = {}, {}

    def fetch(k):
        for s in range(1, chips):
            arriving[k, s, 0] = from_chip(shares[k], s)

    def forward(k, after):
        names = [n for n in arriving if n[0] == k and n[2] == 0] + [
            n for n in arriving if n[0] == k - 1 and n[2] > 0
        ]
        places = [k + 2] if k + 2 < CHUNKS else []
        carried, fresh = share_rows(
            w_gate, w_up, group_word, places, piece, part, [arriving.pop(n) for n in names], after
        )
        fetched.update(zip(names, carried))
        shares.extend(fresh)
        if fresh:
            fetch(k + 2)
        for s in range(1, chips):
            for r in range(1, groups):
                arriving[k, s, r] = from_group(fetched[k, s, 0], r)

    def owner_of(s, first_of):
        table = np.zeros((groups, blocks), np.int64)
        for g in range(groups):
            for p in range(blocks):
                block = (p // CORES + s) % chips * CORES + p % CORES
                table[g, p] = (block * rows + first_of(g)) // features
        return table

    near, far = [], {}

    def far_round(names, after):
        sets = {}
        for s in range(1, chips):
            for r in range(groups):
                table = owner_of(s, lambda g: (g + r) % groups * part)
                kept = [(k, s, q) for k, q in names if q == r]
                sets.setdefault((s, table.tobytes()), (table, []))[1].extend(kept)
        outs = []
        for table, kept in sets.values():
            if kept:
                units = [(fetched[n], fetched[n], hidden_width) for n in kept]
                out = weigh(units, [mine, theirs], after)
                outs.append(out)
                total = reduce_to(out, table)
                for at, n in enumerate(kept):
                    far[n] = total[at * piece : (at + 1) * piece]
        return outs

    fetch(0)
    fetch(1)
    forward(0, [])
    forward(1, [])
    forward(2, [])
    forward(3, [])
    mine, up_out_part = hidden_grads(
        rank_word, below, above, w_down, gate_act, up_act, proj_u, [shares[5], early_part]
    )
    late = lax.all_gather(up_out_part, "tensor", axis=0, tiled=False)
    forward(4, [mine])
    theirs = swap_cores(mine)
    height = rows // split
    done = []
    for which, (both, after) in enumerate(((mine, [shares[6]]), (theirs, []))):
        for j in range(split):
            gate_rows = w_gate[j * height : (j + 1) * height]
            up_rows = w_up[j * height : (j + 1) * height]
            out = weigh([(gate_rows, up_rows, 0)], [both], after)
            done.append(out)
            near.append(reduce_to(out, owner_of(0, lambda g: j * height)))
    forward(5, done)
    outs = far_round([(k, 0) for k in range(5)] + [(k, 1) for k in range(4)], [shares[7]])
    forward(6, outs)
    outs = far_round([(5, 0), (6, 0), (4, 1), (5, 1)], [])
    forward(7, outs)

    early = early.sum(axis=0).astype(jnp.bfloat16)
    late = late.sum(axis=0).astype(jnp.bfloat16).T
    width = late.shape[0]
    slot = width // ranks
    in_up, in_down, out_down = early[:width], early[width : 2 * width], early[2 * width :]
    member = pack_table(doc_lengths, count)
    own = lambda table: lax.dynamic_slice_in_dim(table, rank * slot, slot, 0)
    doc_logs = jnp.stack(
        [doc_outer(member, own(late), in_up), doc_outer(member, own(out_down), in_down)], axis=1
    )

    far_round([(7, 0), (6, 1)], [doc_logs])
    for n in list(arriving):
        fetched[n] = arriving.pop(n)
    far_round([(7, 1)], [])

    first = rank * features
    away = (first // rows // CORES - chip) % chips
    owner = first // rows % CORES == core
    inside = first % rows
    tall = features // part

    def pick(index, options):
        value = options[0]
        for at, option in enumerate(options[1:], 1):
            value = jnp.where(index == at, option, value)
        return value

    options = [
        pick(
            inside // height,
            [jnp.concatenate([near[j], near[split + j]], axis=1) for j in range(split)],
        )
    ]
    for s in range(1, chips):
        by_shift = [
            jnp.concatenate([far[k, s, r] for k in range(CHUNKS)], axis=0) for r in range(groups)
        ]
        options.append(
            jnp.concatenate(
                [
                    pick((inside // part + j - group) % groups, by_shift)
                    for j in range(tall)
                ],
                axis=0,
            )
        )
    total = pick(away, options)
    from_partner = swap_cores(total[:, count:])
    input_grad = jnp.where(owner, total[:, :count], from_partner).T
    return (input_grad, doc_logs)


def solution(mesh):
    placed = (
        P(("groups", "dp"), "tensor"),
        P(("groups", "dp"), "tensor"),
        P(("groups", "dp"), "tensor"),
        P(("groups", "dp"), "tensor"),
        P("dp", "tensor"),
        P("dp", "tensor"),
        P("tensor", None),
        P("tensor", None),
        P("tensor", None),
        P("tensor", None),
        P("tensor", None),
        P(("groups", "dp"), None),
    )
    return jax.shard_map(
        per_device,
        mesh=mesh,
        in_specs=placed,
        out_specs=(P(("groups", "dp"), "tensor"), P(("groups", "dp"), None, "tensor")),
        check_vma=False,
    )
```

```python
import functools

import jax
import jax.numpy as jnp
import numpy as np
from jax import lax
from jax.experimental import pallas as pl
from jax.experimental.pallas import tpu as pltpu
from jax.sharding import PartitionSpec as P

CORES = 2
CHUNKS = 8
VMEM_BYTES = 60 * 1024 * 1024
LIGHT = pl.CostEstimate(flops=1, bytes_accessed=1, transcendentals=0)
ANYWHERE = pl.BlockSpec(memory_space=pl.ANY)


def contract_right(left, right):
    return lax.dot_general(
        left, right, (((1,), (1,)), ((), ())), preferred_element_type=jnp.float32
    )


def project(proj, rows):
    return lax.dot_general(
        proj, rows, (((0,), (1,)), ((), ())), preferred_element_type=jnp.float32
    )


def pack_table(doc_lengths, count):
    lengths = doc_lengths[0]
    ends = jnp.cumsum(lengths)
    starts = ends - lengths
    position = jnp.arange(count, dtype=jnp.int32)[None, :]
    inside = (position >= starts[:, None]) & (position < ends[:, None])
    return inside.astype(jnp.bfloat16)


def doc_outer(member, grad_rows, inputs):
    count = member.shape[1]
    weighted = (member[:, None, :] * grad_rows[None, :, :]).reshape(-1, count)
    table = contract_right(weighted, inputs)
    return table.reshape(member.shape[0], grad_rows.shape[0] * inputs.shape[0])


def swap_cores(value):
    size = lax.axis_size("dp")
    return lax.ppermute(value, "dp", [(i, i ^ 1) for i in range(size)])


def from_chip(value, shift):
    size = lax.axis_size("dp")
    step = shift * CORES
    return lax.ppermute(value, "dp", [((i + step) % size, i) for i in range(size)])


def from_group(value, shift):
    size = lax.axis_size("groups")
    return lax.ppermute(value, "groups", [((i + shift) % size, i) for i in range(size)])


def widest(size, options):
    return next((w for w in options if size % w == 0), size)


def share_rows(w_gate, w_up, group, places, piece, carried, after):
    rows, width = w_gate.shape
    tile = widest(width, (1792, 896, 128))
    kept, waits, fresh = len(carried), len(after), len(places)
    per_group = rows // lax.axis_size("groups") // piece

    def kernel(group_ref, *refs):
        outs = refs[len(refs) - fresh :]
        for at in range(fresh):
            outs[at][0] = refs[2 * at][...]
            outs[at][1] = refs[2 * at + 1][...]

    specs = []
    for k in places:
        at_chunk = functools.partial(lambda k, i, g: (g[0] * per_group + k, i), k)
        specs += [pl.BlockSpec((piece, tile), at_chunk)] * 2
    results = pl.pallas_call(
        kernel,
        grid_spec=pltpu.PrefetchScalarGridSpec(
            num_scalar_prefetch=1,
            grid=(width // tile if places else 1,),
            in_specs=specs + [ANYWHERE] * (kept + waits),
            out_specs=[ANYWHERE] * kept
            + [pl.BlockSpec((2, piece, tile), lambda i, g: (0, 0, i))] * fresh,
        ),
        out_shape=[jax.ShapeDtypeStruct(a.shape, a.dtype) for a in carried]
        + [jax.ShapeDtypeStruct((2, piece, width), w_gate.dtype) for _ in places],
        input_output_aliases={1 + 2 * fresh + i: i for i in range(kept)},
        compiler_params=pltpu.CompilerParams(vmem_limit_bytes=VMEM_BYTES),
        cost_estimate=LIGHT,
        name="share_rows",
    )(group, *[w_gate, w_up] * fresh, *carried, *after)
    return list(results[:kept]), list(results[kept:])


def spread_ranks(value):
    ranks = lax.axis_size("tensor")
    below, above = [value], [value]
    for _ in range(1, ranks):
        below.append(lax.ppermute(below[-1], "tensor", [(i, i + 1) for i in range(ranks - 1)]))
        above.append(lax.ppermute(above[-1], "tensor", [(i + 1, i) for i in range(ranks - 1)]))
    return below, above[1:]


def prepare(gate_act, up_act, proj_h, after):
    count, hidden = gate_act.shape
    narrow = proj_h.shape[0]
    tile = widest(hidden, (512, 256, 128))

    def kernel(gate_ref, up_ref, proj_ref, *refs):
        slope_ref, down_ref = refs[-2:]

        @pl.when(pl.program_id(0) == 0)
        def _():
            down_ref[...] = jnp.zeros_like(down_ref)

        gate = gate_ref[...].astype(jnp.float32).T
        up = up_ref[...].astype(jnp.float32).T
        sigma = jax.nn.sigmoid(gate)
        swish = gate * sigma
        slope_ref[0] = up * sigma * (1.0 + gate * (1.0 - sigma))
        slope_ref[1] = swish
        down_ref[...] += jnp.dot(
            proj_ref[...], (swish * up).astype(jnp.bfloat16), preferred_element_type=jnp.float32
        )

    return pl.pallas_call(
        kernel,
        grid=(hidden // tile,),
        out_shape=[
            jax.ShapeDtypeStruct((2, hidden, count), jnp.float32),
            jax.ShapeDtypeStruct((narrow, count), jnp.float32),
        ],
        in_specs=[
            pl.BlockSpec((count, tile), lambda i: (0, i)),
            pl.BlockSpec((count, tile), lambda i: (0, i)),
            pl.BlockSpec((narrow, tile), lambda i: (0, i)),
        ]
        + [ANYWHERE] * len(after),
        out_specs=[
            pl.BlockSpec((2, tile, count), lambda i: (0, i, 0)),
            pl.BlockSpec((narrow, count), lambda i: (0, 0)),
        ],
        compiler_params=pltpu.CompilerParams(vmem_limit_bytes=VMEM_BYTES),
        cost_estimate=LIGHT,
        name="prepare",
    )(gate_act, up_act, proj_h, *after)


def hidden_grads(rank, below, above, w_down, slopes, proj_u, after):
    ranks = len(below)
    features, count = below[0].shape
    hidden, depth = w_down.shape
    tile = widest(hidden, (512, 256, 128))
    narrow = proj_u.shape[0]

    def kernel(rank_ref, down_ref, slope_ref, proj_ref, *refs):
        both_ref, out_ref, grad_ref, sem = refs[-4:]

        def gather(at, wait):
            block = lax.rem(rank_ref[0] + ranks - at, ranks)
            span = pl.ds(pl.multiple_of(block * features, features), features)
            for source, valid in (
                (refs[at], rank_ref[0] >= at),
                (refs[ranks + ranks - at - 1] if at else None, rank_ref[0] < at),
            ):
                if source is not None:

                    @pl.when(valid)
                    def _():
                        copy = pltpu.make_async_copy(source, grad_ref.at[span, :], sem.at[at])
                        copy.wait() if wait else copy.start()

        @pl.when(pl.program_id(0) == 0)
        def _():
            out_ref[...] = jnp.zeros_like(out_ref)
            for at in range(ranks):
                gather(at, False)
            for at in range(ranks):
                gather(at, True)

        wide = jnp.dot(down_ref[...], grad_ref[...], preferred_element_type=jnp.float32)
        both_ref[0] = (wide * slope_ref[0]).astype(jnp.bfloat16)
        up_grad = (wide * slope_ref[1]).astype(jnp.bfloat16)
        both_ref[1] = up_grad
        out_ref[...] += jnp.dot(proj_ref[...], up_grad, preferred_element_type=jnp.float32)

    return pl.pallas_call(
        kernel,
        grid=(hidden // tile,),
        out_shape=[
            jax.ShapeDtypeStruct((2, hidden, count), jnp.bfloat16),
            jax.ShapeDtypeStruct((narrow, count), jnp.float32),
        ],
        in_specs=[
            pl.BlockSpec(memory_space=pltpu.SMEM),
            pl.BlockSpec((tile, depth), lambda i: (i, 0)),
            pl.BlockSpec((2, tile, count), lambda i: (0, i, 0)),
            pl.BlockSpec((narrow, tile), lambda i: (0, i)),
        ]
        + [ANYWHERE] * (2 * ranks - 1 + len(after)),
        out_specs=[
            pl.BlockSpec((2, tile, count), lambda i: (0, i, 0)),
            pl.BlockSpec((narrow, count), lambda i: (0, 0)),
        ],
        scratch_shapes=[
            pltpu.VMEM((depth, count), jnp.bfloat16),
            pltpu.SemaphoreType.DMA((ranks,)),
        ],
        compiler_params=pltpu.CompilerParams(vmem_limit_bytes=VMEM_BYTES),
        cost_estimate=LIGHT,
        name="hidden_grads",
    )(rank, w_down, slopes, proj_u, *below, *above, *after)


def weigh(units, grads, after):
    hidden = grads[0].shape[1]
    tile = widest(hidden, (512, 256, 128))
    steps = hidden // tile
    counts = [g.shape[2] for g in grads]
    rows, count = sum(u[0].shape[-2] for u in units), sum(counts)
    flat = [w for u in units for w in u]

    def kernel(*refs):
        weights, both = refs[: len(flat)], refs[len(flat) : len(flat) + len(grads)]
        out_ref, total = refs[-2:]
        at = pl.program_id(0)

        @pl.when(at == 0)
        def _():
            total[...] = jnp.zeros_like(total)

        if len(units[0]) == 2:
            gate, up = weights[0][...], weights[1][...]
        else:
            gate = jnp.concatenate([w[0] for w in weights], axis=0)
            up = jnp.concatenate([w[1] for w in weights], axis=0)
        first = 0
        for ref in both:
            span = slice(first, first + ref.shape[2])
            total[:, span] += jnp.dot(
                gate, ref[0], preferred_element_type=jnp.float32
            ) + jnp.dot(up, ref[1], preferred_element_type=jnp.float32)
            first += ref.shape[2]

        @pl.when(at == steps - 1)
        def _():
            out_ref[...] = total[...].astype(jnp.bfloat16)

    specs = []
    for w in flat:
        if w.ndim == 2:
            specs.append(pl.BlockSpec((w.shape[0], tile), lambda i: (0, i)))
        else:
            specs.append(pl.BlockSpec((2, w.shape[1], tile), lambda i: (0, 0, i)))
    for g in grads:
        specs.append(pl.BlockSpec((2, tile, g.shape[2]), lambda i: (0, i, 0)))
    return pl.pallas_call(
        kernel,
        grid=(steps,),
        out_shape=jax.ShapeDtypeStruct((rows, count), jnp.bfloat16),
        in_specs=specs + [ANYWHERE] * len(after),
        out_specs=pl.BlockSpec((rows, count), lambda i: (0, 0)),
        scratch_shapes=[pltpu.VMEM((rows, count), jnp.float32)],
        compiler_params=pltpu.CompilerParams(vmem_limit_bytes=VMEM_BYTES),
        cost_estimate=LIGHT,
        name="weigh_rows",
    )(*flat, *grads, *after)


def scatter_ranks(value):
    ranks, rank = lax.axis_size("tensor"), lax.axis_index("tensor")
    bit = ranks // 2
    while bit:
        half = value.shape[0] // 2
        high = rank & bit != 0
        low_rows, high_rows = value[:half], value[half:]
        got = lax.ppermute(
            jnp.where(high, low_rows, high_rows), "tensor", [(i, i ^ bit) for i in range(ranks)]
        )
        value = jnp.where(high, high_rows, low_rows) + got
        bit //= 2
    return value


def reduce_to(value, owner):
    groups, ranks, blocks = (lax.axis_size(a) for a in ("groups", "tensor", "dp"))
    bit = 1
    while bit < ranks:
        pairs = []
        for g in range(groups):
            for p in range(blocks):
                target = owner[g, p]
                for z in range(ranks):
                    if z % bit == target % bit and (z ^ target) & bit:
                        pairs.append(((g * ranks + z) * blocks + p, (g * ranks + (z ^ bit)) * blocks + p))
        got = lax.ppermute(value, ("groups", "tensor", "dp"), pairs)
        value = (value.astype(jnp.float32) + got.astype(jnp.float32)).astype(jnp.bfloat16)
        bit *= 2
    return value


def per_device(
    layer_input,
    gate_act,
    up_act,
    out_grad,
    w_gate,
    w_up,
    w_down,
    proj_x,
    proj_u,
    proj_h,
    proj_g,
    doc_lengths,
):
    groups, ranks = lax.axis_size("groups"), lax.axis_size("tensor")
    blocks = lax.axis_size("dp")
    chips = blocks // CORES
    group, rank = lax.axis_index("groups"), lax.axis_index("tensor")
    place = lax.axis_index("dp")
    chip, core = place // CORES, place % CORES
    rows = w_gate.shape[0]
    count = layer_input.shape[0]
    features = out_grad.shape[1]
    part = rows // groups
    piece = part // CHUNKS
    split = max(1, ranks // blocks)
    group_word = jnp.full((1,), group, jnp.int32)
    rank_word = jnp.full((1,), rank, jnp.int32)

    below, above = spread_ranks(out_grad.T)
    _, shares = share_rows(w_gate, w_up, group_word, [0, 1], piece, [], [])
    slopes, in_down_part = prepare(gate_act, up_act, proj_h.T, [shares[0]])
    early_part = jnp.concatenate(
        [project(proj_x, layer_input), in_down_part, project(proj_g, out_grad)], axis=0
    )
    early = lax.all_gather(early_part, "tensor", axis=0, tiled=False)

    fetched, arriving = {}, {}

    def fetch(k):
        for s in range(1, chips):
            arriving[k, s, 0] = from_chip(shares[k], s)

    def forward(k, after, held=()):
        names = [n for n in arriving if n[0] == k and n[2] == 0] + [
            n for n in arriving if n[0] == k - 1 and n[2] > 0
        ]
        places = [k + 2] if k + 2 < CHUNKS else []
        carried, fresh = share_rows(
            w_gate, w_up, group_word, places, piece, [arriving.pop(n) for n in names] + list(held), after
        )
        fetched.update(zip(names, carried))
        shares.extend(fresh)
        if fresh:
            fetch(k + 2)
        for s in range(1, chips):
            for r in range(1, groups):
                arriving[k, s, r] = from_group(fetched[k, s, 0], r)
        return carried[len(names) :]

    def owner_of(s, first_of):
        table = np.zeros((groups, blocks), np.int64)
        for g in range(groups):
            for p in range(blocks):
                block = (p // CORES + s) % chips * CORES + p % CORES
                table[g, p] = (block * rows + first_of(g)) // features
        return table

    near, far = [], {}

    def far_round(names, after):
        sets = {}
        for s in range(1, chips):
            for r in range(groups):
                table = owner_of(s, lambda g: (g + r) % groups * part)
                kept = [(k, s, q) for k, q in names if q == r]
                sets.setdefault((s, table.tobytes()), (table, []))[1].extend(kept)
        outs = []
        for table, kept in sets.values():
            if kept:
                units = [(fetched[n],) for n in kept]
                out = weigh(units, [mine, theirs], after)
                outs.append(out)
                total = reduce_to(out, table)
                for at, n in enumerate(kept):
                    far[n] = total[at * piece : (at + 1) * piece]
        return outs

    fetch(0)
    fetch(1)
    forward(0, [slopes])
    forward(1, [early_part])
    forward(2, [])
    forward(3, [])
    mine, up_out_part = hidden_grads(
        rank_word, below, above, w_down, slopes, proj_u.T, [shares[5]]
    )
    up_out = scatter_ranks(up_out_part).astype(jnp.bfloat16)
    forward(4, [mine])
    theirs = swap_cores(mine)
    height = rows // split
    done = []
    for which, (both, after) in enumerate(((mine, [shares[6]]), (theirs, []))):
        for j in range(split):
            gate_rows = w_gate[j * height : (j + 1) * height]
            up_rows = w_up[j * height : (j + 1) * height]
            out = weigh([(gate_rows, up_rows)], [both], after)
            done.append(out)
            near.append(reduce_to(out, owner_of(0, lambda g: j * height)))
    forward(5, done)
    outs = far_round([(k, 0) for k in range(5)] + [(k, 1) for k in range(4)], [shares[7]])
    (early,) = forward(6, outs, [early])
    outs = far_round([(5, 0), (6, 0), (4, 1), (5, 1)], [])
    forward(7, outs)

    early = early.sum(axis=0).astype(jnp.bfloat16)
    width, slot = up_out_part.shape[0], up_out.shape[0]
    in_up, in_down, out_down = early[:width], early[width : 2 * width], early[2 * width :]
    member = pack_table(doc_lengths, count)
    out_down = lax.dynamic_slice_in_dim(out_down, rank * slot, slot, 0)
    doc_logs = jnp.stack(
        [doc_outer(member, up_out, in_up), doc_outer(member, out_down, in_down)], axis=1
    )

    far_round([(7, 0), (6, 1)], [doc_logs])
    for n in list(arriving):
        fetched[n] = arriving.pop(n)
    far_round([(7, 1)], [])

    first = rank * features
    away = (first // rows // CORES - chip) % chips
    owner = first // rows % CORES == core
    inside = first % rows
    tall = features // part

    def pick(index, options):
        value = options[0]
        for at, option in enumerate(options[1:], 1):
            value = jnp.where(index == at, option, value)
        return value

    options = [
        pick(
            inside // height,
            [jnp.concatenate([near[j], near[split + j]], axis=1) for j in range(split)],
        )
    ]
    for s in range(1, chips):
        by_shift = [
            jnp.concatenate([far[k, s, r] for k in range(CHUNKS)], axis=0) for r in range(groups)
        ]
        options.append(
            jnp.concatenate(
                [
                    pick((inside // part + j - group) % groups, by_shift)
                    for j in range(tall)
                ],
                axis=0,
            )
        )
    total = pick(away, options)
    from_partner = swap_cores(total[:, count:])
    input_grad = jnp.where(owner, total[:, :count], from_partner).T
    return (input_grad, doc_logs)


def solution(mesh):
    placed = (
        P(("groups", "dp"), "tensor"),
        P(("groups", "dp"), "tensor"),
        P(("groups", "dp"), "tensor"),
        P(("groups", "dp"), "tensor"),
        P("dp", "tensor"),
        P("dp", "tensor"),
        P("tensor", None),
        P("tensor", None),
        P("tensor", None),
        P("tensor", None),
        P("tensor", None),
        P(("groups", "dp"), None),
    )
    return jax.shard_map(
        per_device,
        mesh=mesh,
        in_specs=placed,
        out_specs=(P(("groups", "dp"), "tensor"), P(("groups", "dp"), None, "tensor")),
        check_vma=False,
    )
```

```python
import functools

import jax
import jax.numpy as jnp
import numpy as np
from jax import lax
from jax.experimental import pallas as pl
from jax.experimental.pallas import tpu as pltpu
from jax.sharding import PartitionSpec as P

CORES = 2
CHUNKS = 8
VMEM_BYTES = 60 * 1024 * 1024
FLOPS_PER_US = 270_000_000
ANYWHERE = pl.BlockSpec(memory_space=pl.ANY)


def contract_right(left, right):
    return lax.dot_general(
        left, right, (((1,), (1,)), ((), ())), preferred_element_type=jnp.float32
    )


def project(proj, rows):
    return lax.dot_general(
        proj, rows, (((0,), (1,)), ((), ())), preferred_element_type=jnp.float32
    )


def pack_table(doc_lengths, count):
    lengths = doc_lengths[0]
    ends = jnp.cumsum(lengths)
    starts = ends - lengths
    position = jnp.arange(count, dtype=jnp.int32)[None, :]
    inside = (position >= starts[:, None]) & (position < ends[:, None])
    return inside.astype(jnp.bfloat16)


def doc_outer(member, grad_rows, inputs):
    count = member.shape[1]
    weighted = (member[:, None, :] * grad_rows[None, :, :]).reshape(-1, count)
    table = contract_right(weighted, inputs)
    return table.reshape(member.shape[0], grad_rows.shape[0] * inputs.shape[0])


def swap_cores(value):
    size = lax.axis_size("dp")
    return lax.ppermute(value, "dp", [(i, i ^ 1) for i in range(size)])


def from_chip(value, shift):
    size = lax.axis_size("dp")
    step = shift * CORES
    return lax.ppermute(value, "dp", [((i + step) % size, i) for i in range(size)])


def from_group(value, shift):
    size = lax.axis_size("groups")
    return lax.ppermute(value, "groups", [((i + shift) % size, i) for i in range(size)])


def cost(us):
    return pl.CostEstimate(flops=int(us * FLOPS_PER_US) + 1, bytes_accessed=1, transcendentals=0)


def widest(size, options):
    return next((w for w in options if size % w == 0), size)


def share_rows(w_gate, w_up, group, places, piece, carried, after):
    rows, width = w_gate.shape
    tile = widest(width, (1792, 896, 128))
    kept, waits, fresh = len(carried), len(after), len(places)
    per_group = rows // lax.axis_size("groups") // piece

    def kernel(group_ref, *refs):
        outs = refs[len(refs) - fresh :] if fresh else []
        for at, out in enumerate(outs):
            out[0] = refs[2 * at][...]
            out[1] = refs[2 * at + 1][...]
        if not fresh:
            refs[-1][...] = jnp.zeros_like(refs[-1])

    specs = []
    for k in places:
        at_chunk = functools.partial(lambda k, i, g: (g[0] * per_group + k, i), k)
        specs += [pl.BlockSpec((piece, tile), at_chunk)] * 2
    results = pl.pallas_call(
        kernel,
        grid_spec=pltpu.PrefetchScalarGridSpec(
            num_scalar_prefetch=1,
            grid=(width // tile if places else 1,),
            in_specs=specs + [ANYWHERE] * (kept + waits),
            out_specs=[ANYWHERE] * kept
            + [pl.BlockSpec((2, piece, tile), lambda i, g: (0, 0, i))] * fresh
            + [pl.BlockSpec((8, 128), lambda i, g: (0, 0))] * (not fresh),
        ),
        out_shape=[jax.ShapeDtypeStruct(a.shape, a.dtype) for a in carried]
        + [jax.ShapeDtypeStruct((2, piece, width), w_gate.dtype) for _ in places]
        + [jax.ShapeDtypeStruct((8, 128), jnp.float32)] * (not fresh),
        input_output_aliases={1 + 2 * fresh + i: i for i in range(kept)},
        compiler_params=pltpu.CompilerParams(vmem_limit_bytes=VMEM_BYTES),
        cost_estimate=cost(2),
        name="share_rows",
    )(group, *[w_gate, w_up] * fresh, *carried, *after)
    return list(results[:kept]), list(results[kept:])


def spread_ranks(value):
    ranks = lax.axis_size("tensor")
    below, above = [value], [value]
    for _ in range(1, ranks):
        below.append(lax.ppermute(below[-1], "tensor", [(i, i + 1) for i in range(ranks - 1)]))
        above.append(lax.ppermute(above[-1], "tensor", [(i + 1, i) for i in range(ranks - 1)]))
    return below, above[1:]


def prepare(gate_act, up_act, proj_h, after):
    count, hidden = gate_act.shape
    narrow = proj_h.shape[0]
    tile = widest(hidden, (512, 256, 128))

    def kernel(gate_ref, up_ref, proj_ref, *refs):
        slope_ref, down_ref = refs[-2:]

        @pl.when(pl.program_id(0) == 0)
        def _():
            down_ref[...] = jnp.zeros_like(down_ref)

        gate = gate_ref[...].astype(jnp.float32).T
        up = up_ref[...].astype(jnp.float32).T
        sigma = jax.nn.sigmoid(gate)
        swish = gate * sigma
        slope_ref[0] = up * sigma * (1.0 + gate * (1.0 - sigma))
        slope_ref[1] = swish
        down_ref[...] += jnp.dot(
            proj_ref[...], (swish * up).astype(jnp.bfloat16), preferred_element_type=jnp.float32
        )

    return pl.pallas_call(
        kernel,
        grid=(hidden // tile,),
        out_shape=[
            jax.ShapeDtypeStruct((2, hidden, count), jnp.float32),
            jax.ShapeDtypeStruct((narrow, count), jnp.float32),
        ],
        in_specs=[
            pl.BlockSpec((count, tile), lambda i: (0, i)),
            pl.BlockSpec((count, tile), lambda i: (0, i)),
            pl.BlockSpec((narrow, tile), lambda i: (0, i)),
        ]
        + [ANYWHERE] * len(after),
        out_specs=[
            pl.BlockSpec((2, tile, count), lambda i: (0, i, 0)),
            pl.BlockSpec((narrow, count), lambda i: (0, 0)),
        ],
        compiler_params=pltpu.CompilerParams(vmem_limit_bytes=VMEM_BYTES),
        cost_estimate=cost(12),
        name="prepare",
    )(gate_act, up_act, proj_h, *after)


def hidden_part(rank, below, above, w_down, first, so_far, slopes, proj_u, after):
    ranks = lax.axis_size("tensor")
    features, count = (below or above)[0].shape
    hidden = w_down.shape[0]
    far = first + len(above) - 1
    own = len(below) - len(above)
    places = own + min(2 * len(above), ranks - first)
    width = widest(features, (512, 256, 128))
    subs = features // width
    tile = widest(hidden, (512, 256, 128))
    finish = slopes is not None
    steps = places * subs
    total_steps = steps + (hidden // tile if finish else 0)

    def counts(z):
        span = far - first + 1
        under = jnp.clip(z - first + 1, 0, span)
        over = jnp.clip(ranks - z - first, 0, span)
        return under, over

    def column(i, rank_ref):
        z = rank_ref[0]
        under, over = counts(z)
        at = jnp.clip(i // subs, 0, jnp.maximum(own + under + over - 1, 0))
        block = jnp.where(at < own + under, z - first - (at - own), z + first + at - own - under)
        if own:
            block = jnp.where(at == 0, z, block)
        block = jnp.clip(block, 0, ranks - 1)
        sub = jnp.where(i // subs > at, subs - 1, lax.rem(i, subs))
        return (0, block * subs + sub)

    def kernel(rank_ref, down_ref, *refs):
        z = rank_ref[0]
        under, over = counts(z)
        sources = refs[: len(below) + len(above)]
        grad_ref, total, sem = refs[-3:]
        i = pl.program_id(0)

        def gather(wait):
            pieces = [(sources[at], True, at) for at in range(own)]
            for t in range(len(above)):
                pieces.append((sources[own + t], t < under, own + t))
                pieces.append((sources[len(below) + t], t < over, own + under + t))
            for at, (source, valid, place) in enumerate(pieces):

                @pl.when(valid)
                def _():
                    rows = pl.ds(pl.multiple_of(place * features, features), features)
                    copy = pltpu.make_async_copy(source, grad_ref.at[rows, :], sem.at[at])
                    copy.wait() if wait else copy.start()

        rest = refs[len(below) + len(above) :]

        @pl.when(i == 0)
        def _():
            gather(False)
            if so_far is not None:
                load = pltpu.make_async_copy(rest[0], total, sem.at[len(sources)])
                load.start()
                load.wait()
            else:
                total[...] = jnp.zeros_like(total)
            gather(True)

        @pl.when((i < steps) & (i // subs < own + under + over))
        def _():
            rows = pl.ds(pl.multiple_of(i * width, width), width)
            total[...] += jnp.dot(
                down_ref[...], grad_ref[rows, :], preferred_element_type=jnp.float32
            )

        if not finish:
            out = refs[-4]

            @pl.when(i == total_steps - 1)
            def _():
                store = pltpu.make_async_copy(total, out, sem.at[len(sources)])
                store.start()
                store.wait()

        else:
            slope_ref, proj_ref = rest[1:3]
            both_ref, out_ref = refs[-5:-3]

            @pl.when(i == 0)
            def _():
                out_ref[...] = jnp.zeros_like(out_ref)

            @pl.when(i >= steps)
            def _():
                rows = pl.ds(pl.multiple_of((i - steps) * tile, tile), tile)
                wide = total[rows, :]
                both_ref[0] = (wide * slope_ref[0]).astype(jnp.bfloat16)
                up_grad = (wide * slope_ref[1]).astype(jnp.bfloat16)
                both_ref[1] = up_grad
                out_ref[...] += jnp.dot(proj_ref[...], up_grad, preferred_element_type=jnp.float32)

    operands = [w_down, *below, *above]
    specs = [pl.BlockSpec((hidden, width), column)] + [ANYWHERE] * (len(below) + len(above))
    if so_far is not None:
        operands.append(so_far)
        specs.append(ANYWHERE)
    if finish:
        narrow = proj_u.shape[0]
        row = lambda i: jnp.maximum(i - steps, 0)
        operands += [slopes, proj_u]
        specs += [
            pl.BlockSpec((2, tile, count), lambda i, r: (0, row(i), 0)),
            pl.BlockSpec((narrow, tile), lambda i, r: (0, row(i))),
        ]
        out_shape = [
            jax.ShapeDtypeStruct((2, hidden, count), jnp.bfloat16),
            jax.ShapeDtypeStruct((narrow, count), jnp.float32),
        ]
        out_specs = [
            pl.BlockSpec((2, tile, count), lambda i, r: (0, row(i), 0)),
            pl.BlockSpec((narrow, count), lambda i, r: (0, 0)),
        ]
    else:
        out_shape = jax.ShapeDtypeStruct((hidden, count), jnp.float32)
        out_specs = ANYWHERE
    return pl.pallas_call(
        kernel,
        grid_spec=pltpu.PrefetchScalarGridSpec(
            num_scalar_prefetch=1,
            grid=(total_steps,),
            in_specs=specs + [ANYWHERE] * len(after),
            out_specs=out_specs,
            scratch_shapes=[
                pltpu.VMEM((places * features, count), jnp.bfloat16),
                pltpu.VMEM((hidden, count), jnp.float32),
                pltpu.SemaphoreType.DMA((len(below) + len(above) + 1,)),
            ],
        ),
        out_shape=out_shape,
        compiler_params=pltpu.CompilerParams(vmem_limit_bytes=VMEM_BYTES),
        cost_estimate=cost(15 if finish else 12),
        name="hidden_part",
    )(rank, *operands, *after)


def weigh(routes, grads, after, price):
    hidden = grads[0].shape[1]
    tile = widest(hidden, (512, 256, 128))
    steps = hidden // tile
    heights = [sum(u[0].shape[-2] for u in units) for units in routes]
    rows, count = sum(heights), sum(g.shape[2] for g in grads)
    units = [u for route in routes for u in route]
    flat = [w for u in units for w in u]

    def kernel(*refs):
        weights, both = list(refs[: len(flat)]), refs[len(flat) : len(flat) + len(grads)]
        outs, total = refs[-1 - len(routes) : -1], refs[-1]
        at = pl.program_id(0)

        @pl.when(at == 0)
        def _():
            total[...] = jnp.zeros_like(total)

        gates, ups = [], []
        for u in units:
            mine, weights = weights[: len(u)], weights[len(u) :]
            gates.append(mine[0][...] if len(u) == 2 else mine[0][0])
            ups.append(mine[1][...] if len(u) == 2 else mine[0][1])
        gate, up = jnp.concatenate(gates, axis=0), jnp.concatenate(ups, axis=0)
        first = 0
        for ref in both:
            span = slice(first, first + ref.shape[2])
            total[:, span] += jnp.dot(
                gate, ref[0], preferred_element_type=jnp.float32
            ) + jnp.dot(up, ref[1], preferred_element_type=jnp.float32)
            first += ref.shape[2]

        @pl.when(at == steps - 1)
        def _():
            top = 0
            for out, height in zip(outs, heights):
                out[...] = total[top : top + height].astype(jnp.bfloat16)
                top += height

    specs = []
    for w in flat:
        if w.ndim == 2:
            specs.append(pl.BlockSpec((w.shape[0], tile), lambda i: (0, i)))
        else:
            specs.append(pl.BlockSpec((2, w.shape[1], tile), lambda i: (0, 0, i)))
    for g in grads:
        specs.append(pl.BlockSpec((2, tile, g.shape[2]), lambda i: (0, i, 0)))
    return pl.pallas_call(
        kernel,
        grid=(steps,),
        out_shape=[jax.ShapeDtypeStruct((h, count), jnp.bfloat16) for h in heights],
        in_specs=specs + [ANYWHERE] * len(after),
        out_specs=[pl.BlockSpec((h, count), lambda i: (0, 0)) for h in heights],
        scratch_shapes=[pltpu.VMEM((rows, count), jnp.float32)],
        compiler_params=pltpu.CompilerParams(vmem_limit_bytes=VMEM_BYTES),
        cost_estimate=cost(price),
        name="weigh_rows",
    )(*flat, *grads, *after)


def add(values, others, heights, after):
    pairs = len(values)
    flat = [h for hs in heights for h in hs]

    def kernel(*refs):
        outs = list(refs[len(refs) - len(flat) :])
        for at in range(pairs):
            top = 0
            for height in heights[at]:
                rows = slice(top, top + height)
                outs.pop(0)[...] = (
                    refs[at][rows].astype(jnp.float32) + refs[pairs + at][rows].astype(jnp.float32)
                ).astype(jnp.bfloat16)
                top += height

    count = values[0].shape[1]
    width = widest(count, (128,))
    specs = [pl.BlockSpec((v.shape[0], width), lambda i: (0, i)) for v in values]
    return pl.pallas_call(
        kernel,
        grid=(count // width,),
        out_shape=[jax.ShapeDtypeStruct((h, count), jnp.bfloat16) for h in flat],
        in_specs=specs + specs + [ANYWHERE] * len(after),
        out_specs=[pl.BlockSpec((h, width), lambda i: (0, i)) for h in flat],
        compiler_params=pltpu.CompilerParams(vmem_limit_bytes=VMEM_BYTES),
        cost_estimate=cost(2),
        name="add_terms",
    )(*values, *others, *after)


def exchange(value, bit):
    ranks = lax.axis_size("tensor")
    return lax.ppermute(value, "tensor", [(i, i ^ bit) for i in range(ranks)])


def halve(value, bit):
    half = value.shape[0] // 2
    high = lax.axis_index("tensor") & bit != 0
    low_rows, high_rows = value[:half], value[half:]
    got = exchange(jnp.where(high, low_rows, high_rows), bit)
    return jnp.where(high, high_rows, low_rows) + got


def toward(value, owner, bit):
    groups, ranks, blocks = (lax.axis_size(a) for a in ("groups", "tensor", "dp"))
    pairs = []
    for g in range(groups):
        for p in range(blocks):
            target = owner[g, p]
            for z in range(ranks):
                if z % bit == target % bit and (z ^ target) & bit:
                    pairs.append(((g * ranks + z) * blocks + p, (g * ranks + (z ^ bit)) * blocks + p))
    return lax.ppermute(value, ("groups", "tensor", "dp"), pairs)


def later_steps(value, owner):
    bit = 2
    got = None
    while bit < lax.axis_size("tensor"):
        if got is not None:
            (value,) = add([value], [got], [[value.shape[0]]], [])
        got = toward(value, owner, bit)
        bit *= 2
    return value, got


def per_device(
    layer_input,
    gate_act,
    up_act,
    out_grad,
    w_gate,
    w_up,
    w_down,
    proj_x,
    proj_u,
    proj_h,
    proj_g,
    doc_lengths,
):
    groups, ranks = lax.axis_size("groups"), lax.axis_size("tensor")
    blocks = lax.axis_size("dp")
    chips = blocks // CORES
    group, rank = lax.axis_index("groups"), lax.axis_index("tensor")
    place = lax.axis_index("dp")
    chip, core = place // CORES, place % CORES
    rows = w_gate.shape[0]
    count = layer_input.shape[0]
    features = out_grad.shape[1]
    part = rows // groups
    piece = part // CHUNKS
    split = max(1, ranks // blocks)
    group_word = jnp.full((1,), group, jnp.int32)
    rank_word = jnp.full((1,), rank, jnp.int32)

    below, above = spread_ranks(out_grad.T)
    _, shares = share_rows(w_gate, w_up, group_word, [0, 1], piece, [], [])
    slopes, in_down_part = prepare(gate_act, up_act, proj_h.T, [shares[0]])
    early_part = jnp.concatenate([project(proj_x, layer_input), in_down_part], axis=0)
    out_down_part = project(proj_g, out_grad)
    fetched, ticks = {}, []

    def fetch(k):
        for s in range(1, chips):
            fetched[k, s, 0] = from_chip(shares[k], s)
            for r in range(1, groups):
                fetched[k, s, r] = from_group(fetched[k, s, 0], r)

    def forward(k, after, held=()):
        waits = [fetched[n] for n in fetched if n[0] == k and n[2] == 0]
        waits += [fetched[n] for n in fetched if n[0] == k - 1 and n[2] > 0]
        waits = [w for w in waits if not any(w is h for h in held)]
        places = [k + 2] if k + 2 < CHUNKS else []
        carried, fresh = share_rows(
            w_gate, w_up, group_word, places, piece, list(held), waits + list(after)
        )
        ticks.append(fresh[0])
        if places:
            shares.extend(fresh)
            fetch(k + 2)
        return carried

    def owner_of(s, first_of):
        table = np.zeros((groups, blocks), np.int64)
        for g in range(groups):
            for p in range(blocks):
                block = (p // CORES + s) % chips * CORES + p % CORES
                table[g, p] = (block * rows + first_of(g)) // features
        return table

    far_routes = []
    for s in range(1, chips):
        for r in range(groups):
            table = owner_of(s, lambda g: (g + r) % groups * part)
            for route in far_routes:
                if route[0] == s and (route[1] == table).all():
                    route[2].append(r)
                    break
            else:
                far_routes.append((s, table, [r]))
    height = rows // split
    near_tables = [owner_of(0, lambda g: j * height) for j in range(split)]
    near_routes = [
        [(w_gate[j * height : (j + 1) * height], w_up[j * height : (j + 1) * height])]
        for j in range(split)
    ]

    def terms(names, grads, after, price, near=False):
        routes = list(zip(near_tables, near_routes, [None] * split)) if near else []
        for s, table, shifts in far_routes:
            units = [(k, s, q) for k, q in names if q in shifts]
            if units:
                routes.append((table, [(fetched[n],) for n in units], units))
        bundles = {}
        for route in routes:
            bundles.setdefault((route[0] % 2).tobytes(), []).append(route)
        bundles = list(bundles.values())
        outs = list(weigh([[u for _, units, _ in b for u in units] for b in bundles], grads, after, price))
        got = [toward(out, b[0][0], 1) for out, b in zip(outs, bundles)]
        return outs, got, bundles

    def carry_on(work, after):
        outs, got, bundles = work
        heights = [[sum(u[0].shape[-2] for u in units) for _, units, _ in b] for b in bundles]
        sums = list(add(outs, got, heights, after))
        ends, at = [], 0
        for b in bundles:
            for table, _, names in b:
                ends.append((names, *later_steps(sums[at], table)))
                at += 1
        return sums, ends

    fetch(0)
    fetch(1)
    forward(0, [slopes])
    forward(1, [early_part, out_down_part])
    forward(2, [])
    so_far = hidden_part(
        rank_word, below[:2], above[:1], w_down, 1, None, None, None, [ticks[2]]
    )
    forward(3, [so_far])
    mine, up_out_part = hidden_part(
        rank_word, below[2:], above[1:], w_down, 2, so_far, slopes, proj_u.T, [ticks[3]]
    )
    bits = [1 << i for i in range(ranks.bit_length() - 1)]
    early = early_part + exchange(early_part, bits[0])
    (mine,) = forward(4, [early], [mine])
    theirs = swap_cores(mine)
    for bit in bits[1:]:
        early = early + exchange(early, bit)
    first_names = [(k, 0) for k in range(5)] + [(k, 1) for k in range(4)]
    first_mine = terms(first_names, [mine], [ticks[4]], 30, near=True)
    (up_out_part,) = forward(5, first_mine[0] + [early], [up_out_part])
    first_theirs = terms(first_names, [theirs], [ticks[5]], 30, near=True)
    sums_mine, end_mine = carry_on(first_mine, first_theirs[0])
    out_parts = jnp.stack([up_out_part, out_down_part]).reshape(2, ranks, -1, count)
    out_parts = halve(out_parts.transpose(1, 0, 2, 3), bits[-1])
    forward(6, sums_mine + [out_parts])
    second_names = [(5, 0), (6, 0), (4, 1), (5, 1)]
    second = terms(second_names, [mine, theirs], [ticks[6]], 18)
    sums_theirs, end_theirs = carry_on(first_theirs, second[0])
    for bit in bits[-2::-1]:
        out_parts = halve(out_parts, bit)
    last_arrived = [(CHUNKS - 1, s, 0) for s in range(1, chips)]
    held = forward(7, sums_theirs + [out_parts], [fetched[n] for n in last_arrived])
    for n, value in zip(last_arrived, held):
        fetched[n] = value
        for r in range(1, groups):
            fetched[n[0], n[1], r] = from_group(value, r)
    third_names = [(7, 0), (6, 1)]
    received = [got for _, _, got in end_mine if got is not None]
    third = terms(third_names, [mine, theirs], [ticks[7]] + received, 0)
    sums_second, end_second = carry_on(second, third[0])

    early = early.astype(jnp.bfloat16)
    width = in_down_part.shape[0]
    in_up, in_down = early[:width], early[width:]
    out_parts = out_parts.astype(jnp.bfloat16)
    up_out, out_down = out_parts[0, 0], out_parts[0, 1]
    member = pack_table(doc_lengths, count)
    doc_logs = jnp.stack(
        [doc_outer(member, up_out, in_up), doc_outer(member, out_down, in_down)], axis=1
    )

    def settle(v, got):
        if got is None:
            return v
        return (v.astype(jnp.float32) + got.astype(jnp.float32)).astype(jnp.bfloat16)

    def pick(index, options):
        value = options[0]
        for at, option in enumerate(options[1:], 1):
            value = jnp.where(index == at, option, value)
        return value

    first = rank * features
    away = (first // rows // CORES - chip) % chips
    owner = first // rows % CORES == core
    inside = first % rows
    tall = features // part
    shifts = [(inside // part + j - group) % groups for j in range(tall)]

    def in_order(near, far):
        options = [pick(inside // height, near)]
        for s in range(1, chips):
            by_shift = [
                jnp.concatenate([far[k, s, r] for k in range(CHUNKS)], axis=0)
                for r in range(groups)
            ]
            options.append(jnp.concatenate([pick(shift, by_shift) for shift in shifts], axis=0))
        return pick(away, options)

    near_half, far_half = [[], []], [{}, {}]
    for at, end in enumerate((end_mine, end_theirs)):
        for names, *pair in end:
            value = settle(*pair)
            if names is None:
                near_half[at].append(value)
            else:
                far_half[at].update(
                    (n, value[i * piece : (i + 1) * piece]) for i, n in enumerate(names)
                )

    sums_third, end_third = carry_on(third, [doc_logs])
    last_names = [(CHUNKS - 1, r) for r in range(1, groups)]
    received = [got for _, _, got in end_theirs if got is not None]
    last = terms(last_names, [mine, theirs], sums_third + received, 10)
    for names, *pair in end_second + end_third:
        value = settle(*pair)
        for i, n in enumerate(names):
            both = value[i * piece : (i + 1) * piece]
            far_half[0][n], far_half[1][n] = both[:, :count], both[:, count:]
    for s in range(1, chips):
        for _, r in last_names:
            for half in far_half:
                half[CHUNKS - 1, s, r] = jnp.zeros((piece, count), jnp.bfloat16)
    total_mine, total_theirs = (in_order(n, f) for n, f in zip(near_half, far_half))
    from_partner = swap_cores(total_theirs)
    _, end_last = carry_on(last, [])
    total = jnp.where(owner, total_mine, from_partner)

    tail = {}
    for names, *pair in end_last:
        value = settle(*pair)
        tail.update((n, value[i * piece : (i + 1) * piece]) for i, n in enumerate(names))
    pieces = jnp.concatenate(
        [
            pick(away - 1, [tail[k, s, r] for s in range(1, chips)])
            for k, r in last_names
        ],
        axis=0,
    )
    pieces = jnp.where(owner, pieces[:, :count], swap_cores(pieces[:, count:]))
    pieces = jnp.where(away > 0, pieces, jnp.zeros_like(pieces))
    parts = []
    for j, shift in enumerate(shifts):
        end = (j + 1) * part
        extra = jnp.zeros((piece, count), jnp.bfloat16)
        for at, (_, r) in enumerate(last_names):
            extra = jnp.where(shift == r, pieces[at * piece : (at + 1) * piece], extra)
        parts += [total[j * part : end - piece], total[end - piece : end] + extra]
    input_grad = jnp.concatenate(parts, axis=0).T
    return (input_grad, doc_logs)


def solution(mesh):
    placed = (
        P(("groups", "dp"), "tensor"),
        P(("groups", "dp"), "tensor"),
        P(("groups", "dp"), "tensor"),
        P(("groups", "dp"), "tensor"),
        P("dp", "tensor"),
        P("dp", "tensor"),
        P("tensor", None),
        P("tensor", None),
        P("tensor", None),
        P("tensor", None),
        P("tensor", None),
        P(("groups", "dp"), None),
    )
    return jax.shard_map(
        per_device,
        mesh=mesh,
        in_specs=placed,
        out_specs=(P(("groups", "dp"), "tensor"), P(("groups", "dp"), None, "tensor")),
        check_vma=False,
    )
```

```python
import functools

import jax
import jax.numpy as jnp
import numpy as np
from jax import lax
from jax.experimental import pallas as pl
from jax.experimental.pallas import tpu as pltpu
from jax.sharding import PartitionSpec as P

CORES = 2
CHUNKS = 8
VMEM_BYTES = 60 * 1024 * 1024
FLOPS_PER_US = 270_000_000
ANYWHERE = pl.BlockSpec(memory_space=pl.ANY)


def contract_right(left, right):
    return lax.dot_general(
        left, right, (((1,), (1,)), ((), ())), preferred_element_type=jnp.float32
    )


def project(proj, rows):
    return lax.dot_general(
        proj, rows, (((0,), (1,)), ((), ())), preferred_element_type=jnp.float32
    )


def pack_table(doc_lengths, count):
    lengths = doc_lengths[0]
    ends = jnp.cumsum(lengths)
    starts = ends - lengths
    position = jnp.arange(count, dtype=jnp.int32)[None, :]
    inside = (position >= starts[:, None]) & (position < ends[:, None])
    return inside.astype(jnp.bfloat16)


def doc_outer(member, grad_rows, inputs):
    count = member.shape[1]
    weighted = (member[:, None, :] * grad_rows[None, :, :]).reshape(-1, count)
    table = contract_right(weighted, inputs)
    return table.reshape(member.shape[0], grad_rows.shape[0] * inputs.shape[0])


def swap_cores(value):
    size = lax.axis_size("dp")
    return lax.ppermute(value, "dp", [(i, i ^ 1) for i in range(size)])


def from_chip(value, shift):
    size = lax.axis_size("dp")
    step = shift * CORES
    return lax.ppermute(value, "dp", [((i + step) % size, i) for i in range(size)])


def from_group(value, shift):
    size = lax.axis_size("groups")
    return lax.ppermute(value, "groups", [((i + shift) % size, i) for i in range(size)])


def cost(us):
    return pl.CostEstimate(flops=int(us * FLOPS_PER_US) + 1, bytes_accessed=1, transcendentals=0)


def widest(size, options):
    return next((w for w in options if size % w == 0), size)


def share_rows(w_gate, w_up, group, places, piece, carried, after):
    rows, width = w_gate.shape
    tile = widest(width, (1792, 896, 128))
    kept, waits, fresh = len(carried), len(after), len(places)
    per_group = rows // lax.axis_size("groups") // piece

    def kernel(group_ref, *refs):
        outs = refs[len(refs) - fresh :] if fresh else []
        for at, out in enumerate(outs):
            out[0] = refs[2 * at][...]
            out[1] = refs[2 * at + 1][...]
        if not fresh:
            refs[-1][...] = jnp.zeros_like(refs[-1])

    specs = []
    for k in places:
        at_chunk = functools.partial(lambda k, i, g: (g[0] * per_group + k, i), k)
        specs += [pl.BlockSpec((piece, tile), at_chunk)] * 2
    results = pl.pallas_call(
        kernel,
        grid_spec=pltpu.PrefetchScalarGridSpec(
            num_scalar_prefetch=1,
            grid=(width // tile if places else 1,),
            in_specs=specs + [ANYWHERE] * (kept + waits),
            out_specs=[ANYWHERE] * kept
            + [pl.BlockSpec((2, piece, tile), lambda i, g: (0, 0, i))] * fresh
            + [pl.BlockSpec((8, 128), lambda i, g: (0, 0))] * (not fresh),
        ),
        out_shape=[jax.ShapeDtypeStruct(a.shape, a.dtype) for a in carried]
        + [jax.ShapeDtypeStruct((2, piece, width), w_gate.dtype) for _ in places]
        + [jax.ShapeDtypeStruct((8, 128), jnp.float32)] * (not fresh),
        input_output_aliases={1 + 2 * fresh + i: i for i in range(kept)},
        compiler_params=pltpu.CompilerParams(vmem_limit_bytes=VMEM_BYTES),
        cost_estimate=cost(2),
        name="share_rows",
    )(group, *[w_gate, w_up] * fresh, *carried, *after)
    return list(results[:kept]), list(results[kept:])


def spread_ranks(value):
    ranks = lax.axis_size("tensor")
    below, above = [value], [value]
    for _ in range(1, ranks):
        below.append(lax.ppermute(below[-1], "tensor", [(i, i + 1) for i in range(ranks - 1)]))
        above.append(lax.ppermute(above[-1], "tensor", [(i + 1, i) for i in range(ranks - 1)]))
    return below, above[1:]


def prepare(gate_act, up_act, proj_h, after):
    count, hidden = gate_act.shape
    narrow = proj_h.shape[0]
    tile = widest(hidden, (512, 256, 128))

    def kernel(gate_ref, up_ref, proj_ref, *refs):
        slope_ref, down_ref = refs[-2:]

        @pl.when(pl.program_id(0) == 0)
        def _():
            down_ref[...] = jnp.zeros_like(down_ref)

        gate = gate_ref[...].astype(jnp.float32).T
        up = up_ref[...].astype(jnp.float32).T
        sigma = jax.nn.sigmoid(gate)
        swish = gate * sigma
        slope_ref[0] = up * sigma * (1.0 + gate * (1.0 - sigma))
        slope_ref[1] = swish
        down_ref[...] += jnp.dot(
            proj_ref[...], (swish * up).astype(jnp.bfloat16), preferred_element_type=jnp.float32
        )

    return pl.pallas_call(
        kernel,
        grid=(hidden // tile,),
        out_shape=[
            jax.ShapeDtypeStruct((2, hidden, count), jnp.float32),
            jax.ShapeDtypeStruct((narrow, count), jnp.float32),
        ],
        in_specs=[
            pl.BlockSpec((count, tile), lambda i: (0, i)),
            pl.BlockSpec((count, tile), lambda i: (0, i)),
            pl.BlockSpec((narrow, tile), lambda i: (0, i)),
        ]
        + [ANYWHERE] * len(after),
        out_specs=[
            pl.BlockSpec((2, tile, count), lambda i: (0, i, 0)),
            pl.BlockSpec((narrow, count), lambda i: (0, 0)),
        ],
        compiler_params=pltpu.CompilerParams(vmem_limit_bytes=VMEM_BYTES),
        cost_estimate=cost(12),
        name="prepare",
    )(gate_act, up_act, proj_h, *after)


def hidden_part(rank, below, above, w_down, first, so_far, slopes, after):
    ranks = lax.axis_size("tensor")
    features, count = (below or above)[0].shape
    hidden = w_down.shape[0]
    own = len(below) - len(above)
    span = len(above)
    slots = own + min(2 * span, ranks - first)
    finish = slopes is not None
    tile = widest(hidden, (896, 512, 128) if finish else (1792, 896, 128))
    sources = [*below, *above]

    def slot_of(z, at):
        if at < own:
            return z, True
        under = jnp.clip(z - first + 1, 0, span)
        over = jnp.clip(ranks - z - first, 0, span)
        at -= own
        block = jnp.where(at < under, z - first - at, z + first + at - under)
        return block, at < under + over

    def column(at, i, rank_ref):
        block, valid = slot_of(rank_ref[0], at)
        if valid is True:
            return (i, block)
        return (jnp.where(valid, i, 0), jnp.where(valid, block, 0))

    def kernel(rank_ref, *refs):
        z = rank_ref[0]
        downs, arrived = refs[:slots], refs[slots : slots + len(sources)]
        grad_ref, total, sem = refs[-3:]
        out = refs[-4]

        def gather(wait):
            under = jnp.clip(z - first + 1, 0, span)
            over = jnp.clip(ranks - z - first, 0, span)
            pieces = [(arrived[at], z >= 0, at) for at in range(own)]
            for t in range(span):
                pieces.append((arrived[own + t], t < under, own + t))
                pieces.append((arrived[len(below) + t], t < over, own + under + t))
            for at, (source, valid, place) in enumerate(pieces):

                @pl.when(valid)
                def _():
                    rows = pl.ds(pl.multiple_of(place * features, features), features)
                    copy = pltpu.make_async_copy(source, grad_ref.at[rows, :], sem.at[at])
                    copy.wait() if wait else copy.start()

        @pl.when(pl.program_id(0) == 0)
        def _():
            gather(False)
            gather(True)

        rest = refs[slots + len(sources) :]
        if so_far is not None:
            total[...] = rest[0][...]
        for at in range(slots):

            def add_slot(at=at):
                term = jnp.dot(
                    downs[at][...],
                    grad_ref[at * features : (at + 1) * features, :],
                    preferred_element_type=jnp.float32,
                )
                if at == 0 and so_far is None:
                    total[...] = term
                else:
                    total[...] += term

            _, valid = slot_of(z, at)
            if valid is True:
                add_slot()
            else:
                pl.when(valid)(add_slot)
        if finish:
            out[0] = (total[...] * rest[1][0]).astype(jnp.bfloat16)
            out[1] = (total[...] * rest[1][1]).astype(jnp.bfloat16)
        else:
            out[...] = total[...]

    operands = [w_down] * slots + sources
    specs = [pl.BlockSpec((tile, features), functools.partial(column, at)) for at in range(slots)]
    specs += [ANYWHERE] * len(sources)
    if so_far is not None:
        operands.append(so_far)
        specs.append(pl.BlockSpec((tile, count), lambda i, r: (i, 0)))
    if finish:
        operands.append(slopes)
        specs.append(pl.BlockSpec((2, tile, count), lambda i, r: (0, i, 0)))
        out_shape = jax.ShapeDtypeStruct((2, hidden, count), jnp.bfloat16)
        out_specs = pl.BlockSpec((2, tile, count), lambda i, r: (0, i, 0))
    else:
        out_shape = jax.ShapeDtypeStruct((hidden, count), jnp.float32)
        out_specs = pl.BlockSpec((tile, count), lambda i, r: (i, 0))
    return pl.pallas_call(
        kernel,
        grid_spec=pltpu.PrefetchScalarGridSpec(
            num_scalar_prefetch=1,
            grid=(hidden // tile,),
            in_specs=specs + [ANYWHERE] * len(after),
            out_specs=out_specs,
            scratch_shapes=[
                pltpu.VMEM((slots * features, count), jnp.bfloat16),
                pltpu.VMEM((tile, count), jnp.float32),
                pltpu.SemaphoreType.DMA((len(sources),)),
            ],
        ),
        out_shape=out_shape,
        compiler_params=pltpu.CompilerParams(vmem_limit_bytes=VMEM_BYTES),
        cost_estimate=cost(12),
        name="hidden_part",
    )(rank, *operands, *after)


def weigh(routes, grads, after, price, extra=None):
    hidden = grads[0].shape[1]
    tile = widest(hidden, (512, 256, 128))
    steps = hidden // tile
    heights = [sum(u[0].shape[-2] for u in units) for units in routes]
    rows, count = sum(heights), sum(g.shape[2] for g in grads)
    units = [u for route in routes for u in route]
    flat = [w for u in units for w in u]
    extras = [] if extra is None else [extra]

    def kernel(*refs):
        weights, both = list(refs[: len(flat)]), refs[len(flat) : len(flat) + len(grads)]
        more = refs[len(flat) + len(grads) : len(flat) + len(grads) + len(extras)]
        outs, total = refs[-1 - len(routes) - len(extras) : -1], refs[-1]
        at = pl.program_id(0)

        @pl.when(at == 0)
        def _():
            total[...] = jnp.zeros_like(total)

        gates, ups = [], []
        for u in units:
            mine, weights = weights[: len(u)], weights[len(u) :]
            gates.append(mine[0][...] if len(u) == 2 else mine[0][0])
            ups.append(mine[1][...] if len(u) == 2 else mine[0][1])
        gate, up = jnp.concatenate(gates, axis=0), jnp.concatenate(ups + [m[...] for m in more], axis=0)
        first = 0
        for ref in both:
            span = slice(first, first + ref.shape[2])
            by_up = jnp.dot(up, ref[1], preferred_element_type=jnp.float32)
            total[:rows, span] += (
                jnp.dot(gate, ref[0], preferred_element_type=jnp.float32) + by_up[:rows]
            )
            if more:
                total[rows:, span] += by_up[rows:]
            first += ref.shape[2]

        @pl.when(at == steps - 1)
        def _():
            top = 0
            for out, height in zip(outs, heights):
                out[...] = total[top : top + height].astype(jnp.bfloat16)
                top += height
            if more:
                outs[-1][...] = total[rows:]

    specs = []
    for w in flat:
        if w.ndim == 2:
            specs.append(pl.BlockSpec((w.shape[0], tile), lambda i: (0, i)))
        else:
            specs.append(pl.BlockSpec((2, w.shape[1], tile), lambda i: (0, 0, i)))
    for g in grads:
        specs.append(pl.BlockSpec((2, tile, g.shape[2]), lambda i: (0, i, 0)))
    shapes = [jax.ShapeDtypeStruct((h, count), jnp.bfloat16) for h in heights]
    for e in extras:
        specs.append(pl.BlockSpec((e.shape[0], tile), lambda i: (0, i)))
        shapes.append(jax.ShapeDtypeStruct((e.shape[0], count), jnp.float32))
    return pl.pallas_call(
        kernel,
        grid=(steps,),
        out_shape=shapes,
        in_specs=specs + [ANYWHERE] * len(after),
        out_specs=[pl.BlockSpec(s.shape, lambda i: (0, 0)) for s in shapes],
        scratch_shapes=[pltpu.VMEM((rows + sum(e.shape[0] for e in extras), count), jnp.float32)],
        compiler_params=pltpu.CompilerParams(vmem_limit_bytes=VMEM_BYTES),
        cost_estimate=cost(price),
        name="weigh_rows",
    )(*flat, *grads, *extras, *after)


def add(values, others, heights, after):
    pairs = len(values)
    flat = [h for hs in heights for h in hs]

    def kernel(*refs):
        outs = list(refs[len(refs) - len(flat) :])
        for at in range(pairs):
            top = 0
            for height in heights[at]:
                rows = slice(top, top + height)
                outs.pop(0)[...] = (
                    refs[at][rows].astype(jnp.float32) + refs[pairs + at][rows].astype(jnp.float32)
                ).astype(jnp.bfloat16)
                top += height

    count = values[0].shape[1]
    whole = pl.BlockSpec(memory_space=pltpu.VMEM)
    return pl.pallas_call(
        kernel,
        out_shape=[jax.ShapeDtypeStruct((h, count), jnp.bfloat16) for h in flat],
        in_specs=[whole] * (2 * pairs) + [ANYWHERE] * len(after),
        out_specs=[whole] * len(flat),
        compiler_params=pltpu.CompilerParams(vmem_limit_bytes=VMEM_BYTES),
        cost_estimate=cost(2),
        name="add_terms",
    )(*values, *others, *after)


def exchange(value, bit):
    ranks = lax.axis_size("tensor")
    return lax.ppermute(value, "tensor", [(i, i ^ bit) for i in range(ranks)])


def halve(value, bit):
    half = value.shape[0] // 2
    high = lax.axis_index("tensor") & bit != 0
    low_rows, high_rows = value[:half], value[half:]
    got = exchange(jnp.where(high, low_rows, high_rows), bit)
    return jnp.where(high, high_rows, low_rows) + got


def hops(owner, bit):
    groups, ranks, blocks = (lax.axis_size(a) for a in ("groups", "tensor", "dp"))
    pairs = []
    for g in range(groups):
        for p in range(blocks):
            target = owner[g, p]
            for z in range(ranks):
                if z % bit == target % bit and (z ^ target) & bit:
                    pairs.append(((g * ranks + z) * blocks + p, (g * ranks + (z ^ bit)) * blocks + p))
    return pairs


def send(value, pairs):
    return lax.ppermute(value, ("groups", "tensor", "dp"), pairs)


def later_steps(values, owners):
    ranks = lax.axis_size("tensor")
    ends = []
    for value, owner in zip(values, owners):
        bit, got = 2, None
        while bit < ranks:
            if got is not None:
                (value,) = add([value], [got], [[value.shape[0]]], [])
            got = send(value, hops(owner, bit))
            bit *= 2
        ends.append((value, got))
    return ends


def per_device(
    layer_input,
    gate_act,
    up_act,
    out_grad,
    w_gate,
    w_up,
    w_down,
    proj_x,
    proj_u,
    proj_h,
    proj_g,
    doc_lengths,
):
    groups, ranks = lax.axis_size("groups"), lax.axis_size("tensor")
    blocks = lax.axis_size("dp")
    chips = blocks // CORES
    group, rank = lax.axis_index("groups"), lax.axis_index("tensor")
    place = lax.axis_index("dp")
    chip, core = place // CORES, place % CORES
    rows = w_gate.shape[0]
    count = layer_input.shape[0]
    features = out_grad.shape[1]
    part = rows // groups
    piece = part // CHUNKS
    split = max(1, ranks // blocks)
    group_word = jnp.full((1,), group, jnp.int32)
    rank_word = jnp.full((1,), rank, jnp.int32)

    below, above = spread_ranks(out_grad.T)
    _, shares = share_rows(w_gate, w_up, group_word, [0, 1], piece, [], [])
    slopes, in_down_part = prepare(gate_act, up_act, proj_h.T, [shares[0]])
    early_part = jnp.concatenate([project(proj_x, layer_input), in_down_part], axis=0)
    out_down_part = project(proj_g, out_grad)
    fetched, ticks = {}, []

    def fetch(k):
        for s in range(1, chips):
            fetched[k, s, 0] = from_chip(shares[k], s)
            for r in range(1, groups):
                fetched[k, s, r] = from_group(fetched[k, s, 0], r)

    def forward(k, after, held=()):
        waits = [fetched[n] for n in fetched if n[0] == k and n[2] == 0]
        waits += [fetched[n] for n in fetched if n[0] == k - 1 and n[2] > 0]
        waits = [w for w in waits if not any(w is h for h in held)]
        places = [k + 2] if k + 2 < CHUNKS else []
        carried, fresh = share_rows(
            w_gate, w_up, group_word, places, piece, list(held), waits + list(after)
        )
        ticks.append(fresh[0])
        if places:
            shares.extend(fresh)
            fetch(k + 2)
        return carried

    def owner_of(s, first_of):
        table = np.zeros((groups, blocks), np.int64)
        for g in range(groups):
            for p in range(blocks):
                block = (p // CORES + s) % chips * CORES + p % CORES
                table[g, p] = (block * rows + first_of(g)) // features
        return table

    far_routes = []
    for s in range(1, chips):
        for r in range(groups):
            table = owner_of(s, lambda g: (g + r) % groups * part)
            for route in far_routes:
                if route[0] == s and (route[1] == table).all():
                    route[2].append(r)
                    break
            else:
                far_routes.append((s, table, [r]))
    height = rows // split
    near_tables = [owner_of(0, lambda g: j * height) for j in range(split)]
    near_routes = [
        [(w_gate[j * height : (j + 1) * height], w_up[j * height : (j + 1) * height])]
        for j in range(split)
    ]

    def terms(names, grads, after, price, near=False, extra=None):
        routes = list(zip(near_tables, near_routes, [None] * split)) if near else []
        for s, table, shifts in far_routes:
            units = [(k, s, q) for k, q in names if q in shifts]
            if units:
                routes.append((table, [(fetched[n],) for n in units], units))
        bundles = {}
        for route in routes:
            bundles.setdefault((route[0] % 2).tobytes(), []).append(route)
        bundles = list(bundles.values())
        joined = [[u for _, units, _ in b for u in units] for b in bundles]
        outs = list(weigh(joined, grads, after, price, extra))
        got = [send(out, hops(b[0][0], 1)) for out, b in zip(outs, bundles)]
        return outs, got, bundles

    def carry_on(work, after):
        outs, got, bundles = work
        heights = [[sum(u[0].shape[-2] for u in units) for _, units, _ in b] for b in bundles]
        sums = list(add(outs, got, heights, after))
        routes = [route for b in bundles for route in b]
        ends = later_steps(sums, [table for table, _, _ in routes])
        return sums, [(names, *end) for (_, _, names), end in zip(routes, ends)]

    fetch(0)
    fetch(1)

    def hold_arrived(k, after, held=()):
        names = [(k, s, 0) for s in range(1, chips)]
        values = forward(k, after, [fetched[n] for n in names] + list(held))
        for n, value in zip(names, values):
            fetched[n] = value
            for r in range(1, groups):
                fetched[k, n[1], r] = from_group(value, r)
        return values[len(names) :]

    bits = [1 << i for i in range(ranks.bit_length() - 1)]
    hold_arrived(0, [slopes])
    so_far = hidden_part(rank_word, below[:2], above[:1], w_down, 1, None, None, [ticks[0]])
    hold_arrived(1, [so_far])
    hold_arrived(2, [below[2], above[1], early_part, out_down_part])
    (early,) = hold_arrived(3, below[3:] + above[2:], [early_part])
    mine = hidden_part(rank_word, below[2:], above[1:], w_down, 2, so_far, slopes, [ticks[3]])
    early = early + exchange(early, bits[0])
    mine, early = hold_arrived(4, [], [mine, early])
    theirs = swap_cores(mine)
    for bit in bits[1:]:
        early = early + exchange(early, bit)
    first_names = [(k, 0) for k in range(5)] + [(k, 1) for k in range(4)]
    first_mine = terms(first_names, [mine], [ticks[4]], 16, near=True, extra=proj_u.T)
    up_out_part = first_mine[0].pop()
    (up_out_part,) = hold_arrived(5, first_mine[0] + [early], [up_out_part])
    first_theirs = terms(first_names, [theirs], [ticks[5]], 16, near=True)
    sums_mine, end_mine = carry_on(first_mine, first_theirs[0])
    out_parts = jnp.stack([up_out_part, out_down_part]).reshape(2, ranks, -1, count)
    out_parts = halve(out_parts.transpose(1, 0, 2, 3), bits[-1])
    (out_parts,) = hold_arrived(6, first_theirs[0], [out_parts])
    second_names = [(5, 0), (6, 0), (4, 1), (5, 1)]
    second = terms(second_names, [mine, theirs], [ticks[6]] + sums_mine, 10)
    sums_theirs, end_theirs = carry_on(first_theirs, second[0])
    for bit in bits[-2::-1]:
        out_parts = halve(out_parts, bit)
    hold_arrived(7, second[0] + [out_parts])
    third_names = [(7, 0), (6, 1)]
    received = [got for _, _, got in end_mine if got is not None]
    third = terms(third_names, [mine, theirs], [ticks[7]] + sums_theirs + received, 4)
    sums_second, end_second = carry_on(second, third[0])

    early = early.astype(jnp.bfloat16)
    width = in_down_part.shape[0]
    in_up, in_down = early[:width], early[width:]
    out_parts = out_parts.astype(jnp.bfloat16)
    up_out, out_down = out_parts[0, 0], out_parts[0, 1]
    member = pack_table(doc_lengths, count)
    doc_logs = jnp.stack(
        [doc_outer(member, up_out, in_up), doc_outer(member, out_down, in_down)], axis=1
    )

    def settle(v, got):
        if got is None:
            return v
        return (v.astype(jnp.float32) + got.astype(jnp.float32)).astype(jnp.bfloat16)

    def pick(index, options):
        value = options[0]
        for at, option in enumerate(options[1:], 1):
            value = jnp.where(index == at, option, value)
        return value

    first = rank * features
    away = (first // rows // CORES - chip) % chips
    owner = first // rows % CORES == core
    inside = first % rows
    tall = features // part
    shifts = [(inside // part + j - group) % groups for j in range(tall)]

    def in_order(near, far):
        options = [pick(inside // height, near)]
        for s in range(1, chips):
            by_shift = [
                jnp.concatenate([far[k, s, r] for k in range(CHUNKS)], axis=0)
                for r in range(groups)
            ]
            options.append(jnp.concatenate([pick(shift, by_shift) for shift in shifts], axis=0))
        return pick(away, options)

    def settle_at_once(end, after):
        if end[0][2] is None:
            return [v for _, v, _ in end]
        mine = [v for _, v, _ in end]
        return add(mine, [got for _, _, got in end], [[v.shape[0]] for v in mine], after)

    sums_third, end_third = carry_on(third, [doc_logs])
    last_names = [(CHUNKS - 1, r) for r in range(1, groups)]
    settled_mine = settle_at_once(end_mine, third[0])
    received = [got for _, _, got in end_theirs if got is not None]
    last = terms(last_names, [mine, theirs], list(settled_mine) + sums_third + received, 20)
    sums_last, end_last = carry_on(last, [])
    settled_theirs = settle_at_once(end_theirs, sums_last)
    later = end_second + end_third
    settled_later = settle_at_once(later, sums_last)

    near_half, far_half = [[], []], [{}, {}]
    for at, (end, settled) in enumerate(
        ((end_mine, settled_mine), (end_theirs, settled_theirs))
    ):
        for (names, _, _), value in zip(end, settled):
            if names is None:
                near_half[at].append(value)
            else:
                far_half[at].update(
                    (n, value[i * piece : (i + 1) * piece]) for i, n in enumerate(names)
                )

    for (names, _, _), value in zip(later, settled_later):
        for i, n in enumerate(names):
            both = value[i * piece : (i + 1) * piece]
            far_half[0][n], far_half[1][n] = both[:, :count], both[:, count:]
    for s in range(1, chips):
        for _, r in last_names:
            for half in far_half:
                half[CHUNKS - 1, s, r] = jnp.zeros((piece, count), jnp.bfloat16)
    total_mine, total_theirs = (in_order(n, f) for n, f in zip(near_half, far_half))
    from_partner = swap_cores(total_theirs)
    total = jnp.where(owner, total_mine, from_partner)

    tail = {}
    for names, *pair in end_last:
        value = settle(*pair)
        tail.update((n, value[i * piece : (i + 1) * piece]) for i, n in enumerate(names))
    pieces = jnp.concatenate(
        [
            pick(away - 1, [tail[k, s, r] for s in range(1, chips)])
            for k, r in last_names
        ],
        axis=0,
    )
    pieces = jnp.where(owner, pieces[:, :count], swap_cores(pieces[:, count:]))
    pieces = jnp.where(away > 0, pieces, jnp.zeros_like(pieces))
    parts = []
    for j, shift in enumerate(shifts):
        end = (j + 1) * part
        extra = jnp.zeros((piece, count), jnp.bfloat16)
        for at, (_, r) in enumerate(last_names):
            extra = jnp.where(shift == r, pieces[at * piece : (at + 1) * piece], extra)
        parts += [total[j * part : end - piece], total[end - piece : end] + extra]
    input_grad = jnp.concatenate(parts, axis=0).T
    return (input_grad, doc_logs)


def solution(mesh):
    placed = (
        P(("groups", "dp"), "tensor"),
        P(("groups", "dp"), "tensor"),
        P(("groups", "dp"), "tensor"),
        P(("groups", "dp"), "tensor"),
        P("dp", "tensor"),
        P("dp", "tensor"),
        P("tensor", None),
        P("tensor", None),
        P("tensor", None),
        P("tensor", None),
        P("tensor", None),
        P(("groups", "dp"), None),
    )
    return jax.shard_map(
        per_device,
        mesh=mesh,
        in_specs=placed,
        out_specs=(P(("groups", "dp"), "tensor"), P(("groups", "dp"), None, "tensor")),
        check_vma=False,
    )
```

```python
import functools

import jax
import jax.numpy as jnp
import numpy as np
from jax import lax
from jax.experimental import pallas as pl
from jax.experimental.pallas import tpu as pltpu
from jax.sharding import PartitionSpec as P

CORES = 2
CHUNKS = 8
VMEM_BYTES = 60 * 1024 * 1024
FLOPS_PER_US = 270_000_000
ANYWHERE = pl.BlockSpec(memory_space=pl.ANY)


def contract_right(left, right):
    return lax.dot_general(
        left, right, (((1,), (1,)), ((), ())), preferred_element_type=jnp.float32
    )


def project(proj, rows):
    return lax.dot_general(
        proj, rows, (((0,), (1,)), ((), ())), preferred_element_type=jnp.float32
    )


def pack_table(doc_lengths, count):
    lengths = doc_lengths[0]
    ends = jnp.cumsum(lengths)
    starts = ends - lengths
    position = jnp.arange(count, dtype=jnp.int32)[None, :]
    inside = (position >= starts[:, None]) & (position < ends[:, None])
    return inside.astype(jnp.bfloat16)


def doc_outer(member, grad_rows, inputs):
    count = member.shape[1]
    weighted = (member[:, None, :] * grad_rows[None, :, :]).reshape(-1, count)
    table = contract_right(weighted, inputs)
    return table.reshape(member.shape[0], grad_rows.shape[0] * inputs.shape[0])


def swap_cores(value):
    size = lax.axis_size("dp")
    return lax.ppermute(value, "dp", [(i, i ^ 1) for i in range(size)])


def from_chip(value, shift):
    size = lax.axis_size("dp")
    step = shift * CORES
    return lax.ppermute(value, "dp", [((i + step) % size, i) for i in range(size)])


def from_group(value, shift):
    size = lax.axis_size("groups")
    return lax.ppermute(value, "groups", [((i + shift) % size, i) for i in range(size)])


def cost(us):
    return pl.CostEstimate(flops=int(us * FLOPS_PER_US) + 1, bytes_accessed=1, transcendentals=0)


def widest(size, options):
    return next((w for w in options if size % w == 0), size)


def share_rows(w_gate, w_up, group, places, piece, carried, after):
    rows, width = w_gate.shape
    tile = widest(width, (1792, 896, 128))
    kept, waits, fresh = len(carried), len(after), len(places)
    per_group = rows // lax.axis_size("groups") // piece

    def kernel(group_ref, *refs):
        outs = refs[len(refs) - fresh :] if fresh else []
        for at, out in enumerate(outs):
            out[0] = refs[2 * at][...]
            out[1] = refs[2 * at + 1][...]
        if not fresh:
            refs[-1][...] = jnp.zeros_like(refs[-1])

    specs = []
    for k in places:
        at_chunk = functools.partial(lambda k, i, g: (g[0] * per_group + k, i), k)
        specs += [pl.BlockSpec((piece, tile), at_chunk)] * 2
    results = pl.pallas_call(
        kernel,
        grid_spec=pltpu.PrefetchScalarGridSpec(
            num_scalar_prefetch=1,
            grid=(width // tile if places else 1,),
            in_specs=specs + [ANYWHERE] * (kept + waits),
            out_specs=[ANYWHERE] * kept
            + [pl.BlockSpec((2, piece, tile), lambda i, g: (0, 0, i))] * fresh
            + [pl.BlockSpec((8, 128), lambda i, g: (0, 0))] * (not fresh),
        ),
        out_shape=[jax.ShapeDtypeStruct(a.shape, a.dtype) for a in carried]
        + [jax.ShapeDtypeStruct((2, piece, width), w_gate.dtype) for _ in places]
        + [jax.ShapeDtypeStruct((8, 128), jnp.float32)] * (not fresh),
        input_output_aliases={1 + 2 * fresh + i: i for i in range(kept)},
        compiler_params=pltpu.CompilerParams(vmem_limit_bytes=VMEM_BYTES),
        cost_estimate=cost(2),
        name="share_rows",
    )(group, *[w_gate, w_up] * fresh, *carried, *after)
    return list(results[:kept]), list(results[kept:])


def spread_ranks(value):
    ranks = lax.axis_size("tensor")
    below, above = [value], [value]
    for _ in range(1, ranks):
        below.append(lax.ppermute(below[-1], "tensor", [(i, i + 1) for i in range(ranks - 1)]))
        above.append(lax.ppermute(above[-1], "tensor", [(i + 1, i) for i in range(ranks - 1)]))
    return below, above[1:]


def prepare(gate_act, up_act, proj_h, after):
    count, hidden = gate_act.shape
    narrow = proj_h.shape[0]
    tile = widest(hidden, (512, 256, 128))

    def kernel(gate_ref, up_ref, proj_ref, *refs):
        slope_ref, down_ref = refs[-2:]

        @pl.when(pl.program_id(0) == 0)
        def _():
            down_ref[...] = jnp.zeros_like(down_ref)

        gate = gate_ref[...].astype(jnp.float32).T
        up = up_ref[...].astype(jnp.float32).T
        sigma = jax.nn.sigmoid(gate)
        swish = gate * sigma
        slope_ref[0] = up * sigma * (1.0 + gate * (1.0 - sigma))
        slope_ref[1] = swish
        down_ref[...] += jnp.dot(
            proj_ref[...], (swish * up).astype(jnp.bfloat16), preferred_element_type=jnp.float32
        )

    return pl.pallas_call(
        kernel,
        grid=(hidden // tile,),
        out_shape=[
            jax.ShapeDtypeStruct((2, hidden, count), jnp.float32),
            jax.ShapeDtypeStruct((narrow, count), jnp.float32),
        ],
        in_specs=[
            pl.BlockSpec((count, tile), lambda i: (0, i)),
            pl.BlockSpec((count, tile), lambda i: (0, i)),
            pl.BlockSpec((narrow, tile), lambda i: (0, i)),
        ]
        + [ANYWHERE] * len(after),
        out_specs=[
            pl.BlockSpec((2, tile, count), lambda i: (0, i, 0)),
            pl.BlockSpec((narrow, count), lambda i: (0, 0)),
        ],
        compiler_params=pltpu.CompilerParams(vmem_limit_bytes=VMEM_BYTES),
        cost_estimate=cost(12),
        name="prepare",
    )(gate_act, up_act, proj_h, *after)


def hidden_part(rank, below, above, w_down, so_far, slopes, proj_u, after):
    ranks = lax.axis_size("tensor")
    features, count = below[0].shape
    hidden = w_down.shape[0]
    finish = so_far is not None
    slots = ranks - 2 if finish else 2
    tile = widest(hidden, (896, 512, 128))
    sources = [(t, -1, below[t]) for t in range(2 if finish else 0, ranks if finish else 2)]
    sources += [(t, 1, above[t - 1]) for t in range(1, ranks if finish else 2)]

    def counts(z):
        both = ((z >= 1) & (z <= ranks - 2)).astype(jnp.int32)
        return both, jnp.maximum(z - 1, 0)

    def place_of(z, t, side):
        if not finish:
            return (0, z >= 0) if t == 0 else (1, z >= 1 if side < 0 else z == 0)
        both, under = counts(z)
        if side < 0:
            return both + t - 2, t <= z
        if t == 1:
            return 0, both == 1
        return both + under + t - 2, z + t <= ranks - 1

    def column(at, i, rank_ref):
        z = rank_ref[0]
        if not finish:
            return (i, z) if at == 0 else (i, jnp.where(z >= 1, z - 1, 1))
        both, under = counts(z)
        block = jnp.where(at < both + under, z - (at - both + 2), z + (at - both - under + 2))
        return (i, jnp.where(at < both, z + 1, block))

    def kernel(rank_ref, *refs):
        z = rank_ref[0]
        downs, arrived = refs[:slots], refs[slots : slots + len(sources)]
        grad_ref, total, sem = refs[-3:]
        rest = refs[slots + len(sources) :]

        def gather(wait):
            for at, (t, side, _) in enumerate(sources):
                place, valid = place_of(z, t, side)

                @pl.when(valid)
                def _():
                    rows = pl.ds(pl.multiple_of(place * features, features), features)
                    copy = pltpu.make_async_copy(arrived[at], grad_ref.at[rows, :], sem.at[at])
                    copy.wait() if wait else copy.start()

        @pl.when(pl.program_id(0) == 0)
        def _():
            gather(False)
            gather(True)

        if finish:
            total[...] = rest[0][...]
        for at in range(slots):
            term = jnp.dot(
                downs[at][...],
                grad_ref[at * features : (at + 1) * features, :],
                preferred_element_type=jnp.float32,
            )
            total[...] = total[...] + term if at or finish else term
        if finish:
            both_ref, out_ref = refs[-5:-3]
            both_ref[0] = (total[...] * rest[1][0]).astype(jnp.bfloat16)
            up_grad = (total[...] * rest[1][1]).astype(jnp.bfloat16)
            both_ref[1] = up_grad
            part = jnp.dot(rest[2][...], up_grad, preferred_element_type=jnp.float32)

            @pl.when(pl.program_id(0) == 0)
            def _():
                out_ref[...] = part

            @pl.when(pl.program_id(0) > 0)
            def _():
                out_ref[...] += part

        else:
            refs[-4][...] = total[...]

    operands = [w_down] * slots + [value for _, _, value in sources]
    specs = [pl.BlockSpec((tile, features), functools.partial(column, at)) for at in range(slots)]
    specs += [ANYWHERE] * len(sources)
    if finish:
        narrow = proj_u.shape[0]
        operands += [so_far, slopes, proj_u]
        specs += [
            pl.BlockSpec((tile, count), lambda i, r: (i, 0)),
            pl.BlockSpec((2, tile, count), lambda i, r: (0, i, 0)),
            pl.BlockSpec((narrow, tile), lambda i, r: (0, i)),
        ]
        out_shape = [
            jax.ShapeDtypeStruct((2, hidden, count), jnp.bfloat16),
            jax.ShapeDtypeStruct((narrow, count), jnp.float32),
        ]
        out_specs = [
            pl.BlockSpec((2, tile, count), lambda i, r: (0, i, 0)),
            pl.BlockSpec((narrow, count), lambda i, r: (0, 0)),
        ]
    else:
        out_shape = jax.ShapeDtypeStruct((hidden, count), jnp.float32)
        out_specs = pl.BlockSpec((tile, count), lambda i, r: (i, 0))
    return pl.pallas_call(
        kernel,
        grid_spec=pltpu.PrefetchScalarGridSpec(
            num_scalar_prefetch=1,
            grid=(hidden // tile,),
            in_specs=specs + [ANYWHERE] * len(after),
            out_specs=out_specs,
            scratch_shapes=[
                pltpu.VMEM((slots * features, count), jnp.bfloat16),
                pltpu.VMEM((tile, count), jnp.float32),
                pltpu.SemaphoreType.DMA((len(sources),)),
            ],
        ),
        out_shape=out_shape,
        compiler_params=pltpu.CompilerParams(vmem_limit_bytes=VMEM_BYTES),
        cost_estimate=cost(12),
        name="hidden_part",
    )(rank, *operands, *after)


def weigh(routes, grads, after, price, extra=None):
    hidden = grads[0].shape[1]
    tile = widest(hidden, (512, 256, 128))
    steps = hidden // tile
    heights = [sum(u[0].shape[-2] for u in units) for units in routes]
    rows, count = sum(heights), sum(g.shape[2] for g in grads)
    units = [u for route in routes for u in route]
    flat = [w for u in units for w in u]
    extras = [] if extra is None else [extra]

    def kernel(*refs):
        weights, both = list(refs[: len(flat)]), refs[len(flat) : len(flat) + len(grads)]
        more = refs[len(flat) + len(grads) : len(flat) + len(grads) + len(extras)]
        outs, total = refs[-1 - len(routes) - len(extras) : -1], refs[-1]
        at = pl.program_id(0)

        @pl.when(at == 0)
        def _():
            total[...] = jnp.zeros_like(total)

        gates, ups = [], []
        for u in units:
            mine, weights = weights[: len(u)], weights[len(u) :]
            gates.append(mine[0][...] if len(u) == 2 else mine[0][0])
            ups.append(mine[1][...] if len(u) == 2 else mine[0][1])
        gate, up = jnp.concatenate(gates, axis=0), jnp.concatenate(ups + [m[...] for m in more], axis=0)
        first = 0
        for ref in both:
            span = slice(first, first + ref.shape[2])
            by_up = jnp.dot(up, ref[1], preferred_element_type=jnp.float32)
            total[:rows, span] += (
                jnp.dot(gate, ref[0], preferred_element_type=jnp.float32) + by_up[:rows]
            )
            if more:
                total[rows:, span] += by_up[rows:]
            first += ref.shape[2]

        @pl.when(at == steps - 1)
        def _():
            top = 0
            for out, height in zip(outs, heights):
                out[...] = total[top : top + height].astype(jnp.bfloat16)
                top += height
            if more:
                outs[-1][...] = total[rows:]

    specs = []
    for w in flat:
        if w.ndim == 2:
            specs.append(pl.BlockSpec((w.shape[0], tile), lambda i: (0, i)))
        else:
            specs.append(pl.BlockSpec((2, w.shape[1], tile), lambda i: (0, 0, i)))
    for g in grads:
        specs.append(pl.BlockSpec((2, tile, g.shape[2]), lambda i: (0, i, 0)))
    shapes = [jax.ShapeDtypeStruct((h, count), jnp.bfloat16) for h in heights]
    for e in extras:
        specs.append(pl.BlockSpec((e.shape[0], tile), lambda i: (0, i)))
        shapes.append(jax.ShapeDtypeStruct((e.shape[0], count), jnp.float32))
    return pl.pallas_call(
        kernel,
        grid=(steps,),
        out_shape=shapes,
        in_specs=specs + [ANYWHERE] * len(after),
        out_specs=[pl.BlockSpec(s.shape, lambda i: (0, 0)) for s in shapes],
        scratch_shapes=[pltpu.VMEM((rows + sum(e.shape[0] for e in extras), count), jnp.float32)],
        compiler_params=pltpu.CompilerParams(vmem_limit_bytes=VMEM_BYTES),
        cost_estimate=cost(price),
        name="weigh_rows",
    )(*flat, *grads, *extras, *after)


def add(values, others, heights, after, price=2):
    pairs = len(values)
    flat = [h for hs in heights for h in hs]

    def kernel(*refs):
        outs = list(refs[len(refs) - len(flat) :])
        for at in range(pairs):
            top = 0
            for height in heights[at]:
                rows = slice(top, top + height)
                outs.pop(0)[...] = (
                    refs[at][rows].astype(jnp.float32) + refs[pairs + at][rows].astype(jnp.float32)
                ).astype(jnp.bfloat16)
                top += height

    count = values[0].shape[1]
    whole = pl.BlockSpec(memory_space=pltpu.VMEM)
    return pl.pallas_call(
        kernel,
        out_shape=[jax.ShapeDtypeStruct((h, count), jnp.bfloat16) for h in flat],
        in_specs=[whole] * (2 * pairs) + [ANYWHERE] * len(after),
        out_specs=[whole] * len(flat),
        compiler_params=pltpu.CompilerParams(vmem_limit_bytes=VMEM_BYTES),
        cost_estimate=cost(price),
        name="add_terms",
    )(*values, *others, *after)


def assemble(words, count, features, part, near, far, chips, after):
    groups = lax.axis_size("groups")
    height = near[0][0][0].shape[0]
    tall = features // part
    arrays, index = [], {}

    def at_of(value):
        if id(value) not in index:
            index[id(value)] = len(arrays)
            arrays.append(value)
        return index[id(value)]

    near_at = [[[at_of(v) for v in pair] for pair in half] for half in near]
    far_at = {
        n: (row, [([at_of(v) for v in pair], first) for pair, first in halves])
        for n, (row, halves) in far.items()
    }
    chunks = 1 + max(n[0] for n in far)
    piece = part // CHUNKS

    def kernel(words_ref, *refs):
        outs = refs[-2:]
        away, group, inside = words_ref[0], words_ref[1], words_ref[2]

        def total(pair, rows, cols):
            one, two = (refs[at][rows, cols].astype(jnp.float32) for at in pair)
            return (one + two).astype(jnp.bfloat16)

        for j in range(len(near[0])):

            @pl.when((away == 0) & (inside == j * height))
            def _(j=j):
                for half in range(2):
                    outs[half][...] = total(near_at[half][j], slice(0, height), slice(0, count))

        for s in range(1, chips):
            for g in range(groups):
                for h in range(0, groups, tall):

                    @pl.when((away == s) & (group == g) & (inside == h * part))
                    def _(s=s, g=g, h=h):
                        for j in range(tall):
                            shift = (h + j - g) % groups
                            for k in range(CHUNKS):
                                top = j * part + k * piece
                                for half in range(2):
                                    if (k, s, shift) in far_at:
                                        row, halves = far_at[k, s, shift]
                                        pair, first = halves[half]
                                        value = total(
                                            pair, slice(row, row + piece), slice(first, first + count)
                                        )
                                    else:
                                        value = jnp.zeros((piece, count), jnp.bfloat16)
                                    outs[half][top : top + piece] = value

    whole = pl.BlockSpec(memory_space=pltpu.VMEM)
    return pl.pallas_call(
        kernel,
        out_shape=[jax.ShapeDtypeStruct((features, count), jnp.bfloat16)] * 2,
        in_specs=[pl.BlockSpec(memory_space=pltpu.SMEM)]
        + [whole] * len(arrays)
        + [ANYWHERE] * len(after),
        out_specs=[whole] * 2,
        compiler_params=pltpu.CompilerParams(vmem_limit_bytes=VMEM_BYTES),
        cost_estimate=cost(5),
        name="assemble",
    )(words, *arrays, *after)


def finish(words, part, mine, theirs, late_mine, late_theirs, late, chips):
    features, count = mine.shape
    groups = lax.axis_size("groups")
    tall = features // part
    piece = part // CHUNKS

    def kernel(words_ref, mine_ref, theirs_ref, late_mine_ref, late_theirs_ref, out_ref, rows_ref):
        away, group, inside = words_ref[0], words_ref[1], words_ref[2]
        for own, base, extra in ((1, mine_ref, late_mine_ref), (0, theirs_ref, late_theirs_ref)):

            @pl.when(words_ref[3] == own)
            def _(base=base, extra=extra):
                rows_ref[...] = base[...]
                for g in range(groups):
                    for h in range(0, groups, tall):

                        @pl.when((away > 0) & (group == g) & (inside == h * part))
                        def _(g=g, h=h):
                            for j in range(tall):
                                for at, (k, r) in enumerate(late):
                                    if (h + j - g) % groups == r:
                                        top = j * part + k * piece
                                        rows_ref[top : top + piece] = extra[
                                            at * piece : (at + 1) * piece
                                        ]

        out_ref[...] = rows_ref[...].T

    return pl.pallas_call(
        kernel,
        out_shape=jax.ShapeDtypeStruct((count, features), mine.dtype),
        in_specs=[pl.BlockSpec(memory_space=pltpu.SMEM)] + [pl.BlockSpec(memory_space=pltpu.VMEM)] * 4,
        out_specs=pl.BlockSpec(memory_space=pltpu.VMEM),
        scratch_shapes=[pltpu.VMEM((features, count), mine.dtype)],
        compiler_params=pltpu.CompilerParams(vmem_limit_bytes=VMEM_BYTES),
        cost_estimate=cost(3),
        name="finish",
    )(words, mine, theirs, late_mine, late_theirs)


def exchange(value, bit):
    ranks = lax.axis_size("tensor")
    return lax.ppermute(value, "tensor", [(i, i ^ bit) for i in range(ranks)])


def halve(value, bit):
    half = value.shape[0] // 2
    high = lax.axis_index("tensor") & bit != 0
    low_rows, high_rows = value[:half], value[half:]
    got = exchange(jnp.where(high, low_rows, high_rows), bit)
    return jnp.where(high, high_rows, low_rows) + got


def hops(owner, bit):
    groups, ranks, blocks = (lax.axis_size(a) for a in ("groups", "tensor", "dp"))
    pairs = []
    for g in range(groups):
        for p in range(blocks):
            target = owner[g, p]
            for z in range(ranks):
                if z % bit == target % bit and (z ^ target) & bit:
                    pairs.append(((g * ranks + z) * blocks + p, (g * ranks + (z ^ bit)) * blocks + p))
    return pairs


def send(value, pairs):
    return lax.ppermute(value, ("groups", "tensor", "dp"), pairs)


def later_steps(values, owners):
    ranks = lax.axis_size("tensor")
    ends = []
    for value, owner in zip(values, owners):
        bit, got = 2, None
        while bit < ranks:
            if got is not None:
                (value,) = add([value], [got], [[value.shape[0]]], [])
            got = send(value, hops(owner, bit))
            bit *= 2
        ends.append((value, got))
    return ends


def per_device(
    layer_input,
    gate_act,
    up_act,
    out_grad,
    w_gate,
    w_up,
    w_down,
    proj_x,
    proj_u,
    proj_h,
    proj_g,
    doc_lengths,
):
    groups, ranks = lax.axis_size("groups"), lax.axis_size("tensor")
    blocks = lax.axis_size("dp")
    chips = blocks // CORES
    group, rank = lax.axis_index("groups"), lax.axis_index("tensor")
    place = lax.axis_index("dp")
    chip, core = place // CORES, place % CORES
    rows = w_gate.shape[0]
    count = layer_input.shape[0]
    features = out_grad.shape[1]
    part = rows // groups
    piece = part // CHUNKS
    split = max(1, ranks // blocks)
    group_word = jnp.full((1,), group, jnp.int32)
    rank_word = jnp.full((1,), rank, jnp.int32)

    below, above = spread_ranks(out_grad.T)
    _, shares = share_rows(w_gate, w_up, group_word, [0, 1], piece, [], [])
    slopes, in_down_part = prepare(gate_act, up_act, proj_h.T, [shares[0]])
    early_part = jnp.concatenate([project(proj_x, layer_input), in_down_part], axis=0)
    out_down_part = project(proj_g, out_grad)
    fetched, ticks = {}, []

    def fetch(k):
        for s in range(1, chips):
            fetched[k, s, 0] = from_chip(shares[k], s)
            for r in range(1, groups):
                fetched[k, s, r] = from_group(fetched[k, s, 0], r)

    def forward(k, after, held=()):
        waits = [fetched[n] for n in fetched if n[0] == k and n[2] == 0]
        waits += [fetched[n] for n in fetched if n[0] == k - 1 and n[2] > 0]
        waits = [w for w in waits if not any(w is h for h in held)]
        places = [k + 2] if k + 2 < CHUNKS else []
        carried, fresh = share_rows(
            w_gate, w_up, group_word, places, piece, list(held), waits + list(after)
        )
        ticks.append(fresh[0])
        if places:
            shares.extend(fresh)
            fetch(k + 2)
        return carried

    def owner_of(s, first_of):
        table = np.zeros((groups, blocks), np.int64)
        for g in range(groups):
            for p in range(blocks):
                block = (p // CORES + s) % chips * CORES + p % CORES
                table[g, p] = (block * rows + first_of(g)) // features
        return table

    far_routes = []
    for s in range(1, chips):
        for r in range(groups):
            table = owner_of(s, lambda g: (g + r) % groups * part)
            for route in far_routes:
                if route[0] == s and (route[1] == table).all():
                    route[2].append(r)
                    break
            else:
                far_routes.append((s, table, [r]))
    height = rows // split
    near_tables = [owner_of(0, lambda g: j * height) for j in range(split)]
    near_routes = [
        [(w_gate[j * height : (j + 1) * height], w_up[j * height : (j + 1) * height])]
        for j in range(split)
    ]

    def terms(names, grads, after, price, near=False, extra=None):
        routes = list(zip(near_tables, near_routes, [None] * split)) if near else []
        for s, table, shifts in far_routes:
            units = [(k, s, q) for k, q in names if q in shifts]
            if units:
                routes.append((table, [(fetched[n],) for n in units], units))
        bundles = {}
        for route in routes:
            bundles.setdefault((route[0] % 2).tobytes(), []).append(route)
        bundles = list(bundles.values())
        joined = [[u for _, units, _ in b for u in units] for b in bundles]
        outs = list(weigh(joined, grads, after, price, extra))
        got = [send(out, hops(b[0][0], 1)) for out, b in zip(outs, bundles)]
        return outs, got, bundles

    def carry_on(work, after, price=2):
        outs, got, bundles = work
        heights = [[sum(u[0].shape[-2] for u in units) for _, units, _ in b] for b in bundles]
        sums = list(add(outs, got, heights, after, price))
        routes = [route for b in bundles for route in b]
        ends = later_steps(sums, [table for table, _, _ in routes])
        return sums, [(names, *end) for (_, _, names), end in zip(routes, ends)]

    fetch(0)
    fetch(1)

    def hold_arrived(k, after, held=()):
        names = [(k, s, 0) for s in range(1, chips)]
        values = forward(k, after, [fetched[n] for n in names] + list(held))
        for n, value in zip(names, values):
            fetched[n] = value
            for r in range(1, groups):
                fetched[k, n[1], r] = from_group(value, r)
        return values[len(names) :]

    bits = [1 << i for i in range(ranks.bit_length() - 1)]
    hold_arrived(0, [slopes])
    so_far = hidden_part(rank_word, below, above, w_down, None, None, None, [ticks[0]])
    hold_arrived(1, [so_far])
    forward(2, [below[2], above[1], early_part, out_down_part])
    (early,) = forward(3, below[3:] + above[2:], [early_part])
    mine, up_out_part = hidden_part(
        rank_word, below, above, w_down, so_far, slopes, proj_u.T, [ticks[3]]
    )
    early = early + exchange(early, bits[0])
    mine, early = forward(4, [], [mine, early])
    theirs = swap_cores(mine)

    out_parts = jnp.stack([up_out_part, out_down_part]).reshape(2, ranks, -1, count)
    out_parts = out_parts.transpose(1, 0, 2, 3).reshape(-1, count)
    half = out_parts.shape[0] // 2
    high = rank & bits[-1] != 0
    width = early.shape[0]
    got = exchange(
        jnp.concatenate([early, jnp.where(high, out_parts[:half], out_parts[half:])], axis=0),
        bits[-1],
    )
    early = early + got[:width]
    out_parts = jnp.where(high, out_parts[half:], out_parts[:half]) + got[width:]
    for bit in bits[1:-1]:
        early = early + exchange(early, bit)

    first_names = [(k, 0) for k in range(5)] + [(k, 1) for k in range(4)]
    first_mine = terms(first_names, [mine], [ticks[4]], 16, near=True)
    (out_parts,) = forward(5, first_mine[0] + [early], [out_parts])
    first_theirs = terms(first_names, [theirs], [ticks[5]], 16, near=True)
    sums_mine, end_mine = carry_on(first_mine, first_theirs[0])
    hold_arrived(6, first_theirs[0])
    second_names = [(5, 0), (6, 0), (4, 1), (5, 1)]
    second = terms(second_names, [mine, theirs], [ticks[6]] + sums_mine, 10)
    sums_theirs, end_theirs = carry_on(first_theirs, second[0])
    (out_parts,) = hold_arrived(7, second[0], [out_parts])
    third_names = [(7, 0), (6, 1)]
    received = [got for _, _, got in end_mine]
    third = terms(third_names, [mine, theirs], [ticks[7]] + sums_theirs + received, 4)
    sums_second, end_second = carry_on(second, third[0])

    for bit in bits[-2::-1]:
        out_parts = halve(out_parts, bit)
    early = early.astype(jnp.bfloat16)
    width = in_down_part.shape[0]
    in_up, in_down = early[:width], early[width:]
    out_parts = out_parts.astype(jnp.bfloat16)
    slot = out_parts.shape[0] // 2
    up_out, out_down = out_parts[:slot], out_parts[slot:]
    member = pack_table(doc_lengths, count)
    doc_logs = jnp.stack(
        [doc_outer(member, up_out, in_up), doc_outer(member, out_down, in_down)], axis=1
    )

    sums_third, end_third = carry_on(third, [])
    last_names = [(CHUNKS - 1, r) for r in range(1, groups)]
    received = [got for _, _, got in end_theirs]
    last = terms(last_names, [mine, theirs], sums_third + received, 20)
    sums_last, end_last = carry_on(last, [], 40)

    first = rank * features
    away = (first // rows // CORES - chip) % chips
    owner = first // rows % CORES == core
    inside = first % rows
    near, far = [[], []], {}
    for (names, *m), (_, *t) in zip(end_mine, end_theirs):
        if names is None:
            near[0].append(m)
            near[1].append(t)
        else:
            far.update((n, (i * piece, [(m, 0), (t, 0)])) for i, n in enumerate(names))
    for names, *pair in end_second:
        far.update((n, (i * piece, [(pair, 0), (pair, count)])) for i, n in enumerate(names))
    words = jnp.stack([away, group, inside, owner]).astype(jnp.int32)
    total_mine, total_theirs = assemble(
        words, count, features, part, near, far, chips, last[0]
    )
    from_partner = swap_cores(total_theirs)

    def pick(index, options):
        value = options[0]
        for at, option in enumerate(options[1:], 1):
            value = jnp.where(index == at, option, value)
        return value

    tail = {}
    for names, value, got in end_third + end_last:
        value = (value.astype(jnp.float32) + got.astype(jnp.float32)).astype(jnp.bfloat16)
        tail.update((n, value[i * piece : (i + 1) * piece]) for i, n in enumerate(names))
    late = sorted({(k, r) for k, _, r in tail})
    pieces = jnp.concatenate(
        [pick(away - 1, [tail[k, s, r] for s in range(1, chips)]) for k, r in late], axis=0
    )
    input_grad = finish(
        words,
        part,
        total_mine,
        from_partner,
        pieces[:, :count],
        swap_cores(pieces[:, count:]),
        late,
        chips,
    )
    return (input_grad, doc_logs)


def solution(mesh):
    placed = (
        P(("groups", "dp"), "tensor"),
        P(("groups", "dp"), "tensor"),
        P(("groups", "dp"), "tensor"),
        P(("groups", "dp"), "tensor"),
        P("dp", "tensor"),
        P("dp", "tensor"),
        P("tensor", None),
        P("tensor", None),
        P("tensor", None),
        P("tensor", None),
        P("tensor", None),
        P(("groups", "dp"), None),
    )
    return jax.shard_map(
        per_device,
        mesh=mesh,
        in_specs=placed,
        out_specs=(P(("groups", "dp"), "tensor"), P(("groups", "dp"), None, "tensor")),
        check_vma=False,
    )
```

```python
import functools

import jax
import jax.numpy as jnp
import numpy as np
from jax import lax
from jax.experimental import pallas as pl
from jax.experimental.pallas import tpu as pltpu
from jax.sharding import PartitionSpec as P

CORES = 2
CHUNKS = (2, 2, 2, 2, 3, 3, 2)
VMEM_BYTES = 60 * 1024 * 1024
FLOPS_PER_US = 270_000_000
ANYWHERE = pl.BlockSpec(memory_space=pl.ANY)


def contract_right(left, right):
    return lax.dot_general(
        left, right, (((1,), (1,)), ((), ())), preferred_element_type=jnp.float32
    )


def project(proj, rows):
    return lax.dot_general(
        proj, rows, (((0,), (1,)), ((), ())), preferred_element_type=jnp.float32
    )


def pack_table(doc_lengths, count):
    lengths = doc_lengths[0]
    ends = jnp.cumsum(lengths)
    starts = ends - lengths
    position = jnp.arange(count, dtype=jnp.int32)[None, :]
    inside = (position >= starts[:, None]) & (position < ends[:, None])
    return inside.astype(jnp.bfloat16)


def doc_outer(member, grad_rows, inputs):
    count = member.shape[1]
    weighted = (member[:, None, :] * grad_rows[None, :, :]).reshape(-1, count)
    table = contract_right(weighted, inputs)
    return table.reshape(member.shape[0], grad_rows.shape[0] * inputs.shape[0])


def swap_cores(value):
    size = lax.axis_size("dp")
    return lax.ppermute(value, "dp", [(i, i ^ 1) for i in range(size)])


def from_chip(value, shift):
    size = lax.axis_size("dp")
    step = shift * CORES
    return lax.ppermute(value, "dp", [((i + step) % size, i) for i in range(size)])


def from_group(value, shift):
    size = lax.axis_size("groups")
    return lax.ppermute(value, "groups", [((i + shift) % size, i) for i in range(size)])


def chunk_edges(part):
    return [part // 16 * sum(CHUNKS[:k]) for k in range(len(CHUNKS) + 1)]


def cost(us):
    return pl.CostEstimate(flops=int(us * FLOPS_PER_US) + 1, bytes_accessed=1, transcendentals=0)


def widest(size, options):
    return next((w for w in options if size % w == 0), size)


def share_rows(w_gate, w_up, group, spans, carried, after):
    rows, width = w_gate.shape
    part = rows // lax.axis_size("groups")
    step = part // 16
    kept, waits, fresh = len(carried), len(after), len(spans)
    steps = max([(last - first) // step for first, last in spans], default=1)

    def kernel(group_ref, *refs):
        outs = refs[len(refs) - fresh :] if fresh else []
        for at, out in enumerate(outs):
            out[0] = refs[2 * at][...]
            out[1] = refs[2 * at + 1][...]
        if not fresh:
            refs[-1][...] = jnp.zeros_like(refs[-1])

    in_specs, out_specs = [], [ANYWHERE] * kept
    shapes = [jax.ShapeDtypeStruct(a.shape, a.dtype) for a in carried]
    for first, last in spans:
        at_rows = functools.partial(lambda f, i, g: (g[0] * (part // step) + f // step + i, 0), first)
        in_specs += [pl.BlockSpec((step, width), at_rows)] * 2
        out_specs.append(pl.BlockSpec((2, step, width), lambda i, g: (0, i, 0)))
        shapes.append(jax.ShapeDtypeStruct((2, last - first, width), w_gate.dtype))
    if not fresh:
        out_specs.append(pl.BlockSpec((8, 128), lambda i, g: (0, 0)))
        shapes.append(jax.ShapeDtypeStruct((8, 128), jnp.float32))
    results = pl.pallas_call(
        kernel,
        grid_spec=pltpu.PrefetchScalarGridSpec(
            num_scalar_prefetch=1,
            grid=(steps,),
            in_specs=in_specs + [ANYWHERE] * (kept + waits),
            out_specs=out_specs,
        ),
        out_shape=shapes,
        input_output_aliases={1 + 2 * fresh + i: i for i in range(kept)},
        compiler_params=pltpu.CompilerParams(vmem_limit_bytes=VMEM_BYTES),
        cost_estimate=cost(2),
        name="share_rows",
    )(group, *[w_gate, w_up] * fresh, *carried, *after)
    return list(results[:kept]), list(results[kept:])


def spread_ranks(value):
    ranks = lax.axis_size("tensor")
    below, above = [value], [value]
    for _ in range(1, ranks):
        below.append(lax.ppermute(below[-1], "tensor", [(i, i + 1) for i in range(ranks - 1)]))
        above.append(lax.ppermute(above[-1], "tensor", [(i + 1, i) for i in range(ranks - 1)]))
    return below, above[1:]


def prepare(gate_act, up_act, proj_h, after):
    count, hidden = gate_act.shape
    narrow = proj_h.shape[0]
    tile = widest(hidden, (512, 256, 128))

    def kernel(gate_ref, up_ref, proj_ref, *refs):
        slope_ref, down_ref = refs[-2:]

        @pl.when(pl.program_id(0) == 0)
        def _():
            down_ref[...] = jnp.zeros_like(down_ref)

        gate = gate_ref[...].astype(jnp.float32).T
        up = up_ref[...].astype(jnp.float32).T
        sigma = jax.nn.sigmoid(gate)
        swish = gate * sigma
        slope_ref[0] = up * sigma * (1.0 + gate * (1.0 - sigma))
        slope_ref[1] = swish
        down_ref[...] += jnp.dot(
            proj_ref[...], (swish * up).astype(jnp.bfloat16), preferred_element_type=jnp.float32
        )

    return pl.pallas_call(
        kernel,
        grid=(hidden // tile,),
        out_shape=[
            jax.ShapeDtypeStruct((2, hidden, count), jnp.float32),
            jax.ShapeDtypeStruct((narrow, count), jnp.float32),
        ],
        in_specs=[
            pl.BlockSpec((count, tile), lambda i: (0, i)),
            pl.BlockSpec((count, tile), lambda i: (0, i)),
            pl.BlockSpec((narrow, tile), lambda i: (0, i)),
        ]
        + [ANYWHERE] * len(after),
        out_specs=[
            pl.BlockSpec((2, tile, count), lambda i: (0, i, 0)),
            pl.BlockSpec((narrow, count), lambda i: (0, 0)),
        ],
        compiler_params=pltpu.CompilerParams(vmem_limit_bytes=VMEM_BYTES),
        cost_estimate=cost(12),
        name="prepare",
    )(gate_act, up_act, proj_h, *after)


def hidden_part(rank, below, above, w_down, so_far, slopes, proj_u, after):
    ranks = lax.axis_size("tensor")
    features, count = below[0].shape
    hidden = w_down.shape[0]
    finish = so_far is not None
    slots = ranks - 2 if finish else 2
    tile = widest(hidden, (896, 512, 128))
    sources = [(t, -1, below[t]) for t in range(2 if finish else 0, ranks if finish else 2)]
    sources += [(t, 1, above[t - 1]) for t in range(1, ranks if finish else 2)]

    def counts(z):
        both = ((z >= 1) & (z <= ranks - 2)).astype(jnp.int32)
        return both, jnp.maximum(z - 1, 0)

    def place_of(z, t, side):
        if not finish:
            return (0, z >= 0) if t == 0 else (1, z >= 1 if side < 0 else z == 0)
        both, under = counts(z)
        if side < 0:
            return both + t - 2, t <= z
        if t == 1:
            return 0, both == 1
        return both + under + t - 2, z + t <= ranks - 1

    def column(at, i, rank_ref):
        z = rank_ref[0]
        if not finish:
            return (i, z) if at == 0 else (i, jnp.where(z >= 1, z - 1, 1))
        both, under = counts(z)
        block = jnp.where(at < both + under, z - (at - both + 2), z + (at - both - under + 2))
        return (i, jnp.where(at < both, z + 1, block))

    def kernel(rank_ref, *refs):
        z = rank_ref[0]
        downs, arrived = refs[:slots], refs[slots : slots + len(sources)]
        grad_ref, sem = refs[-2:]
        rest = refs[slots + len(sources) :]

        def gather(wait):
            for at, (t, side, _) in enumerate(sources):
                place, valid = place_of(z, t, side)

                @pl.when(valid)
                def _():
                    rows = pl.ds(pl.multiple_of(place * features, features), features)
                    copy = pltpu.make_async_copy(arrived[at], grad_ref.at[rows, :], sem.at[at])
                    copy.wait() if wait else copy.start()

        @pl.when(pl.program_id(0) == 0)
        def _():
            gather(False)
            gather(True)

        wide = None
        for at in range(slots):
            term = jnp.dot(
                downs[at][...],
                grad_ref[at * features : (at + 1) * features, :],
                preferred_element_type=jnp.float32,
            )
            wide = term if wide is None else wide + term
        if finish:
            both_ref, out_ref = refs[-4:-2]
            wide = wide + rest[0][...]
            both_ref[0] = (wide * rest[1][0]).astype(jnp.bfloat16)
            up_grad = (wide * rest[1][1]).astype(jnp.bfloat16)
            both_ref[1] = up_grad
            part = jnp.dot(rest[2][...], up_grad, preferred_element_type=jnp.float32)

            @pl.when(pl.program_id(0) == 0)
            def _():
                out_ref[...] = part

            @pl.when(pl.program_id(0) > 0)
            def _():
                out_ref[...] += part

        else:
            refs[-3][...] = wide

    operands = [w_down] * slots + [value for _, _, value in sources]
    specs = [pl.BlockSpec((tile, features), functools.partial(column, at)) for at in range(slots)]
    specs += [ANYWHERE] * len(sources)
    if finish:
        narrow = proj_u.shape[0]
        operands += [so_far, slopes, proj_u]
        specs += [
            pl.BlockSpec((tile, count), lambda i, r: (i, 0)),
            pl.BlockSpec((2, tile, count), lambda i, r: (0, i, 0)),
            pl.BlockSpec((narrow, tile), lambda i, r: (0, i)),
        ]
        out_shape = [
            jax.ShapeDtypeStruct((2, hidden, count), jnp.bfloat16),
            jax.ShapeDtypeStruct((narrow, count), jnp.float32),
        ]
        out_specs = [
            pl.BlockSpec((2, tile, count), lambda i, r: (0, i, 0)),
            pl.BlockSpec((narrow, count), lambda i, r: (0, 0)),
        ]
    else:
        out_shape = jax.ShapeDtypeStruct((hidden, count), jnp.float32)
        out_specs = pl.BlockSpec((tile, count), lambda i, r: (i, 0))
    return pl.pallas_call(
        kernel,
        grid_spec=pltpu.PrefetchScalarGridSpec(
            num_scalar_prefetch=1,
            grid=(hidden // tile,),
            in_specs=specs + [ANYWHERE] * len(after),
            out_specs=out_specs,
            scratch_shapes=[
                pltpu.VMEM((slots * features, count), jnp.bfloat16),
                pltpu.SemaphoreType.DMA((len(sources),)),
            ],
        ),
        out_shape=out_shape,
        compiler_params=pltpu.CompilerParams(vmem_limit_bytes=VMEM_BYTES),
        cost_estimate=cost(12),
        name="hidden_part",
    )(rank, *operands, *after)


def weigh(routes, grads, after, price, extra=None):
    hidden = grads[0].shape[1]
    tile = widest(hidden, (512, 256, 128))
    steps = hidden // tile
    heights = [sum(u[0].shape[-2] for u in units) for units in routes]
    rows, count = sum(heights), sum(g.shape[2] for g in grads)
    units = [u for route in routes for u in route]
    flat = [w for u in units for w in u]
    extras = [] if extra is None else [extra]

    def kernel(*refs):
        weights, both = list(refs[: len(flat)]), refs[len(flat) : len(flat) + len(grads)]
        more = refs[len(flat) + len(grads) : len(flat) + len(grads) + len(extras)]
        outs, total = refs[-1 - len(routes) - len(extras) : -1], refs[-1]
        at = pl.program_id(0)

        @pl.when(at == 0)
        def _():
            total[...] = jnp.zeros_like(total)

        gates, ups = [], []
        for u in units:
            mine, weights = weights[: len(u)], weights[len(u) :]
            gates.append(mine[0][...] if len(u) == 2 else mine[0][0])
            ups.append(mine[1][...] if len(u) == 2 else mine[0][1])
        gate, up = jnp.concatenate(gates, axis=0), jnp.concatenate(ups + [m[...] for m in more], axis=0)
        first = 0
        for ref in both:
            span = slice(first, first + ref.shape[2])
            by_up = jnp.dot(up, ref[1], preferred_element_type=jnp.float32)
            total[:rows, span] += (
                jnp.dot(gate, ref[0], preferred_element_type=jnp.float32) + by_up[:rows]
            )
            if more:
                total[rows:, span] += by_up[rows:]
            first += ref.shape[2]

        @pl.when(at == steps - 1)
        def _():
            top = 0
            for out, height in zip(outs, heights):
                out[...] = total[top : top + height].astype(jnp.bfloat16)
                top += height
            if more:
                outs[-1][...] = total[rows:]

    specs = []
    for w in flat:
        if w.ndim == 2:
            specs.append(pl.BlockSpec((w.shape[0], tile), lambda i: (0, i)))
        else:
            specs.append(pl.BlockSpec((2, w.shape[1], tile), lambda i: (0, 0, i)))
    for g in grads:
        specs.append(pl.BlockSpec((2, tile, g.shape[2]), lambda i: (0, i, 0)))
    shapes = [jax.ShapeDtypeStruct((h, count), jnp.bfloat16) for h in heights]
    for e in extras:
        specs.append(pl.BlockSpec((e.shape[0], tile), lambda i: (0, i)))
        shapes.append(jax.ShapeDtypeStruct((e.shape[0], count), jnp.float32))
    return pl.pallas_call(
        kernel,
        grid=(steps,),
        out_shape=shapes,
        in_specs=specs + [ANYWHERE] * len(after),
        out_specs=[pl.BlockSpec(s.shape, lambda i: (0, 0)) for s in shapes],
        scratch_shapes=[pltpu.VMEM((rows + sum(e.shape[0] for e in extras), count), jnp.float32)],
        compiler_params=pltpu.CompilerParams(vmem_limit_bytes=VMEM_BYTES),
        cost_estimate=cost(price),
        name="weigh_rows",
    )(*flat, *grads, *extras, *after)


def add(values, others, heights, after, price=2):
    pairs = len(values)
    flat = [h for hs in heights for h in hs]

    def kernel(*refs):
        outs = list(refs[len(refs) - len(flat) :])
        for at in range(pairs):
            top = 0
            for height in heights[at]:
                rows = slice(top, top + height)
                outs.pop(0)[...] = (
                    refs[at][rows].astype(jnp.float32) + refs[pairs + at][rows].astype(jnp.float32)
                ).astype(jnp.bfloat16)
                top += height

    count = values[0].shape[1]
    whole = pl.BlockSpec(memory_space=pltpu.VMEM)
    return pl.pallas_call(
        kernel,
        out_shape=[jax.ShapeDtypeStruct((h, count), jnp.bfloat16) for h in flat],
        in_specs=[whole] * (2 * pairs) + [ANYWHERE] * len(after),
        out_specs=[whole] * len(flat),
        compiler_params=pltpu.CompilerParams(vmem_limit_bytes=VMEM_BYTES),
        cost_estimate=cost(price),
        name="add_terms",
    )(*values, *others, *after)


def assemble(words, count, features, part, near, far, chips, after):
    groups = lax.axis_size("groups")
    height = near[0][0][0].shape[0]
    tall = features // part
    arrays, index = [], {}

    def at_of(value):
        if id(value) not in index:
            index[id(value)] = len(arrays)
            arrays.append(value)
        return index[id(value)]

    near_at = [[[at_of(v) for v in pair] for pair in half] for half in near]
    far_at = {
        n: (row, [([at_of(v) for v in pair], first) for pair, first in halves])
        for n, (row, halves) in far.items()
    }
    edges = chunk_edges(part)

    def kernel(words_ref, *refs):
        outs = refs[-2:]
        away, group, inside = words_ref[0], words_ref[1], words_ref[2]

        def total(pair, rows, cols):
            one, two = (refs[at][rows, cols].astype(jnp.float32) for at in pair)
            return (one + two).astype(jnp.bfloat16)

        for j in range(len(near[0])):

            @pl.when((away == 0) & (inside == j * height))
            def _(j=j):
                for half in range(2):
                    outs[half][...] = total(near_at[half][j], slice(0, height), slice(0, count))

        for s in range(1, chips):
            for g in range(groups):
                for h in range(0, groups, tall):

                    @pl.when((away == s) & (group == g) & (inside == h * part))
                    def _(s=s, g=g, h=h):
                        for j in range(tall):
                            shift = (h + j - g) % groups
                            for k in range(len(CHUNKS)):
                                top = j * part + edges[k]
                                piece = edges[k + 1] - edges[k]
                                for half in range(2):
                                    if (k, s, shift) in far_at:
                                        row, halves = far_at[k, s, shift]
                                        pair, first = halves[half]
                                        value = total(
                                            pair, slice(row, row + piece), slice(first, first + count)
                                        )
                                    else:
                                        value = jnp.zeros((piece, count), jnp.bfloat16)
                                    outs[half][top : top + piece] = value

    whole = pl.BlockSpec(memory_space=pltpu.VMEM)
    return pl.pallas_call(
        kernel,
        out_shape=[jax.ShapeDtypeStruct((features, count), jnp.bfloat16)] * 2,
        in_specs=[pl.BlockSpec(memory_space=pltpu.SMEM)]
        + [whole] * len(arrays)
        + [ANYWHERE] * len(after),
        out_specs=[whole] * 2,
        compiler_params=pltpu.CompilerParams(vmem_limit_bytes=VMEM_BYTES),
        cost_estimate=cost(5),
        name="assemble",
    )(words, *arrays, *after)


def finish(words, part, mine, theirs, late_mine, late_theirs, late, chips):
    features, count = mine.shape
    groups = lax.axis_size("groups")
    tall = features // part
    edges = chunk_edges(part)

    def kernel(words_ref, mine_ref, theirs_ref, late_mine_ref, late_theirs_ref, out_ref, rows_ref):
        away, group, inside = words_ref[0], words_ref[1], words_ref[2]
        for own, base, extra in ((1, mine_ref, late_mine_ref), (0, theirs_ref, late_theirs_ref)):

            @pl.when(words_ref[3] == own)
            def _(base=base, extra=extra):
                rows_ref[...] = base[...]
                for g in range(groups):
                    for h in range(0, groups, tall):

                        @pl.when((away > 0) & (group == g) & (inside == h * part))
                        def _(g=g, h=h):
                            for j in range(tall):
                                row = 0
                                for k, r in late:
                                    top, piece = j * part + edges[k], edges[k + 1] - edges[k]
                                    if (h + j - g) % groups == r:
                                        rows_ref[top : top + piece] = extra[row : row + piece]
                                    row += piece

        out_ref[...] = rows_ref[...].T

    return pl.pallas_call(
        kernel,
        out_shape=jax.ShapeDtypeStruct((count, features), mine.dtype),
        in_specs=[pl.BlockSpec(memory_space=pltpu.SMEM)] + [pl.BlockSpec(memory_space=pltpu.VMEM)] * 4,
        out_specs=pl.BlockSpec(memory_space=pltpu.VMEM),
        scratch_shapes=[pltpu.VMEM((features, count), mine.dtype)],
        compiler_params=pltpu.CompilerParams(vmem_limit_bytes=VMEM_BYTES),
        cost_estimate=cost(3),
        name="finish",
    )(words, mine, theirs, late_mine, late_theirs)


def exchange(value, bit):
    ranks = lax.axis_size("tensor")
    return lax.ppermute(value, "tensor", [(i, i ^ bit) for i in range(ranks)])


def halve(value, bit):
    half = value.shape[0] // 2
    high = lax.axis_index("tensor") & bit != 0
    low_rows, high_rows = value[:half], value[half:]
    got = exchange(jnp.where(high, low_rows, high_rows), bit)
    return jnp.where(high, high_rows, low_rows) + got


def hops(owner, bit):
    groups, ranks, blocks = (lax.axis_size(a) for a in ("groups", "tensor", "dp"))
    pairs = []
    for g in range(groups):
        for p in range(blocks):
            target = owner[g, p]
            for z in range(ranks):
                if z % bit == target % bit and (z ^ target) & bit:
                    pairs.append(((g * ranks + z) * blocks + p, (g * ranks + (z ^ bit)) * blocks + p))
    return pairs


def send(value, pairs):
    return lax.ppermute(value, ("groups", "tensor", "dp"), pairs)


def later_steps(values, owners):
    ranks = lax.axis_size("tensor")
    ends = []
    for value, owner in zip(values, owners):
        bit, got = 2, None
        while bit < ranks:
            if got is not None:
                (value,) = add([value], [got], [[value.shape[0]]], [])
            got = send(value, hops(owner, bit))
            bit *= 2
        ends.append((value, got))
    return ends


def per_device(
    layer_input,
    gate_act,
    up_act,
    out_grad,
    w_gate,
    w_up,
    w_down,
    proj_x,
    proj_u,
    proj_h,
    proj_g,
    doc_lengths,
):
    groups, ranks = lax.axis_size("groups"), lax.axis_size("tensor")
    blocks = lax.axis_size("dp")
    chips = blocks // CORES
    group, rank = lax.axis_index("groups"), lax.axis_index("tensor")
    place = lax.axis_index("dp")
    chip, core = place // CORES, place % CORES
    rows = w_gate.shape[0]
    count = layer_input.shape[0]
    features = out_grad.shape[1]
    part = rows // groups
    edges = chunk_edges(part)
    chunks = len(CHUNKS)
    split = max(1, ranks // blocks)
    group_word = jnp.full((1,), group, jnp.int32)
    rank_word = jnp.full((1,), rank, jnp.int32)

    below, above = spread_ranks(out_grad.T)
    spans = list(zip(edges, edges[1:]))
    _, shares = share_rows(w_gate, w_up, group_word, spans[:2], [], [])
    slopes, in_down_part = prepare(gate_act, up_act, proj_h.T, [shares[0]])
    early_part = jnp.concatenate([project(proj_x, layer_input), in_down_part], axis=0)
    out_down_part = project(proj_g, out_grad)
    fetched, ticks = {}, []

    def fetch(k):
        for s in range(1, chips):
            fetched[k, s, 0] = from_chip(shares[k], s)
            for r in range(1, groups):
                fetched[k, s, r] = from_group(fetched[k, s, 0], r)

    def forward(k, waits, after, held=()):
        names = [(k, 0)] + waits
        arrived = [fetched[n] for n in fetched if (n[0], n[2]) in names]
        arrived = [a for a in arrived if not any(a is h for h in held)]
        carried, fresh = share_rows(
            w_gate, w_up, group_word, spans[k + 2 : k + 3], list(held), arrived + list(after)
        )
        ticks.append(fresh[0])
        if k + 2 < chunks:
            shares.extend(fresh)
            fetch(k + 2)
        return carried

    def owner_of(s, first_of):
        table = np.zeros((groups, blocks), np.int64)
        for g in range(groups):
            for p in range(blocks):
                block = (p // CORES + s) % chips * CORES + p % CORES
                table[g, p] = (block * rows + first_of(g)) // features
        return table

    far_routes = []
    for s in range(1, chips):
        for r in range(groups):
            table = owner_of(s, lambda g: (g + r) % groups * part)
            for route in far_routes:
                if route[0] == s and (route[1] == table).all():
                    route[2].append(r)
                    break
            else:
                far_routes.append((s, table, [r]))
    height = rows // split
    near_tables = [owner_of(0, lambda g: j * height) for j in range(split)]
    near_routes = [
        [(w_gate[j * height : (j + 1) * height], w_up[j * height : (j + 1) * height])]
        for j in range(split)
    ]

    def terms(names, grads, after, price, near=False, extra=None):
        routes = list(zip(near_tables, near_routes, [None] * split)) if near else []
        for s, table, shifts in far_routes:
            units = [(k, s, q) for k, q in names if q in shifts]
            if units:
                routes.append((table, [(fetched[n],) for n in units], units))
        bundles = {}
        for route in routes:
            bundles.setdefault((route[0] % 2).tobytes(), []).append(route)
        bundles = list(bundles.values())
        joined = [[u for _, units, _ in b for u in units] for b in bundles]
        outs = list(weigh(joined, grads, after, price, extra))
        got = [send(out, hops(b[0][0], 1)) for out, b in zip(outs, bundles)]
        return outs, got, bundles

    def carry_on(work, after, price=2):
        outs, got, bundles = work
        heights = [[sum(u[0].shape[-2] for u in units) for _, units, _ in b] for b in bundles]
        sums = list(add(outs, got, heights, after, price))
        routes = [route for b in bundles for route in b]
        ends = later_steps(sums, [table for table, _, _ in routes])
        return sums, [(names, *end) for (_, _, names), end in zip(routes, ends)]

    fetch(0)
    fetch(1)

    def hold_arrived(k, waits, after, held=()):
        names = [(k, s, 0) for s in range(1, chips)]
        values = forward(k, waits, after, [fetched[n] for n in names] + list(held))
        for n, value in zip(names, values):
            fetched[n] = value
            for r in range(1, groups):
                fetched[k, n[1], r] = from_group(value, r)
        return values[len(names) :]

    def chunks_of(numbers, shifts):
        return [(k, r) for r in shifts for k in numbers]

    others = range(1, groups)
    bits = [1 << i for i in range(ranks.bit_length() - 1)]
    hold_arrived(0, [], [slopes])
    hold_arrived(1, chunks_of([0], others), [below[1], above[0]])
    so_far = hidden_part(rank_word, below, above, w_down, None, None, None, [ticks[1]])
    forward(
        2, chunks_of([1], others), [so_far, below[2], above[1], early_part, out_down_part]
    )
    (early,) = forward(3, chunks_of([2], others), below[3:] + above[2:], [early_part])
    mine, up_out_part = hidden_part(
        rank_word, below, above, w_down, so_far, slopes, proj_u.T, [ticks[3]]
    )
    early = early + exchange(early, bits[0])
    mine, early = forward(4, chunks_of([3], others), [], [mine, early])
    theirs = swap_cores(mine)

    out_parts = jnp.stack([up_out_part, out_down_part]).reshape(2, ranks, -1, count)
    out_parts = out_parts.transpose(1, 0, 2, 3).reshape(-1, count)
    half = out_parts.shape[0] // 2
    high = rank & bits[-1] != 0
    width = early.shape[0]
    got = exchange(
        jnp.concatenate([early, jnp.where(high, out_parts[:half], out_parts[half:])], axis=0),
        bits[-1],
    )
    early = early + got[:width]
    out_parts = jnp.where(high, out_parts[half:], out_parts[:half]) + got[width:]
    for bit in bits[1:-1]:
        early = early + exchange(early, bit)

    first_names = chunks_of(range(5), [0]) + chunks_of(range(4), others)
    first_mine = terms(first_names, [mine], [ticks[4]], 32, near=True)
    (out_parts,) = hold_arrived(5, chunks_of([4], others), first_mine[0] + [early], [out_parts])
    first_theirs = terms(first_names, [theirs], [ticks[5]], 60, near=True)
    sums_mine, end_mine = carry_on(first_mine, first_theirs[0])
    hold_arrived(6, [], first_theirs[0])
    second_names = chunks_of([5, 6], [0]) + chunks_of([4, 5], others)
    near_received = [got for names, _, got in end_mine if names is None]
    far_received = [got for names, _, got in end_mine if names is not None]
    second = terms(second_names, [mine, theirs], [ticks[6]] + far_received, 40)
    sums_theirs, end_theirs = carry_on(first_theirs, second[0] + near_received)

    last_names = chunks_of([6], others)
    come = [fetched[n] for n in fetched if (n[0], n[2]) in last_names]
    sums_second, end_second = carry_on(second, sums_theirs + come)
    last = terms(last_names, [mine, theirs], sums_second, 60)
    far_received = [got for names, _, got in end_theirs if names is not None]
    sums_last, end_last = carry_on(last, far_received, 8)

    (out_parts,), _ = share_rows(w_gate, w_up, group_word, [], [out_parts], sums_second)
    for bit in bits[-2::-1]:
        out_parts = halve(out_parts, bit)
    early = early.astype(jnp.bfloat16)
    width = in_down_part.shape[0]
    in_up, in_down = early[:width], early[width:]
    out_parts = out_parts.astype(jnp.bfloat16)
    slot = out_parts.shape[0] // 2
    up_out, out_down = out_parts[:slot], out_parts[slot:]
    member = pack_table(doc_lengths, count)
    doc_logs = jnp.stack(
        [doc_outer(member, up_out, in_up), doc_outer(member, out_down, in_down)], axis=1
    )

    first = rank * features
    away = (first // rows // CORES - chip) % chips
    owner = first // rows % CORES == core
    inside = first % rows
    def tops(names):
        sizes = [edges[n[0] + 1] - edges[n[0]] for n in names]
        return [(sum(sizes[:i]), n) for i, n in enumerate(names)]

    near, far = [[], []], {}
    for (names, *m), (_, *t) in zip(end_mine, end_theirs):
        if names is None:
            near[0].append(m)
            near[1].append(t)
        else:
            far.update((n, (row, [(m, 0), (t, 0)])) for row, n in tops(names))
    for names, *pair in end_second:
        far.update((n, (row, [(pair, 0), (pair, count)])) for row, n in tops(names))
    words = jnp.stack([away, group, inside, owner]).astype(jnp.int32)
    total_mine, total_theirs = assemble(
        words, count, features, part, near, far, chips, last[0]
    )
    from_partner = swap_cores(total_theirs)

    def pick(index, options):
        value = options[0]
        for at, option in enumerate(options[1:], 1):
            value = jnp.where(index == at, option, value)
        return value

    tail = {}
    for names, value, got in end_last:
        value = (value.astype(jnp.float32) + got.astype(jnp.float32)).astype(jnp.bfloat16)
        tail.update(
            (n, value[row : row + edges[n[0] + 1] - edges[n[0]]]) for row, n in tops(names)
        )
    late = sorted({(k, r) for k, _, r in tail})
    pieces = jnp.concatenate(
        [pick(away - 1, [tail[k, s, r] for s in range(1, chips)]) for k, r in late], axis=0
    )
    input_grad = finish(
        words,
        part,
        total_mine,
        from_partner,
        pieces[:, :count],
        swap_cores(pieces[:, count:]),
        late,
        chips,
    )
    return (input_grad, doc_logs)


def solution(mesh):
    placed = (
        P(("groups", "dp"), "tensor"),
        P(("groups", "dp"), "tensor"),
        P(("groups", "dp"), "tensor"),
        P(("groups", "dp"), "tensor"),
        P("dp", "tensor"),
        P("dp", "tensor"),
        P("tensor", None),
        P("tensor", None),
        P("tensor", None),
        P("tensor", None),
        P("tensor", None),
        P(("groups", "dp"), None),
    )
    return jax.shard_map(
        per_device,
        mesh=mesh,
        in_specs=placed,
        out_specs=(P(("groups", "dp"), "tensor"), P(("groups", "dp"), None, "tensor")),
        check_vma=False,
    )
```

```python
import functools

import jax
import jax.numpy as jnp
import numpy as np
from jax import lax
from jax.experimental import pallas as pl
from jax.experimental.pallas import tpu as pltpu
from jax.sharding import PartitionSpec as P

CORES = 2
CHUNKS = (2,) * 8
VMEM_BYTES = 60 * 1024 * 1024
FLOPS_PER_US = 270_000_000
ANYWHERE = pl.BlockSpec(memory_space=pl.ANY)


def contract_right(left, right):
    return lax.dot_general(
        left, right, (((1,), (1,)), ((), ())), preferred_element_type=jnp.float32
    )


def project(proj, rows):
    return lax.dot_general(
        proj, rows, (((0,), (1,)), ((), ())), preferred_element_type=jnp.float32
    )


def pack_table(doc_lengths, count):
    lengths = doc_lengths[0]
    ends = jnp.cumsum(lengths)
    starts = ends - lengths
    position = jnp.arange(count, dtype=jnp.int32)[None, :]
    inside = (position >= starts[:, None]) & (position < ends[:, None])
    return inside.astype(jnp.bfloat16)


def doc_outer(member, grad_rows, inputs):
    count = member.shape[1]
    weighted = (member[:, None, :] * grad_rows[None, :, :]).reshape(-1, count)
    table = contract_right(weighted, inputs)
    return table.reshape(member.shape[0], grad_rows.shape[0] * inputs.shape[0])


def swap_cores(value):
    size = lax.axis_size("dp")
    return lax.ppermute(value, "dp", [(i, i ^ 1) for i in range(size)])


def from_chip(value, shift):
    size = lax.axis_size("dp")
    step = shift * CORES
    return lax.ppermute(value, "dp", [((i + step) % size, i) for i in range(size)])


def from_group(value, shift):
    size = lax.axis_size("groups")
    return lax.ppermute(value, "groups", [((i + shift) % size, i) for i in range(size)])


def chunk_edges(part):
    return [part // 16 * sum(CHUNKS[:k]) for k in range(len(CHUNKS) + 1)]


def cost(us):
    return pl.CostEstimate(flops=int(us * FLOPS_PER_US) + 1, bytes_accessed=1, transcendentals=0)


def widest(size, options):
    return next((w for w in options if size % w == 0), size)


def share_rows(w_gate, w_up, group, spans, carried, after):
    rows, width = w_gate.shape
    part = rows // lax.axis_size("groups")
    step = part // 16
    kept, waits, fresh = len(carried), len(after), len(spans)
    steps = max([(last - first) // step for first, last in spans], default=1)

    def kernel(group_ref, *refs):
        outs = refs[len(refs) - fresh :] if fresh else []
        for at, out in enumerate(outs):
            out[0] = refs[2 * at][...]
            out[1] = refs[2 * at + 1][...]
        if not fresh:
            refs[-1][...] = jnp.zeros_like(refs[-1])

    in_specs, out_specs = [], [ANYWHERE] * kept
    shapes = [jax.ShapeDtypeStruct(a.shape, a.dtype) for a in carried]
    for first, last in spans:
        at_rows = functools.partial(lambda f, i, g: (g[0] * (part // step) + f // step + i, 0), first)
        in_specs += [pl.BlockSpec((step, width), at_rows)] * 2
        out_specs.append(pl.BlockSpec((2, step, width), lambda i, g: (0, i, 0)))
        shapes.append(jax.ShapeDtypeStruct((2, last - first, width), w_gate.dtype))
    if not fresh:
        out_specs.append(pl.BlockSpec((8, 128), lambda i, g: (0, 0)))
        shapes.append(jax.ShapeDtypeStruct((8, 128), jnp.float32))
    results = pl.pallas_call(
        kernel,
        grid_spec=pltpu.PrefetchScalarGridSpec(
            num_scalar_prefetch=1,
            grid=(steps,),
            in_specs=in_specs + [ANYWHERE] * (kept + waits),
            out_specs=out_specs,
        ),
        out_shape=shapes,
        input_output_aliases={1 + 2 * fresh + i: i for i in range(kept)},
        compiler_params=pltpu.CompilerParams(vmem_limit_bytes=VMEM_BYTES),
        cost_estimate=cost(2),
        name="share_rows",
    )(group, *[w_gate, w_up] * fresh, *carried, *after)
    return list(results[:kept]), list(results[kept:])


def spread_ranks(value):
    ranks = lax.axis_size("tensor")
    below, above = [value], [value]
    for _ in range(1, ranks):
        below.append(lax.ppermute(below[-1], "tensor", [(i, i + 1) for i in range(ranks - 1)]))
        above.append(lax.ppermute(above[-1], "tensor", [(i + 1, i) for i in range(ranks - 1)]))
    return below, above[1:]


def prepare(gate_act, up_act, proj_h, after):
    count, hidden = gate_act.shape
    narrow = proj_h.shape[0]
    tile = widest(hidden, (512, 256, 128))

    def kernel(gate_ref, up_ref, proj_ref, *refs):
        slope_ref, down_ref = refs[-2:]

        @pl.when(pl.program_id(0) == 0)
        def _():
            down_ref[...] = jnp.zeros_like(down_ref)

        gate = gate_ref[...].astype(jnp.float32).T
        up = up_ref[...].astype(jnp.float32).T
        sigma = jax.nn.sigmoid(gate)
        swish = gate * sigma
        slope_ref[0] = up * sigma * (1.0 + gate * (1.0 - sigma))
        slope_ref[1] = swish
        down_ref[...] += jnp.dot(
            proj_ref[...], (swish * up).astype(jnp.bfloat16), preferred_element_type=jnp.float32
        )

    return pl.pallas_call(
        kernel,
        grid=(hidden // tile,),
        out_shape=[
            jax.ShapeDtypeStruct((2, hidden, count), jnp.float32),
            jax.ShapeDtypeStruct((narrow, count), jnp.float32),
        ],
        in_specs=[
            pl.BlockSpec((count, tile), lambda i: (0, i)),
            pl.BlockSpec((count, tile), lambda i: (0, i)),
            pl.BlockSpec((narrow, tile), lambda i: (0, i)),
        ]
        + [ANYWHERE] * len(after),
        out_specs=[
            pl.BlockSpec((2, tile, count), lambda i: (0, i, 0)),
            pl.BlockSpec((narrow, count), lambda i: (0, 0)),
        ],
        compiler_params=pltpu.CompilerParams(vmem_limit_bytes=VMEM_BYTES),
        cost_estimate=cost(12),
        name="prepare",
    )(gate_act, up_act, proj_h, *after)


def hidden_part(rank, below, above, w_down, so_far, slopes, proj_u, after):
    ranks = lax.axis_size("tensor")
    features, count = below[0].shape
    hidden = w_down.shape[0]
    finish = so_far is not None
    slots = ranks - 2 if finish else 2
    tile = widest(hidden, (896, 512, 128))
    sources = [(t, -1, below[t]) for t in range(2 if finish else 0, ranks if finish else 2)]
    sources += [(t, 1, above[t - 1]) for t in range(1, ranks if finish else 2)]

    def counts(z):
        both = ((z >= 1) & (z <= ranks - 2)).astype(jnp.int32)
        return both, jnp.maximum(z - 1, 0)

    def place_of(z, t, side):
        if not finish:
            return (0, z >= 0) if t == 0 else (1, z >= 1 if side < 0 else z == 0)
        both, under = counts(z)
        if side < 0:
            return both + t - 2, t <= z
        if t == 1:
            return 0, both == 1
        return both + under + t - 2, z + t <= ranks - 1

    def column(at, i, rank_ref):
        z = rank_ref[0]
        if not finish:
            return (i, z) if at == 0 else (i, jnp.where(z >= 1, z - 1, 1))
        both, under = counts(z)
        block = jnp.where(at < both + under, z - (at - both + 2), z + (at - both - under + 2))
        return (i, jnp.where(at < both, z + 1, block))

    def kernel(rank_ref, *refs):
        z = rank_ref[0]
        downs, arrived = refs[:slots], refs[slots : slots + len(sources)]
        grad_ref, sem = refs[-2:]
        rest = refs[slots + len(sources) :]

        def gather(wait):
            for at, (t, side, _) in enumerate(sources):
                place, valid = place_of(z, t, side)

                @pl.when(valid)
                def _():
                    rows = pl.ds(pl.multiple_of(place * features, features), features)
                    copy = pltpu.make_async_copy(arrived[at], grad_ref.at[rows, :], sem.at[at])
                    copy.wait() if wait else copy.start()

        @pl.when(pl.program_id(0) == 0)
        def _():
            gather(False)
            gather(True)

        wide = None
        for at in range(slots):
            term = jnp.dot(
                downs[at][...],
                grad_ref[at * features : (at + 1) * features, :],
                preferred_element_type=jnp.float32,
            )
            wide = term if wide is None else wide + term
        if finish:
            both_ref, out_ref = refs[-4:-2]
            wide = wide + rest[0][...]
            both_ref[0] = (wide * rest[1][0]).astype(jnp.bfloat16)
            up_grad = (wide * rest[1][1]).astype(jnp.bfloat16)
            both_ref[1] = up_grad
            part = jnp.dot(rest[2][...], up_grad, preferred_element_type=jnp.float32)

            @pl.when(pl.program_id(0) == 0)
            def _():
                out_ref[...] = part

            @pl.when(pl.program_id(0) > 0)
            def _():
                out_ref[...] += part

        else:
            refs[-3][...] = wide

    operands = [w_down] * slots + [value for _, _, value in sources]
    specs = [pl.BlockSpec((tile, features), functools.partial(column, at)) for at in range(slots)]
    specs += [ANYWHERE] * len(sources)
    if finish:
        narrow = proj_u.shape[0]
        operands += [so_far, slopes, proj_u]
        specs += [
            pl.BlockSpec((tile, count), lambda i, r: (i, 0)),
            pl.BlockSpec((2, tile, count), lambda i, r: (0, i, 0)),
            pl.BlockSpec((narrow, tile), lambda i, r: (0, i)),
        ]
        out_shape = [
            jax.ShapeDtypeStruct((2, hidden, count), jnp.bfloat16),
            jax.ShapeDtypeStruct((narrow, count), jnp.float32),
        ]
        out_specs = [
            pl.BlockSpec((2, tile, count), lambda i, r: (0, i, 0)),
            pl.BlockSpec((narrow, count), lambda i, r: (0, 0)),
        ]
    else:
        out_shape = jax.ShapeDtypeStruct((hidden, count), jnp.float32)
        out_specs = pl.BlockSpec((tile, count), lambda i, r: (i, 0))
    return pl.pallas_call(
        kernel,
        grid_spec=pltpu.PrefetchScalarGridSpec(
            num_scalar_prefetch=1,
            grid=(hidden // tile,),
            in_specs=specs + [ANYWHERE] * len(after),
            out_specs=out_specs,
            scratch_shapes=[
                pltpu.VMEM((slots * features, count), jnp.bfloat16),
                pltpu.SemaphoreType.DMA((len(sources),)),
            ],
        ),
        out_shape=out_shape,
        compiler_params=pltpu.CompilerParams(vmem_limit_bytes=VMEM_BYTES),
        cost_estimate=cost(12),
        name="hidden_part",
    )(rank, *operands, *after)


def weigh(routes, grads, after, price, extra=None):
    hidden = grads[0].shape[1]
    tile = widest(hidden, (512, 256, 128))
    steps = hidden // tile
    heights = [sum(u[0].shape[-2] for u in units) for units in routes]
    rows, count = sum(heights), sum(g.shape[2] for g in grads)
    units = [u for route in routes for u in route]
    flat = [w for u in units for w in u]
    extras = [] if extra is None else [extra]

    def kernel(*refs):
        weights, both = list(refs[: len(flat)]), refs[len(flat) : len(flat) + len(grads)]
        more = refs[len(flat) + len(grads) : len(flat) + len(grads) + len(extras)]
        outs, total = refs[-1 - len(routes) - len(extras) : -1], refs[-1]
        at = pl.program_id(0)

        @pl.when(at == 0)
        def _():
            total[...] = jnp.zeros_like(total)

        gates, ups = [], []
        for u in units:
            mine, weights = weights[: len(u)], weights[len(u) :]
            gates.append(mine[0][...] if len(u) == 2 else mine[0][0])
            ups.append(mine[1][...] if len(u) == 2 else mine[0][1])
        gate, up = jnp.concatenate(gates, axis=0), jnp.concatenate(ups + [m[...] for m in more], axis=0)
        first = 0
        for ref in both:
            span = slice(first, first + ref.shape[2])
            by_up = jnp.dot(up, ref[1], preferred_element_type=jnp.float32)
            total[:rows, span] += (
                jnp.dot(gate, ref[0], preferred_element_type=jnp.float32) + by_up[:rows]
            )
            if more:
                total[rows:, span] += by_up[rows:]
            first += ref.shape[2]

        @pl.when(at == steps - 1)
        def _():
            top = 0
            for out, height in zip(outs, heights):
                out[...] = total[top : top + height].astype(jnp.bfloat16)
                top += height
            if more:
                outs[-1][...] = total[rows:]

    specs = []
    for w in flat:
        if w.ndim == 2:
            specs.append(pl.BlockSpec((w.shape[0], tile), lambda i: (0, i)))
        else:
            specs.append(pl.BlockSpec((2, w.shape[1], tile), lambda i: (0, 0, i)))
    for g in grads:
        specs.append(pl.BlockSpec((2, tile, g.shape[2]), lambda i: (0, i, 0)))
    shapes = [jax.ShapeDtypeStruct((h, count), jnp.bfloat16) for h in heights]
    for e in extras:
        specs.append(pl.BlockSpec((e.shape[0], tile), lambda i: (0, i)))
        shapes.append(jax.ShapeDtypeStruct((e.shape[0], count), jnp.float32))
    return pl.pallas_call(
        kernel,
        grid=(steps,),
        out_shape=shapes,
        in_specs=specs + [ANYWHERE] * len(after),
        out_specs=[pl.BlockSpec(s.shape, lambda i: (0, 0)) for s in shapes],
        scratch_shapes=[pltpu.VMEM((rows + sum(e.shape[0] for e in extras), count), jnp.float32)],
        compiler_params=pltpu.CompilerParams(vmem_limit_bytes=VMEM_BYTES),
        cost_estimate=cost(price),
        name="weigh_rows",
    )(*flat, *grads, *extras, *after)


def add(values, others, heights, after, price=2):
    pairs = len(values)
    flat = [h for hs in heights for h in hs]

    def kernel(*refs):
        outs = list(refs[len(refs) - len(flat) :])
        for at in range(pairs):
            top = 0
            for height in heights[at]:
                rows = slice(top, top + height)
                outs.pop(0)[...] = (
                    refs[at][rows].astype(jnp.float32) + refs[pairs + at][rows].astype(jnp.float32)
                ).astype(jnp.bfloat16)
                top += height

    count = values[0].shape[1]
    whole = pl.BlockSpec(memory_space=pltpu.VMEM)
    return pl.pallas_call(
        kernel,
        out_shape=[jax.ShapeDtypeStruct((h, count), jnp.bfloat16) for h in flat],
        in_specs=[whole] * (2 * pairs) + [ANYWHERE] * len(after),
        out_specs=[whole] * len(flat),
        compiler_params=pltpu.CompilerParams(vmem_limit_bytes=VMEM_BYTES),
        cost_estimate=cost(price),
        name="add_terms",
    )(*values, *others, *after)


def assemble(words, count, features, part, near, far, chips, after):
    groups = lax.axis_size("groups")
    height = near[0][0].shape[0]
    tall = features // part
    arrays, index = [], {}

    def at_of(value):
        if id(value) not in index:
            index[id(value)] = len(arrays)
            arrays.append(value)
        return index[id(value)]

    near_at = [[at_of(v) for v in pair] for pair in near]
    far_at = {n: (row, [at_of(v) for v in pair], first) for n, (row, pair, first) in far.items()}
    edges = chunk_edges(part)

    def kernel(words_ref, *refs):
        out = refs[-1]
        away, group, inside = words_ref[0], words_ref[1], words_ref[2]

        def total(pair, rows, cols):
            one, two = (refs[at][rows, cols].astype(jnp.float32) for at in pair)
            return (one + two).astype(jnp.bfloat16)

        for j in range(len(near)):

            @pl.when((away == 0) & (inside == j * height))
            def _(j=j):
                out[...] = total(near_at[j], slice(0, height), slice(0, count))

        for s in range(1, chips):
            for g in range(groups):
                for h in range(0, groups, tall):

                    @pl.when((away == s) & (group == g) & (inside == h * part))
                    def _(s=s, g=g, h=h):
                        for j in range(tall):
                            shift = (h + j - g) % groups
                            for k in range(len(CHUNKS)):
                                top = j * part + edges[k]
                                piece = edges[k + 1] - edges[k]
                                if (k, s, shift) in far_at:
                                    row, pair, first = far_at[k, s, shift]
                                    value = total(
                                        pair, slice(row, row + piece), slice(first, first + count)
                                    )
                                else:
                                    value = jnp.zeros((piece, count), jnp.bfloat16)
                                out[top : top + piece] = value

    whole = pl.BlockSpec(memory_space=pltpu.VMEM)
    return pl.pallas_call(
        kernel,
        out_shape=jax.ShapeDtypeStruct((features, count), jnp.bfloat16),
        in_specs=[pl.BlockSpec(memory_space=pltpu.SMEM)]
        + [whole] * len(arrays)
        + [ANYWHERE] * len(after),
        out_specs=whole,
        compiler_params=pltpu.CompilerParams(vmem_limit_bytes=VMEM_BYTES),
        cost_estimate=cost(5),
        name="assemble",
    )(words, *arrays, *after)


def finish(words, part, mine, theirs, late_mine, late_theirs, late, chips):
    features, count = mine.shape
    groups = lax.axis_size("groups")
    tall = features // part
    edges = chunk_edges(part)

    def kernel(words_ref, mine_ref, theirs_ref, late_mine_ref, late_theirs_ref, out_ref, rows_ref):
        away, group, inside = words_ref[0], words_ref[1], words_ref[2]
        for own, base, extra in ((1, mine_ref, late_mine_ref), (0, theirs_ref, late_theirs_ref)):

            @pl.when(words_ref[3] == own)
            def _(base=base, extra=extra):
                rows_ref[...] = base[...]
                for g in range(groups):
                    for h in range(0, groups, tall):

                        @pl.when((away > 0) & (group == g) & (inside == h * part))
                        def _(g=g, h=h):
                            for j in range(tall):
                                row = 0
                                for k, r in late:
                                    top, piece = j * part + edges[k], edges[k + 1] - edges[k]
                                    if (h + j - g) % groups == r:
                                        rows_ref[top : top + piece] = extra[row : row + piece]
                                    row += piece

        out_ref[...] = rows_ref[...].T

    return pl.pallas_call(
        kernel,
        out_shape=jax.ShapeDtypeStruct((count, features), mine.dtype),
        in_specs=[pl.BlockSpec(memory_space=pltpu.SMEM)] + [pl.BlockSpec(memory_space=pltpu.VMEM)] * 4,
        out_specs=pl.BlockSpec(memory_space=pltpu.VMEM),
        scratch_shapes=[pltpu.VMEM((features, count), mine.dtype)],
        compiler_params=pltpu.CompilerParams(vmem_limit_bytes=VMEM_BYTES),
        cost_estimate=cost(3),
        name="finish",
    )(words, mine, theirs, late_mine, late_theirs)


def exchange(value, bit):
    ranks = lax.axis_size("tensor")
    return lax.ppermute(value, "tensor", [(i, i ^ bit) for i in range(ranks)])


def halve(value, bit):
    half = value.shape[0] // 2
    high = lax.axis_index("tensor") & bit != 0
    low_rows, high_rows = value[:half], value[half:]
    got = exchange(jnp.where(high, low_rows, high_rows), bit)
    return jnp.where(high, high_rows, low_rows) + got


def hops(owner, bit):
    groups, ranks, blocks = (lax.axis_size(a) for a in ("groups", "tensor", "dp"))
    pairs = []
    for g in range(groups):
        for p in range(blocks):
            target = owner[g, p]
            for z in range(ranks):
                if z % bit == target % bit and (z ^ target) & bit:
                    pairs.append(((g * ranks + z) * blocks + p, (g * ranks + (z ^ bit)) * blocks + p))
    return pairs


def send(value, pairs):
    return lax.ppermute(value, ("groups", "tensor", "dp"), pairs)


def later_steps(values, owners):
    ranks = lax.axis_size("tensor")
    ends = []
    for value, owner in zip(values, owners):
        bit, got = 2, None
        while bit < ranks:
            if got is not None:
                (value,) = add([value], [got], [[value.shape[0]]], [])
            got = send(value, hops(owner, bit))
            bit *= 2
        ends.append((value, got))
    return ends


def per_device(
    layer_input,
    gate_act,
    up_act,
    out_grad,
    w_gate,
    w_up,
    w_down,
    proj_x,
    proj_u,
    proj_h,
    proj_g,
    doc_lengths,
):
    groups, ranks = lax.axis_size("groups"), lax.axis_size("tensor")
    blocks = lax.axis_size("dp")
    chips = blocks // CORES
    group, rank = lax.axis_index("groups"), lax.axis_index("tensor")
    place = lax.axis_index("dp")
    chip, core = place // CORES, place % CORES
    rows = w_gate.shape[0]
    count = layer_input.shape[0]
    features = out_grad.shape[1]
    part = rows // groups
    edges = chunk_edges(part)
    chunks = len(CHUNKS)
    split = max(1, ranks // blocks)
    group_word = jnp.full((1,), group, jnp.int32)
    rank_word = jnp.full((1,), rank, jnp.int32)

    below, above = spread_ranks(out_grad.T)
    spans = list(zip(edges, edges[1:]))
    _, shares = share_rows(w_gate, w_up, group_word, spans[:2], [], [])
    slopes, in_down_part = prepare(gate_act, up_act, proj_h.T, [shares[0]])
    early_part = jnp.concatenate([project(proj_x, layer_input), in_down_part], axis=0)
    out_down_part = project(proj_g, out_grad)
    fetched, ticks = {}, []

    def fetch(k):
        for s in range(1, chips):
            fetched[k, s, 0] = from_chip(shares[k], s)
            for r in range(1, groups):
                fetched[k, s, r] = from_group(fetched[k, s, 0], r)

    def forward(k, waits, after, held=()):
        names = [(k, 0)] + waits
        arrived = [fetched[n] for n in fetched if (n[0], n[2]) in names]
        arrived = [a for a in arrived if not any(a is h for h in held)]
        carried, fresh = share_rows(
            w_gate, w_up, group_word, spans[k + 2 : k + 3], list(held), arrived + list(after)
        )
        ticks.append(fresh[0])
        if k + 2 < chunks:
            shares.extend(fresh)
            fetch(k + 2)
        return carried

    def owner_of(s, first_of):
        table = np.zeros((groups, blocks), np.int64)
        for g in range(groups):
            for p in range(blocks):
                block = (p // CORES + s) % chips * CORES + p % CORES
                table[g, p] = (block * rows + first_of(g)) // features
        return table

    far_routes = []
    for s in range(1, chips):
        for r in range(groups):
            table = owner_of(s, lambda g: (g + r) % groups * part)
            for route in far_routes:
                if route[0] == s and (route[1] == table).all():
                    route[2].append(r)
                    break
            else:
                far_routes.append((s, table, [r]))
    height = rows // split
    near_tables = [owner_of(0, lambda g: j * height) for j in range(split)]
    near_routes = [
        [(w_gate[j * height : (j + 1) * height], w_up[j * height : (j + 1) * height])]
        for j in range(split)
    ]

    def terms(names, grads, after, price, near=False, extra=None):
        routes = list(zip(near_tables, near_routes, [None] * split)) if near else []
        for s, table, shifts in far_routes:
            units = [(k, s, q) for k, q in names if q in shifts]
            if units:
                routes.append((table, [(fetched[n],) for n in units], units))
        bundles = {}
        for route in routes:
            bundles.setdefault((route[0] % 2).tobytes(), []).append(route)
        bundles = list(bundles.values())
        joined = [[u for _, units, _ in b for u in units] for b in bundles]
        outs = list(weigh(joined, grads, after, price, extra))
        got = [send(out, hops(b[0][0], 1)) for out, b in zip(outs, bundles)]
        return outs, got, bundles

    def carry_on(work, after, price=2):
        outs, got, bundles = work
        heights = [[sum(u[0].shape[-2] for u in units) for _, units, _ in b] for b in bundles]
        sums = list(add(outs, got, heights, after, price))
        routes = [route for b in bundles for route in b]
        ends = later_steps(sums, [table for table, _, _ in routes])
        return sums, [(names, *end) for (_, _, names), end in zip(routes, ends)]

    fetch(0)
    fetch(1)

    def hold_arrived(k, waits, after, held=()):
        names = [(k, s, 0) for s in range(1, chips)]
        values = forward(k, waits, after, [fetched[n] for n in names] + list(held))
        for n, value in zip(names, values):
            fetched[n] = value
            for r in range(1, groups):
                fetched[k, n[1], r] = from_group(value, r)
        return values[len(names) :]

    def chunks_of(numbers, shifts):
        return [(k, r) for r in shifts for k in numbers]

    others = range(1, groups)
    bits = [1 << i for i in range(ranks.bit_length() - 1)]
    hold_arrived(0, [], [slopes])
    so_far = hidden_part(rank_word, below, above, w_down, None, None, None, [ticks[0]])
    hold_arrived(1, chunks_of([0], others), [so_far])
    hold_arrived(2, chunks_of([1], others), [below[2], above[1], early_part, out_down_part])
    (early,) = hold_arrived(3, chunks_of([2], others), below[3:] + above[2:], [early_part])
    mine, up_out_part = hidden_part(
        rank_word, below, above, w_down, so_far, slopes, proj_u.T, [ticks[3]]
    )
    early = early + exchange(early, bits[0])
    mine, early = forward(4, chunks_of([3], others) + [(5, 0)], [], [mine, early])
    theirs = swap_cores(mine)

    out_parts = jnp.stack([up_out_part, out_down_part]).reshape(2, ranks, -1, count)
    out_parts = out_parts.transpose(1, 0, 2, 3).reshape(-1, count)
    half = out_parts.shape[0] // 2
    high = rank & bits[-1] != 0
    width = early.shape[0]
    got = exchange(
        jnp.concatenate([early, jnp.where(high, out_parts[:half], out_parts[half:])], axis=0),
        bits[-1],
    )
    early = early + got[:width]
    out_parts = jnp.where(high, out_parts[half:], out_parts[:half]) + got[width:]
    for bit in bits[1:-1]:
        early = early + exchange(early, bit)

    first_names = chunks_of(range(5), [0]) + chunks_of(range(4), others)
    first_mine = terms(first_names, [mine], [ticks[4]], 32, near=True)
    (out_parts,) = forward(
        5, chunks_of([4], others) + [(6, 0)], first_mine[0] + [early], [out_parts]
    )
    first_theirs = terms(first_names, [theirs], [ticks[5]], 60, near=True)
    sums_mine, end_mine = carry_on(first_mine, first_theirs[0])
    forward(6, chunks_of([5], others) + [(7, 0)], first_theirs[0])
    second_names = chunks_of([5, 6, 7], [0]) + chunks_of([4, 5, 6], others)
    near_received = [got for names, _, got in end_mine if names is None]
    far_received = [got for names, _, got in end_mine if names is not None]
    second = terms(second_names, [mine, theirs], [ticks[6]] + far_received, 40)
    sums_theirs, end_theirs = carry_on(first_theirs, second[0] + near_received)

    last_names = chunks_of([7], others)
    come = [fetched[n] for n in fetched if (n[0], n[2]) in last_names]
    sums_second, end_second = carry_on(second, sums_theirs + come)
    last = terms(last_names, [mine, theirs], sums_second, 60)
    far_received = [got for names, _, got in end_theirs if names is not None]
    sums_last, end_last = carry_on(last, far_received, 8)

    (out_parts,), _ = share_rows(w_gate, w_up, group_word, [], [out_parts], sums_second)
    for bit in bits[-2::-1]:
        out_parts = halve(out_parts, bit)
    early = early.astype(jnp.bfloat16)
    width = in_down_part.shape[0]
    in_up, in_down = early[:width], early[width:]
    out_parts = out_parts.astype(jnp.bfloat16)
    slot = out_parts.shape[0] // 2
    up_out, out_down = out_parts[:slot], out_parts[slot:]
    member = pack_table(doc_lengths, count)
    doc_logs = jnp.stack(
        [doc_outer(member, up_out, in_up), doc_outer(member, out_down, in_down)], axis=1
    )

    first = rank * features
    away = (first // rows // CORES - chip) % chips
    owner = first // rows % CORES == core
    inside = first % rows
    def tops(names):
        sizes = [edges[n[0] + 1] - edges[n[0]] for n in names]
        return [(sum(sizes[:i]), n) for i, n in enumerate(names)]

    words = jnp.stack([away, group, inside, owner]).astype(jnp.int32)

    def assembled(end, first, after):
        near = [pair for names, *pair in end if names is None]
        far = {}
        for names, *pair in end:
            if names is not None:
                far.update((n, (row, pair, 0)) for row, n in tops(names))
        for names, *pair in end_second:
            far.update((n, (row, pair, first)) for row, n in tops(names))
        return assemble(words, count, features, part, near, far, chips, after)

    received = [got for _, _, got in end_last]
    total_theirs = assembled(end_theirs, count, received)
    total_mine = assembled(end_mine, 0, [total_theirs])
    from_partner = swap_cores(total_theirs)

    def pick(index, options):
        value = options[0]
        for at, option in enumerate(options[1:], 1):
            value = jnp.where(index == at, option, value)
        return value

    tail = {}
    for names, value, got in end_last:
        value = (value.astype(jnp.float32) + got.astype(jnp.float32)).astype(jnp.bfloat16)
        tail.update(
            (n, value[row : row + edges[n[0] + 1] - edges[n[0]]]) for row, n in tops(names)
        )
    late = sorted({(k, r) for k, _, r in tail})
    pieces = jnp.concatenate(
        [pick(away - 1, [tail[k, s, r] for s in range(1, chips)]) for k, r in late], axis=0
    )
    input_grad = finish(
        words,
        part,
        total_mine,
        from_partner,
        pieces[:, :count],
        swap_cores(pieces[:, count:]),
        late,
        chips,
    )
    return (input_grad, doc_logs)


def solution(mesh):
    placed = (
        P(("groups", "dp"), "tensor"),
        P(("groups", "dp"), "tensor"),
        P(("groups", "dp"), "tensor"),
        P(("groups", "dp"), "tensor"),
        P("dp", "tensor"),
        P("dp", "tensor"),
        P("tensor", None),
        P("tensor", None),
        P("tensor", None),
        P("tensor", None),
        P("tensor", None),
        P(("groups", "dp"), None),
    )
    return jax.shard_map(
        per_device,
        mesh=mesh,
        in_specs=placed,
        out_specs=(P(("groups", "dp"), "tensor"), P(("groups", "dp"), None, "tensor")),
        check_vma=False,
    )
```

```python
import functools

import jax
import jax.numpy as jnp
import numpy as np
from jax import lax
from jax.experimental import pallas as pl
from jax.experimental.pallas import tpu as pltpu
from jax.sharding import PartitionSpec as P

CORES = 2
CHUNKS = (2,) * 8
VMEM_BYTES = 60 * 1024 * 1024
FLOPS_PER_US = 270_000_000
ANYWHERE = pl.BlockSpec(memory_space=pl.ANY)


def contract_right(left, right):
    return lax.dot_general(
        left, right, (((1,), (1,)), ((), ())), preferred_element_type=jnp.float32
    )


def project(proj, rows):
    return lax.dot_general(
        proj, rows, (((0,), (1,)), ((), ())), preferred_element_type=jnp.float32
    )


def pack_table(doc_lengths, count):
    lengths = doc_lengths[0]
    ends = jnp.cumsum(lengths)
    starts = ends - lengths
    position = jnp.arange(count, dtype=jnp.int32)[None, :]
    inside = (position >= starts[:, None]) & (position < ends[:, None])
    return inside.astype(jnp.bfloat16)


def doc_outer(member, grad_rows, inputs):
    count = member.shape[1]
    weighted = (member[:, None, :] * grad_rows[None, :, :]).reshape(-1, count)
    table = contract_right(weighted, inputs)
    return table.reshape(member.shape[0], grad_rows.shape[0] * inputs.shape[0])


def swap_cores(value):
    size = lax.axis_size("dp")
    return lax.ppermute(value, "dp", [(i, i ^ 1) for i in range(size)])


def from_chip(value, shift):
    size = lax.axis_size("dp")
    step = shift * CORES
    return lax.ppermute(value, "dp", [((i + step) % size, i) for i in range(size)])


def from_group(value, shift):
    size = lax.axis_size("groups")
    return lax.ppermute(value, "groups", [((i + shift) % size, i) for i in range(size)])


def chunk_edges(part):
    return [part // 16 * sum(CHUNKS[:k]) for k in range(len(CHUNKS) + 1)]


def cost(us):
    return pl.CostEstimate(flops=int(us * FLOPS_PER_US) + 1, bytes_accessed=1, transcendentals=0)


def widest(size, options):
    return next((w for w in options if size % w == 0), size)


def share_rows(w_gate, w_up, group, spans, carried, after):
    rows, width = w_gate.shape
    part = rows // lax.axis_size("groups")
    step = part // 16
    kept, waits, fresh = len(carried), len(after), len(spans)
    steps = max([(last - first) // step for first, last in spans], default=1)

    def kernel(group_ref, *refs):
        outs = refs[len(refs) - fresh :] if fresh else []
        for at, out in enumerate(outs):
            out[0] = refs[2 * at][...]
            out[1] = refs[2 * at + 1][...]
        if not fresh:
            refs[-1][...] = jnp.zeros_like(refs[-1])

    in_specs, out_specs = [], [ANYWHERE] * kept
    shapes = [jax.ShapeDtypeStruct(a.shape, a.dtype) for a in carried]
    for first, last in spans:
        at_rows = functools.partial(lambda f, i, g: (g[0] * (part // step) + f // step + i, 0), first)
        in_specs += [pl.BlockSpec((step, width), at_rows)] * 2
        out_specs.append(pl.BlockSpec((2, step, width), lambda i, g: (0, i, 0)))
        shapes.append(jax.ShapeDtypeStruct((2, last - first, width), w_gate.dtype))
    if not fresh:
        out_specs.append(pl.BlockSpec((8, 128), lambda i, g: (0, 0)))
        shapes.append(jax.ShapeDtypeStruct((8, 128), jnp.float32))
    results = pl.pallas_call(
        kernel,
        grid_spec=pltpu.PrefetchScalarGridSpec(
            num_scalar_prefetch=1,
            grid=(steps,),
            in_specs=in_specs + [ANYWHERE] * (kept + waits),
            out_specs=out_specs,
        ),
        out_shape=shapes,
        input_output_aliases={1 + 2 * fresh + i: i for i in range(kept)},
        compiler_params=pltpu.CompilerParams(vmem_limit_bytes=VMEM_BYTES),
        cost_estimate=cost(2),
        name="share_rows",
    )(group, *[w_gate, w_up] * fresh, *carried, *after)
    return list(results[:kept]), list(results[kept:])


def spread_ranks(value):
    ranks = lax.axis_size("tensor")
    below, above = [value], [value]
    for _ in range(1, ranks):
        below.append(lax.ppermute(below[-1], "tensor", [(i, i + 1) for i in range(ranks - 1)]))
        above.append(lax.ppermute(above[-1], "tensor", [(i + 1, i) for i in range(ranks - 1)]))
    return below, above[1:]


def prepare(gate_act, up_act, proj_h, after):
    count, hidden = gate_act.shape
    narrow = proj_h.shape[0]
    tile = widest(hidden, (512, 256, 128))

    def kernel(gate_ref, up_ref, proj_ref, *refs):
        slope_ref, down_ref = refs[-2:]

        @pl.when(pl.program_id(0) == 0)
        def _():
            down_ref[...] = jnp.zeros_like(down_ref)

        gate = gate_ref[...].astype(jnp.float32).T
        up = up_ref[...].astype(jnp.float32).T
        sigma = jax.nn.sigmoid(gate)
        swish = gate * sigma
        slope_ref[0] = up * sigma * (1.0 + gate * (1.0 - sigma))
        slope_ref[1] = swish
        down_ref[...] += jnp.dot(
            proj_ref[...], (swish * up).astype(jnp.bfloat16), preferred_element_type=jnp.float32
        )

    return pl.pallas_call(
        kernel,
        grid=(hidden // tile,),
        out_shape=[
            jax.ShapeDtypeStruct((2, hidden, count), jnp.float32),
            jax.ShapeDtypeStruct((narrow, count), jnp.float32),
        ],
        in_specs=[
            pl.BlockSpec((count, tile), lambda i: (0, i)),
            pl.BlockSpec((count, tile), lambda i: (0, i)),
            pl.BlockSpec((narrow, tile), lambda i: (0, i)),
        ]
        + [ANYWHERE] * len(after),
        out_specs=[
            pl.BlockSpec((2, tile, count), lambda i: (0, i, 0)),
            pl.BlockSpec((narrow, count), lambda i: (0, 0)),
        ],
        compiler_params=pltpu.CompilerParams(vmem_limit_bytes=VMEM_BYTES),
        cost_estimate=cost(12),
        name="prepare",
    )(gate_act, up_act, proj_h, *after)


def hidden_part(rank, below, above, w_down, so_far, slopes, proj_u, after):
    ranks = lax.axis_size("tensor")
    features, count = below[0].shape
    hidden = w_down.shape[0]
    finish = so_far is not None
    slots = ranks - 2 if finish else 2
    tile = widest(hidden, (896, 512, 128))
    sources = [(t, -1, below[t]) for t in range(2 if finish else 0, ranks if finish else 2)]
    sources += [(t, 1, above[t - 1]) for t in range(1, ranks if finish else 2)]

    def counts(z):
        both = ((z >= 1) & (z <= ranks - 2)).astype(jnp.int32)
        return both, jnp.maximum(z - 1, 0)

    def place_of(z, t, side):
        if not finish:
            return (0, z >= 0) if t == 0 else (1, z >= 1 if side < 0 else z == 0)
        both, under = counts(z)
        if side < 0:
            return both + t - 2, t <= z
        if t == 1:
            return 0, both == 1
        return both + under + t - 2, z + t <= ranks - 1

    def column(at, i, rank_ref):
        z = rank_ref[0]
        if not finish:
            return (i, z) if at == 0 else (i, jnp.where(z >= 1, z - 1, 1))
        both, under = counts(z)
        block = jnp.where(at < both + under, z - (at - both + 2), z + (at - both - under + 2))
        return (i, jnp.where(at < both, z + 1, block))

    def kernel(rank_ref, *refs):
        z = rank_ref[0]
        downs, arrived = refs[:slots], refs[slots : slots + len(sources)]
        grad_ref, sem = refs[-2:]
        rest = refs[slots + len(sources) :]

        def gather(wait):
            for at, (t, side, _) in enumerate(sources):
                place, valid = place_of(z, t, side)

                @pl.when(valid)
                def _():
                    rows = pl.ds(pl.multiple_of(place * features, features), features)
                    copy = pltpu.make_async_copy(arrived[at], grad_ref.at[rows, :], sem.at[at])
                    copy.wait() if wait else copy.start()

        @pl.when(pl.program_id(0) == 0)
        def _():
            gather(False)
            gather(True)

        wide = None
        for at in range(slots):
            term = jnp.dot(
                downs[at][...],
                grad_ref[at * features : (at + 1) * features, :],
                preferred_element_type=jnp.float32,
            )
            wide = term if wide is None else wide + term
        if finish:
            both_ref, out_ref = refs[-4:-2]
            wide = wide + rest[0][...]
            both_ref[0] = (wide * rest[1][0]).astype(jnp.bfloat16)
            up_grad = (wide * rest[1][1]).astype(jnp.bfloat16)
            both_ref[1] = up_grad
            part = jnp.dot(rest[2][...], up_grad, preferred_element_type=jnp.float32)

            @pl.when(pl.program_id(0) == 0)
            def _():
                out_ref[...] = part

            @pl.when(pl.program_id(0) > 0)
            def _():
                out_ref[...] += part

        else:
            refs[-3][...] = wide

    operands = [w_down] * slots + [value for _, _, value in sources]
    specs = [pl.BlockSpec((tile, features), functools.partial(column, at)) for at in range(slots)]
    specs += [ANYWHERE] * len(sources)
    if finish:
        narrow = proj_u.shape[0]
        operands += [so_far, slopes, proj_u]
        specs += [
            pl.BlockSpec((tile, count), lambda i, r: (i, 0)),
            pl.BlockSpec((2, tile, count), lambda i, r: (0, i, 0)),
            pl.BlockSpec((narrow, tile), lambda i, r: (0, i)),
        ]
        out_shape = [
            jax.ShapeDtypeStruct((2, hidden, count), jnp.bfloat16),
            jax.ShapeDtypeStruct((narrow, count), jnp.float32),
        ]
        out_specs = [
            pl.BlockSpec((2, tile, count), lambda i, r: (0, i, 0)),
            pl.BlockSpec((narrow, count), lambda i, r: (0, 0)),
        ]
    else:
        out_shape = jax.ShapeDtypeStruct((hidden, count), jnp.float32)
        out_specs = pl.BlockSpec((tile, count), lambda i, r: (i, 0))
    return pl.pallas_call(
        kernel,
        grid_spec=pltpu.PrefetchScalarGridSpec(
            num_scalar_prefetch=1,
            grid=(hidden // tile,),
            in_specs=specs + [ANYWHERE] * len(after),
            out_specs=out_specs,
            scratch_shapes=[
                pltpu.VMEM((slots * features, count), jnp.bfloat16),
                pltpu.SemaphoreType.DMA((len(sources),)),
            ],
        ),
        out_shape=out_shape,
        compiler_params=pltpu.CompilerParams(vmem_limit_bytes=VMEM_BYTES),
        cost_estimate=cost(12),
        name="hidden_part",
    )(rank, *operands, *after)


def weigh(routes, grads, after, price, extra=None):
    hidden = grads[0].shape[1]
    tile = widest(hidden, (512, 256, 128))
    steps = hidden // tile
    heights = [sum(u[0].shape[-2] for u in units) for units in routes]
    rows, count = sum(heights), sum(g.shape[2] for g in grads)
    units = [u for route in routes for u in route]
    flat = [w for u in units for w in u]
    extras = [] if extra is None else [extra]

    def kernel(*refs):
        weights, both = list(refs[: len(flat)]), refs[len(flat) : len(flat) + len(grads)]
        more = refs[len(flat) + len(grads) : len(flat) + len(grads) + len(extras)]
        outs, total = refs[-1 - len(routes) - len(extras) : -1], refs[-1]
        at = pl.program_id(0)

        @pl.when(at == 0)
        def _():
            total[...] = jnp.zeros_like(total)

        gates, ups = [], []
        for u in units:
            mine, weights = weights[: len(u)], weights[len(u) :]
            gates.append(mine[0][...] if len(u) == 2 else mine[0][0])
            ups.append(mine[1][...] if len(u) == 2 else mine[0][1])
        gate, up = jnp.concatenate(gates, axis=0), jnp.concatenate(ups + [m[...] for m in more], axis=0)
        first = 0
        for ref in both:
            span = slice(first, first + ref.shape[2])
            by_up = jnp.dot(up, ref[1], preferred_element_type=jnp.float32)
            total[:rows, span] += (
                jnp.dot(gate, ref[0], preferred_element_type=jnp.float32) + by_up[:rows]
            )
            if more:
                total[rows:, span] += by_up[rows:]
            first += ref.shape[2]

        @pl.when(at == steps - 1)
        def _():
            top = 0
            for out, height in zip(outs, heights):
                out[...] = total[top : top + height].astype(jnp.bfloat16)
                top += height
            if more:
                outs[-1][...] = total[rows:]

    specs = []
    for w in flat:
        if w.ndim == 2:
            specs.append(pl.BlockSpec((w.shape[0], tile), lambda i: (0, i)))
        else:
            specs.append(pl.BlockSpec((2, w.shape[1], tile), lambda i: (0, 0, i)))
    for g in grads:
        specs.append(pl.BlockSpec((2, tile, g.shape[2]), lambda i: (0, i, 0)))
    shapes = [jax.ShapeDtypeStruct((h, count), jnp.bfloat16) for h in heights]
    for e in extras:
        specs.append(pl.BlockSpec((e.shape[0], tile), lambda i: (0, i)))
        shapes.append(jax.ShapeDtypeStruct((e.shape[0], count), jnp.float32))
    return pl.pallas_call(
        kernel,
        grid=(steps,),
        out_shape=shapes,
        in_specs=specs + [ANYWHERE] * len(after),
        out_specs=[pl.BlockSpec(s.shape, lambda i: (0, 0)) for s in shapes],
        scratch_shapes=[pltpu.VMEM((rows + sum(e.shape[0] for e in extras), count), jnp.float32)],
        compiler_params=pltpu.CompilerParams(vmem_limit_bytes=VMEM_BYTES),
        cost_estimate=cost(price),
        name="weigh_rows",
    )(*flat, *grads, *extras, *after)


def add(values, others, heights, after, price=2):
    pairs = len(values)
    flat = [h for hs in heights for h in hs]

    def kernel(*refs):
        outs = list(refs[len(refs) - len(flat) :])
        for at in range(pairs):
            top = 0
            for height in heights[at]:
                rows = slice(top, top + height)
                outs.pop(0)[...] = (
                    refs[at][rows].astype(jnp.float32) + refs[pairs + at][rows].astype(jnp.float32)
                ).astype(jnp.bfloat16)
                top += height

    count = values[0].shape[1]
    whole = pl.BlockSpec(memory_space=pltpu.VMEM)
    return pl.pallas_call(
        kernel,
        out_shape=[jax.ShapeDtypeStruct((h, count), jnp.bfloat16) for h in flat],
        in_specs=[whole] * (2 * pairs) + [ANYWHERE] * len(after),
        out_specs=[whole] * len(flat),
        compiler_params=pltpu.CompilerParams(vmem_limit_bytes=VMEM_BYTES),
        cost_estimate=cost(price),
        name="add_terms",
    )(*values, *others, *after)


def assemble(words, count, features, part, near, far, chips, after):
    groups = lax.axis_size("groups")
    height = near[0][0].shape[0]
    tall = features // part
    arrays, index = [], {}

    def at_of(value):
        if id(value) not in index:
            index[id(value)] = len(arrays)
            arrays.append(value)
        return index[id(value)]

    near_at = [[at_of(v) for v in pair] for pair in near]
    far_at = {n: (row, [at_of(v) for v in pair], first) for n, (row, pair, first) in far.items()}
    edges = chunk_edges(part)

    def kernel(words_ref, *refs):
        out = refs[-1]
        away, group, inside = words_ref[0], words_ref[1], words_ref[2]

        def total(pair, rows, cols):
            one, two = (refs[at][rows, cols].astype(jnp.float32) for at in pair)
            return (one + two).astype(jnp.bfloat16)

        for j in range(len(near)):

            @pl.when((away == 0) & (inside == j * height))
            def _(j=j):
                out[...] = total(near_at[j], slice(0, height), slice(0, count))

        for s in range(1, chips):
            for g in range(groups):
                for h in range(0, groups, tall):

                    @pl.when((away == s) & (group == g) & (inside == h * part))
                    def _(s=s, g=g, h=h):
                        for j in range(tall):
                            shift = (h + j - g) % groups
                            for k in range(len(CHUNKS)):
                                top = j * part + edges[k]
                                piece = edges[k + 1] - edges[k]
                                if (k, s, shift) in far_at:
                                    row, pair, first = far_at[k, s, shift]
                                    value = total(
                                        pair, slice(row, row + piece), slice(first, first + count)
                                    )
                                else:
                                    value = jnp.zeros((piece, count), jnp.bfloat16)
                                out[top : top + piece] = value

    whole = pl.BlockSpec(memory_space=pltpu.VMEM)
    return pl.pallas_call(
        kernel,
        out_shape=jax.ShapeDtypeStruct((features, count), jnp.bfloat16),
        in_specs=[pl.BlockSpec(memory_space=pltpu.SMEM)]
        + [whole] * len(arrays)
        + [ANYWHERE] * len(after),
        out_specs=whole,
        compiler_params=pltpu.CompilerParams(vmem_limit_bytes=VMEM_BYTES),
        cost_estimate=cost(5),
        name="assemble",
    )(words, *arrays, *after)


def finish(words, part, mine, theirs, late_mine, late_theirs, late, chips):
    features, count = mine.shape
    groups = lax.axis_size("groups")
    tall = features // part
    edges = chunk_edges(part)

    def kernel(words_ref, mine_ref, theirs_ref, late_mine_ref, late_theirs_ref, out_ref, rows_ref):
        away, group, inside = words_ref[0], words_ref[1], words_ref[2]
        for own, base, extra in ((1, mine_ref, late_mine_ref), (0, theirs_ref, late_theirs_ref)):

            @pl.when(words_ref[3] == own)
            def _(base=base, extra=extra):
                rows_ref[...] = base[...]
                for g in range(groups):
                    for h in range(0, groups, tall):

                        @pl.when((away > 0) & (group == g) & (inside == h * part))
                        def _(g=g, h=h):
                            for j in range(tall):
                                row = 0
                                for k, r in late:
                                    top, piece = j * part + edges[k], edges[k + 1] - edges[k]
                                    if (h + j - g) % groups == r:
                                        rows_ref[top : top + piece] = extra[row : row + piece]
                                    row += piece

        out_ref[...] = rows_ref[...].T

    return pl.pallas_call(
        kernel,
        out_shape=jax.ShapeDtypeStruct((count, features), mine.dtype),
        in_specs=[pl.BlockSpec(memory_space=pltpu.SMEM)] + [pl.BlockSpec(memory_space=pltpu.VMEM)] * 4,
        out_specs=pl.BlockSpec(memory_space=pltpu.VMEM),
        scratch_shapes=[pltpu.VMEM((features, count), mine.dtype)],
        compiler_params=pltpu.CompilerParams(vmem_limit_bytes=VMEM_BYTES),
        cost_estimate=cost(3),
        name="finish",
    )(words, mine, theirs, late_mine, late_theirs)


def exchange(value, bit):
    ranks = lax.axis_size("tensor")
    return lax.ppermute(value, "tensor", [(i, i ^ bit) for i in range(ranks)])


def halve(value, bit):
    half = value.shape[0] // 2
    high = lax.axis_index("tensor") & bit != 0
    low_rows, high_rows = value[:half], value[half:]
    got = exchange(jnp.where(high, low_rows, high_rows), bit)
    return jnp.where(high, high_rows, low_rows) + got


def hops(owner, bit):
    groups, ranks, blocks = (lax.axis_size(a) for a in ("groups", "tensor", "dp"))
    pairs = []
    for g in range(groups):
        for p in range(blocks):
            target = owner[g, p]
            for z in range(ranks):
                if z % bit == target % bit and (z ^ target) & bit:
                    pairs.append(((g * ranks + z) * blocks + p, (g * ranks + (z ^ bit)) * blocks + p))
    return pairs


def send(value, pairs):
    return lax.ppermute(value, ("groups", "tensor", "dp"), pairs)


def later_steps(values, owners):
    ranks = lax.axis_size("tensor")
    if ranks == 4 and len(values) == 2:
        one, two = hops(owners[0], 2), hops(owners[1], 2)
        if all(not {x[i] for x in one} & {x[i] for x in two} for i in range(2)):
            rank, group, place = (lax.axis_index(a) for a in ("tensor", "groups", "dp"))
            target = jnp.asarray(owners[0], jnp.int32)[group, place]
            height = max(v.shape[0] for v in values)
            high = [jnp.pad(v, ((0, height - v.shape[0]), (0, 0))) for v in values]
            got = send(jnp.where((rank ^ target) & 2 != 0, *high), sorted(one + two))
            return [(v, got) for v in values]
    ends = []
    for value, owner in zip(values, owners):
        bit, got = 2, None
        while bit < ranks:
            if got is not None:
                (value,) = add([value], [got], [[value.shape[0]]], [])
            got = send(value, hops(owner, bit))
            bit *= 2
        ends.append((value, got))
    return ends


def per_device(
    layer_input,
    gate_act,
    up_act,
    out_grad,
    w_gate,
    w_up,
    w_down,
    proj_x,
    proj_u,
    proj_h,
    proj_g,
    doc_lengths,
):
    groups, ranks = lax.axis_size("groups"), lax.axis_size("tensor")
    blocks = lax.axis_size("dp")
    chips = blocks // CORES
    group, rank = lax.axis_index("groups"), lax.axis_index("tensor")
    place = lax.axis_index("dp")
    chip, core = place // CORES, place % CORES
    rows = w_gate.shape[0]
    count = layer_input.shape[0]
    features = out_grad.shape[1]
    part = rows // groups
    edges = chunk_edges(part)
    chunks = len(CHUNKS)
    split = max(1, ranks // blocks)
    group_word = jnp.full((1,), group, jnp.int32)
    rank_word = jnp.full((1,), rank, jnp.int32)

    below, above = spread_ranks(out_grad.T)
    spans = list(zip(edges, edges[1:]))
    _, shares = share_rows(w_gate, w_up, group_word, spans[:2], [], [])
    slopes, in_down_part = prepare(gate_act, up_act, proj_h.T, [shares[0]])
    early_part = jnp.concatenate([project(proj_x, layer_input), in_down_part], axis=0)
    out_down_part = project(proj_g, out_grad)
    fetched, ticks = {}, []

    def fetch(k):
        for s in range(1, chips):
            fetched[k, s, 0] = from_chip(shares[k], s)
            for r in range(1, groups):
                fetched[k, s, r] = from_group(fetched[k, s, 0], r)

    def forward(k, waits, after, held=()):
        names = [(k, 0)] + waits
        arrived = [fetched[n] for n in fetched if (n[0], n[2]) in names]
        arrived = [a for a in arrived if not any(a is h for h in held)]
        carried, fresh = share_rows(
            w_gate, w_up, group_word, spans[k + 2 : k + 3], list(held), arrived + list(after)
        )
        ticks.append(fresh[0])
        if k + 2 < chunks:
            shares.extend(fresh)
            fetch(k + 2)
        return carried

    def owner_of(s, first_of):
        table = np.zeros((groups, blocks), np.int64)
        for g in range(groups):
            for p in range(blocks):
                block = (p // CORES + s) % chips * CORES + p % CORES
                table[g, p] = (block * rows + first_of(g)) // features
        return table

    far_routes = []
    for s in range(1, chips):
        for r in range(groups):
            table = owner_of(s, lambda g: (g + r) % groups * part)
            for route in far_routes:
                if route[0] == s and (route[1] == table).all():
                    route[2].append(r)
                    break
            else:
                far_routes.append((s, table, [r]))
    height = rows // split
    near_tables = [owner_of(0, lambda g: j * height) for j in range(split)]
    near_routes = [
        [(w_gate[j * height : (j + 1) * height], w_up[j * height : (j + 1) * height])]
        for j in range(split)
    ]

    def terms(names, grads, after, price, near=False, extra=None):
        routes = list(zip(near_tables, near_routes, [None] * split)) if near else []
        for s, table, shifts in far_routes:
            units = [(k, s, q) for k, q in names if q in shifts]
            if units:
                routes.append((table, [(fetched[n],) for n in units], units))
        bundles = {}
        for route in routes:
            bundles.setdefault((route[0] % 2).tobytes(), []).append(route)
        bundles = list(bundles.values())
        joined = [[u for _, units, _ in b for u in units] for b in bundles]
        outs = list(weigh(joined, grads, after, price, extra))
        got = [send(out, hops(b[0][0], 1)) for out, b in zip(outs, bundles)]
        return outs, got, bundles

    def carry_on(works, after, price=2):
        outs, got, bundles = ([v for work in works for v in work[i]] for i in range(3))
        heights = [[sum(u[0].shape[-2] for u in units) for _, units, _ in b] for b in bundles]
        sums = list(add(outs, got, heights, after, price))
        routes = [route for b in bundles for route in b]
        ends = later_steps(sums, [table for table, _, _ in routes])
        return sums, [(names, *end) for (_, _, names), end in zip(routes, ends)]

    fetch(0)
    fetch(1)

    def hold_arrived(k, waits, after, held=()):
        names = [(k, s, 0) for s in range(1, chips)]
        values = forward(k, waits, after, [fetched[n] for n in names] + list(held))
        for n, value in zip(names, values):
            fetched[n] = value
            for r in range(1, groups):
                fetched[k, n[1], r] = from_group(value, r)
        return values[len(names) :]

    def chunks_of(numbers, shifts):
        return [(k, r) for r in shifts for k in numbers]

    others = range(1, groups)
    bits = [1 << i for i in range(ranks.bit_length() - 1)]
    hold_arrived(0, [], [slopes])
    so_far = hidden_part(rank_word, below, above, w_down, None, None, None, [ticks[0]])
    hold_arrived(1, chunks_of([0], others), [so_far])
    hold_arrived(2, chunks_of([1], others), [below[2], above[1], early_part, out_down_part])
    (early,) = hold_arrived(3, chunks_of([2], others), below[3:] + above[2:], [early_part])
    mine, up_out_part = hidden_part(
        rank_word, below, above, w_down, so_far, slopes, proj_u.T, [ticks[3]]
    )
    early = early + exchange(early, bits[0])
    mine, early = forward(4, chunks_of([3], others) + [(5, 0)], [], [mine, early])
    theirs = swap_cores(mine)

    out_parts = jnp.stack([up_out_part, out_down_part]).reshape(2, ranks, -1, count)
    out_parts = out_parts.transpose(1, 0, 2, 3).reshape(-1, count)
    half = out_parts.shape[0] // 2
    high = rank & bits[-1] != 0
    width = early.shape[0]
    got = exchange(
        jnp.concatenate([early, jnp.where(high, out_parts[:half], out_parts[half:])], axis=0),
        bits[-1],
    )
    early = early + got[:width]
    out_parts = jnp.where(high, out_parts[half:], out_parts[:half]) + got[width:]
    for bit in bits[1:-1]:
        early = early + exchange(early, bit)

    first_names = chunks_of(range(5), [0]) + chunks_of(range(4), others)
    first_mine = terms(first_names, [mine], [ticks[4]], 32, near=True)
    (out_parts,) = forward(
        5, chunks_of([4], others) + [(6, 0)], first_mine[0] + [early], [out_parts]
    )
    near_theirs = terms([], [theirs], [ticks[5]], 44, near=True)
    sums_mine, end_mine = carry_on([first_mine], near_theirs[0])
    far_theirs = terms(first_names, [theirs], sums_mine, 40)
    forward(6, chunks_of([5], others) + [(7, 0)], far_theirs[0])
    come = [fetched[n] for n in fetched if n[0] == 6 and n[2] > 0]
    sums_theirs, end_theirs = carry_on([near_theirs, far_theirs], [ticks[6]] + come)
    second_names = chunks_of([5, 6, 7], [0]) + chunks_of([4, 5, 6], others)
    last_names = chunks_of([7], others)
    received = [got for _, _, got in end_mine]
    second = terms(second_names, [mine, theirs], [ticks[6]] + sums_theirs + received, 40)
    come = [fetched[n] for n in fetched if (n[0], n[2]) in last_names]
    come += [got for _, _, got in end_theirs]
    sums_second, end_second = carry_on([second], come)
    last = terms(last_names, [mine, theirs], sums_second, 60)
    sums_last, end_last = carry_on([last], [], 8)

    (out_parts,), _ = share_rows(w_gate, w_up, group_word, [], [out_parts], sums_second)
    for bit in bits[-2::-1]:
        out_parts = halve(out_parts, bit)
    early = early.astype(jnp.bfloat16)
    width = in_down_part.shape[0]
    in_up, in_down = early[:width], early[width:]
    out_parts = out_parts.astype(jnp.bfloat16)
    slot = out_parts.shape[0] // 2
    up_out, out_down = out_parts[:slot], out_parts[slot:]
    member = pack_table(doc_lengths, count)
    doc_logs = jnp.stack(
        [doc_outer(member, up_out, in_up), doc_outer(member, out_down, in_down)], axis=1
    )

    first = rank * features
    away = (first // rows // CORES - chip) % chips
    owner = first // rows % CORES == core
    inside = first % rows
    def tops(names):
        sizes = [edges[n[0] + 1] - edges[n[0]] for n in names]
        return [(sum(sizes[:i]), n) for i, n in enumerate(names)]

    words = jnp.stack([away, group, inside, owner]).astype(jnp.int32)

    def assembled(end, first, after):
        near = [pair for names, *pair in end if names is None]
        far = {}
        for names, *pair in end:
            if names is not None:
                far.update((n, (row, pair, 0)) for row, n in tops(names))
        for names, *pair in end_second:
            far.update((n, (row, pair, first)) for row, n in tops(names))
        return assemble(words, count, features, part, near, far, chips, after)

    received = [got for _, _, got in end_last]
    total_theirs = assembled(end_theirs, count, received)
    total_mine = assembled(end_mine, 0, [total_theirs])
    from_partner = swap_cores(total_theirs)

    def pick(index, options):
        value = options[0]
        for at, option in enumerate(options[1:], 1):
            value = jnp.where(index == at, option, value)
        return value

    tail = {}
    for names, value, got in end_last:
        value = (value.astype(jnp.float32) + got.astype(jnp.float32)).astype(jnp.bfloat16)
        tail.update(
            (n, value[row : row + edges[n[0] + 1] - edges[n[0]]]) for row, n in tops(names)
        )
    late = sorted({(k, r) for k, _, r in tail})
    pieces = jnp.concatenate(
        [pick(away - 1, [tail[k, s, r] for s in range(1, chips)]) for k, r in late], axis=0
    )
    input_grad = finish(
        words,
        part,
        total_mine,
        from_partner,
        pieces[:, :count],
        swap_cores(pieces[:, count:]),
        late,
        chips,
    )
    return (input_grad, doc_logs)


def solution(mesh):
    placed = (
        P(("groups", "dp"), "tensor"),
        P(("groups", "dp"), "tensor"),
        P(("groups", "dp"), "tensor"),
        P(("groups", "dp"), "tensor"),
        P("dp", "tensor"),
        P("dp", "tensor"),
        P("tensor", None),
        P("tensor", None),
        P("tensor", None),
        P("tensor", None),
        P("tensor", None),
        P(("groups", "dp"), None),
    )
    return jax.shard_map(
        per_device,
        mesh=mesh,
        in_specs=placed,
        out_specs=(P(("groups", "dp"), "tensor"), P(("groups", "dp"), None, "tensor")),
        check_vma=False,
    )
```

```python
import functools

import jax
import jax.numpy as jnp
import numpy as np
from jax import lax
from jax.experimental import pallas as pl
from jax.experimental.pallas import tpu as pltpu
from jax.sharding import PartitionSpec as P

CORES = 2
CHUNKS = (2,) * 8
VMEM_BYTES = 60 * 1024 * 1024
FLOPS_PER_US = 270_000_000
ANYWHERE = pl.BlockSpec(memory_space=pl.ANY)


def contract_right(left, right):
    return lax.dot_general(
        left, right, (((1,), (1,)), ((), ())), preferred_element_type=jnp.float32
    )


def project(proj, rows):
    return lax.dot_general(
        proj, rows, (((0,), (1,)), ((), ())), preferred_element_type=jnp.float32
    )


def pack_table(doc_lengths, count):
    lengths = doc_lengths[0]
    ends = jnp.cumsum(lengths)
    starts = ends - lengths
    position = jnp.arange(count, dtype=jnp.int32)[None, :]
    inside = (position >= starts[:, None]) & (position < ends[:, None])
    return inside.astype(jnp.bfloat16)


def doc_outer(member, grad_rows, inputs):
    count = member.shape[1]
    weighted = (member[:, None, :] * grad_rows[None, :, :]).reshape(-1, count)
    table = contract_right(weighted, inputs)
    return table.reshape(member.shape[0], grad_rows.shape[0] * inputs.shape[0])


def swap_cores(value):
    size = lax.axis_size("dp")
    return lax.ppermute(value, "dp", [(i, i ^ 1) for i in range(size)])


def from_chip(value, shift):
    size = lax.axis_size("dp")
    step = shift * CORES
    return lax.ppermute(value, "dp", [((i + step) % size, i) for i in range(size)])


def from_group(value, shift):
    size = lax.axis_size("groups")
    return lax.ppermute(value, "groups", [((i + shift) % size, i) for i in range(size)])


def chunk_edges(part):
    return [part // 16 * sum(CHUNKS[:k]) for k in range(len(CHUNKS) + 1)]


def cost(us):
    return pl.CostEstimate(flops=int(us * FLOPS_PER_US) + 1, bytes_accessed=1, transcendentals=0)


def widest(size, options):
    return next((w for w in options if size % w == 0), size)


def share_rows(w_gate, w_up, group, spans, carried, after):
    rows, width = w_gate.shape
    part = rows // lax.axis_size("groups")
    step = part // 16
    kept, waits, fresh = len(carried), len(after), len(spans)
    steps = max([(last - first) // step for first, last in spans], default=1)

    def kernel(group_ref, *refs):
        outs = refs[len(refs) - fresh :] if fresh else []
        for at, out in enumerate(outs):
            out[0] = refs[2 * at][...]
            out[1] = refs[2 * at + 1][...]
        if not fresh:
            refs[-1][...] = jnp.zeros_like(refs[-1])

    in_specs, out_specs = [], [ANYWHERE] * kept
    shapes = [jax.ShapeDtypeStruct(a.shape, a.dtype) for a in carried]
    for first, last in spans:
        at_rows = functools.partial(lambda f, i, g: (g[0] * (part // step) + f // step + i, 0), first)
        in_specs += [pl.BlockSpec((step, width), at_rows)] * 2
        out_specs.append(pl.BlockSpec((2, step, width), lambda i, g: (0, i, 0)))
        shapes.append(jax.ShapeDtypeStruct((2, last - first, width), w_gate.dtype))
    if not fresh:
        out_specs.append(pl.BlockSpec((8, 128), lambda i, g: (0, 0)))
        shapes.append(jax.ShapeDtypeStruct((8, 128), jnp.float32))
    results = pl.pallas_call(
        kernel,
        grid_spec=pltpu.PrefetchScalarGridSpec(
            num_scalar_prefetch=1,
            grid=(steps,),
            in_specs=in_specs + [ANYWHERE] * (kept + waits),
            out_specs=out_specs,
        ),
        out_shape=shapes,
        input_output_aliases={1 + 2 * fresh + i: i for i in range(kept)},
        compiler_params=pltpu.CompilerParams(vmem_limit_bytes=VMEM_BYTES),
        cost_estimate=cost(2),
        name="share_rows",
    )(group, *[w_gate, w_up] * fresh, *carried, *after)
    return list(results[:kept]), list(results[kept:])


def spread_ranks(value):
    ranks = lax.axis_size("tensor")
    below, above = [value], [value]
    for _ in range(1, ranks):
        below.append(lax.ppermute(below[-1], "tensor", [(i, i + 1) for i in range(ranks - 1)]))
        above.append(lax.ppermute(above[-1], "tensor", [(i + 1, i) for i in range(ranks - 1)]))
    return below, above[1:]


def prepare(gate_act, up_act, proj_h, after):
    count, hidden = gate_act.shape
    narrow = proj_h.shape[0]
    tile = widest(hidden, (512, 256, 128))

    def kernel(gate_ref, up_ref, proj_ref, *refs):
        slope_ref, down_ref = refs[-2:]

        @pl.when(pl.program_id(0) == 0)
        def _():
            down_ref[...] = jnp.zeros_like(down_ref)

        gate = gate_ref[...].astype(jnp.float32).T
        up = up_ref[...].astype(jnp.float32).T
        sigma = jax.nn.sigmoid(gate)
        swish = gate * sigma
        slope_ref[0] = up * sigma * (1.0 + gate * (1.0 - sigma))
        slope_ref[1] = swish
        down_ref[...] += jnp.dot(
            proj_ref[...], (swish * up).astype(jnp.bfloat16), preferred_element_type=jnp.float32
        )

    return pl.pallas_call(
        kernel,
        grid=(hidden // tile,),
        out_shape=[
            jax.ShapeDtypeStruct((2, hidden, count), jnp.float32),
            jax.ShapeDtypeStruct((narrow, count), jnp.float32),
        ],
        in_specs=[
            pl.BlockSpec((count, tile), lambda i: (0, i)),
            pl.BlockSpec((count, tile), lambda i: (0, i)),
            pl.BlockSpec((narrow, tile), lambda i: (0, i)),
        ]
        + [ANYWHERE] * len(after),
        out_specs=[
            pl.BlockSpec((2, tile, count), lambda i: (0, i, 0)),
            pl.BlockSpec((narrow, count), lambda i: (0, 0)),
        ],
        compiler_params=pltpu.CompilerParams(vmem_limit_bytes=VMEM_BYTES),
        cost_estimate=cost(12),
        name="prepare",
    )(gate_act, up_act, proj_h, *after)


def hidden_part(rank, below, above, w_down, so_far, slopes, proj_u, after):
    ranks = lax.axis_size("tensor")
    features, count = below[0].shape
    hidden = w_down.shape[0]
    finish = so_far is not None
    slots = ranks - 2 if finish else 2
    tile = widest(hidden, (896, 512, 128))
    sources = [(t, -1, below[t]) for t in range(2 if finish else 0, ranks if finish else 2)]
    sources += [(t, 1, above[t - 1]) for t in range(1, ranks if finish else 2)]

    def counts(z):
        both = ((z >= 1) & (z <= ranks - 2)).astype(jnp.int32)
        return both, jnp.maximum(z - 1, 0)

    def place_of(z, t, side):
        if not finish:
            return (0, z >= 0) if t == 0 else (1, z >= 1 if side < 0 else z == 0)
        both, under = counts(z)
        if side < 0:
            return both + t - 2, t <= z
        if t == 1:
            return 0, both == 1
        return both + under + t - 2, z + t <= ranks - 1

    def column(at, i, rank_ref):
        z = rank_ref[0]
        if not finish:
            return (i, z) if at == 0 else (i, jnp.where(z >= 1, z - 1, 1))
        both, under = counts(z)
        block = jnp.where(at < both + under, z - (at - both + 2), z + (at - both - under + 2))
        return (i, jnp.where(at < both, z + 1, block))

    def kernel(rank_ref, *refs):
        z = rank_ref[0]
        downs, arrived = refs[:slots], refs[slots : slots + len(sources)]
        grad_ref, sem = refs[-2:]
        rest = refs[slots + len(sources) :]

        def gather(wait):
            for at, (t, side, _) in enumerate(sources):
                place, valid = place_of(z, t, side)

                @pl.when(valid)
                def _():
                    rows = pl.ds(pl.multiple_of(place * features, features), features)
                    copy = pltpu.make_async_copy(arrived[at], grad_ref.at[rows, :], sem.at[at])
                    copy.wait() if wait else copy.start()

        @pl.when(pl.program_id(0) == 0)
        def _():
            gather(False)
            gather(True)

        wide = None
        for at in range(slots):
            term = jnp.dot(
                downs[at][...],
                grad_ref[at * features : (at + 1) * features, :],
                preferred_element_type=jnp.float32,
            )
            wide = term if wide is None else wide + term
        if finish:
            both_ref, out_ref = refs[-4:-2]
            wide = wide + rest[0][...]
            both_ref[0] = (wide * rest[1][0]).astype(jnp.bfloat16)
            up_grad = (wide * rest[1][1]).astype(jnp.bfloat16)
            both_ref[1] = up_grad
            part = jnp.dot(rest[2][...], up_grad, preferred_element_type=jnp.float32)

            @pl.when(pl.program_id(0) == 0)
            def _():
                out_ref[...] = part

            @pl.when(pl.program_id(0) > 0)
            def _():
                out_ref[...] += part

        else:
            refs[-3][...] = wide

    operands = [w_down] * slots + [value for _, _, value in sources]
    specs = [pl.BlockSpec((tile, features), functools.partial(column, at)) for at in range(slots)]
    specs += [ANYWHERE] * len(sources)
    if finish:
        narrow = proj_u.shape[0]
        operands += [so_far, slopes, proj_u]
        specs += [
            pl.BlockSpec((tile, count), lambda i, r: (i, 0)),
            pl.BlockSpec((2, tile, count), lambda i, r: (0, i, 0)),
            pl.BlockSpec((narrow, tile), lambda i, r: (0, i)),
        ]
        out_shape = [
            jax.ShapeDtypeStruct((2, hidden, count), jnp.bfloat16),
            jax.ShapeDtypeStruct((narrow, count), jnp.float32),
        ]
        out_specs = [
            pl.BlockSpec((2, tile, count), lambda i, r: (0, i, 0)),
            pl.BlockSpec((narrow, count), lambda i, r: (0, 0)),
        ]
    else:
        out_shape = jax.ShapeDtypeStruct((hidden, count), jnp.float32)
        out_specs = pl.BlockSpec((tile, count), lambda i, r: (i, 0))
    return pl.pallas_call(
        kernel,
        grid_spec=pltpu.PrefetchScalarGridSpec(
            num_scalar_prefetch=1,
            grid=(hidden // tile,),
            in_specs=specs + [ANYWHERE] * len(after),
            out_specs=out_specs,
            scratch_shapes=[
                pltpu.VMEM((slots * features, count), jnp.bfloat16),
                pltpu.SemaphoreType.DMA((len(sources),)),
            ],
        ),
        out_shape=out_shape,
        compiler_params=pltpu.CompilerParams(vmem_limit_bytes=VMEM_BYTES),
        cost_estimate=cost(12),
        name="hidden_part",
    )(rank, *operands, *after)


def weigh(routes, grads, after, price, extra=None):
    hidden = grads[0].shape[1]
    tile = widest(hidden, (512, 256, 128))
    steps = hidden // tile
    heights = [sum(u[0].shape[-2] for u in units) for units in routes]
    rows, count = sum(heights), sum(g.shape[2] for g in grads)
    units = [u for route in routes for u in route]
    flat = [w for u in units for w in u]
    extras = [] if extra is None else [extra]

    def kernel(*refs):
        weights, both = list(refs[: len(flat)]), refs[len(flat) : len(flat) + len(grads)]
        more = refs[len(flat) + len(grads) : len(flat) + len(grads) + len(extras)]
        outs, total = refs[-1 - len(routes) - len(extras) : -1], refs[-1]
        at = pl.program_id(0)

        @pl.when(at == 0)
        def _():
            total[...] = jnp.zeros_like(total)

        gates, ups = [], []
        for u in units:
            mine, weights = weights[: len(u)], weights[len(u) :]
            gates.append(mine[0][...] if len(u) == 2 else mine[0][0])
            ups.append(mine[1][...] if len(u) == 2 else mine[0][1])
        gate, up = jnp.concatenate(gates, axis=0), jnp.concatenate(ups + [m[...] for m in more], axis=0)
        first = 0
        for ref in both:
            span = slice(first, first + ref.shape[2])
            by_up = jnp.dot(up, ref[1], preferred_element_type=jnp.float32)
            total[:rows, span] += (
                jnp.dot(gate, ref[0], preferred_element_type=jnp.float32) + by_up[:rows]
            )
            if more:
                total[rows:, span] += by_up[rows:]
            first += ref.shape[2]

        @pl.when(at == steps - 1)
        def _():
            top = 0
            for out, height in zip(outs, heights):
                out[...] = total[top : top + height].astype(jnp.bfloat16)
                top += height
            if more:
                outs[-1][...] = total[rows:]

    specs = []
    for w in flat:
        if w.ndim == 2:
            specs.append(pl.BlockSpec((w.shape[0], tile), lambda i: (0, i)))
        else:
            specs.append(pl.BlockSpec((2, w.shape[1], tile), lambda i: (0, 0, i)))
    for g in grads:
        specs.append(pl.BlockSpec((2, tile, g.shape[2]), lambda i: (0, i, 0)))
    shapes = [jax.ShapeDtypeStruct((h, count), jnp.bfloat16) for h in heights]
    for e in extras:
        specs.append(pl.BlockSpec((e.shape[0], tile), lambda i: (0, i)))
        shapes.append(jax.ShapeDtypeStruct((e.shape[0], count), jnp.float32))
    return pl.pallas_call(
        kernel,
        grid=(steps,),
        out_shape=shapes,
        in_specs=specs + [ANYWHERE] * len(after),
        out_specs=[pl.BlockSpec(s.shape, lambda i: (0, 0)) for s in shapes],
        scratch_shapes=[pltpu.VMEM((rows + sum(e.shape[0] for e in extras), count), jnp.float32)],
        compiler_params=pltpu.CompilerParams(vmem_limit_bytes=VMEM_BYTES),
        cost_estimate=cost(price),
        name="weigh_rows",
    )(*flat, *grads, *extras, *after)


def add(values, others, heights, after, price=2):
    pairs = len(values)
    flat = [h for hs in heights for h in hs]

    def kernel(*refs):
        outs = list(refs[len(refs) - len(flat) :])
        for at in range(pairs):
            top = 0
            for height in heights[at]:
                rows = slice(top, top + height)
                outs.pop(0)[...] = (
                    refs[at][rows].astype(jnp.float32) + refs[pairs + at][rows].astype(jnp.float32)
                ).astype(jnp.bfloat16)
                top += height

    count = values[0].shape[1]
    whole = pl.BlockSpec(memory_space=pltpu.VMEM)
    return pl.pallas_call(
        kernel,
        out_shape=[jax.ShapeDtypeStruct((h, count), jnp.bfloat16) for h in flat],
        in_specs=[whole] * (2 * pairs) + [ANYWHERE] * len(after),
        out_specs=[whole] * len(flat),
        compiler_params=pltpu.CompilerParams(vmem_limit_bytes=VMEM_BYTES),
        cost_estimate=cost(price),
        name="add_terms",
    )(*values, *others, *after)


def assemble(words, count, features, part, near, far, chips, after):
    groups = lax.axis_size("groups")
    height = near[0][0].shape[0]
    tall = features // part
    arrays, index = [], {}

    def at_of(value):
        if id(value) not in index:
            index[id(value)] = len(arrays)
            arrays.append(value)
        return index[id(value)]

    near_at = [[at_of(v) for v in pair] for pair in near]
    far_at = {n: (row, [at_of(v) for v in pair], first) for n, (row, pair, first) in far.items()}
    edges = chunk_edges(part)

    def kernel(words_ref, *refs):
        out = refs[-1]
        away, group, inside = words_ref[0], words_ref[1], words_ref[2]

        def total(pair, rows, cols):
            one, two = (refs[at][rows, cols].astype(jnp.float32) for at in pair)
            return (one + two).astype(jnp.bfloat16)

        for j in range(len(near)):

            @pl.when((away == 0) & (inside == j * height))
            def _(j=j):
                out[...] = total(near_at[j], slice(0, height), slice(0, count))

        for s in range(1, chips):
            for g in range(groups):
                for h in range(0, groups, tall):

                    @pl.when((away == s) & (group == g) & (inside == h * part))
                    def _(s=s, g=g, h=h):
                        for j in range(tall):
                            shift = (h + j - g) % groups
                            for k in range(len(CHUNKS)):
                                top = j * part + edges[k]
                                piece = edges[k + 1] - edges[k]
                                if (k, s, shift) in far_at:
                                    row, pair, first = far_at[k, s, shift]
                                    value = total(
                                        pair, slice(row, row + piece), slice(first, first + count)
                                    )
                                else:
                                    value = jnp.zeros((piece, count), jnp.bfloat16)
                                out[top : top + piece] = value

    whole = pl.BlockSpec(memory_space=pltpu.VMEM)
    return pl.pallas_call(
        kernel,
        out_shape=jax.ShapeDtypeStruct((features, count), jnp.bfloat16),
        in_specs=[pl.BlockSpec(memory_space=pltpu.SMEM)]
        + [whole] * len(arrays)
        + [ANYWHERE] * len(after),
        out_specs=whole,
        compiler_params=pltpu.CompilerParams(vmem_limit_bytes=VMEM_BYTES),
        cost_estimate=cost(5),
        name="assemble",
    )(words, *arrays, *after)


def finish(words, part, mine, theirs, late_mine, late_theirs, late, chips):
    features, count = mine.shape
    groups = lax.axis_size("groups")
    tall = features // part
    edges = chunk_edges(part)

    def kernel(words_ref, mine_ref, theirs_ref, late_mine_ref, late_theirs_ref, out_ref, rows_ref):
        away, group, inside = words_ref[0], words_ref[1], words_ref[2]
        for own, base, extra in ((1, mine_ref, late_mine_ref), (0, theirs_ref, late_theirs_ref)):

            @pl.when(words_ref[3] == own)
            def _(base=base, extra=extra):
                rows_ref[...] = base[...]
                for g in range(groups):
                    for h in range(0, groups, tall):

                        @pl.when((away > 0) & (group == g) & (inside == h * part))
                        def _(g=g, h=h):
                            for j in range(tall):
                                row = 0
                                for k, r in late:
                                    top, piece = j * part + edges[k], edges[k + 1] - edges[k]
                                    if (h + j - g) % groups == r:
                                        rows_ref[top : top + piece] = extra[row : row + piece]
                                    row += piece

        out_ref[...] = rows_ref[...].T

    return pl.pallas_call(
        kernel,
        out_shape=jax.ShapeDtypeStruct((count, features), mine.dtype),
        in_specs=[pl.BlockSpec(memory_space=pltpu.SMEM)] + [pl.BlockSpec(memory_space=pltpu.VMEM)] * 4,
        out_specs=pl.BlockSpec(memory_space=pltpu.VMEM),
        scratch_shapes=[pltpu.VMEM((features, count), mine.dtype)],
        compiler_params=pltpu.CompilerParams(vmem_limit_bytes=VMEM_BYTES),
        cost_estimate=cost(3),
        name="finish",
    )(words, mine, theirs, late_mine, late_theirs)


def exchange(value, bit):
    ranks = lax.axis_size("tensor")
    got = lax.ppermute(value.astype(jnp.bfloat16), "tensor", [(i, i ^ bit) for i in range(ranks)])
    return got.astype(jnp.float32)


def halve(value, bit):
    half = value.shape[0] // 2
    high = lax.axis_index("tensor") & bit != 0
    low_rows, high_rows = value[:half], value[half:]
    got = exchange(jnp.where(high, low_rows, high_rows), bit)
    return jnp.where(high, high_rows, low_rows) + got


def hops(owner, bit):
    groups, ranks, blocks = (lax.axis_size(a) for a in ("groups", "tensor", "dp"))
    pairs = []
    for g in range(groups):
        for p in range(blocks):
            target = owner[g, p]
            for z in range(ranks):
                if z % bit == target % bit and (z ^ target) & bit:
                    pairs.append(((g * ranks + z) * blocks + p, (g * ranks + (z ^ bit)) * blocks + p))
    return pairs


def send(value, pairs):
    return lax.ppermute(value, ("groups", "tensor", "dp"), pairs)


def later_steps(values, owners, at_once):
    ranks = lax.axis_size("tensor")
    if at_once and ranks == 4 and len(values) == 2:
        one, two = hops(owners[0], 2), hops(owners[1], 2)
        if all(not {x[i] for x in one} & {x[i] for x in two} for i in range(2)):
            rank, group, place = (lax.axis_index(a) for a in ("tensor", "groups", "dp"))
            target = jnp.asarray(owners[0], jnp.int32)[group, place]
            height = max(v.shape[0] for v in values)
            high = [jnp.pad(v, ((0, height - v.shape[0]), (0, 0))) for v in values]
            got = send(jnp.where((rank ^ target) & 2 != 0, *high), sorted(one + two))
            return [(v, got) for v in values]
    ends = []
    for value, owner in zip(values, owners):
        bit, got = 2, None
        while bit < ranks:
            if got is not None:
                (value,) = add([value], [got], [[value.shape[0]]], [])
            got = send(value, hops(owner, bit))
            bit *= 2
        ends.append((value, got))
    return ends


def per_device(
    layer_input,
    gate_act,
    up_act,
    out_grad,
    w_gate,
    w_up,
    w_down,
    proj_x,
    proj_u,
    proj_h,
    proj_g,
    doc_lengths,
):
    groups, ranks = lax.axis_size("groups"), lax.axis_size("tensor")
    blocks = lax.axis_size("dp")
    chips = blocks // CORES
    group, rank = lax.axis_index("groups"), lax.axis_index("tensor")
    place = lax.axis_index("dp")
    chip, core = place // CORES, place % CORES
    rows = w_gate.shape[0]
    count = layer_input.shape[0]
    features = out_grad.shape[1]
    part = rows // groups
    edges = chunk_edges(part)
    chunks = len(CHUNKS)
    split = max(1, ranks // blocks)
    group_word = jnp.full((1,), group, jnp.int32)
    rank_word = jnp.full((1,), rank, jnp.int32)

    below, above = spread_ranks(out_grad.T)
    spans = list(zip(edges, edges[1:]))
    _, shares = share_rows(w_gate, w_up, group_word, spans[:2], [], [])
    slopes, in_down_part = prepare(gate_act, up_act, proj_h.T, [shares[0]])
    early_part = jnp.concatenate([project(proj_x, layer_input), in_down_part], axis=0)
    out_down_part = project(proj_g, out_grad)
    fetched, ticks = {}, []

    def fetch(k):
        for s in range(1, chips):
            fetched[k, s, 0] = from_chip(shares[k], s)
            for r in range(1, groups):
                fetched[k, s, r] = from_group(fetched[k, s, 0], r)

    def forward(k, waits, after, held=()):
        names = [(k, 0)] + waits
        arrived = [fetched[n] for n in fetched if (n[0], n[2]) in names]
        arrived = [a for a in arrived if not any(a is h for h in held)]
        carried, fresh = share_rows(
            w_gate, w_up, group_word, spans[k + 2 : k + 3], list(held), arrived + list(after)
        )
        ticks.append(fresh[0])
        if k + 2 < chunks:
            shares.extend(fresh)
            fetch(k + 2)
        return carried

    def owner_of(s, first_of):
        table = np.zeros((groups, blocks), np.int64)
        for g in range(groups):
            for p in range(blocks):
                block = (p // CORES + s) % chips * CORES + p % CORES
                table[g, p] = (block * rows + first_of(g)) // features
        return table

    far_routes = []
    for s in range(1, chips):
        for r in range(groups):
            table = owner_of(s, lambda g: (g + r) % groups * part)
            for route in far_routes:
                if route[0] == s and (route[1] == table).all():
                    route[2].append(r)
                    break
            else:
                far_routes.append((s, table, [r]))
    height = rows // split
    near_tables = [owner_of(0, lambda g: j * height) for j in range(split)]
    near_routes = [
        [(w_gate[j * height : (j + 1) * height], w_up[j * height : (j + 1) * height])]
        for j in range(split)
    ]

    def terms(names, grads, after, price, near=False, extra=None):
        routes = list(zip(near_tables, near_routes, [None] * split)) if near else []
        for s, table, shifts in far_routes:
            units = [(k, s, q) for k, q in names if q in shifts]
            if units:
                routes.append((table, [(fetched[n],) for n in units], units))
        bundles = {}
        for route in routes:
            bundles.setdefault((route[0] % 2).tobytes(), []).append(route)
        bundles = list(bundles.values())
        joined = [[u for _, units, _ in b for u in units] for b in bundles]
        outs = list(weigh(joined, grads, after, price, extra))
        got = [send(out, hops(b[0][0], 1)) for out, b in zip(outs, bundles)]
        return outs, got, bundles

    def carry_on(works, after, price=2, at_once=False):
        outs, got, bundles = ([v for work in works for v in work[i]] for i in range(3))
        heights = [[sum(u[0].shape[-2] for u in units) for _, units, _ in b] for b in bundles]
        sums = list(add(outs, got, heights, after, price))
        routes = [route for b in bundles for route in b]
        ends = later_steps(sums, [table for table, _, _ in routes], at_once)
        return sums, [(names, *end) for (_, _, names), end in zip(routes, ends)]

    fetch(0)
    fetch(1)

    def hold_arrived(k, waits, after, held=()):
        names = [(k, s, 0) for s in range(1, chips)]
        values = forward(k, waits, after, [fetched[n] for n in names] + list(held))
        for n, value in zip(names, values):
            fetched[n] = value
            for r in range(1, groups):
                fetched[k, n[1], r] = from_group(value, r)
        return values[len(names) :]

    def chunks_of(numbers, shifts):
        return [(k, r) for r in shifts for k in numbers]

    others = range(1, groups)
    bits = [1 << i for i in range(ranks.bit_length() - 1)]
    hold_arrived(0, [], [slopes])
    so_far = hidden_part(rank_word, below, above, w_down, None, None, None, [ticks[0]])
    hold_arrived(1, chunks_of([0], others), [so_far])
    hold_arrived(2, chunks_of([1], others), [below[2], above[1], out_down_part, early_part])
    mine, up_out_part = hidden_part(
        rank_word, below, above, w_down, so_far, slopes, proj_u.T, [ticks[2]]
    )
    mine, early = forward(3, chunks_of([2, 3], others) + [(4, 0)], [], [mine, early_part])
    theirs = swap_cores(mine)
    early = early + exchange(early, bits[0])
    first_names = chunks_of(range(5), [0]) + chunks_of(range(4), others)
    near_mine = terms([], [mine], [ticks[3]], 24, near=True)
    early, up_out_part = forward(
        4, chunks_of([4], others) + [(5, 0)], near_mine[0], [early, up_out_part]
    )

    out_parts = jnp.stack([up_out_part, out_down_part]).reshape(2, ranks, -1, count)
    out_parts = out_parts.transpose(1, 0, 2, 3).reshape(-1, count)
    half = out_parts.shape[0] // 2
    high = rank & bits[-1] != 0
    width = early.shape[0]
    got = exchange(
        jnp.concatenate([early, jnp.where(high, out_parts[:half], out_parts[half:])], axis=0),
        bits[-1],
    )
    early = early + got[:width]
    out_parts = jnp.where(high, out_parts[half:], out_parts[:half]) + got[width:]
    for bit in bits[1:-1]:
        early = early + exchange(early, bit)

    far_mine = terms(first_names, [mine], [ticks[4]], 6)
    near_theirs = terms([], [theirs], far_mine[0] + [early], 11, near=True)
    held = forward(
        5, chunks_of([5], others), near_theirs[0], [fetched[6, s, 0] for s in range(1, chips)]
    )
    for s, value in enumerate(held, 1):
        fetched[6, s, 0] = value
        for r in range(1, groups):
            fetched[6, s, r] = from_group(value, r)
    sums_mine, end_mine = carry_on([near_mine, far_mine], near_theirs[0], at_once=True)
    far_theirs = terms(first_names, [theirs], [ticks[5]] + sums_mine, 16)
    (out_parts,) = forward(
        6, chunks_of([6], others) + [(7, 0)], far_theirs[0], [out_parts]
    )
    second_names = chunks_of([5, 6], [0]) + chunks_of([4, 5], others)
    last_names = chunks_of([7], [0]) + chunks_of([6, 7], others)
    second = terms(second_names, [mine, theirs], [ticks[6]], 9)
    received = [got for _, _, got in end_mine]
    sums_theirs, end_theirs = carry_on([near_theirs, far_theirs], second[0] + received)
    sums_second, end_second = carry_on([second], sums_theirs)
    last = terms(last_names, [mine, theirs], sums_second, 60)
    received = [got for names, _, got in end_theirs + end_second if names is not None]
    sums_last, end_last = carry_on([last], received, 2)

    for bit in bits[-2::-1]:
        out_parts = halve(out_parts, bit)
    early = early.astype(jnp.bfloat16)
    width = in_down_part.shape[0]
    in_up, in_down = early[:width], early[width:]
    out_parts = out_parts.astype(jnp.bfloat16)
    slot = out_parts.shape[0] // 2
    up_out, out_down = out_parts[:slot], out_parts[slot:]
    member = pack_table(doc_lengths, count)
    doc_logs = jnp.stack(
        [doc_outer(member, up_out, in_up), doc_outer(member, out_down, in_down)], axis=1
    )

    first = rank * features
    away = (first // rows // CORES - chip) % chips
    owner = first // rows % CORES == core
    inside = first % rows
    def tops(names):
        sizes = [edges[n[0] + 1] - edges[n[0]] for n in names]
        return [(sum(sizes[:i]), n) for i, n in enumerate(names)]

    words = jnp.stack([away, group, inside, owner]).astype(jnp.int32)

    def assembled(end, first, after):
        near = [pair for names, *pair in end if names is None]
        far = {}
        for names, *pair in end:
            if names is not None:
                far.update((n, (row, pair, 0)) for row, n in tops(names))
        for names, *pair in end_second:
            far.update((n, (row, pair, first)) for row, n in tops(names))
        return assemble(words, count, features, part, near, far, chips, after)

    received = [got for _, _, got in end_last]
    total_theirs = assembled(end_theirs, count, received)
    total_mine = assembled(end_mine, 0, [total_theirs])
    from_partner = swap_cores(total_theirs)

    def pick(index, options):
        value = options[0]
        for at, option in enumerate(options[1:], 1):
            value = jnp.where(index == at, option, value)
        return value

    tail = {}
    for names, value, got in end_last:
        value = (value.astype(jnp.float32) + got.astype(jnp.float32)).astype(jnp.bfloat16)
        tail.update(
            (n, value[row : row + edges[n[0] + 1] - edges[n[0]]]) for row, n in tops(names)
        )
    late = sorted({(k, r) for k, _, r in tail})
    pieces = jnp.concatenate(
        [pick(away - 1, [tail[k, s, r] for s in range(1, chips)]) for k, r in late], axis=0
    )
    input_grad = finish(
        words,
        part,
        total_mine,
        from_partner,
        pieces[:, :count],
        swap_cores(pieces[:, count:]),
        late,
        chips,
    )
    return (input_grad, doc_logs)


def solution(mesh):
    placed = (
        P(("groups", "dp"), "tensor"),
        P(("groups", "dp"), "tensor"),
        P(("groups", "dp"), "tensor"),
        P(("groups", "dp"), "tensor"),
        P("dp", "tensor"),
        P("dp", "tensor"),
        P("tensor", None),
        P("tensor", None),
        P("tensor", None),
        P("tensor", None),
        P("tensor", None),
        P(("groups", "dp"), None),
    )
    return jax.shard_map(
        per_device,
        mesh=mesh,
        in_specs=placed,
        out_specs=(P(("groups", "dp"), "tensor"), P(("groups", "dp"), None, "tensor")),
        check_vma=False,
    )
```

```python
import functools

import jax
import jax.numpy as jnp
import numpy as np
from jax import lax
from jax.experimental import pallas as pl
from jax.experimental.pallas import tpu as pltpu
from jax.sharding import PartitionSpec as P

CORES = 2
CHUNKS = (2,) * 8
VMEM_BYTES = 60 * 1024 * 1024
FLOPS_PER_US = 270_000_000
ANYWHERE = pl.BlockSpec(memory_space=pl.ANY)


def contract_right(left, right):
    return lax.dot_general(
        left, right, (((1,), (1,)), ((), ())), preferred_element_type=jnp.float32
    )


def project(proj, rows):
    return lax.dot_general(
        proj, rows, (((0,), (1,)), ((), ())), preferred_element_type=jnp.float32
    )


def pack_table(doc_lengths, count):
    lengths = doc_lengths[0]
    ends = jnp.cumsum(lengths)
    starts = ends - lengths
    position = jnp.arange(count, dtype=jnp.int32)[None, :]
    inside = (position >= starts[:, None]) & (position < ends[:, None])
    return inside.astype(jnp.bfloat16)


def doc_outer(member, grad_rows, inputs):
    count = member.shape[1]
    weighted = (member[:, None, :] * grad_rows[None, :, :]).reshape(-1, count)
    table = contract_right(weighted, inputs)
    return table.reshape(member.shape[0], grad_rows.shape[0] * inputs.shape[0])


def swap_cores(value):
    size = lax.axis_size("dp")
    return lax.ppermute(value, "dp", [(i, i ^ 1) for i in range(size)])


def from_chip(value, shift):
    size = lax.axis_size("dp")
    step = shift * CORES
    return lax.ppermute(value, "dp", [((i + step) % size, i) for i in range(size)])


def from_group(value, shift):
    size = lax.axis_size("groups")
    return lax.ppermute(value, "groups", [((i + shift) % size, i) for i in range(size)])


def chunk_edges(part):
    return [part // 16 * sum(CHUNKS[:k]) for k in range(len(CHUNKS) + 1)]


def cost(us):
    return pl.CostEstimate(flops=int(us * FLOPS_PER_US) + 1, bytes_accessed=1, transcendentals=0)


def widest(size, options):
    return next((w for w in options if size % w == 0), size)


def share_rows(w_gate, w_up, group, spans, carried, after):
    rows, width = w_gate.shape
    part = rows // lax.axis_size("groups")
    step = part // 16
    kept, waits, fresh = len(carried), len(after), len(spans)
    steps = max([(last - first) // step for first, last in spans], default=1)

    def kernel(group_ref, *refs):
        outs = refs[len(refs) - fresh :] if fresh else []
        for at, out in enumerate(outs):
            out[0] = refs[2 * at][...]
            out[1] = refs[2 * at + 1][...]
        if not fresh:
            refs[-1][...] = jnp.zeros_like(refs[-1])

    in_specs, out_specs = [], [ANYWHERE] * kept
    shapes = [jax.ShapeDtypeStruct(a.shape, a.dtype) for a in carried]
    for first, last in spans:
        at_rows = functools.partial(lambda f, i, g: (g[0] * (part // step) + f // step + i, 0), first)
        in_specs += [pl.BlockSpec((step, width), at_rows)] * 2
        out_specs.append(pl.BlockSpec((2, step, width), lambda i, g: (0, i, 0)))
        shapes.append(jax.ShapeDtypeStruct((2, last - first, width), w_gate.dtype))
    if not fresh:
        out_specs.append(pl.BlockSpec((8, 128), lambda i, g: (0, 0)))
        shapes.append(jax.ShapeDtypeStruct((8, 128), jnp.float32))
    results = pl.pallas_call(
        kernel,
        grid_spec=pltpu.PrefetchScalarGridSpec(
            num_scalar_prefetch=1,
            grid=(steps,),
            in_specs=in_specs + [ANYWHERE] * (kept + waits),
            out_specs=out_specs,
        ),
        out_shape=shapes,
        input_output_aliases={1 + 2 * fresh + i: i for i in range(kept)},
        compiler_params=pltpu.CompilerParams(vmem_limit_bytes=VMEM_BYTES),
        cost_estimate=cost(2),
        name="share_rows",
    )(group, *[w_gate, w_up] * fresh, *carried, *after)
    return list(results[:kept]), list(results[kept:])


def spread_ranks(value):
    ranks = lax.axis_size("tensor")
    below, above = [value], [value]
    for _ in range(1, ranks):
        below.append(lax.ppermute(below[-1], "tensor", [(i, i + 1) for i in range(ranks - 1)]))
        above.append(lax.ppermute(above[-1], "tensor", [(i + 1, i) for i in range(ranks - 1)]))
    return below, above[1:]


def prepare(gate_act, up_act, proj_h, after):
    count, hidden = gate_act.shape
    narrow = proj_h.shape[0]
    tile = widest(hidden, (512, 256, 128))

    def kernel(gate_ref, up_ref, proj_ref, *refs):
        slope_ref, down_ref = refs[-2:]

        @pl.when(pl.program_id(0) == 0)
        def _():
            down_ref[...] = jnp.zeros_like(down_ref)

        gate = gate_ref[...].astype(jnp.float32).T
        up = up_ref[...].astype(jnp.float32).T
        sigma = jax.nn.sigmoid(gate)
        swish = gate * sigma
        slope_ref[0] = up * sigma * (1.0 + gate * (1.0 - sigma))
        slope_ref[1] = swish
        down_ref[...] += jnp.dot(
            proj_ref[...], (swish * up).astype(jnp.bfloat16), preferred_element_type=jnp.float32
        )

    return pl.pallas_call(
        kernel,
        grid=(hidden // tile,),
        out_shape=[
            jax.ShapeDtypeStruct((2, hidden, count), jnp.float32),
            jax.ShapeDtypeStruct((narrow, count), jnp.float32),
        ],
        in_specs=[
            pl.BlockSpec((count, tile), lambda i: (0, i)),
            pl.BlockSpec((count, tile), lambda i: (0, i)),
            pl.BlockSpec((narrow, tile), lambda i: (0, i)),
        ]
        + [ANYWHERE] * len(after),
        out_specs=[
            pl.BlockSpec((2, tile, count), lambda i: (0, i, 0)),
            pl.BlockSpec((narrow, count), lambda i: (0, 0)),
        ],
        compiler_params=pltpu.CompilerParams(vmem_limit_bytes=VMEM_BYTES),
        cost_estimate=cost(12),
        name="prepare",
    )(gate_act, up_act, proj_h, *after)


def hidden_part(rank, below, above, w_down, so_far, slopes, proj_u, after):
    ranks = lax.axis_size("tensor")
    features, count = below[0].shape
    hidden = w_down.shape[0]
    finish = so_far is not None
    slots = ranks - 2 if finish else 2
    tile = widest(hidden, (896, 512, 128))
    sources = [(t, -1, below[t]) for t in range(2 if finish else 0, ranks if finish else 2)]
    sources += [(t, 1, above[t - 1]) for t in range(1, ranks if finish else 2)]

    def counts(z):
        both = ((z >= 1) & (z <= ranks - 2)).astype(jnp.int32)
        return both, jnp.maximum(z - 1, 0)

    def place_of(z, t, side):
        if not finish:
            return (0, z >= 0) if t == 0 else (1, z >= 1 if side < 0 else z == 0)
        both, under = counts(z)
        if side < 0:
            return both + t - 2, t <= z
        if t == 1:
            return 0, both == 1
        return both + under + t - 2, z + t <= ranks - 1

    def column(at, i, rank_ref):
        z = rank_ref[0]
        if not finish:
            return (i, z) if at == 0 else (i, jnp.where(z >= 1, z - 1, 1))
        both, under = counts(z)
        block = jnp.where(at < both + under, z - (at - both + 2), z + (at - both - under + 2))
        return (i, jnp.where(at < both, z + 1, block))

    def kernel(rank_ref, *refs):
        z = rank_ref[0]
        downs, arrived = refs[:slots], refs[slots : slots + len(sources)]
        grad_ref, sem = refs[-2:]
        rest = refs[slots + len(sources) :]

        def gather(wait):
            for at, (t, side, _) in enumerate(sources):
                place, valid = place_of(z, t, side)

                @pl.when(valid)
                def _():
                    rows = pl.ds(pl.multiple_of(place * features, features), features)
                    copy = pltpu.make_async_copy(arrived[at], grad_ref.at[rows, :], sem.at[at])
                    copy.wait() if wait else copy.start()

        @pl.when(pl.program_id(0) == 0)
        def _():
            gather(False)
            gather(True)

        wide = None
        for at in range(slots):
            term = jnp.dot(
                downs[at][...],
                grad_ref[at * features : (at + 1) * features, :],
                preferred_element_type=jnp.float32,
            )
            wide = term if wide is None else wide + term
        if finish:
            both_ref, out_ref = refs[-4:-2]
            wide = wide + rest[0][...]
            both_ref[0] = (wide * rest[1][0]).astype(jnp.bfloat16)
            up_grad = (wide * rest[1][1]).astype(jnp.bfloat16)
            both_ref[1] = up_grad
            part = jnp.dot(rest[2][...], up_grad, preferred_element_type=jnp.float32)

            @pl.when(pl.program_id(0) == 0)
            def _():
                out_ref[...] = part

            @pl.when(pl.program_id(0) > 0)
            def _():
                out_ref[...] += part

        else:
            refs[-3][...] = wide

    operands = [w_down] * slots + [value for _, _, value in sources]
    specs = [pl.BlockSpec((tile, features), functools.partial(column, at)) for at in range(slots)]
    specs += [ANYWHERE] * len(sources)
    if finish:
        narrow = proj_u.shape[0]
        operands += [so_far, slopes, proj_u]
        specs += [
            pl.BlockSpec((tile, count), lambda i, r: (i, 0)),
            pl.BlockSpec((2, tile, count), lambda i, r: (0, i, 0)),
            pl.BlockSpec((narrow, tile), lambda i, r: (0, i)),
        ]
        out_shape = [
            jax.ShapeDtypeStruct((2, hidden, count), jnp.bfloat16),
            jax.ShapeDtypeStruct((narrow, count), jnp.float32),
        ]
        out_specs = [
            pl.BlockSpec((2, tile, count), lambda i, r: (0, i, 0)),
            pl.BlockSpec((narrow, count), lambda i, r: (0, 0)),
        ]
    else:
        out_shape = jax.ShapeDtypeStruct((hidden, count), jnp.float32)
        out_specs = pl.BlockSpec((tile, count), lambda i, r: (i, 0))
    return pl.pallas_call(
        kernel,
        grid_spec=pltpu.PrefetchScalarGridSpec(
            num_scalar_prefetch=1,
            grid=(hidden // tile,),
            in_specs=specs + [ANYWHERE] * len(after),
            out_specs=out_specs,
            scratch_shapes=[
                pltpu.VMEM((slots * features, count), jnp.bfloat16),
                pltpu.SemaphoreType.DMA((len(sources),)),
            ],
        ),
        out_shape=out_shape,
        compiler_params=pltpu.CompilerParams(vmem_limit_bytes=VMEM_BYTES),
        cost_estimate=cost(12),
        name="hidden_part",
    )(rank, *operands, *after)


def weigh(routes, grads, after, price, extra=None):
    hidden = grads[0].shape[1]
    tile = widest(hidden, (512, 256, 128))
    steps = hidden // tile
    heights = [sum(u[0].shape[-2] for u in units) for units in routes]
    rows, count = sum(heights), sum(g.shape[2] for g in grads)
    units = [u for route in routes for u in route]
    flat = [w for u in units for w in u]
    extras = [] if extra is None else [extra]

    def kernel(*refs):
        weights, both = list(refs[: len(flat)]), refs[len(flat) : len(flat) + len(grads)]
        more = refs[len(flat) + len(grads) : len(flat) + len(grads) + len(extras)]
        outs, total = refs[-1 - len(routes) - len(extras) : -1], refs[-1]
        at = pl.program_id(0)

        @pl.when(at == 0)
        def _():
            total[...] = jnp.zeros_like(total)

        gates, ups = [], []
        for u in units:
            mine, weights = weights[: len(u)], weights[len(u) :]
            gates.append(mine[0][...] if len(u) == 2 else mine[0][0])
            ups.append(mine[1][...] if len(u) == 2 else mine[0][1])
        gate, up = jnp.concatenate(gates, axis=0), jnp.concatenate(ups + [m[...] for m in more], axis=0)
        first = 0
        for ref in both:
            span = slice(first, first + ref.shape[2])
            by_up = jnp.dot(up, ref[1], preferred_element_type=jnp.float32)
            total[:rows, span] += (
                jnp.dot(gate, ref[0], preferred_element_type=jnp.float32) + by_up[:rows]
            )
            if more:
                total[rows:, span] += by_up[rows:]
            first += ref.shape[2]

        @pl.when(at == steps - 1)
        def _():
            top = 0
            for out, height in zip(outs, heights):
                out[...] = total[top : top + height].astype(jnp.bfloat16)
                top += height
            if more:
                outs[-1][...] = total[rows:]

    specs = []
    for w in flat:
        if w.ndim == 2:
            specs.append(pl.BlockSpec((w.shape[0], tile), lambda i: (0, i)))
        else:
            specs.append(pl.BlockSpec((2, w.shape[1], tile), lambda i: (0, 0, i)))
    for g in grads:
        specs.append(pl.BlockSpec((2, tile, g.shape[2]), lambda i: (0, i, 0)))
    shapes = [jax.ShapeDtypeStruct((h, count), jnp.bfloat16) for h in heights]
    for e in extras:
        specs.append(pl.BlockSpec((e.shape[0], tile), lambda i: (0, i)))
        shapes.append(jax.ShapeDtypeStruct((e.shape[0], count), jnp.float32))
    return pl.pallas_call(
        kernel,
        grid=(steps,),
        out_shape=shapes,
        in_specs=specs + [ANYWHERE] * len(after),
        out_specs=[pl.BlockSpec(s.shape, lambda i: (0, 0)) for s in shapes],
        scratch_shapes=[pltpu.VMEM((rows + sum(e.shape[0] for e in extras), count), jnp.float32)],
        compiler_params=pltpu.CompilerParams(vmem_limit_bytes=VMEM_BYTES),
        cost_estimate=cost(price),
        name="weigh_rows",
    )(*flat, *grads, *extras, *after)


def add(values, others, heights, after, price=2):
    pairs = len(values)
    flat = [h for hs in heights for h in hs]

    def kernel(*refs):
        outs = list(refs[len(refs) - len(flat) :])
        for at in range(pairs):
            top = 0
            for height in heights[at]:
                rows = slice(top, top + height)
                outs.pop(0)[...] = (
                    refs[at][rows].astype(jnp.float32) + refs[pairs + at][rows].astype(jnp.float32)
                ).astype(jnp.bfloat16)
                top += height

    count = values[0].shape[1]
    whole = pl.BlockSpec(memory_space=pltpu.VMEM)
    return pl.pallas_call(
        kernel,
        out_shape=[jax.ShapeDtypeStruct((h, count), jnp.bfloat16) for h in flat],
        in_specs=[whole] * (2 * pairs) + [ANYWHERE] * len(after),
        out_specs=[whole] * len(flat),
        compiler_params=pltpu.CompilerParams(vmem_limit_bytes=VMEM_BYTES),
        cost_estimate=cost(price),
        name="add_terms",
    )(*values, *others, *after)


def assemble(words, count, features, part, near, far, chips, after):
    groups = lax.axis_size("groups")
    height = near[0][0].shape[0]
    tall = features // part
    arrays, index = [], {}

    def at_of(value):
        if id(value) not in index:
            index[id(value)] = len(arrays)
            arrays.append(value)
        return index[id(value)]

    near_at = [[at_of(v) for v in pair] for pair in near]
    far_at = {n: (row, [at_of(v) for v in pair], first) for n, (row, pair, first) in far.items()}
    edges = chunk_edges(part)

    def kernel(words_ref, *refs):
        out = refs[-1]
        away, group, inside = words_ref[0], words_ref[1], words_ref[2]

        def total(pair, rows, cols):
            one, two = (refs[at][rows, cols].astype(jnp.float32) for at in pair)
            return (one + two).astype(jnp.bfloat16)

        for j in range(len(near)):

            @pl.when((away == 0) & (inside == j * height))
            def _(j=j):
                out[...] = total(near_at[j], slice(0, height), slice(0, count))

        for s in range(1, chips):
            for g in range(groups):
                for h in range(0, groups, tall):

                    @pl.when((away == s) & (group == g) & (inside == h * part))
                    def _(s=s, g=g, h=h):
                        for j in range(tall):
                            shift = (h + j - g) % groups
                            for k in range(len(CHUNKS)):
                                top = j * part + edges[k]
                                piece = edges[k + 1] - edges[k]
                                if (k, s, shift) in far_at:
                                    row, pair, first = far_at[k, s, shift]
                                    value = total(
                                        pair, slice(row, row + piece), slice(first, first + count)
                                    )
                                else:
                                    value = jnp.zeros((piece, count), jnp.bfloat16)
                                out[top : top + piece] = value

    whole = pl.BlockSpec(memory_space=pltpu.VMEM)
    return pl.pallas_call(
        kernel,
        out_shape=jax.ShapeDtypeStruct((features, count), jnp.bfloat16),
        in_specs=[pl.BlockSpec(memory_space=pltpu.SMEM)]
        + [whole] * len(arrays)
        + [ANYWHERE] * len(after),
        out_specs=whole,
        compiler_params=pltpu.CompilerParams(vmem_limit_bytes=VMEM_BYTES),
        cost_estimate=cost(5),
        name="assemble",
    )(words, *arrays, *after)


def finish(words, part, mine, theirs, late_mine, late_theirs, late, chips):
    features, count = mine.shape
    groups = lax.axis_size("groups")
    tall = features // part
    edges = chunk_edges(part)

    def kernel(words_ref, mine_ref, theirs_ref, late_mine_ref, late_theirs_ref, out_ref, rows_ref):
        away, group, inside = words_ref[0], words_ref[1], words_ref[2]
        for own, base, extra in ((1, mine_ref, late_mine_ref), (0, theirs_ref, late_theirs_ref)):

            @pl.when(words_ref[3] == own)
            def _(base=base, extra=extra):
                rows_ref[...] = base[...]
                for g in range(groups):
                    for h in range(0, groups, tall):

                        @pl.when((away > 0) & (group == g) & (inside == h * part))
                        def _(g=g, h=h):
                            for j in range(tall):
                                row = 0
                                for k, r in late:
                                    top, piece = j * part + edges[k], edges[k + 1] - edges[k]
                                    if (h + j - g) % groups == r:
                                        rows_ref[top : top + piece] = extra[row : row + piece]
                                    row += piece

        out_ref[...] = rows_ref[...].T

    return pl.pallas_call(
        kernel,
        out_shape=jax.ShapeDtypeStruct((count, features), mine.dtype),
        in_specs=[pl.BlockSpec(memory_space=pltpu.SMEM)] + [pl.BlockSpec(memory_space=pltpu.VMEM)] * 4,
        out_specs=pl.BlockSpec(memory_space=pltpu.VMEM),
        scratch_shapes=[pltpu.VMEM((features, count), mine.dtype)],
        compiler_params=pltpu.CompilerParams(vmem_limit_bytes=VMEM_BYTES),
        cost_estimate=cost(3),
        name="finish",
    )(words, mine, theirs, late_mine, late_theirs)


def exchange(value, bit):
    ranks = lax.axis_size("tensor")
    return lax.ppermute(value.astype(jnp.bfloat16), "tensor", [(i, i ^ bit) for i in range(ranks)])


def halve(value, bit):
    half = value.shape[0] // 2
    high = lax.axis_index("tensor") & bit != 0
    low_rows, high_rows = value[:half], value[half:]
    got = exchange(jnp.where(high, low_rows, high_rows), bit)
    return jnp.where(high, high_rows, low_rows), got


def hops(owner, bit):
    groups, ranks, blocks = (lax.axis_size(a) for a in ("groups", "tensor", "dp"))
    pairs = []
    for g in range(groups):
        for p in range(blocks):
            target = owner[g, p]
            for z in range(ranks):
                if z % bit == target % bit and (z ^ target) & bit:
                    pairs.append(((g * ranks + z) * blocks + p, (g * ranks + (z ^ bit)) * blocks + p))
    return pairs


def send(value, pairs):
    return lax.ppermute(value, ("groups", "tensor", "dp"), pairs)


def later_steps(values, owners, at_once):
    ranks = lax.axis_size("tensor")
    if at_once and ranks == 4 and len(values) == 2:
        one, two = hops(owners[0], 2), hops(owners[1], 2)
        if all(not {x[i] for x in one} & {x[i] for x in two} for i in range(2)):
            rank, group, place = (lax.axis_index(a) for a in ("tensor", "groups", "dp"))
            target = jnp.asarray(owners[0], jnp.int32)[group, place]
            height = max(v.shape[0] for v in values)
            high = [jnp.pad(v, ((0, height - v.shape[0]), (0, 0))) for v in values]
            got = send(jnp.where((rank ^ target) & 2 != 0, *high), sorted(one + two))
            return [(v, got) for v in values]
    ends = []
    for value, owner in zip(values, owners):
        bit, got = 2, None
        while bit < ranks:
            if got is not None:
                (value,) = add([value], [got], [[value.shape[0]]], [])
            got = send(value, hops(owner, bit))
            bit *= 2
        ends.append((value, got))
    return ends


def per_device(
    layer_input,
    gate_act,
    up_act,
    out_grad,
    w_gate,
    w_up,
    w_down,
    proj_x,
    proj_u,
    proj_h,
    proj_g,
    doc_lengths,
):
    groups, ranks = lax.axis_size("groups"), lax.axis_size("tensor")
    blocks = lax.axis_size("dp")
    chips = blocks // CORES
    group, rank = lax.axis_index("groups"), lax.axis_index("tensor")
    place = lax.axis_index("dp")
    chip, core = place // CORES, place % CORES
    rows = w_gate.shape[0]
    count = layer_input.shape[0]
    features = out_grad.shape[1]
    part = rows // groups
    edges = chunk_edges(part)
    chunks = len(CHUNKS)
    split = max(1, ranks // blocks)
    group_word = jnp.full((1,), group, jnp.int32)
    rank_word = jnp.full((1,), rank, jnp.int32)

    below, above = spread_ranks(out_grad.T)
    spans = list(zip(edges, edges[1:]))
    _, shares = share_rows(w_gate, w_up, group_word, spans[:2], [], [])
    slopes, in_down_part = prepare(gate_act, up_act, proj_h.T, [shares[0]])
    early_part = jnp.concatenate([project(proj_x, layer_input), in_down_part], axis=0)
    out_down_part = project(proj_g, out_grad)
    fetched, ticks = {}, []

    def fetch(k):
        for s in range(1, chips):
            fetched[k, s, 0] = from_chip(shares[k], s)
            for r in range(1, groups):
                fetched[k, s, r] = from_group(fetched[k, s, 0], r)

    def forward(k, waits, after, held=()):
        names = [(k, 0)] + waits
        arrived = [fetched[n] for n in fetched if (n[0], n[2]) in names]
        arrived = [a for a in arrived if not any(a is h for h in held)]
        carried, fresh = share_rows(
            w_gate, w_up, group_word, spans[k + 2 : k + 3], list(held), arrived + list(after)
        )
        ticks.append(fresh[0])
        if k + 2 < chunks:
            shares.extend(fresh)
            fetch(k + 2)
        return carried

    def owner_of(s, first_of):
        table = np.zeros((groups, blocks), np.int64)
        for g in range(groups):
            for p in range(blocks):
                block = (p // CORES + s) % chips * CORES + p % CORES
                table[g, p] = (block * rows + first_of(g)) // features
        return table

    far_routes = []
    for s in range(1, chips):
        for r in range(groups):
            table = owner_of(s, lambda g: (g + r) % groups * part)
            for route in far_routes:
                if route[0] == s and (route[1] == table).all():
                    route[2].append(r)
                    break
            else:
                far_routes.append((s, table, [r]))
    height = rows // split
    near_tables = [owner_of(0, lambda g: j * height) for j in range(split)]
    near_routes = [
        [(w_gate[j * height : (j + 1) * height], w_up[j * height : (j + 1) * height])]
        for j in range(split)
    ]

    def terms(names, grads, after, price, near=False, extra=None):
        routes = list(zip(near_tables, near_routes, [None] * split)) if near else []
        for s, table, shifts in far_routes:
            units = [(k, s, q) for k, q in names if q in shifts]
            if units:
                routes.append((table, [(fetched[n],) for n in units], units))
        bundles = {}
        for route in routes:
            bundles.setdefault((route[0] % 2).tobytes(), []).append(route)
        bundles = list(bundles.values())
        joined = [[u for _, units, _ in b for u in units] for b in bundles]
        outs = list(weigh(joined, grads, after, price, extra))
        got = [send(out, hops(b[0][0], 1)) for out, b in zip(outs, bundles)]
        return outs, got, bundles

    def carry_on(works, after, price=2, at_once=False):
        outs, got, bundles = ([v for work in works for v in work[i]] for i in range(3))
        heights = [[sum(u[0].shape[-2] for u in units) for _, units, _ in b] for b in bundles]
        sums = list(add(outs, got, heights, after, price))
        routes = [route for b in bundles for route in b]
        ends = later_steps(sums, [table for table, _, _ in routes], at_once)
        return sums, [(names, *end) for (_, _, names), end in zip(routes, ends)]

    fetch(0)
    fetch(1)

    def hold_arrived(k, waits, after, held=()):
        names = [(k, s, 0) for s in range(1, chips)]
        values = forward(k, waits, after, [fetched[n] for n in names] + list(held))
        for n, value in zip(names, values):
            fetched[n] = value
            for r in range(1, groups):
                fetched[k, n[1], r] = from_group(value, r)
        return values[len(names) :]

    def chunks_of(numbers, shifts):
        return [(k, r) for r in shifts for k in numbers]

    others = range(1, groups)
    bits = [1 << i for i in range(ranks.bit_length() - 1)]
    hold_arrived(0, [], [slopes])
    so_far = hidden_part(rank_word, below, above, w_down, None, None, None, [ticks[0]])
    hold_arrived(1, chunks_of([0], others), [so_far])
    hold_arrived(2, chunks_of([1], others), [below[2], above[1], out_down_part, early_part])
    mine, up_out_part = hidden_part(
        rank_word, below, above, w_down, so_far, slopes, proj_u.T, [ticks[2]]
    )
    mine, early = forward(3, chunks_of([2], others) + [(4, 0)], [], [mine, early_part])
    theirs = swap_cores(mine)
    got = exchange(early, bits[0])
    first_names = chunks_of(range(5), [0]) + chunks_of(range(3), others)
    first_mine = terms(first_names, [mine], [ticks[3]], 24, near=True)
    early, got, up_out_part = forward(
        4, chunks_of([3], others) + [(5, 0)], first_mine[0], [early, got, up_out_part]
    )
    early = early + got

    out_parts = jnp.stack([up_out_part, out_down_part]).reshape(2, ranks, -1, count)
    out_parts = out_parts.transpose(1, 0, 2, 3).reshape(-1, count)
    half = out_parts.shape[0] // 2
    high = rank & bits[-1] != 0
    width = early.shape[0]
    got = exchange(
        jnp.concatenate([early, jnp.where(high, out_parts[:half], out_parts[half:])], axis=0),
        bits[-1],
    )
    first_theirs = terms(first_names, [theirs], [ticks[4]], 24, near=True)
    (got,) = forward(5, chunks_of([4], others) + [(6, 0)], first_theirs[0], [got])
    early = early + got[:width]
    out_parts = jnp.where(high, out_parts[half:], out_parts[:half]) + got[width:]
    for bit in bits[1:-1]:
        early = early + exchange(early, bit)
    for bit in bits[-2:0:-1]:
        out_parts, got = halve(out_parts, bit)
        out_parts = out_parts + got
    out_parts, got = halve(out_parts, bits[0])
    sums_mine, end_mine = carry_on([first_mine], first_theirs[0], at_once=True)
    second_names = chunks_of([5, 6], [0]) + chunks_of([3, 4, 5], others)
    last_names = chunks_of([7], [0]) + chunks_of([6, 7], others)
    second = terms(second_names, [mine, theirs], [ticks[5]] + sums_mine, 16)
    held = [fetched[7, s, 0] for s in range(1, chips)]
    got, *held = forward(6, chunks_of([5], others), second[0], [got] + held)
    for s, value in enumerate(held, 1):
        fetched[7, s, 0] = value
        for r in range(1, groups):
            fetched[7, s, r] = from_group(value, r)
    out_parts = out_parts + got
    received = [got for _, _, got in end_mine]
    received += [fetched[n] for n in fetched if n[0] == 6 and n[2] > 0]
    sums_theirs, end_theirs = carry_on([first_theirs], [ticks[6]] + received)
    sums_second, end_second = carry_on([second], sums_theirs)
    last = terms(last_names, [mine, theirs], sums_second, 60)
    received = [got for names, _, got in end_theirs + end_second if names is not None]
    sums_last, end_last = carry_on([last], received, 2)

    early = early.astype(jnp.bfloat16)
    width = in_down_part.shape[0]
    in_up, in_down = early[:width], early[width:]
    out_parts = out_parts.astype(jnp.bfloat16)
    slot = out_parts.shape[0] // 2
    up_out, out_down = out_parts[:slot], out_parts[slot:]
    member = pack_table(doc_lengths, count)
    doc_logs = jnp.stack(
        [doc_outer(member, up_out, in_up), doc_outer(member, out_down, in_down)], axis=1
    )

    first = rank * features
    away = (first // rows // CORES - chip) % chips
    owner = first // rows % CORES == core
    inside = first % rows
    def tops(names):
        sizes = [edges[n[0] + 1] - edges[n[0]] for n in names]
        return [(sum(sizes[:i]), n) for i, n in enumerate(names)]

    words = jnp.stack([away, group, inside, owner]).astype(jnp.int32)

    def assembled(end, first, after):
        near = [pair for names, *pair in end if names is None]
        far = {}
        for names, *pair in end:
            if names is not None:
                far.update((n, (row, pair, 0)) for row, n in tops(names))
        for names, *pair in end_second:
            far.update((n, (row, pair, first)) for row, n in tops(names))
        return assemble(words, count, features, part, near, far, chips, after)

    received = [got for _, _, got in end_last]
    total_theirs = assembled(end_theirs, count, received)
    total_mine = assembled(end_mine, 0, [total_theirs])
    from_partner = swap_cores(total_theirs)

    def pick(index, options):
        value = options[0]
        for at, option in enumerate(options[1:], 1):
            value = jnp.where(index == at, option, value)
        return value

    tail = {}
    for names, value, got in end_last:
        value = (value.astype(jnp.float32) + got.astype(jnp.float32)).astype(jnp.bfloat16)
        tail.update(
            (n, value[row : row + edges[n[0] + 1] - edges[n[0]]]) for row, n in tops(names)
        )
    late = sorted({(k, r) for k, _, r in tail})
    pieces = jnp.concatenate(
        [pick(away - 1, [tail[k, s, r] for s in range(1, chips)]) for k, r in late], axis=0
    )
    input_grad = finish(
        words,
        part,
        total_mine,
        from_partner,
        pieces[:, :count],
        swap_cores(pieces[:, count:]),
        late,
        chips,
    )
    return (input_grad, doc_logs)


def solution(mesh):
    placed = (
        P(("groups", "dp"), "tensor"),
        P(("groups", "dp"), "tensor"),
        P(("groups", "dp"), "tensor"),
        P(("groups", "dp"), "tensor"),
        P("dp", "tensor"),
        P("dp", "tensor"),
        P("tensor", None),
        P("tensor", None),
        P("tensor", None),
        P("tensor", None),
        P("tensor", None),
        P(("groups", "dp"), None),
    )
    return jax.shard_map(
        per_device,
        mesh=mesh,
        in_specs=placed,
        out_specs=(P(("groups", "dp"), "tensor"), P(("groups", "dp"), None, "tensor")),
        check_vma=False,
    )
```

```python
import functools

import jax
import jax.numpy as jnp
import numpy as np
from jax import lax
from jax.experimental import pallas as pl
from jax.experimental.pallas import tpu as pltpu
from jax.sharding import PartitionSpec as P

CORES = 2
CHUNKS = (2,) * 8
VMEM_BYTES = 60 * 1024 * 1024
FLOPS_PER_US = 270_000_000
ANYWHERE = pl.BlockSpec(memory_space=pl.ANY)


def contract_right(left, right):
    return lax.dot_general(
        left, right, (((1,), (1,)), ((), ())), preferred_element_type=jnp.float32
    )


def project(proj, rows):
    return lax.dot_general(
        proj, rows, (((0,), (1,)), ((), ())), preferred_element_type=jnp.float32
    )


def pack_table(doc_lengths, count):
    lengths = doc_lengths[0]
    ends = jnp.cumsum(lengths)
    starts = ends - lengths
    position = jnp.arange(count, dtype=jnp.int32)[None, :]
    inside = (position >= starts[:, None]) & (position < ends[:, None])
    return inside.astype(jnp.bfloat16)


def doc_outer(member, grad_rows, inputs):
    count = member.shape[1]
    weighted = (member[:, None, :] * grad_rows[None, :, :]).reshape(-1, count)
    table = contract_right(weighted, inputs)
    return table.reshape(member.shape[0], grad_rows.shape[0] * inputs.shape[0])


def swap_cores(value):
    size = lax.axis_size("dp")
    return lax.ppermute(value, "dp", [(i, i ^ 1) for i in range(size)])


def from_chip(value, shift):
    size = lax.axis_size("dp")
    step = shift * CORES
    return lax.ppermute(value, "dp", [((i + step) % size, i) for i in range(size)])


def from_group(value, shift):
    size = lax.axis_size("groups")
    return lax.ppermute(value, "groups", [((i + shift) % size, i) for i in range(size)])


def chunk_edges(part):
    return [part // 16 * sum(CHUNKS[:k]) for k in range(len(CHUNKS) + 1)]


def cost(us):
    return pl.CostEstimate(flops=int(us * FLOPS_PER_US) + 1, bytes_accessed=1, transcendentals=0)


def widest(size, options):
    return next((w for w in options if size % w == 0), size)


def share_rows(w_gate, w_up, group, spans, carried, after):
    rows, width = w_gate.shape
    part = rows // lax.axis_size("groups")
    step = part // 16
    kept, waits, fresh = len(carried), len(after), len(spans)
    steps = max([(last - first) // step for first, last in spans], default=1)

    def kernel(group_ref, *refs):
        outs = refs[len(refs) - fresh :] if fresh else []
        for at, out in enumerate(outs):
            out[0] = refs[2 * at][...]
            out[1] = refs[2 * at + 1][...]
        if not fresh:
            refs[-1][...] = jnp.zeros_like(refs[-1])

    in_specs, out_specs = [], [ANYWHERE] * kept
    shapes = [jax.ShapeDtypeStruct(a.shape, a.dtype) for a in carried]
    for first, last in spans:
        at_rows = functools.partial(lambda f, i, g: (g[0] * (part // step) + f // step + i, 0), first)
        in_specs += [pl.BlockSpec((step, width), at_rows)] * 2
        out_specs.append(pl.BlockSpec((2, step, width), lambda i, g: (0, i, 0)))
        shapes.append(jax.ShapeDtypeStruct((2, last - first, width), w_gate.dtype))
    if not fresh:
        out_specs.append(pl.BlockSpec((8, 128), lambda i, g: (0, 0)))
        shapes.append(jax.ShapeDtypeStruct((8, 128), jnp.float32))
    results = pl.pallas_call(
        kernel,
        grid_spec=pltpu.PrefetchScalarGridSpec(
            num_scalar_prefetch=1,
            grid=(steps,),
            in_specs=in_specs + [ANYWHERE] * (kept + waits),
            out_specs=out_specs,
        ),
        out_shape=shapes,
        input_output_aliases={1 + 2 * fresh + i: i for i in range(kept)},
        compiler_params=pltpu.CompilerParams(vmem_limit_bytes=VMEM_BYTES),
        cost_estimate=cost(2),
        name="share_rows",
    )(group, *[w_gate, w_up] * fresh, *carried, *after)
    return list(results[:kept]), list(results[kept:])


def spread_ranks(value):
    ranks = lax.axis_size("tensor")
    below, above = [value], [value]
    for _ in range(1, ranks):
        below.append(lax.ppermute(below[-1], "tensor", [(i, i + 1) for i in range(ranks - 1)]))
        above.append(lax.ppermute(above[-1], "tensor", [(i + 1, i) for i in range(ranks - 1)]))
    return below, above[1:]


def prepare(gate_act, up_act, proj_h, after):
    count, hidden = gate_act.shape
    narrow = proj_h.shape[0]
    tile = widest(hidden, (512, 256, 128))

    def kernel(gate_ref, up_ref, proj_ref, *refs):
        slope_ref, down_ref = refs[-2:]

        @pl.when(pl.program_id(0) == 0)
        def _():
            down_ref[...] = jnp.zeros_like(down_ref)

        gate = gate_ref[...].astype(jnp.float32).T
        up = up_ref[...].astype(jnp.float32).T
        sigma = jax.nn.sigmoid(gate)
        swish = gate * sigma
        slope_ref[0] = up * sigma * (1.0 + gate * (1.0 - sigma))
        slope_ref[1] = swish
        down_ref[...] += jnp.dot(
            proj_ref[...], (swish * up).astype(jnp.bfloat16), preferred_element_type=jnp.float32
        )

    return pl.pallas_call(
        kernel,
        grid=(hidden // tile,),
        out_shape=[
            jax.ShapeDtypeStruct((2, hidden, count), jnp.float32),
            jax.ShapeDtypeStruct((narrow, count), jnp.float32),
        ],
        in_specs=[
            pl.BlockSpec((count, tile), lambda i: (0, i)),
            pl.BlockSpec((count, tile), lambda i: (0, i)),
            pl.BlockSpec((narrow, tile), lambda i: (0, i)),
        ]
        + [ANYWHERE] * len(after),
        out_specs=[
            pl.BlockSpec((2, tile, count), lambda i: (0, i, 0)),
            pl.BlockSpec((narrow, count), lambda i: (0, 0)),
        ],
        compiler_params=pltpu.CompilerParams(vmem_limit_bytes=VMEM_BYTES),
        cost_estimate=cost(12),
        name="prepare",
    )(gate_act, up_act, proj_h, *after)


def hidden_part(rank, below, above, w_down, so_far, slopes, proj_u, after):
    ranks = lax.axis_size("tensor")
    features, count = below[0].shape
    hidden = w_down.shape[0]
    finish = so_far is not None
    slots = ranks - 2 if finish else 2
    tile = widest(hidden, (896, 512, 128))
    sources = [(t, -1, below[t]) for t in range(2 if finish else 0, ranks if finish else 2)]
    sources += [(t, 1, above[t - 1]) for t in range(1, ranks if finish else 2)]

    def counts(z):
        both = ((z >= 1) & (z <= ranks - 2)).astype(jnp.int32)
        return both, jnp.maximum(z - 1, 0)

    def place_of(z, t, side):
        if not finish:
            return (0, z >= 0) if t == 0 else (1, z >= 1 if side < 0 else z == 0)
        both, under = counts(z)
        if side < 0:
            return both + t - 2, t <= z
        if t == 1:
            return 0, both == 1
        return both + under + t - 2, z + t <= ranks - 1

    def column(at, i, rank_ref):
        z = rank_ref[0]
        if not finish:
            return (i, z) if at == 0 else (i, jnp.where(z >= 1, z - 1, 1))
        both, under = counts(z)
        block = jnp.where(at < both + under, z - (at - both + 2), z + (at - both - under + 2))
        return (i, jnp.where(at < both, z + 1, block))

    def kernel(rank_ref, *refs):
        z = rank_ref[0]
        downs, arrived = refs[:slots], refs[slots : slots + len(sources)]
        grad_ref, sem = refs[-2:]
        rest = refs[slots + len(sources) :]

        def gather(wait):
            for at, (t, side, _) in enumerate(sources):
                place, valid = place_of(z, t, side)

                @pl.when(valid)
                def _():
                    rows = pl.ds(pl.multiple_of(place * features, features), features)
                    copy = pltpu.make_async_copy(arrived[at], grad_ref.at[rows, :], sem.at[at])
                    copy.wait() if wait else copy.start()

        @pl.when(pl.program_id(0) == 0)
        def _():
            gather(False)
            gather(True)

        wide = None
        for at in range(slots):
            term = jnp.dot(
                downs[at][...],
                grad_ref[at * features : (at + 1) * features, :],
                preferred_element_type=jnp.float32,
            )
            wide = term if wide is None else wide + term
        if finish:
            both_ref, out_ref = refs[-4:-2]
            wide = wide + rest[0][...]
            both_ref[0] = (wide * rest[1][0]).astype(jnp.bfloat16)
            up_grad = (wide * rest[1][1]).astype(jnp.bfloat16)
            both_ref[1] = up_grad
            part = jnp.dot(rest[2][...], up_grad, preferred_element_type=jnp.float32)

            @pl.when(pl.program_id(0) == 0)
            def _():
                out_ref[...] = part

            @pl.when(pl.program_id(0) > 0)
            def _():
                out_ref[...] += part

        else:
            refs[-3][...] = wide

    operands = [w_down] * slots + [value for _, _, value in sources]
    specs = [pl.BlockSpec((tile, features), functools.partial(column, at)) for at in range(slots)]
    specs += [ANYWHERE] * len(sources)
    if finish:
        narrow = proj_u.shape[0]
        operands += [so_far, slopes, proj_u]
        specs += [
            pl.BlockSpec((tile, count), lambda i, r: (i, 0)),
            pl.BlockSpec((2, tile, count), lambda i, r: (0, i, 0)),
            pl.BlockSpec((narrow, tile), lambda i, r: (0, i)),
        ]
        out_shape = [
            jax.ShapeDtypeStruct((2, hidden, count), jnp.bfloat16),
            jax.ShapeDtypeStruct((narrow, count), jnp.float32),
        ]
        out_specs = [
            pl.BlockSpec((2, tile, count), lambda i, r: (0, i, 0)),
            pl.BlockSpec((narrow, count), lambda i, r: (0, 0)),
        ]
    else:
        out_shape = jax.ShapeDtypeStruct((hidden, count), jnp.float32)
        out_specs = pl.BlockSpec((tile, count), lambda i, r: (i, 0))
    return pl.pallas_call(
        kernel,
        grid_spec=pltpu.PrefetchScalarGridSpec(
            num_scalar_prefetch=1,
            grid=(hidden // tile,),
            in_specs=specs + [ANYWHERE] * len(after),
            out_specs=out_specs,
            scratch_shapes=[
                pltpu.VMEM((slots * features, count), jnp.bfloat16),
                pltpu.SemaphoreType.DMA((len(sources),)),
            ],
        ),
        out_shape=out_shape,
        compiler_params=pltpu.CompilerParams(vmem_limit_bytes=VMEM_BYTES),
        cost_estimate=cost(12),
        name="hidden_part",
    )(rank, *operands, *after)


def weigh(routes, grads, after, price, extra=None):
    hidden = grads[0].shape[1]
    tile = widest(hidden, (512, 256, 128))
    steps = hidden // tile
    heights = [sum(u[0].shape[-2] for u in units) for units in routes]
    rows, count = sum(heights), sum(g.shape[2] for g in grads)
    units = [u for route in routes for u in route]
    flat = [w for u in units for w in u]
    extras = [] if extra is None else [extra]

    def kernel(*refs):
        weights, both = list(refs[: len(flat)]), refs[len(flat) : len(flat) + len(grads)]
        more = refs[len(flat) + len(grads) : len(flat) + len(grads) + len(extras)]
        outs, total = refs[-1 - len(routes) - len(extras) : -1], refs[-1]
        at = pl.program_id(0)

        @pl.when(at == 0)
        def _():
            total[...] = jnp.zeros_like(total)

        gates, ups = [], []
        for u in units:
            mine, weights = weights[: len(u)], weights[len(u) :]
            gates.append(mine[0][...] if len(u) == 2 else mine[0][0])
            ups.append(mine[1][...] if len(u) == 2 else mine[0][1])
        gate, up = jnp.concatenate(gates, axis=0), jnp.concatenate(ups + [m[...] for m in more], axis=0)
        first = 0
        for ref in both:
            span = slice(first, first + ref.shape[2])
            by_up = jnp.dot(up, ref[1], preferred_element_type=jnp.float32)
            total[:rows, span] += (
                jnp.dot(gate, ref[0], preferred_element_type=jnp.float32) + by_up[:rows]
            )
            if more:
                total[rows:, span] += by_up[rows:]
            first += ref.shape[2]

        @pl.when(at == steps - 1)
        def _():
            top = 0
            for out, height in zip(outs, heights):
                out[...] = total[top : top + height].astype(jnp.bfloat16)
                top += height
            if more:
                outs[-1][...] = total[rows:]

    specs = []
    for w in flat:
        if w.ndim == 2:
            specs.append(pl.BlockSpec((w.shape[0], tile), lambda i: (0, i)))
        else:
            specs.append(pl.BlockSpec((2, w.shape[1], tile), lambda i: (0, 0, i)))
    for g in grads:
        specs.append(pl.BlockSpec((2, tile, g.shape[2]), lambda i: (0, i, 0)))
    shapes = [jax.ShapeDtypeStruct((h, count), jnp.bfloat16) for h in heights]
    for e in extras:
        specs.append(pl.BlockSpec((e.shape[0], tile), lambda i: (0, i)))
        shapes.append(jax.ShapeDtypeStruct((e.shape[0], count), jnp.float32))
    return pl.pallas_call(
        kernel,
        grid=(steps,),
        out_shape=shapes,
        in_specs=specs + [ANYWHERE] * len(after),
        out_specs=[pl.BlockSpec(s.shape, lambda i: (0, 0)) for s in shapes],
        scratch_shapes=[pltpu.VMEM((rows + sum(e.shape[0] for e in extras), count), jnp.float32)],
        compiler_params=pltpu.CompilerParams(vmem_limit_bytes=VMEM_BYTES),
        cost_estimate=cost(price),
        name="weigh_rows",
    )(*flat, *grads, *extras, *after)


def add(values, others, heights, after, price=2, first=None):
    pairs = len(values)
    flat = [h for hs in heights for h in hs]
    words = [] if first is None else [first]

    def kernel(*refs):
        ins = refs[len(words) :]
        outs = refs[len(refs) - len(flat) - len(words) :]
        at_out = 0
        for at in range(pairs):
            top = 0
            for height in heights[at]:
                rows = slice(top, top + height)
                outs[at_out][...] = (
                    ins[at][rows].astype(jnp.float32) + ins[pairs + at][rows].astype(jnp.float32)
                ).astype(jnp.bfloat16)
                top += height
                at_out += 1
        for at in range(2 * len(words)):

            @pl.when(refs[0][0] == 1 - at)
            def _(at=at):
                outs[-1][: flat[at]] = outs[at][...]
                if flat[at] < max(flat):
                    outs[-1][flat[at] :] = jnp.zeros((max(flat) - flat[at], count), jnp.bfloat16)

    count = values[0].shape[1]
    whole = pl.BlockSpec(memory_space=pltpu.VMEM)
    shapes = [jax.ShapeDtypeStruct((h, count), jnp.bfloat16) for h in flat + [max(flat)] * len(words)]
    return pl.pallas_call(
        kernel,
        out_shape=shapes,
        in_specs=[pl.BlockSpec(memory_space=pltpu.SMEM)] * len(words)
        + [whole] * (2 * pairs)
        + [ANYWHERE] * len(after),
        out_specs=[whole] * len(shapes),
        compiler_params=pltpu.CompilerParams(vmem_limit_bytes=VMEM_BYTES),
        cost_estimate=cost(price),
        name="add_terms",
    )(*words, *values, *others, *after)


def assemble(words, count, features, part, near, far, chips, after):
    groups = lax.axis_size("groups")
    height = near[0][0].shape[0]
    tall = features // part
    arrays, index = [], {}

    def at_of(value):
        if id(value) not in index:
            index[id(value)] = len(arrays)
            arrays.append(value)
        return index[id(value)]

    near_at = [[at_of(v) for v in pair] for pair in near]
    far_at = {n: (row, [at_of(v) for v in pair], first) for n, (row, pair, first) in far.items()}
    edges = chunk_edges(part)

    def kernel(words_ref, *refs):
        out = refs[-1]
        away, group, inside = words_ref[0], words_ref[1], words_ref[2]

        def total(pair, rows, cols):
            one, two = (refs[at][rows, cols].astype(jnp.float32) for at in pair)
            return (one + two).astype(jnp.bfloat16)

        for j in range(len(near)):

            @pl.when((away == 0) & (inside == j * height))
            def _(j=j):
                out[...] = total(near_at[j], slice(0, height), slice(0, count))

        for s in range(1, chips):
            for g in range(groups):
                for h in range(0, groups, tall):

                    @pl.when((away == s) & (group == g) & (inside == h * part))
                    def _(s=s, g=g, h=h):
                        for j in range(tall):
                            shift = (h + j - g) % groups
                            for k in range(len(CHUNKS)):
                                top = j * part + edges[k]
                                piece = edges[k + 1] - edges[k]
                                if (k, s, shift) in far_at:
                                    row, pair, first = far_at[k, s, shift]
                                    value = total(
                                        pair, slice(row, row + piece), slice(first, first + count)
                                    )
                                else:
                                    value = jnp.zeros((piece, count), jnp.bfloat16)
                                out[top : top + piece] = value

    whole = pl.BlockSpec(memory_space=pltpu.VMEM)
    return pl.pallas_call(
        kernel,
        out_shape=jax.ShapeDtypeStruct((features, count), jnp.bfloat16),
        in_specs=[pl.BlockSpec(memory_space=pltpu.SMEM)]
        + [whole] * len(arrays)
        + [ANYWHERE] * len(after),
        out_specs=whole,
        compiler_params=pltpu.CompilerParams(vmem_limit_bytes=VMEM_BYTES),
        cost_estimate=cost(5),
        name="assemble",
    )(words, *arrays, *after)


def finish(words, part, mine, theirs, late_mine, late_theirs, late, chips):
    features, count = mine.shape
    groups = lax.axis_size("groups")
    tall = features // part
    edges = chunk_edges(part)

    def kernel(words_ref, mine_ref, theirs_ref, late_mine_ref, late_theirs_ref, out_ref, rows_ref):
        away, group, inside = words_ref[0], words_ref[1], words_ref[2]
        for own, base, extra in ((1, mine_ref, late_mine_ref), (0, theirs_ref, late_theirs_ref)):

            @pl.when(words_ref[3] == own)
            def _(base=base, extra=extra):
                rows_ref[...] = base[...]
                for g in range(groups):
                    for h in range(0, groups, tall):

                        @pl.when((away > 0) & (group == g) & (inside == h * part))
                        def _(g=g, h=h):
                            for j in range(tall):
                                row = 0
                                for k, r in late:
                                    top, piece = j * part + edges[k], edges[k + 1] - edges[k]
                                    if (h + j - g) % groups == r:
                                        rows_ref[top : top + piece] = extra[row : row + piece]
                                    row += piece

        out_ref[...] = rows_ref[...].T

    return pl.pallas_call(
        kernel,
        out_shape=jax.ShapeDtypeStruct((count, features), mine.dtype),
        in_specs=[pl.BlockSpec(memory_space=pltpu.SMEM)] + [pl.BlockSpec(memory_space=pltpu.VMEM)] * 4,
        out_specs=pl.BlockSpec(memory_space=pltpu.VMEM),
        scratch_shapes=[pltpu.VMEM((features, count), mine.dtype)],
        compiler_params=pltpu.CompilerParams(vmem_limit_bytes=VMEM_BYTES),
        cost_estimate=cost(3),
        name="finish",
    )(words, mine, theirs, late_mine, late_theirs)


def exchange(value, bit):
    ranks = lax.axis_size("tensor")
    return lax.ppermute(value.astype(jnp.bfloat16), "tensor", [(i, i ^ bit) for i in range(ranks)])


def halve(value, bit):
    half = value.shape[0] // 2
    high = lax.axis_index("tensor") & bit != 0
    low_rows, high_rows = value[:half], value[half:]
    got = exchange(jnp.where(high, low_rows, high_rows), bit)
    return jnp.where(high, high_rows, low_rows), got


def hops(owner, bit):
    groups, ranks, blocks = (lax.axis_size(a) for a in ("groups", "tensor", "dp"))
    pairs = []
    for g in range(groups):
        for p in range(blocks):
            target = owner[g, p]
            for z in range(ranks):
                if z % bit == target % bit and (z ^ target) & bit:
                    pairs.append(((g * ranks + z) * blocks + p, (g * ranks + (z ^ bit)) * blocks + p))
    return pairs


def send(value, pairs):
    return lax.ppermute(value, ("groups", "tensor", "dp"), pairs)


def exchangeable(owners):
    if lax.axis_size("tensor") != 4 or len(owners) != 2:
        return False
    one, two = hops(owners[0], 2), hops(owners[1], 2)
    return all(not {x[i] for x in one} & {x[i] for x in two} for i in range(2))


def later_steps(values, owners):
    ranks = lax.axis_size("tensor")
    ends = []
    for value, owner in zip(values, owners):
        bit, got = 2, None
        while bit < ranks:
            if got is not None:
                (value,) = add([value], [got], [[value.shape[0]]], [])
            got = send(value, hops(owner, bit))
            bit *= 2
        ends.append((value, got))
    return ends


def per_device(
    layer_input,
    gate_act,
    up_act,
    out_grad,
    w_gate,
    w_up,
    w_down,
    proj_x,
    proj_u,
    proj_h,
    proj_g,
    doc_lengths,
):
    groups, ranks = lax.axis_size("groups"), lax.axis_size("tensor")
    blocks = lax.axis_size("dp")
    chips = blocks // CORES
    group, rank = lax.axis_index("groups"), lax.axis_index("tensor")
    place = lax.axis_index("dp")
    chip, core = place // CORES, place % CORES
    rows = w_gate.shape[0]
    count = layer_input.shape[0]
    features = out_grad.shape[1]
    part = rows // groups
    edges = chunk_edges(part)
    chunks = len(CHUNKS)
    split = max(1, ranks // blocks)
    group_word = jnp.full((1,), group, jnp.int32)
    rank_word = jnp.full((1,), rank, jnp.int32)

    below, above = spread_ranks(out_grad.T)
    spans = list(zip(edges, edges[1:]))
    _, shares = share_rows(w_gate, w_up, group_word, spans[:2], [], [])
    slopes, in_down_part = prepare(gate_act, up_act, proj_h.T, [shares[0]])
    early_part = jnp.concatenate([project(proj_x, layer_input), in_down_part], axis=0)
    out_down_part = project(proj_g, out_grad)
    fetched, ticks = {}, []

    def fetch(k):
        for s in range(1, chips):
            fetched[k, s, 0] = from_chip(shares[k], s)
            for r in range(1, groups):
                fetched[k, s, r] = from_group(fetched[k, s, 0], r)

    def forward(k, waits, after, held=()):
        names = [(k, 0)] + waits
        arrived = [fetched[n] for n in fetched if (n[0], n[2]) in names]
        arrived = [a for a in arrived if not any(a is h for h in held)]
        carried, fresh = share_rows(
            w_gate, w_up, group_word, spans[k + 2 : k + 3], list(held), arrived + list(after)
        )
        ticks.append(fresh[0])
        if k + 2 < chunks:
            shares.extend(fresh)
            fetch(k + 2)
        return carried

    def owner_of(s, first_of):
        table = np.zeros((groups, blocks), np.int64)
        for g in range(groups):
            for p in range(blocks):
                block = (p // CORES + s) % chips * CORES + p % CORES
                table[g, p] = (block * rows + first_of(g)) // features
        return table

    far_routes = []
    for s in range(1, chips):
        for r in range(groups):
            table = owner_of(s, lambda g: (g + r) % groups * part)
            for route in far_routes:
                if route[0] == s and (route[1] == table).all():
                    route[2].append(r)
                    break
            else:
                far_routes.append((s, table, [r]))
    height = rows // split
    near_tables = [owner_of(0, lambda g: j * height) for j in range(split)]
    near_routes = [
        [(w_gate[j * height : (j + 1) * height], w_up[j * height : (j + 1) * height])]
        for j in range(split)
    ]

    def terms(names, grads, after, price, near=False, extra=None):
        routes = list(zip(near_tables, near_routes, [None] * split)) if near else []
        for s, table, shifts in far_routes:
            units = [(k, s, q) for k, q in names if q in shifts]
            if units:
                routes.append((table, [(fetched[n],) for n in units], units))
        bundles = {}
        for route in routes:
            bundles.setdefault((route[0] % 2).tobytes(), []).append(route)
        bundles = list(bundles.values())
        joined = [[u for _, units, _ in b for u in units] for b in bundles]
        outs = list(weigh(joined, grads, after, price, extra))
        got = [send(out, hops(b[0][0], 1)) for out, b in zip(outs, bundles)]
        return outs, got, bundles

    def carry_on(works, after, price=2, at_once=False):
        outs, got, bundles = ([v for work in works for v in work[i]] for i in range(3))
        heights = [[sum(u[0].shape[-2] for u in units) for _, units, _ in b] for b in bundles]
        routes = [route for b in bundles for route in b]
        owners = [table for table, _, _ in routes]
        if at_once and exchangeable(owners):
            target = place * rows // features
            first = ((rank ^ target) & 2 != 0).astype(jnp.int32).reshape(1)
            *sums, sent = add(outs, got, heights, after, price, first)
            came = send(sent, sorted(hops(owners[0], 2) + hops(owners[1], 2)))
            ends = [(v, came) for v in sums]
        else:
            sums = list(add(outs, got, heights, after, price))
            ends = later_steps(sums, owners)
        return sums, [(names, *end) for (_, _, names), end in zip(routes, ends)]

    fetch(0)
    fetch(1)

    def hold_arrived(k, waits, after, held=()):
        names = [(k, s, 0) for s in range(1, chips)]
        values = forward(k, waits, after, [fetched[n] for n in names] + list(held))
        for n, value in zip(names, values):
            fetched[n] = value
            for r in range(1, groups):
                fetched[k, n[1], r] = from_group(value, r)
        return values[len(names) :]

    def chunks_of(numbers, shifts):
        return [(k, r) for r in shifts for k in numbers]

    others = range(1, groups)
    bits = [1 << i for i in range(ranks.bit_length() - 1)]
    hold_arrived(0, [], [slopes])
    so_far = hidden_part(rank_word, below, above, w_down, None, None, None, [ticks[0]])
    hold_arrived(1, chunks_of([0], others), [so_far])
    hold_arrived(2, chunks_of([1], others), [below[2], above[1], out_down_part, early_part])
    mine, up_out_part = hidden_part(
        rank_word, below, above, w_down, so_far, slopes, proj_u.T, [ticks[2]]
    )
    mine, early = forward(3, chunks_of([2], others) + [(4, 0)], [], [mine, early_part])
    theirs = swap_cores(mine)
    got = exchange(early, bits[0])
    first_names = chunks_of(range(5), [0]) + chunks_of(range(3), others)
    first_mine = terms(first_names, [mine], [ticks[3]], 24, near=True)
    early, got, up_out_part = forward(
        4, chunks_of([3], others) + [(5, 0)], first_mine[0], [early, got, up_out_part]
    )
    early = early + got

    out_parts = jnp.stack([up_out_part, out_down_part]).reshape(2, ranks, -1, count)
    out_parts = out_parts.transpose(1, 0, 2, 3).reshape(-1, count)
    half = out_parts.shape[0] // 2
    high = rank & bits[-1] != 0
    width = early.shape[0]
    got = exchange(
        jnp.concatenate([early, jnp.where(high, out_parts[:half], out_parts[half:])], axis=0),
        bits[-1],
    )
    first_theirs = terms(first_names, [theirs], [ticks[4]], 24, near=True)
    got, *held = forward(
        5, chunks_of([4], others), first_theirs[0], [got] + [fetched[6, s, 0] for s in range(1, chips)]
    )
    for s, value in enumerate(held, 1):
        fetched[6, s, 0] = value
        for r in range(1, groups):
            fetched[6, s, r] = from_group(value, r)
    early = early + got[:width]
    out_parts = jnp.where(high, out_parts[half:], out_parts[:half]) + got[width:]
    for bit in bits[1:-1]:
        early = early + exchange(early, bit)
    for bit in bits[-2:0:-1]:
        out_parts, got = halve(out_parts, bit)
        out_parts = out_parts + got
    out_parts, got = halve(out_parts, bits[0])
    sums_mine, end_mine = carry_on([first_mine], first_theirs[0], at_once=True)
    second_names = chunks_of([5, 6], [0]) + chunks_of([3, 4, 5], others)
    last_names = chunks_of([7], [0]) + chunks_of([6, 7], others)
    second = terms(second_names, [mine, theirs], [ticks[5]] + sums_mine, 16)
    held = [fetched[7, s, 0] for s in range(1, chips)]
    got, *held = forward(6, chunks_of([5], others), second[0], [got] + held)
    for s, value in enumerate(held, 1):
        fetched[7, s, 0] = value
        for r in range(1, groups):
            fetched[7, s, r] = from_group(value, r)
    out_parts = out_parts + got
    received = [got for _, _, got in end_mine]
    received += [fetched[n] for n in fetched if n[0] == 6 and n[2] > 0]
    sums_theirs, end_theirs = carry_on([first_theirs], [ticks[6]] + received)
    sums_second, end_second = carry_on([second], sums_theirs)
    last = terms(last_names, [mine, theirs], sums_second, 60)
    received = [got for names, _, got in end_theirs + end_second if names is not None]
    sums_last, end_last = carry_on([last], received, 2)

    early = early.astype(jnp.bfloat16)
    width = in_down_part.shape[0]
    in_up, in_down = early[:width], early[width:]
    out_parts = out_parts.astype(jnp.bfloat16)
    slot = out_parts.shape[0] // 2
    up_out, out_down = out_parts[:slot], out_parts[slot:]
    member = pack_table(doc_lengths, count)
    doc_logs = jnp.stack(
        [doc_outer(member, up_out, in_up), doc_outer(member, out_down, in_down)], axis=1
    )

    first = rank * features
    away = (first // rows // CORES - chip) % chips
    owner = first // rows % CORES == core
    inside = first % rows
    def tops(names):
        sizes = [edges[n[0] + 1] - edges[n[0]] for n in names]
        return [(sum(sizes[:i]), n) for i, n in enumerate(names)]

    words = jnp.stack([away, group, inside, owner]).astype(jnp.int32)

    def assembled(end, first, after):
        near = [pair for names, *pair in end if names is None]
        far = {}
        for names, *pair in end:
            if names is not None:
                far.update((n, (row, pair, 0)) for row, n in tops(names))
        for names, *pair in end_second:
            far.update((n, (row, pair, first)) for row, n in tops(names))
        return assemble(words, count, features, part, near, far, chips, after)

    received = [got for _, _, got in end_last]
    total_theirs = assembled(end_theirs, count, received)
    total_mine = assembled(end_mine, 0, [total_theirs])
    from_partner = swap_cores(total_theirs)

    def pick(index, options):
        value = options[0]
        for at, option in enumerate(options[1:], 1):
            value = jnp.where(index == at, option, value)
        return value

    tail = {}
    for names, value, got in end_last:
        value = (value.astype(jnp.float32) + got.astype(jnp.float32)).astype(jnp.bfloat16)
        tail.update(
            (n, value[row : row + edges[n[0] + 1] - edges[n[0]]]) for row, n in tops(names)
        )
    late = sorted({(k, r) for k, _, r in tail})
    pieces = jnp.concatenate(
        [pick(away - 1, [tail[k, s, r] for s in range(1, chips)]) for k, r in late], axis=0
    )
    input_grad = finish(
        words,
        part,
        total_mine,
        from_partner,
        pieces[:, :count],
        swap_cores(pieces[:, count:]),
        late,
        chips,
    )
    return (input_grad, doc_logs)


def solution(mesh):
    placed = (
        P(("groups", "dp"), "tensor"),
        P(("groups", "dp"), "tensor"),
        P(("groups", "dp"), "tensor"),
        P(("groups", "dp"), "tensor"),
        P("dp", "tensor"),
        P("dp", "tensor"),
        P("tensor", None),
        P("tensor", None),
        P("tensor", None),
        P("tensor", None),
        P("tensor", None),
        P(("groups", "dp"), None),
    )
    return jax.shard_map(
        per_device,
        mesh=mesh,
        in_specs=placed,
        out_specs=(P(("groups", "dp"), "tensor"), P(("groups", "dp"), None, "tensor")),
        check_vma=False,
    )
```

```python
import functools

import jax
import jax.numpy as jnp
import numpy as np
from jax import lax
from jax.experimental import pallas as pl
from jax.experimental.pallas import tpu as pltpu
from jax.sharding import PartitionSpec as P

CORES = 2
CHUNKS = (2,) * 8
VMEM_BYTES = 60 * 1024 * 1024
FLOPS_PER_US = 270_000_000
ANYWHERE = pl.BlockSpec(memory_space=pl.ANY)


def contract_right(left, right):
    return lax.dot_general(
        left, right, (((1,), (1,)), ((), ())), preferred_element_type=jnp.float32
    )


def project(proj, rows):
    return lax.dot_general(
        proj, rows, (((0,), (1,)), ((), ())), preferred_element_type=jnp.float32
    )


def pack_table(doc_lengths, count):
    lengths = doc_lengths[0]
    ends = jnp.cumsum(lengths)
    starts = ends - lengths
    position = jnp.arange(count, dtype=jnp.int32)[None, :]
    inside = (position >= starts[:, None]) & (position < ends[:, None])
    return inside.astype(jnp.bfloat16)


def doc_outer(member, grad_rows, inputs):
    count = member.shape[1]
    weighted = (member[:, None, :] * grad_rows[None, :, :]).reshape(-1, count)
    table = contract_right(weighted, inputs)
    return table.reshape(member.shape[0], grad_rows.shape[0] * inputs.shape[0])


def swap_cores(value):
    size = lax.axis_size("dp")
    return lax.ppermute(value, "dp", [(i, i ^ 1) for i in range(size)])


def from_chip(value, shift):
    size = lax.axis_size("dp")
    step = shift * CORES
    return lax.ppermute(value, "dp", [((i + step) % size, i) for i in range(size)])


def from_group(value, shift):
    size = lax.axis_size("groups")
    return lax.ppermute(value, "groups", [((i + shift) % size, i) for i in range(size)])


def chunk_edges(part):
    return [part // 16 * sum(CHUNKS[:k]) for k in range(len(CHUNKS) + 1)]


def cost(us):
    return pl.CostEstimate(flops=int(us * FLOPS_PER_US) + 1, bytes_accessed=1, transcendentals=0)


def widest(size, options):
    return next((w for w in options if size % w == 0), size)


def share_rows(w_gate, w_up, group, spans, carried, after):
    rows, width = w_gate.shape
    part = rows // lax.axis_size("groups")
    step = part // 16
    kept, waits, fresh = len(carried), len(after), len(spans)
    steps = max([(last - first) // step for first, last in spans], default=1)

    def kernel(group_ref, *refs):
        outs = refs[len(refs) - fresh :] if fresh else []
        for at, out in enumerate(outs):
            out[0] = refs[2 * at][...]
            out[1] = refs[2 * at + 1][...]
        if not fresh:
            refs[-1][...] = jnp.zeros_like(refs[-1])

    in_specs, out_specs = [], [ANYWHERE] * kept
    shapes = [jax.ShapeDtypeStruct(a.shape, a.dtype) for a in carried]
    for first, last in spans:
        at_rows = functools.partial(lambda f, i, g: (g[0] * (part // step) + f // step + i, 0), first)
        in_specs += [pl.BlockSpec((step, width), at_rows)] * 2
        out_specs.append(pl.BlockSpec((2, step, width), lambda i, g: (0, i, 0)))
        shapes.append(jax.ShapeDtypeStruct((2, last - first, width), w_gate.dtype))
    if not fresh:
        out_specs.append(pl.BlockSpec((8, 128), lambda i, g: (0, 0)))
        shapes.append(jax.ShapeDtypeStruct((8, 128), jnp.float32))
    results = pl.pallas_call(
        kernel,
        grid_spec=pltpu.PrefetchScalarGridSpec(
            num_scalar_prefetch=1,
            grid=(steps,),
            in_specs=in_specs + [ANYWHERE] * (kept + waits),
            out_specs=out_specs,
        ),
        out_shape=shapes,
        input_output_aliases={1 + 2 * fresh + i: i for i in range(kept)},
        compiler_params=pltpu.CompilerParams(vmem_limit_bytes=VMEM_BYTES),
        cost_estimate=cost(2),
        name="share_rows",
    )(group, *[w_gate, w_up] * fresh, *carried, *after)
    return list(results[:kept]), list(results[kept:])


def spread_ranks(value):
    ranks = lax.axis_size("tensor")
    below, above = [value], [value]
    for _ in range(1, ranks):
        below.append(lax.ppermute(below[-1], "tensor", [(i, i + 1) for i in range(ranks - 1)]))
        above.append(lax.ppermute(above[-1], "tensor", [(i + 1, i) for i in range(ranks - 1)]))
    return below, above[1:]


def prepare(gate_act, up_act, proj_h, after):
    count, hidden = gate_act.shape
    narrow = proj_h.shape[0]
    tile = widest(hidden, (512, 256, 128))

    def kernel(gate_ref, up_ref, proj_ref, *refs):
        slope_ref, down_ref = refs[-2:]

        @pl.when(pl.program_id(0) == 0)
        def _():
            down_ref[...] = jnp.zeros_like(down_ref)

        gate = gate_ref[...].astype(jnp.float32).T
        up = up_ref[...].astype(jnp.float32).T
        sigma = jax.nn.sigmoid(gate)
        swish = gate * sigma
        slope_ref[0] = up * sigma * (1.0 + gate * (1.0 - sigma))
        slope_ref[1] = swish
        down_ref[...] += jnp.dot(
            proj_ref[...], (swish * up).astype(jnp.bfloat16), preferred_element_type=jnp.float32
        )

    return pl.pallas_call(
        kernel,
        grid=(hidden // tile,),
        out_shape=[
            jax.ShapeDtypeStruct((2, hidden, count), jnp.float32),
            jax.ShapeDtypeStruct((narrow, count), jnp.float32),
        ],
        in_specs=[
            pl.BlockSpec((count, tile), lambda i: (0, i)),
            pl.BlockSpec((count, tile), lambda i: (0, i)),
            pl.BlockSpec((narrow, tile), lambda i: (0, i)),
        ]
        + [ANYWHERE] * len(after),
        out_specs=[
            pl.BlockSpec((2, tile, count), lambda i: (0, i, 0)),
            pl.BlockSpec((narrow, count), lambda i: (0, 0)),
        ],
        compiler_params=pltpu.CompilerParams(vmem_limit_bytes=VMEM_BYTES),
        cost_estimate=cost(12),
        name="prepare",
    )(gate_act, up_act, proj_h, *after)


def hidden_part(rank, below, above, w_down, so_far, slopes, proj_u, after):
    ranks = lax.axis_size("tensor")
    features, count = below[0].shape
    hidden = w_down.shape[0]
    finish = so_far is not None
    slots = ranks - 2 if finish else 2
    tile = widest(hidden, (896, 512, 128))
    sources = [(t, -1, below[t]) for t in range(2 if finish else 0, ranks if finish else 2)]
    sources += [(t, 1, above[t - 1]) for t in range(1, ranks if finish else 2)]

    def counts(z):
        both = ((z >= 1) & (z <= ranks - 2)).astype(jnp.int32)
        return both, jnp.maximum(z - 1, 0)

    def place_of(z, t, side):
        if not finish:
            return (0, z >= 0) if t == 0 else (1, z >= 1 if side < 0 else z == 0)
        both, under = counts(z)
        if side < 0:
            return both + t - 2, t <= z
        if t == 1:
            return 0, both == 1
        return both + under + t - 2, z + t <= ranks - 1

    def column(at, i, rank_ref):
        z = rank_ref[0]
        if not finish:
            return (i, z) if at == 0 else (i, jnp.where(z >= 1, z - 1, 1))
        both, under = counts(z)
        block = jnp.where(at < both + under, z - (at - both + 2), z + (at - both - under + 2))
        return (i, jnp.where(at < both, z + 1, block))

    def kernel(rank_ref, *refs):
        z = rank_ref[0]
        downs, arrived = refs[:slots], refs[slots : slots + len(sources)]
        grad_ref, sem = refs[-2:]
        rest = refs[slots + len(sources) :]

        def gather(wait):
            for at, (t, side, _) in enumerate(sources):
                place, valid = place_of(z, t, side)

                @pl.when(valid)
                def _():
                    rows = pl.ds(pl.multiple_of(place * features, features), features)
                    copy = pltpu.make_async_copy(arrived[at], grad_ref.at[rows, :], sem.at[at])
                    copy.wait() if wait else copy.start()

        @pl.when(pl.program_id(0) == 0)
        def _():
            gather(False)
            gather(True)

        wide = None
        for at in range(slots):
            term = jnp.dot(
                downs[at][...],
                grad_ref[at * features : (at + 1) * features, :],
                preferred_element_type=jnp.float32,
            )
            wide = term if wide is None else wide + term
        if finish:
            both_ref, out_ref = refs[-4:-2]
            wide = wide + rest[0][...]
            both_ref[0] = (wide * rest[1][0]).astype(jnp.bfloat16)
            up_grad = (wide * rest[1][1]).astype(jnp.bfloat16)
            both_ref[1] = up_grad
            part = jnp.dot(rest[2][...], up_grad, preferred_element_type=jnp.float32)

            @pl.when(pl.program_id(0) == 0)
            def _():
                out_ref[...] = part

            @pl.when(pl.program_id(0) > 0)
            def _():
                out_ref[...] += part

        else:
            refs[-3][...] = wide

    operands = [w_down] * slots + [value for _, _, value in sources]
    specs = [pl.BlockSpec((tile, features), functools.partial(column, at)) for at in range(slots)]
    specs += [ANYWHERE] * len(sources)
    if finish:
        narrow = proj_u.shape[0]
        operands += [so_far, slopes, proj_u]
        specs += [
            pl.BlockSpec((tile, count), lambda i, r: (i, 0)),
            pl.BlockSpec((2, tile, count), lambda i, r: (0, i, 0)),
            pl.BlockSpec((narrow, tile), lambda i, r: (0, i)),
        ]
        out_shape = [
            jax.ShapeDtypeStruct((2, hidden, count), jnp.bfloat16),
            jax.ShapeDtypeStruct((narrow, count), jnp.float32),
        ]
        out_specs = [
            pl.BlockSpec((2, tile, count), lambda i, r: (0, i, 0)),
            pl.BlockSpec((narrow, count), lambda i, r: (0, 0)),
        ]
    else:
        out_shape = jax.ShapeDtypeStruct((hidden, count), jnp.float32)
        out_specs = pl.BlockSpec((tile, count), lambda i, r: (i, 0))
    return pl.pallas_call(
        kernel,
        grid_spec=pltpu.PrefetchScalarGridSpec(
            num_scalar_prefetch=1,
            grid=(hidden // tile,),
            in_specs=specs + [ANYWHERE] * len(after),
            out_specs=out_specs,
            scratch_shapes=[
                pltpu.VMEM((slots * features, count), jnp.bfloat16),
                pltpu.SemaphoreType.DMA((len(sources),)),
            ],
        ),
        out_shape=out_shape,
        compiler_params=pltpu.CompilerParams(vmem_limit_bytes=VMEM_BYTES),
        cost_estimate=cost(12),
        name="hidden_part",
    )(rank, *operands, *after)


def weigh(routes, grads, after, price, extra=None):
    hidden = grads[0].shape[1]
    tile = widest(hidden, (512, 256, 128))
    steps = hidden // tile
    heights = [sum(u[0].shape[-2] for u in units) for units in routes]
    rows, count = sum(heights), sum(g.shape[2] for g in grads)
    units = [u for route in routes for u in route]
    flat = [w for u in units for w in u]
    extras = [] if extra is None else [extra]

    def kernel(*refs):
        weights, both = list(refs[: len(flat)]), refs[len(flat) : len(flat) + len(grads)]
        more = refs[len(flat) + len(grads) : len(flat) + len(grads) + len(extras)]
        outs, total = refs[-1 - len(routes) - len(extras) : -1], refs[-1]
        at = pl.program_id(0)

        @pl.when(at == 0)
        def _():
            total[...] = jnp.zeros_like(total)

        gates, ups = [], []
        for u in units:
            mine, weights = weights[: len(u)], weights[len(u) :]
            gates.append(mine[0][...] if len(u) == 2 else mine[0][0])
            ups.append(mine[1][...] if len(u) == 2 else mine[0][1])
        gate, up = jnp.concatenate(gates, axis=0), jnp.concatenate(ups + [m[...] for m in more], axis=0)
        first = 0
        for ref in both:
            span = slice(first, first + ref.shape[2])
            by_up = jnp.dot(up, ref[1], preferred_element_type=jnp.float32)
            total[:rows, span] += (
                jnp.dot(gate, ref[0], preferred_element_type=jnp.float32) + by_up[:rows]
            )
            if more:
                total[rows:, span] += by_up[rows:]
            first += ref.shape[2]

        @pl.when(at == steps - 1)
        def _():
            top = 0
            for out, height in zip(outs, heights):
                out[...] = total[top : top + height].astype(jnp.bfloat16)
                top += height
            if more:
                outs[-1][...] = total[rows:]

    specs = []
    for w in flat:
        if w.ndim == 2:
            specs.append(pl.BlockSpec((w.shape[0], tile), lambda i: (0, i)))
        else:
            specs.append(pl.BlockSpec((2, w.shape[1], tile), lambda i: (0, 0, i)))
    for g in grads:
        specs.append(pl.BlockSpec((2, tile, g.shape[2]), lambda i: (0, i, 0)))
    shapes = [jax.ShapeDtypeStruct((h, count), jnp.bfloat16) for h in heights]
    for e in extras:
        specs.append(pl.BlockSpec((e.shape[0], tile), lambda i: (0, i)))
        shapes.append(jax.ShapeDtypeStruct((e.shape[0], count), jnp.float32))
    return pl.pallas_call(
        kernel,
        grid=(steps,),
        out_shape=shapes,
        in_specs=specs + [ANYWHERE] * len(after),
        out_specs=[pl.BlockSpec(s.shape, lambda i: (0, 0)) for s in shapes],
        scratch_shapes=[pltpu.VMEM((rows + sum(e.shape[0] for e in extras), count), jnp.float32)],
        compiler_params=pltpu.CompilerParams(vmem_limit_bytes=VMEM_BYTES),
        cost_estimate=cost(price),
        name="weigh_rows",
    )(*flat, *grads, *extras, *after)


def add(values, others, heights, after, price=2, first=None):
    pairs = len(values)
    flat = [h for hs in heights for h in hs]
    words = [] if first is None else [first]

    def kernel(*refs):
        ins = refs[len(words) :]
        outs = refs[len(refs) - len(flat) - len(words) :]
        at_out = 0
        for at in range(pairs):
            top = 0
            for height in heights[at]:
                rows = slice(top, top + height)
                outs[at_out][...] = (
                    ins[at][rows].astype(jnp.float32) + ins[pairs + at][rows].astype(jnp.float32)
                ).astype(jnp.bfloat16)
                top += height
                at_out += 1
        for at in range(2 * len(words)):

            @pl.when(refs[0][0] == 1 - at)
            def _(at=at):
                outs[-1][: flat[at]] = outs[at][...]
                if flat[at] < max(flat):
                    outs[-1][flat[at] :] = jnp.zeros((max(flat) - flat[at], count), jnp.bfloat16)

    count = values[0].shape[1]
    whole = pl.BlockSpec(memory_space=pltpu.VMEM)
    shapes = [jax.ShapeDtypeStruct((h, count), jnp.bfloat16) for h in flat + [max(flat)] * len(words)]
    return pl.pallas_call(
        kernel,
        out_shape=shapes,
        in_specs=[pl.BlockSpec(memory_space=pltpu.SMEM)] * len(words)
        + [whole] * (2 * pairs)
        + [ANYWHERE] * len(after),
        out_specs=[whole] * len(shapes),
        compiler_params=pltpu.CompilerParams(vmem_limit_bytes=VMEM_BYTES),
        cost_estimate=cost(price),
        name="add_terms",
    )(*words, *values, *others, *after)


def assemble(words, count, features, part, near, far, chips, after, cuts):
    groups = lax.axis_size("groups")
    height = near[0][0].shape[0]
    tall = features // part
    arrays, index = [], {}

    def at_of(value):
        if id(value) not in index:
            index[id(value)] = len(arrays)
            arrays.append(value)
        return index[id(value)]

    near_at = [[at_of(v) for v in pair] for pair in near]
    far_at = {n: (row, [at_of(v) for v in pair], first) for n, (row, pair, first) in far.items()}
    edges = chunk_edges(part)
    height_out = features // cuts

    def kernel(words_ref, *refs):
        outs = refs[-cuts:]
        away, group, inside = words_ref[0], words_ref[1], words_ref[2]

        def total(pair, rows, cols):
            one, two = (refs[at][rows, cols].astype(jnp.float32) for at in pair)
            return (one + two).astype(jnp.bfloat16)

        for j in range(len(near)):

            @pl.when((away == 0) & (inside == j * height))
            def _(j=j):
                for at, out in enumerate(outs):
                    out[...] = total(
                        near_at[j], slice(at * height_out, (at + 1) * height_out), slice(0, count)
                    )

        for s in range(1, chips):
            for g in range(groups):
                for h in range(0, groups, tall):

                    @pl.when((away == s) & (group == g) & (inside == h * part))
                    def _(s=s, g=g, h=h):
                        for j in range(tall):
                            shift = (h + j - g) % groups
                            for k in range(len(CHUNKS)):
                                top = j * part + edges[k]
                                piece = edges[k + 1] - edges[k]
                                if (k, s, shift) in far_at:
                                    row, pair, first = far_at[k, s, shift]
                                    value = total(
                                        pair, slice(row, row + piece), slice(first, first + count)
                                    )
                                else:
                                    value = jnp.zeros((piece, count), jnp.bfloat16)
                                at = top % height_out
                                outs[top // height_out][at : at + piece] = value

    whole = pl.BlockSpec(memory_space=pltpu.VMEM)
    return pl.pallas_call(
        kernel,
        out_shape=[jax.ShapeDtypeStruct((height_out, count), jnp.bfloat16)] * cuts,
        in_specs=[pl.BlockSpec(memory_space=pltpu.SMEM)]
        + [whole] * len(arrays)
        + [ANYWHERE] * len(after),
        out_specs=[whole] * cuts,
        compiler_params=pltpu.CompilerParams(vmem_limit_bytes=VMEM_BYTES),
        cost_estimate=cost(1),
        name="assemble",
    )(words, *arrays, *after)


def finish(words, part, mine, theirs, late_mine, late_theirs, late, chips):
    count = mine[0].shape[1]
    features = sum(m.shape[0] for m in mine)
    groups = lax.axis_size("groups")
    tall = features // part
    edges = chunk_edges(part)

    def kernel(words_ref, *refs):
        mine_refs, theirs_refs = refs[: len(mine)], refs[len(mine) : len(mine) + len(theirs)]
        late_mine_ref, late_theirs_ref, out_ref, rows_ref = refs[-4:]
        away, group, inside = words_ref[0], words_ref[1], words_ref[2]
        for own, bases, extra in (
            (1, mine_refs, late_mine_ref),
            (0, theirs_refs, late_theirs_ref),
        ):

            @pl.when(words_ref[3] == own)
            def _(bases=bases, extra=extra):
                first = 0
                for base in bases:
                    rows_ref[first : first + base.shape[0]] = base[...]
                    first += base.shape[0]
                for g in range(groups):
                    for h in range(0, groups, tall):

                        @pl.when((away > 0) & (group == g) & (inside == h * part))
                        def _(g=g, h=h):
                            for j in range(tall):
                                row = 0
                                for k, r in late:
                                    top, piece = j * part + edges[k], edges[k + 1] - edges[k]
                                    if (h + j - g) % groups == r:
                                        rows_ref[top : top + piece] = extra[row : row + piece]
                                    row += piece

        out_ref[...] = rows_ref[...].T

    whole = pl.BlockSpec(memory_space=pltpu.VMEM)
    return pl.pallas_call(
        kernel,
        out_shape=jax.ShapeDtypeStruct((count, features), jnp.bfloat16),
        in_specs=[pl.BlockSpec(memory_space=pltpu.SMEM)] + [whole] * (len(mine) + len(theirs) + 2),
        out_specs=whole,
        scratch_shapes=[pltpu.VMEM((features, count), jnp.bfloat16)],
        compiler_params=pltpu.CompilerParams(vmem_limit_bytes=VMEM_BYTES),
        cost_estimate=cost(3),
        name="finish",
    )(words, *mine, *theirs, late_mine, late_theirs)


def exchange(value, bit):
    ranks = lax.axis_size("tensor")
    return lax.ppermute(value.astype(jnp.bfloat16), "tensor", [(i, i ^ bit) for i in range(ranks)])


def halve(value, bit):
    half = value.shape[0] // 2
    high = lax.axis_index("tensor") & bit != 0
    low_rows, high_rows = value[:half], value[half:]
    got = exchange(jnp.where(high, low_rows, high_rows), bit)
    return jnp.where(high, high_rows, low_rows), got


def hops(owner, bit):
    groups, ranks, blocks = (lax.axis_size(a) for a in ("groups", "tensor", "dp"))
    pairs = []
    for g in range(groups):
        for p in range(blocks):
            target = owner[g, p]
            for z in range(ranks):
                if z % bit == target % bit and (z ^ target) & bit:
                    pairs.append(((g * ranks + z) * blocks + p, (g * ranks + (z ^ bit)) * blocks + p))
    return pairs


def send(value, pairs):
    return lax.ppermute(value, ("groups", "tensor", "dp"), pairs)


def exchangeable(owners):
    if lax.axis_size("tensor") != 4 or len(owners) != 2:
        return False
    one, two = hops(owners[0], 2), hops(owners[1], 2)
    return all(not {x[i] for x in one} & {x[i] for x in two} for i in range(2))


def later_steps(values, owners):
    ranks = lax.axis_size("tensor")
    ends = []
    for value, owner in zip(values, owners):
        bit, got = 2, None
        while bit < ranks:
            if got is not None:
                (value,) = add([value], [got], [[value.shape[0]]], [])
            got = send(value, hops(owner, bit))
            bit *= 2
        ends.append((value, got))
    return ends


def per_device(
    layer_input,
    gate_act,
    up_act,
    out_grad,
    w_gate,
    w_up,
    w_down,
    proj_x,
    proj_u,
    proj_h,
    proj_g,
    doc_lengths,
):
    groups, ranks = lax.axis_size("groups"), lax.axis_size("tensor")
    blocks = lax.axis_size("dp")
    chips = blocks // CORES
    group, rank = lax.axis_index("groups"), lax.axis_index("tensor")
    place = lax.axis_index("dp")
    chip, core = place // CORES, place % CORES
    rows = w_gate.shape[0]
    count = layer_input.shape[0]
    features = out_grad.shape[1]
    part = rows // groups
    edges = chunk_edges(part)
    chunks = len(CHUNKS)
    split = max(1, ranks // blocks)
    group_word = jnp.full((1,), group, jnp.int32)
    rank_word = jnp.full((1,), rank, jnp.int32)

    below, above = spread_ranks(out_grad.T)
    spans = list(zip(edges, edges[1:]))
    _, shares = share_rows(w_gate, w_up, group_word, spans[:2], [], [])
    slopes, in_down_part = prepare(gate_act, up_act, proj_h.T, [shares[0]])
    early_part = jnp.concatenate([project(proj_x, layer_input), in_down_part], axis=0)
    out_down_part = project(proj_g, out_grad)
    fetched, ticks = {}, []

    def fetch(k):
        for s in range(1, chips):
            fetched[k, s, 0] = from_chip(shares[k], s)
            for r in range(1, groups):
                fetched[k, s, r] = from_group(fetched[k, s, 0], r)

    def forward(k, waits, after, held=()):
        names = [(k, 0)] + waits
        arrived = [fetched[n] for n in fetched if (n[0], n[2]) in names]
        arrived = [a for a in arrived if not any(a is h for h in held)]
        carried, fresh = share_rows(
            w_gate, w_up, group_word, spans[k + 2 : k + 3], list(held), arrived + list(after)
        )
        ticks.append(fresh[0])
        if k + 2 < chunks:
            shares.extend(fresh)
            fetch(k + 2)
        return carried

    def owner_of(s, first_of):
        table = np.zeros((groups, blocks), np.int64)
        for g in range(groups):
            for p in range(blocks):
                block = (p // CORES + s) % chips * CORES + p % CORES
                table[g, p] = (block * rows + first_of(g)) // features
        return table

    far_routes = []
    for s in range(1, chips):
        for r in range(groups):
            table = owner_of(s, lambda g: (g + r) % groups * part)
            for route in far_routes:
                if route[0] == s and (route[1] == table).all():
                    route[2].append(r)
                    break
            else:
                far_routes.append((s, table, [r]))
    height = rows // split
    near_tables = [owner_of(0, lambda g: j * height) for j in range(split)]
    near_routes = [
        [(w_gate[j * height : (j + 1) * height], w_up[j * height : (j + 1) * height])]
        for j in range(split)
    ]

    def terms(names, grads, after, price, near=False, extra=None):
        routes = list(zip(near_tables, near_routes, [None] * split)) if near else []
        for s, table, shifts in far_routes:
            units = [(k, s, q) for k, q in names if q in shifts]
            if units:
                routes.append((table, [(fetched[n],) for n in units], units))
        bundles = {}
        for route in routes:
            bundles.setdefault((route[0] % 2).tobytes(), []).append(route)
        bundles = list(bundles.values())
        joined = [[u for _, units, _ in b for u in units] for b in bundles]
        outs = list(weigh(joined, grads, after, price, extra))
        got = [send(out, hops(b[0][0], 1)) for out, b in zip(outs, bundles)]
        return outs, got, bundles

    def carry_on(works, after, price=2, at_once=False):
        outs, got, bundles = ([v for work in works for v in work[i]] for i in range(3))
        heights = [[sum(u[0].shape[-2] for u in units) for _, units, _ in b] for b in bundles]
        routes = [route for b in bundles for route in b]
        owners = [table for table, _, _ in routes]
        if at_once and exchangeable(owners):
            target = place * rows // features
            first = ((rank ^ target) & 2 != 0).astype(jnp.int32).reshape(1)
            *sums, sent = add(outs, got, heights, after, price, first)
            came = send(sent, sorted(hops(owners[0], 2) + hops(owners[1], 2)))
            ends = [(v, came) for v in sums]
        else:
            sums = list(add(outs, got, heights, after, price))
            ends = later_steps(sums, owners)
        return sums, [(names, *end) for (_, _, names), end in zip(routes, ends)]

    fetch(0)
    fetch(1)

    def hold_arrived(k, waits, after, held=()):
        names = [(k, s, 0) for s in range(1, chips)]
        values = forward(k, waits, after, [fetched[n] for n in names] + list(held))
        for n, value in zip(names, values):
            fetched[n] = value
            for r in range(1, groups):
                fetched[k, n[1], r] = from_group(value, r)
        return values[len(names) :]

    def chunks_of(numbers, shifts):
        return [(k, r) for r in shifts for k in numbers]

    others = range(1, groups)
    bits = [1 << i for i in range(ranks.bit_length() - 1)]
    hold_arrived(0, [], [slopes])
    so_far = hidden_part(rank_word, below, above, w_down, None, None, None, [ticks[0]])
    hold_arrived(1, chunks_of([0], others), [so_far])
    hold_arrived(2, chunks_of([1], others), [below[2], above[1], out_down_part, early_part])
    mine, up_out_part = hidden_part(
        rank_word, below, above, w_down, so_far, slopes, proj_u.T, [ticks[2]]
    )
    mine, early = forward(3, chunks_of([2], others) + [(4, 0)], [], [mine, early_part])
    theirs = swap_cores(mine)
    got = exchange(early, bits[0])
    first_names = chunks_of(range(5), [0]) + chunks_of(range(3), others)
    first_mine = terms(first_names, [mine], [ticks[3]], 24, near=True)
    early, got, up_out_part = forward(
        4, chunks_of([3], others) + [(5, 0)], first_mine[0], [early, got, up_out_part]
    )
    early = early + got

    out_parts = jnp.stack([up_out_part, out_down_part]).reshape(2, ranks, -1, count)
    out_parts = out_parts.transpose(1, 0, 2, 3).reshape(-1, count)
    half = out_parts.shape[0] // 2
    high = rank & bits[-1] != 0
    width = early.shape[0]
    got = exchange(
        jnp.concatenate([early, jnp.where(high, out_parts[:half], out_parts[half:])], axis=0),
        bits[-1],
    )
    first_theirs = terms(first_names, [theirs], [ticks[4]], 24, near=True)
    got, *held = forward(
        5, chunks_of([4], others), first_theirs[0], [got] + [fetched[6, s, 0] for s in range(1, chips)]
    )
    for s, value in enumerate(held, 1):
        fetched[6, s, 0] = value
        for r in range(1, groups):
            fetched[6, s, r] = from_group(value, r)
    early = early + got[:width]
    out_parts = jnp.where(high, out_parts[half:], out_parts[:half]) + got[width:]
    for bit in bits[1:-1]:
        early = early + exchange(early, bit)
    for bit in bits[-2:0:-1]:
        out_parts, got = halve(out_parts, bit)
        out_parts = out_parts + got
    out_parts, got = halve(out_parts, bits[0])
    sums_mine, end_mine = carry_on([first_mine], first_theirs[0], at_once=True)
    second_names = chunks_of([5, 6], [0]) + chunks_of([3, 4, 5], others)
    last_names = chunks_of([7], [0]) + chunks_of([6, 7], others)
    second = terms(second_names, [mine, theirs], [ticks[5]] + sums_mine, 16)
    held = [fetched[7, s, 0] for s in range(1, chips)]
    got, *held = forward(6, chunks_of([5], others), second[0], [got] + held)
    for s, value in enumerate(held, 1):
        fetched[7, s, 0] = value
        for r in range(1, groups):
            fetched[7, s, r] = from_group(value, r)
    out_parts = out_parts + got
    received = [got for _, _, got in end_mine]
    received += [fetched[n] for n in fetched if n[0] == 6 and n[2] > 0]
    sums_theirs, end_theirs = carry_on([first_theirs], [ticks[6]] + received)
    sums_second, end_second = carry_on([second], sums_theirs)
    last = terms(last_names, [mine, theirs], sums_second, 60)
    received = [got for names, _, got in end_theirs + end_second if names is not None]
    sums_last, end_last = carry_on([last], received, 2)

    early = early.astype(jnp.bfloat16)
    width = in_down_part.shape[0]
    in_up, in_down = early[:width], early[width:]
    out_parts = out_parts.astype(jnp.bfloat16)
    slot = out_parts.shape[0] // 2
    up_out, out_down = out_parts[:slot], out_parts[slot:]
    member = pack_table(doc_lengths, count)
    doc_logs = jnp.stack(
        [doc_outer(member, up_out, in_up), doc_outer(member, out_down, in_down)], axis=1
    )

    first = rank * features
    away = (first // rows // CORES - chip) % chips
    owner = first // rows % CORES == core
    inside = first % rows
    def tops(names):
        sizes = [edges[n[0] + 1] - edges[n[0]] for n in names]
        return [(sum(sizes[:i]), n) for i, n in enumerate(names)]

    words = jnp.stack([away, group, inside, owner]).astype(jnp.int32)

    def assembled(end, first, after, cuts):
        near = [pair for names, *pair in end if names is None]
        far = {}
        for names, *pair in end:
            if names is not None:
                far.update((n, (row, pair, 0)) for row, n in tops(names))
        for names, *pair in end_second:
            far.update((n, (row, pair, first)) for row, n in tops(names))
        return assemble(words, count, features, part, near, far, chips, after, cuts)

    total_theirs = assembled(end_theirs, count, sums_last, 2)
    total_mine = assembled(end_mine, 0, total_theirs, 1)
    from_partner = [swap_cores(v) for v in total_theirs]

    def pick(index, options):
        value = options[0]
        for at, option in enumerate(options[1:], 1):
            value = jnp.where(index == at, option, value)
        return value

    tail = {}
    settled = add(
        [v for _, v, _ in end_last],
        [got for _, _, got in end_last],
        [[v.shape[0]] for _, v, _ in end_last],
        total_mine,
    )
    for (names, _, _), value in zip(end_last, settled):
        tail.update(
            (n, value[row : row + edges[n[0] + 1] - edges[n[0]]]) for row, n in tops(names)
        )
    late = sorted({(k, r) for k, _, r in tail})
    pieces = jnp.concatenate(
        [pick(away - 1, [tail[k, s, r] for s in range(1, chips)]) for k, r in late], axis=0
    )
    input_grad = finish(
        words,
        part,
        total_mine,
        from_partner,
        pieces[:, :count],
        swap_cores(pieces[:, count:]),
        late,
        chips,
    )
    return (input_grad, doc_logs)


def solution(mesh):
    placed = (
        P(("groups", "dp"), "tensor"),
        P(("groups", "dp"), "tensor"),
        P(("groups", "dp"), "tensor"),
        P(("groups", "dp"), "tensor"),
        P("dp", "tensor"),
        P("dp", "tensor"),
        P("tensor", None),
        P("tensor", None),
        P("tensor", None),
        P("tensor", None),
        P("tensor", None),
        P(("groups", "dp"), None),
    )
    return jax.shard_map(
        per_device,
        mesh=mesh,
        in_specs=placed,
        out_specs=(P(("groups", "dp"), "tensor"), P(("groups", "dp"), None, "tensor")),
        check_vma=False,
    )
```

```python
import functools

import jax
import jax.numpy as jnp
import numpy as np
from jax import lax
from jax.experimental import pallas as pl
from jax.experimental.pallas import tpu as pltpu
from jax.sharding import PartitionSpec as P

CORES = 2
CHUNKS = (2,) * 8
VMEM_BYTES = 60 * 1024 * 1024
FLOPS_PER_US = 270_000_000
ANYWHERE = pl.BlockSpec(memory_space=pl.ANY)


def contract_right(left, right):
    return lax.dot_general(
        left, right, (((1,), (1,)), ((), ())), preferred_element_type=jnp.float32
    )


def project(proj, rows):
    return lax.dot_general(
        proj, rows, (((0,), (1,)), ((), ())), preferred_element_type=jnp.float32
    )


def pack_table(doc_lengths, count):
    lengths = doc_lengths[0]
    ends = jnp.cumsum(lengths)
    starts = ends - lengths
    position = jnp.arange(count, dtype=jnp.int32)[None, :]
    inside = (position >= starts[:, None]) & (position < ends[:, None])
    return inside.astype(jnp.bfloat16)


def doc_outer(member, grad_rows, inputs):
    count = member.shape[1]
    weighted = (member[:, None, :] * grad_rows[None, :, :]).reshape(-1, count)
    table = contract_right(weighted, inputs)
    return table.reshape(member.shape[0], grad_rows.shape[0] * inputs.shape[0])


def swap_cores(value):
    size = lax.axis_size("dp")
    return lax.ppermute(value, "dp", [(i, i ^ 1) for i in range(size)])


def from_chip(value, shift):
    size = lax.axis_size("dp")
    step = shift * CORES
    return lax.ppermute(value, "dp", [((i + step) % size, i) for i in range(size)])


def from_group(value, shift):
    size = lax.axis_size("groups")
    return lax.ppermute(value, "groups", [((i + shift) % size, i) for i in range(size)])


def chunk_edges(part):
    return [part // 16 * sum(CHUNKS[:k]) for k in range(len(CHUNKS) + 1)]


def cost(us):
    return pl.CostEstimate(flops=int(us * FLOPS_PER_US) + 1, bytes_accessed=1, transcendentals=0)


def widest(size, options):
    return next((w for w in options if size % w == 0), size)


def share_rows(w_gate, w_up, group, spans, carried, after):
    rows, width = w_gate.shape
    part = rows // lax.axis_size("groups")
    step = part // 16
    kept, waits, fresh = len(carried), len(after), len(spans)
    steps = max([(last - first) // step for first, last in spans], default=1)

    def kernel(group_ref, *refs):
        outs = refs[len(refs) - fresh :] if fresh else []
        for at, out in enumerate(outs):
            out[0] = refs[2 * at][...]
            out[1] = refs[2 * at + 1][...]
        if not fresh:
            refs[-1][...] = jnp.zeros_like(refs[-1])

    in_specs, out_specs = [], [ANYWHERE] * kept
    shapes = [jax.ShapeDtypeStruct(a.shape, a.dtype) for a in carried]
    for first, last in spans:
        at_rows = functools.partial(lambda f, i, g: (g[0] * (part // step) + f // step + i, 0), first)
        in_specs += [pl.BlockSpec((step, width), at_rows)] * 2
        out_specs.append(pl.BlockSpec((2, step, width), lambda i, g: (0, i, 0)))
        shapes.append(jax.ShapeDtypeStruct((2, last - first, width), w_gate.dtype))
    if not fresh:
        out_specs.append(pl.BlockSpec((8, 128), lambda i, g: (0, 0)))
        shapes.append(jax.ShapeDtypeStruct((8, 128), jnp.float32))
    results = pl.pallas_call(
        kernel,
        grid_spec=pltpu.PrefetchScalarGridSpec(
            num_scalar_prefetch=1,
            grid=(steps,),
            in_specs=in_specs + [ANYWHERE] * (kept + waits),
            out_specs=out_specs,
        ),
        out_shape=shapes,
        input_output_aliases={1 + 2 * fresh + i: i for i in range(kept)},
        compiler_params=pltpu.CompilerParams(vmem_limit_bytes=VMEM_BYTES),
        cost_estimate=cost(2),
        name="share_rows",
    )(group, *[w_gate, w_up] * fresh, *carried, *after)
    return list(results[:kept]), list(results[kept:])


def spread_ranks(value):
    ranks = lax.axis_size("tensor")
    below, above = [value], [value]
    for _ in range(1, ranks):
        below.append(lax.ppermute(below[-1], "tensor", [(i, i + 1) for i in range(ranks - 1)]))
        above.append(lax.ppermute(above[-1], "tensor", [(i + 1, i) for i in range(ranks - 1)]))
    return below, above[1:]


def prepare(gate_act, up_act, proj_h, after):
    count, hidden = gate_act.shape
    narrow = proj_h.shape[0]
    tile = widest(hidden, (512, 256, 128))

    def kernel(gate_ref, up_ref, proj_ref, *refs):
        slope_ref, down_ref = refs[-2:]

        @pl.when(pl.program_id(0) == 0)
        def _():
            down_ref[...] = jnp.zeros_like(down_ref)

        gate = gate_ref[...].astype(jnp.float32).T
        up = up_ref[...].astype(jnp.float32).T
        sigma = jax.nn.sigmoid(gate)
        swish = gate * sigma
        slope_ref[0] = up * sigma * (1.0 + gate * (1.0 - sigma))
        slope_ref[1] = swish
        down_ref[...] += jnp.dot(
            proj_ref[...], (swish * up).astype(jnp.bfloat16), preferred_element_type=jnp.float32
        )

    return pl.pallas_call(
        kernel,
        grid=(hidden // tile,),
        out_shape=[
            jax.ShapeDtypeStruct((2, hidden, count), jnp.float32),
            jax.ShapeDtypeStruct((narrow, count), jnp.float32),
        ],
        in_specs=[
            pl.BlockSpec((count, tile), lambda i: (0, i)),
            pl.BlockSpec((count, tile), lambda i: (0, i)),
            pl.BlockSpec((narrow, tile), lambda i: (0, i)),
        ]
        + [ANYWHERE] * len(after),
        out_specs=[
            pl.BlockSpec((2, tile, count), lambda i: (0, i, 0)),
            pl.BlockSpec((narrow, count), lambda i: (0, 0)),
        ],
        compiler_params=pltpu.CompilerParams(vmem_limit_bytes=VMEM_BYTES),
        cost_estimate=cost(12),
        name="prepare",
    )(gate_act, up_act, proj_h, *after)


def hidden_part(rank, below, above, w_down, so_far, slopes, proj_u, after):
    ranks = lax.axis_size("tensor")
    features, count = below[0].shape
    hidden = w_down.shape[0]
    finish = so_far is not None
    slots = ranks - 2 if finish else 2
    tile = widest(hidden, (896, 512, 128))
    sources = [(t, -1, below[t]) for t in range(2 if finish else 0, ranks if finish else 2)]
    sources += [(t, 1, above[t - 1]) for t in range(1, ranks if finish else 2)]

    def counts(z):
        both = ((z >= 1) & (z <= ranks - 2)).astype(jnp.int32)
        return both, jnp.maximum(z - 1, 0)

    def place_of(z, t, side):
        if not finish:
            return (0, z >= 0) if t == 0 else (1, z >= 1 if side < 0 else z == 0)
        both, under = counts(z)
        if side < 0:
            return both + t - 2, t <= z
        if t == 1:
            return 0, both == 1
        return both + under + t - 2, z + t <= ranks - 1

    def column(at, i, rank_ref):
        z = rank_ref[0]
        if not finish:
            return (i, z) if at == 0 else (i, jnp.where(z >= 1, z - 1, 1))
        both, under = counts(z)
        block = jnp.where(at < both + under, z - (at - both + 2), z + (at - both - under + 2))
        return (i, jnp.where(at < both, z + 1, block))

    def kernel(rank_ref, *refs):
        z = rank_ref[0]
        downs, arrived = refs[:slots], refs[slots : slots + len(sources)]
        grad_ref, sem = refs[-2:]
        rest = refs[slots + len(sources) :]

        def gather(wait):
            for at, (t, side, _) in enumerate(sources):
                place, valid = place_of(z, t, side)

                @pl.when(valid)
                def _():
                    rows = pl.ds(pl.multiple_of(place * features, features), features)
                    copy = pltpu.make_async_copy(arrived[at], grad_ref.at[rows, :], sem.at[at])
                    copy.wait() if wait else copy.start()

        @pl.when(pl.program_id(0) == 0)
        def _():
            gather(False)
            gather(True)

        wide = None
        for at in range(slots):
            term = jnp.dot(
                downs[at][...],
                grad_ref[at * features : (at + 1) * features, :],
                preferred_element_type=jnp.float32,
            )
            wide = term if wide is None else wide + term
        if finish:
            both_ref, out_ref = refs[-4:-2]
            wide = wide + rest[0][...]
            both_ref[0] = (wide * rest[1][0]).astype(jnp.bfloat16)
            up_grad = (wide * rest[1][1]).astype(jnp.bfloat16)
            both_ref[1] = up_grad
            part = jnp.dot(rest[2][...], up_grad, preferred_element_type=jnp.float32)

            @pl.when(pl.program_id(0) == 0)
            def _():
                out_ref[...] = part

            @pl.when(pl.program_id(0) > 0)
            def _():
                out_ref[...] += part

        else:
            refs[-3][...] = wide

    operands = [w_down] * slots + [value for _, _, value in sources]
    specs = [pl.BlockSpec((tile, features), functools.partial(column, at)) for at in range(slots)]
    specs += [ANYWHERE] * len(sources)
    if finish:
        narrow = proj_u.shape[0]
        operands += [so_far, slopes, proj_u]
        specs += [
            pl.BlockSpec((tile, count), lambda i, r: (i, 0)),
            pl.BlockSpec((2, tile, count), lambda i, r: (0, i, 0)),
            pl.BlockSpec((narrow, tile), lambda i, r: (0, i)),
        ]
        out_shape = [
            jax.ShapeDtypeStruct((2, hidden, count), jnp.bfloat16),
            jax.ShapeDtypeStruct((narrow, count), jnp.float32),
        ]
        out_specs = [
            pl.BlockSpec((2, tile, count), lambda i, r: (0, i, 0)),
            pl.BlockSpec((narrow, count), lambda i, r: (0, 0)),
        ]
    else:
        out_shape = jax.ShapeDtypeStruct((hidden, count), jnp.float32)
        out_specs = pl.BlockSpec((tile, count), lambda i, r: (i, 0))
    return pl.pallas_call(
        kernel,
        grid_spec=pltpu.PrefetchScalarGridSpec(
            num_scalar_prefetch=1,
            grid=(hidden // tile,),
            in_specs=specs + [ANYWHERE] * len(after),
            out_specs=out_specs,
            scratch_shapes=[
                pltpu.VMEM((slots * features, count), jnp.bfloat16),
                pltpu.SemaphoreType.DMA((len(sources),)),
            ],
        ),
        out_shape=out_shape,
        compiler_params=pltpu.CompilerParams(vmem_limit_bytes=VMEM_BYTES),
        cost_estimate=cost(12),
        name="hidden_part",
    )(rank, *operands, *after)


def weigh(routes, grads, after, price, extra=None):
    hidden = grads[0].shape[1]
    tile = widest(hidden, (512, 256, 128))
    steps = hidden // tile
    heights = [sum(u[0].shape[-2] for u in units) for units in routes]
    rows, count = sum(heights), sum(g.shape[2] for g in grads)
    units = [u for route in routes for u in route]
    flat = [w for u in units for w in u]
    extras = [] if extra is None else [extra]

    def kernel(*refs):
        weights, both = list(refs[: len(flat)]), refs[len(flat) : len(flat) + len(grads)]
        more = refs[len(flat) + len(grads) : len(flat) + len(grads) + len(extras)]
        outs, total = refs[-1 - len(routes) - len(extras) : -1], refs[-1]
        at = pl.program_id(0)

        @pl.when(at == 0)
        def _():
            total[...] = jnp.zeros_like(total)

        gates, ups = [], []
        for u in units:
            mine, weights = weights[: len(u)], weights[len(u) :]
            gates.append(mine[0][...] if len(u) == 2 else mine[0][0])
            ups.append(mine[1][...] if len(u) == 2 else mine[0][1])
        gate, up = jnp.concatenate(gates, axis=0), jnp.concatenate(ups + [m[...] for m in more], axis=0)
        first = 0
        for ref in both:
            span = slice(first, first + ref.shape[2])
            by_up = jnp.dot(up, ref[1], preferred_element_type=jnp.float32)
            total[:rows, span] += (
                jnp.dot(gate, ref[0], preferred_element_type=jnp.float32) + by_up[:rows]
            )
            if more:
                total[rows:, span] += by_up[rows:]
            first += ref.shape[2]

        @pl.when(at == steps - 1)
        def _():
            top = 0
            for out, height in zip(outs, heights):
                out[...] = total[top : top + height].astype(jnp.bfloat16)
                top += height
            if more:
                outs[-1][...] = total[rows:]

    specs = []
    for w in flat:
        if w.ndim == 2:
            specs.append(pl.BlockSpec((w.shape[0], tile), lambda i: (0, i)))
        else:
            specs.append(pl.BlockSpec((2, w.shape[1], tile), lambda i: (0, 0, i)))
    for g in grads:
        specs.append(pl.BlockSpec((2, tile, g.shape[2]), lambda i: (0, i, 0)))
    shapes = [jax.ShapeDtypeStruct((h, count), jnp.bfloat16) for h in heights]
    for e in extras:
        specs.append(pl.BlockSpec((e.shape[0], tile), lambda i: (0, i)))
        shapes.append(jax.ShapeDtypeStruct((e.shape[0], count), jnp.float32))
    return pl.pallas_call(
        kernel,
        grid=(steps,),
        out_shape=shapes,
        in_specs=specs + [ANYWHERE] * len(after),
        out_specs=[pl.BlockSpec(s.shape, lambda i: (0, 0)) for s in shapes],
        scratch_shapes=[pltpu.VMEM((rows + sum(e.shape[0] for e in extras), count), jnp.float32)],
        compiler_params=pltpu.CompilerParams(vmem_limit_bytes=VMEM_BYTES),
        cost_estimate=cost(price),
        name="weigh_rows",
    )(*flat, *grads, *extras, *after)


def add(values, others, heights, after, price=2, first=None):
    pairs = len(values)
    flat = [h for hs in heights for h in hs]
    words = [] if first is None else [first]

    def kernel(*refs):
        ins = refs[len(words) :]
        outs = refs[len(refs) - len(flat) - len(words) :]
        at_out = 0
        for at in range(pairs):
            top = 0
            for height in heights[at]:
                rows = slice(top, top + height)
                outs[at_out][...] = (
                    ins[at][rows].astype(jnp.float32) + ins[pairs + at][rows].astype(jnp.float32)
                ).astype(jnp.bfloat16)
                top += height
                at_out += 1
        for at in range(2 * len(words)):

            @pl.when(refs[0][0] == 1 - at)
            def _(at=at):
                outs[-1][: flat[at]] = outs[at][...]
                if flat[at] < max(flat):
                    outs[-1][flat[at] :] = jnp.zeros((max(flat) - flat[at], count), jnp.bfloat16)

    count = values[0].shape[1]
    whole = pl.BlockSpec(memory_space=pltpu.VMEM)
    shapes = [jax.ShapeDtypeStruct((h, count), jnp.bfloat16) for h in flat + [max(flat)] * len(words)]
    return pl.pallas_call(
        kernel,
        out_shape=shapes,
        in_specs=[pl.BlockSpec(memory_space=pltpu.SMEM)] * len(words)
        + [whole] * (2 * pairs)
        + [ANYWHERE] * len(after),
        out_specs=[whole] * len(shapes),
        compiler_params=pltpu.CompilerParams(vmem_limit_bytes=VMEM_BYTES),
        cost_estimate=cost(price),
        name="add_terms",
    )(*words, *values, *others, *after)


def assemble(words, count, features, part, near, far, chips, after, cuts):
    groups = lax.axis_size("groups")
    height = near[0][0].shape[0]
    tall = features // part
    arrays, index = [], {}

    def at_of(value):
        if id(value) not in index:
            index[id(value)] = len(arrays)
            arrays.append(value)
        return index[id(value)]

    near_at = [[at_of(v) for v in pair] for pair in near]
    far_at = {n: (row, [at_of(v) for v in pair], first) for n, (row, pair, first) in far.items()}
    edges = chunk_edges(part)
    height_out = features // cuts

    def kernel(words_ref, *refs):
        outs = refs[-cuts:]
        away, group, inside = words_ref[0], words_ref[1], words_ref[2]

        def total(pair, rows, cols):
            one, two = (refs[at][rows, cols].astype(jnp.float32) for at in pair)
            return (one + two).astype(jnp.bfloat16)

        for j in range(len(near)):

            @pl.when((away == 0) & (inside == j * height))
            def _(j=j):
                for at, out in enumerate(outs):
                    out[...] = total(
                        near_at[j], slice(at * height_out, (at + 1) * height_out), slice(0, count)
                    )

        for s in range(1, chips):
            for g in range(groups):
                for h in range(0, groups, tall):

                    @pl.when((away == s) & (group == g) & (inside == h * part))
                    def _(s=s, g=g, h=h):
                        for j in range(tall):
                            shift = (h + j - g) % groups
                            for k in range(len(CHUNKS)):
                                top = j * part + edges[k]
                                piece = edges[k + 1] - edges[k]
                                if (k, s, shift) in far_at:
                                    row, pair, first = far_at[k, s, shift]
                                    value = total(
                                        pair, slice(row, row + piece), slice(first, first + count)
                                    )
                                else:
                                    value = jnp.zeros((piece, count), jnp.bfloat16)
                                at = top % height_out
                                outs[top // height_out][at : at + piece] = value

    whole = pl.BlockSpec(memory_space=pltpu.VMEM)
    return pl.pallas_call(
        kernel,
        out_shape=[jax.ShapeDtypeStruct((height_out, count), jnp.bfloat16)] * cuts,
        in_specs=[pl.BlockSpec(memory_space=pltpu.SMEM)]
        + [whole] * len(arrays)
        + [ANYWHERE] * len(after),
        out_specs=[whole] * cuts,
        compiler_params=pltpu.CompilerParams(vmem_limit_bytes=VMEM_BYTES),
        cost_estimate=cost(1),
        name="assemble",
    )(words, *arrays, *after)


def finish(words, part, mine, theirs, late_mine, late_theirs, late, chips):
    count = mine[0].shape[1]
    features = sum(m.shape[0] for m in mine)
    groups = lax.axis_size("groups")
    tall = features // part
    edges = chunk_edges(part)

    def kernel(words_ref, *refs):
        mine_refs, theirs_refs = refs[: len(mine)], refs[len(mine) : len(mine) + len(theirs)]
        late_mine_ref, late_theirs_ref, out_ref, rows_ref = refs[-4:]
        away, group, inside = words_ref[0], words_ref[1], words_ref[2]
        for own, bases, extra in (
            (1, mine_refs, late_mine_ref),
            (0, theirs_refs, late_theirs_ref),
        ):

            @pl.when(words_ref[3] == own)
            def _(bases=bases, extra=extra):
                first = 0
                for base in bases:
                    rows_ref[first : first + base.shape[0]] = base[...]
                    first += base.shape[0]
                for g in range(groups):
                    for h in range(0, groups, tall):

                        @pl.when((away > 0) & (group == g) & (inside == h * part))
                        def _(g=g, h=h):
                            for j in range(tall):
                                row = 0
                                for k, r in late:
                                    top, piece = j * part + edges[k], edges[k + 1] - edges[k]
                                    if (h + j - g) % groups == r:
                                        rows_ref[top : top + piece] = extra[row : row + piece]
                                    row += piece

        out_ref[...] = rows_ref[...].T

    whole = pl.BlockSpec(memory_space=pltpu.VMEM)
    return pl.pallas_call(
        kernel,
        out_shape=jax.ShapeDtypeStruct((count, features), jnp.bfloat16),
        in_specs=[pl.BlockSpec(memory_space=pltpu.SMEM)] + [whole] * (len(mine) + len(theirs) + 2),
        out_specs=whole,
        scratch_shapes=[pltpu.VMEM((features, count), jnp.bfloat16)],
        compiler_params=pltpu.CompilerParams(vmem_limit_bytes=VMEM_BYTES),
        cost_estimate=cost(3),
        name="finish",
    )(words, *mine, *theirs, late_mine, late_theirs)


def exchange(value, bit):
    ranks = lax.axis_size("tensor")
    return lax.ppermute(value.astype(jnp.bfloat16), "tensor", [(i, i ^ bit) for i in range(ranks)])


def halve(value, bit):
    half = value.shape[0] // 2
    high = lax.axis_index("tensor") & bit != 0
    low_rows, high_rows = value[:half], value[half:]
    got = exchange(jnp.where(high, low_rows, high_rows), bit)
    return jnp.where(high, high_rows, low_rows), got


def hops(owner, bit):
    groups, ranks, blocks = (lax.axis_size(a) for a in ("groups", "tensor", "dp"))
    pairs = []
    for g in range(groups):
        for p in range(blocks):
            target = owner[g, p]
            for z in range(ranks):
                if z % bit == target % bit and (z ^ target) & bit:
                    pairs.append(((g * ranks + z) * blocks + p, (g * ranks + (z ^ bit)) * blocks + p))
    return pairs


def send(value, pairs):
    return lax.ppermute(value, ("groups", "tensor", "dp"), pairs)


def exchangeable(owners):
    if lax.axis_size("tensor") != 4 or len(owners) != 2:
        return False
    one, two = hops(owners[0], 2), hops(owners[1], 2)
    return all(not {x[i] for x in one} & {x[i] for x in two} for i in range(2))


def later_steps(values, owners):
    ranks = lax.axis_size("tensor")
    ends = []
    for value, owner in zip(values, owners):
        bit, got = 2, None
        while bit < ranks:
            if got is not None:
                (value,) = add([value], [got], [[value.shape[0]]], [])
            got = send(value, hops(owner, bit))
            bit *= 2
        ends.append((value, got))
    return ends


def per_device(
    layer_input,
    gate_act,
    up_act,
    out_grad,
    w_gate,
    w_up,
    w_down,
    proj_x,
    proj_u,
    proj_h,
    proj_g,
    doc_lengths,
):
    groups, ranks = lax.axis_size("groups"), lax.axis_size("tensor")
    blocks = lax.axis_size("dp")
    chips = blocks // CORES
    group, rank = lax.axis_index("groups"), lax.axis_index("tensor")
    place = lax.axis_index("dp")
    chip, core = place // CORES, place % CORES
    rows = w_gate.shape[0]
    count = layer_input.shape[0]
    features = out_grad.shape[1]
    part = rows // groups
    edges = chunk_edges(part)
    chunks = len(CHUNKS)
    split = max(1, ranks // blocks)
    group_word = jnp.full((1,), group, jnp.int32)
    rank_word = jnp.full((1,), rank, jnp.int32)

    below, above = spread_ranks(out_grad.T)
    spans = list(zip(edges, edges[1:]))
    _, shares = share_rows(w_gate, w_up, group_word, spans[:2], [], [])
    slopes, in_down_part = prepare(gate_act, up_act, proj_h.T, [shares[0]])
    early_part = jnp.concatenate([project(proj_x, layer_input), in_down_part], axis=0)
    out_down_part = project(proj_g, out_grad)
    fetched, ticks = {}, []

    def fetch(k):
        for s in range(1, chips):
            fetched[k, s, 0] = from_chip(shares[k], s)
            for r in range(1, groups):
                fetched[k, s, r] = from_group(fetched[k, s, 0], r)

    def forward(k, waits, after, held=()):
        names = [(k, 0)] + waits
        arrived = [fetched[n] for n in fetched if (n[0], n[2]) in names]
        arrived = [a for a in arrived if not any(a is h for h in held)]
        carried, fresh = share_rows(
            w_gate, w_up, group_word, spans[k + 2 : k + 3], list(held), arrived + list(after)
        )
        ticks.append(fresh[0])
        if k + 2 < chunks:
            shares.extend(fresh)
            fetch(k + 2)
        return carried

    def owner_of(s, first_of):
        table = np.zeros((groups, blocks), np.int64)
        for g in range(groups):
            for p in range(blocks):
                block = (p // CORES + s) % chips * CORES + p % CORES
                table[g, p] = (block * rows + first_of(g)) // features
        return table

    far_routes = []
    for s in range(1, chips):
        for r in range(groups):
            table = owner_of(s, lambda g: (g + r) % groups * part)
            for route in far_routes:
                if route[0] == s and (route[1] == table).all():
                    route[2].append(r)
                    break
            else:
                far_routes.append((s, table, [r]))
    height = rows // split
    near_tables = [owner_of(0, lambda g: j * height) for j in range(split)]
    near_routes = [
        [(w_gate[j * height : (j + 1) * height], w_up[j * height : (j + 1) * height])]
        for j in range(split)
    ]

    def terms(names, grads, after, price, near=False, extra=None):
        routes = list(zip(near_tables, near_routes, [None] * split)) if near else []
        for s, table, shifts in far_routes:
            units = [(k, s, q) for k, q in names if q in shifts]
            if units:
                routes.append((table, [(fetched[n],) for n in units], units))
        bundles = {}
        for route in routes:
            bundles.setdefault((route[0] % 2).tobytes(), []).append(route)
        bundles = list(bundles.values())
        joined = [[u for _, units, _ in b for u in units] for b in bundles]
        outs = list(weigh(joined, grads, after, price, extra))
        got = [send(out, hops(b[0][0], 1)) for out, b in zip(outs, bundles)]
        return outs, got, bundles

    def carry_on(works, after, price=2, at_once=False):
        outs, got, bundles = ([v for work in works for v in work[i]] for i in range(3))
        heights = [[sum(u[0].shape[-2] for u in units) for _, units, _ in b] for b in bundles]
        routes = [route for b in bundles for route in b]
        owners = [table for table, _, _ in routes]
        if at_once and exchangeable(owners):
            target = place * rows // features
            first = ((rank ^ target) & 2 != 0).astype(jnp.int32).reshape(1)
            *sums, sent = add(outs, got, heights, after, price, first)
            came = send(sent, sorted(hops(owners[0], 2) + hops(owners[1], 2)))
            ends = [(v, came) for v in sums]
        else:
            sums = list(add(outs, got, heights, after, price))
            ends = later_steps(sums, owners)
        return sums, [(names, *end) for (_, _, names), end in zip(routes, ends)]

    fetch(0)
    fetch(1)

    def hold_arrived(k, waits, after, held=()):
        names = [(k, s, 0) for s in range(1, chips)]
        values = forward(k, waits, after, [fetched[n] for n in names] + list(held))
        for n, value in zip(names, values):
            fetched[n] = value
            for r in range(1, groups):
                fetched[k, n[1], r] = from_group(value, r)
        return values[len(names) :]

    def chunks_of(numbers, shifts):
        return [(k, r) for r in shifts for k in numbers]

    others = range(1, groups)
    bits = [1 << i for i in range(ranks.bit_length() - 1)]
    hold_arrived(0, [], [slopes])
    so_far = hidden_part(rank_word, below, above, w_down, None, None, None, [ticks[0]])
    hold_arrived(1, chunks_of([0], others), [so_far])
    hold_arrived(2, chunks_of([1], others), [below[2], above[1], out_down_part, early_part])
    mine, up_out_part = hidden_part(
        rank_word, below, above, w_down, so_far, slopes, proj_u.T, [ticks[2]]
    )
    mine, early = forward(3, chunks_of([2], others) + [(4, 0)], [], [mine, early_part])
    theirs = swap_cores(mine)
    got = exchange(early, bits[0])
    first_names = chunks_of(range(5), [0]) + chunks_of(range(3), others)
    first_mine = terms(first_names, [mine], [ticks[3]], 24, near=True)
    early, got, up_out_part = forward(
        4, chunks_of([3], others) + [(5, 0)], first_mine[0], [early, got, up_out_part]
    )
    early = early + got

    out_parts = jnp.stack([up_out_part, out_down_part]).reshape(2, ranks, -1, count)
    out_parts = out_parts.transpose(1, 0, 2, 3).reshape(-1, count)
    half = out_parts.shape[0] // 2
    high = rank & bits[-1] != 0
    width = early.shape[0]
    got = exchange(
        jnp.concatenate([early, jnp.where(high, out_parts[:half], out_parts[half:])], axis=0),
        bits[-1],
    )
    first_theirs = terms(first_names, [theirs], [ticks[4]], 24, near=True)
    got, *held = forward(
        5, chunks_of([4], others), first_theirs[0], [got] + [fetched[6, s, 0] for s in range(1, chips)]
    )
    for s, value in enumerate(held, 1):
        fetched[6, s, 0] = value
        for r in range(1, groups):
            fetched[6, s, r] = from_group(value, r)
    sums_mine, end_mine = carry_on([first_mine], first_theirs[0], at_once=True)
    second_names = chunks_of([5, 6], [0]) + chunks_of([3, 4, 5], others)
    last_names = chunks_of([7], [0]) + chunks_of([6, 7], others)
    second = terms(second_names, [mine, theirs], [ticks[5]] + sums_mine, 16)
    held = [fetched[7, s, 0] for s in range(1, chips)]
    got, *held = forward(6, chunks_of([5], others), second[0], [got] + held)
    for s, value in enumerate(held, 1):
        fetched[7, s, 0] = value
        for r in range(1, groups):
            fetched[7, s, r] = from_group(value, r)
    early = early + got[:width]
    out_parts = jnp.where(high, out_parts[half:], out_parts[:half]) + got[width:]
    for bit in bits[1:-1]:
        early = early + exchange(early, bit)
    for bit in bits[-2::-1]:
        out_parts, got = halve(out_parts, bit)
        out_parts = out_parts + got
    received = [got for _, _, got in end_mine]
    received += [fetched[n] for n in fetched if n[0] == 6 and n[2] > 0]
    sums_theirs, end_theirs = carry_on([first_theirs], [ticks[6]] + received)
    sums_second, end_second = carry_on([second], sums_theirs)
    last = terms(last_names, [mine, theirs], sums_second, 60)
    received = [got for names, _, got in end_theirs + end_second if names is not None]
    sums_last, end_last = carry_on([last], received, 2)

    early = early.astype(jnp.bfloat16)
    width = in_down_part.shape[0]
    in_up, in_down = early[:width], early[width:]
    out_parts = out_parts.astype(jnp.bfloat16)
    slot = out_parts.shape[0] // 2
    up_out, out_down = out_parts[:slot], out_parts[slot:]
    member = pack_table(doc_lengths, count)
    doc_logs = jnp.stack(
        [doc_outer(member, up_out, in_up), doc_outer(member, out_down, in_down)], axis=1
    )

    first = rank * features
    away = (first // rows // CORES - chip) % chips
    owner = first // rows % CORES == core
    inside = first % rows
    def tops(names):
        sizes = [edges[n[0] + 1] - edges[n[0]] for n in names]
        return [(sum(sizes[:i]), n) for i, n in enumerate(names)]

    words = jnp.stack([away, group, inside, owner]).astype(jnp.int32)

    def assembled(end, first, after, cuts):
        near = [pair for names, *pair in end if names is None]
        far = {}
        for names, *pair in end:
            if names is not None:
                far.update((n, (row, pair, 0)) for row, n in tops(names))
        for names, *pair in end_second:
            far.update((n, (row, pair, first)) for row, n in tops(names))
        return assemble(words, count, features, part, near, far, chips, after, cuts)

    total_theirs = assembled(end_theirs, count, sums_last, 2)
    total_mine = assembled(end_mine, 0, total_theirs, 1)
    from_partner = [swap_cores(v) for v in total_theirs]

    def pick(index, options):
        value = options[0]
        for at, option in enumerate(options[1:], 1):
            value = jnp.where(index == at, option, value)
        return value

    tail = {}
    settled = add(
        [v for _, v, _ in end_last],
        [got for _, _, got in end_last],
        [[v.shape[0]] for _, v, _ in end_last],
        total_mine,
    )
    for (names, _, _), value in zip(end_last, settled):
        tail.update(
            (n, value[row : row + edges[n[0] + 1] - edges[n[0]]]) for row, n in tops(names)
        )
    late = sorted({(k, r) for k, _, r in tail})
    pieces = jnp.concatenate(
        [pick(away - 1, [tail[k, s, r] for s in range(1, chips)]) for k, r in late], axis=0
    )
    input_grad = finish(
        words,
        part,
        total_mine,
        from_partner,
        pieces[:, :count],
        swap_cores(pieces[:, count:]),
        late,
        chips,
    )
    return (input_grad, doc_logs)


def solution(mesh):
    placed = (
        P(("groups", "dp"), "tensor"),
        P(("groups", "dp"), "tensor"),
        P(("groups", "dp"), "tensor"),
        P(("groups", "dp"), "tensor"),
        P("dp", "tensor"),
        P("dp", "tensor"),
        P("tensor", None),
        P("tensor", None),
        P("tensor", None),
        P("tensor", None),
        P("tensor", None),
        P(("groups", "dp"), None),
    )
    return jax.shard_map(
        per_device,
        mesh=mesh,
        in_specs=placed,
        out_specs=(P(("groups", "dp"), "tensor"), P(("groups", "dp"), None, "tensor")),
        check_vma=False,
    )
```

```python
import functools

import jax
import jax.numpy as jnp
import numpy as np
from jax import lax
from jax.experimental import pallas as pl
from jax.experimental.pallas import tpu as pltpu
from jax.sharding import PartitionSpec as P

CORES = 2
CHUNKS = (2,) * 8
VMEM_BYTES = 60 * 1024 * 1024
FLOPS_PER_US = 270_000_000
ANYWHERE = pl.BlockSpec(memory_space=pl.ANY)


def contract_right(left, right):
    return lax.dot_general(
        left, right, (((1,), (1,)), ((), ())), preferred_element_type=jnp.float32
    )


def project(proj, rows):
    return lax.dot_general(
        proj, rows, (((0,), (1,)), ((), ())), preferred_element_type=jnp.float32
    )


def pack_table(doc_lengths, count):
    lengths = doc_lengths[0]
    ends = jnp.cumsum(lengths)
    starts = ends - lengths
    position = jnp.arange(count, dtype=jnp.int32)[None, :]
    inside = (position >= starts[:, None]) & (position < ends[:, None])
    return inside.astype(jnp.bfloat16)


def doc_outer(member, grad_rows, inputs):
    count = member.shape[1]
    weighted = (member[:, None, :] * grad_rows[None, :, :]).reshape(-1, count)
    table = contract_right(weighted, inputs)
    return table.reshape(member.shape[0], grad_rows.shape[0] * inputs.shape[0])


def swap_cores(value):
    size = lax.axis_size("dp")
    return lax.ppermute(value, "dp", [(i, i ^ 1) for i in range(size)])


def from_chip(value, shift):
    size = lax.axis_size("dp")
    step = shift * CORES
    return lax.ppermute(value, "dp", [((i + step) % size, i) for i in range(size)])


def from_group(value, shift):
    size = lax.axis_size("groups")
    return lax.ppermute(value, "groups", [((i + shift) % size, i) for i in range(size)])


def chunk_edges(part):
    return [part // 16 * sum(CHUNKS[:k]) for k in range(len(CHUNKS) + 1)]


def cost(us):
    return pl.CostEstimate(flops=int(us * FLOPS_PER_US) + 1, bytes_accessed=1, transcendentals=0)


def widest(size, options):
    return next((w for w in options if size % w == 0), size)


def share_rows(w_gate, w_up, group, spans, carried, after):
    rows, width = w_gate.shape
    part = rows // lax.axis_size("groups")
    step = part // 16
    kept, waits, fresh = len(carried), len(after), len(spans)
    steps = max([(last - first) // step for first, last in spans], default=1)

    def kernel(group_ref, *refs):
        outs = refs[len(refs) - fresh :] if fresh else []
        for at, out in enumerate(outs):
            out[0] = refs[2 * at][...]
            out[1] = refs[2 * at + 1][...]
        if not fresh:
            refs[-1][...] = jnp.zeros_like(refs[-1])

    in_specs, out_specs = [], [ANYWHERE] * kept
    shapes = [jax.ShapeDtypeStruct(a.shape, a.dtype) for a in carried]
    for first, last in spans:
        at_rows = functools.partial(lambda f, i, g: (g[0] * (part // step) + f // step + i, 0), first)
        in_specs += [pl.BlockSpec((step, width), at_rows)] * 2
        out_specs.append(pl.BlockSpec((2, step, width), lambda i, g: (0, i, 0)))
        shapes.append(jax.ShapeDtypeStruct((2, last - first, width), w_gate.dtype))
    if not fresh:
        out_specs.append(pl.BlockSpec((8, 128), lambda i, g: (0, 0)))
        shapes.append(jax.ShapeDtypeStruct((8, 128), jnp.float32))
    results = pl.pallas_call(
        kernel,
        grid_spec=pltpu.PrefetchScalarGridSpec(
            num_scalar_prefetch=1,
            grid=(steps,),
            in_specs=in_specs + [ANYWHERE] * (kept + waits),
            out_specs=out_specs,
        ),
        out_shape=shapes,
        input_output_aliases={1 + 2 * fresh + i: i for i in range(kept)},
        compiler_params=pltpu.CompilerParams(vmem_limit_bytes=VMEM_BYTES),
        cost_estimate=cost(2),
        name="share_rows",
    )(group, *[w_gate, w_up] * fresh, *carried, *after)
    return list(results[:kept]), list(results[kept:])


def spread_ranks(value):
    ranks = lax.axis_size("tensor")
    below, above = [value], [value]
    for _ in range(1, ranks):
        below.append(lax.ppermute(below[-1], "tensor", [(i, i + 1) for i in range(ranks - 1)]))
        above.append(lax.ppermute(above[-1], "tensor", [(i + 1, i) for i in range(ranks - 1)]))
    return below, above[1:]


def prepare(gate_act, up_act, proj_h, after):
    count, hidden = gate_act.shape
    narrow = proj_h.shape[0]
    tile = widest(hidden, (512, 256, 128))

    def kernel(gate_ref, up_ref, proj_ref, *refs):
        slope_ref, down_ref = refs[-2:]

        @pl.when(pl.program_id(0) == 0)
        def _():
            down_ref[...] = jnp.zeros_like(down_ref)

        gate = gate_ref[...].astype(jnp.float32).T
        up = up_ref[...].astype(jnp.float32).T
        sigma = jax.nn.sigmoid(gate)
        swish = gate * sigma
        slope_ref[0] = up * sigma * (1.0 + gate * (1.0 - sigma))
        slope_ref[1] = swish
        down_ref[...] += jnp.dot(
            proj_ref[...], (swish * up).astype(jnp.bfloat16), preferred_element_type=jnp.float32
        )

    return pl.pallas_call(
        kernel,
        grid=(hidden // tile,),
        out_shape=[
            jax.ShapeDtypeStruct((2, hidden, count), jnp.float32),
            jax.ShapeDtypeStruct((narrow, count), jnp.float32),
        ],
        in_specs=[
            pl.BlockSpec((count, tile), lambda i: (0, i)),
            pl.BlockSpec((count, tile), lambda i: (0, i)),
            pl.BlockSpec((narrow, tile), lambda i: (0, i)),
        ]
        + [ANYWHERE] * len(after),
        out_specs=[
            pl.BlockSpec((2, tile, count), lambda i: (0, i, 0)),
            pl.BlockSpec((narrow, count), lambda i: (0, 0)),
        ],
        compiler_params=pltpu.CompilerParams(vmem_limit_bytes=VMEM_BYTES),
        cost_estimate=cost(12),
        name="prepare",
    )(gate_act, up_act, proj_h, *after)


def hidden_part(rank, below, above, w_down, so_far, slopes, proj_u, after):
    ranks = lax.axis_size("tensor")
    features, count = below[0].shape
    hidden = w_down.shape[0]
    finish = so_far is not None
    slots = ranks - 2 if finish else 2
    tile = widest(hidden, (896, 512, 128))
    sources = [(t, -1, below[t]) for t in range(2 if finish else 0, ranks if finish else 2)]
    sources += [(t, 1, above[t - 1]) for t in range(1, ranks if finish else 2)]

    def counts(z):
        both = ((z >= 1) & (z <= ranks - 2)).astype(jnp.int32)
        return both, jnp.maximum(z - 1, 0)

    def place_of(z, t, side):
        if not finish:
            return (0, z >= 0) if t == 0 else (1, z >= 1 if side < 0 else z == 0)
        both, under = counts(z)
        if side < 0:
            return both + t - 2, t <= z
        if t == 1:
            return 0, both == 1
        return both + under + t - 2, z + t <= ranks - 1

    def column(at, i, rank_ref):
        z = rank_ref[0]
        if not finish:
            return (i, z) if at == 0 else (i, jnp.where(z >= 1, z - 1, 1))
        both, under = counts(z)
        block = jnp.where(at < both + under, z - (at - both + 2), z + (at - both - under + 2))
        return (i, jnp.where(at < both, z + 1, block))

    def kernel(rank_ref, *refs):
        z = rank_ref[0]
        downs, arrived = refs[:slots], refs[slots : slots + len(sources)]
        grad_ref, sem = refs[-2:]
        rest = refs[slots + len(sources) :]

        def gather(wait):
            for at, (t, side, _) in enumerate(sources):
                place, valid = place_of(z, t, side)

                @pl.when(valid)
                def _():
                    rows = pl.ds(pl.multiple_of(place * features, features), features)
                    copy = pltpu.make_async_copy(arrived[at], grad_ref.at[rows, :], sem.at[at])
                    copy.wait() if wait else copy.start()

        @pl.when(pl.program_id(0) == 0)
        def _():
            gather(False)
            gather(True)

        wide = None
        for at in range(slots):
            term = jnp.dot(
                downs[at][...],
                grad_ref[at * features : (at + 1) * features, :],
                preferred_element_type=jnp.float32,
            )
            wide = term if wide is None else wide + term
        if finish:
            both_ref, out_ref = refs[-4:-2]
            wide = wide + rest[0][...]
            both_ref[0] = (wide * rest[1][0]).astype(jnp.bfloat16)
            up_grad = (wide * rest[1][1]).astype(jnp.bfloat16)
            both_ref[1] = up_grad
            part = jnp.dot(rest[2][...], up_grad, preferred_element_type=jnp.float32)

            @pl.when(pl.program_id(0) == 0)
            def _():
                out_ref[...] = part

            @pl.when(pl.program_id(0) > 0)
            def _():
                out_ref[...] += part

        else:
            refs[-3][...] = wide

    operands = [w_down] * slots + [value for _, _, value in sources]
    specs = [pl.BlockSpec((tile, features), functools.partial(column, at)) for at in range(slots)]
    specs += [ANYWHERE] * len(sources)
    if finish:
        narrow = proj_u.shape[0]
        operands += [so_far, slopes, proj_u]
        specs += [
            pl.BlockSpec((tile, count), lambda i, r: (i, 0)),
            pl.BlockSpec((2, tile, count), lambda i, r: (0, i, 0)),
            pl.BlockSpec((narrow, tile), lambda i, r: (0, i)),
        ]
        out_shape = [
            jax.ShapeDtypeStruct((2, hidden, count), jnp.bfloat16),
            jax.ShapeDtypeStruct((narrow, count), jnp.float32),
        ]
        out_specs = [
            pl.BlockSpec((2, tile, count), lambda i, r: (0, i, 0)),
            pl.BlockSpec((narrow, count), lambda i, r: (0, 0)),
        ]
    else:
        out_shape = jax.ShapeDtypeStruct((hidden, count), jnp.float32)
        out_specs = pl.BlockSpec((tile, count), lambda i, r: (i, 0))
    return pl.pallas_call(
        kernel,
        grid_spec=pltpu.PrefetchScalarGridSpec(
            num_scalar_prefetch=1,
            grid=(hidden // tile,),
            in_specs=specs + [ANYWHERE] * len(after),
            out_specs=out_specs,
            scratch_shapes=[
                pltpu.VMEM((slots * features, count), jnp.bfloat16),
                pltpu.SemaphoreType.DMA((len(sources),)),
            ],
        ),
        out_shape=out_shape,
        compiler_params=pltpu.CompilerParams(vmem_limit_bytes=VMEM_BYTES),
        cost_estimate=cost(12),
        name="hidden_part",
    )(rank, *operands, *after)


def weigh(routes, grads, after, price, extra=None):
    hidden = grads[0].shape[1]
    tile = widest(hidden, (512, 256, 128))
    steps = hidden // tile
    heights = [sum(u[0].shape[-2] for u in units) for units in routes]
    rows, count = sum(heights), sum(g.shape[2] for g in grads)
    units = [u for route in routes for u in route]
    flat = [w for u in units for w in u]
    extras = [] if extra is None else [extra]

    def kernel(*refs):
        weights, both = list(refs[: len(flat)]), refs[len(flat) : len(flat) + len(grads)]
        more = refs[len(flat) + len(grads) : len(flat) + len(grads) + len(extras)]
        outs, total = refs[-1 - len(routes) - len(extras) : -1], refs[-1]
        at = pl.program_id(0)

        @pl.when(at == 0)
        def _():
            total[...] = jnp.zeros_like(total)

        gates, ups = [], []
        for u in units:
            mine, weights = weights[: len(u)], weights[len(u) :]
            gates.append(mine[0][...] if len(u) == 2 else mine[0][0])
            ups.append(mine[1][...] if len(u) == 2 else mine[0][1])
        gate, up = jnp.concatenate(gates, axis=0), jnp.concatenate(ups + [m[...] for m in more], axis=0)
        first = 0
        for ref in both:
            span = slice(first, first + ref.shape[2])
            by_up = jnp.dot(up, ref[1], preferred_element_type=jnp.float32)
            total[:rows, span] += (
                jnp.dot(gate, ref[0], preferred_element_type=jnp.float32) + by_up[:rows]
            )
            if more:
                total[rows:, span] += by_up[rows:]
            first += ref.shape[2]

        @pl.when(at == steps - 1)
        def _():
            top = 0
            for out, height in zip(outs, heights):
                out[...] = total[top : top + height].astype(jnp.bfloat16)
                top += height
            if more:
                outs[-1][...] = total[rows:]

    specs = []
    for w in flat:
        if w.ndim == 2:
            specs.append(pl.BlockSpec((w.shape[0], tile), lambda i: (0, i)))
        else:
            specs.append(pl.BlockSpec((2, w.shape[1], tile), lambda i: (0, 0, i)))
    for g in grads:
        specs.append(pl.BlockSpec((2, tile, g.shape[2]), lambda i: (0, i, 0)))
    shapes = [jax.ShapeDtypeStruct((h, count), jnp.bfloat16) for h in heights]
    for e in extras:
        specs.append(pl.BlockSpec((e.shape[0], tile), lambda i: (0, i)))
        shapes.append(jax.ShapeDtypeStruct((e.shape[0], count), jnp.float32))
    return pl.pallas_call(
        kernel,
        grid=(steps,),
        out_shape=shapes,
        in_specs=specs + [ANYWHERE] * len(after),
        out_specs=[pl.BlockSpec(s.shape, lambda i: (0, 0)) for s in shapes],
        scratch_shapes=[pltpu.VMEM((rows + sum(e.shape[0] for e in extras), count), jnp.float32)],
        compiler_params=pltpu.CompilerParams(vmem_limit_bytes=VMEM_BYTES),
        cost_estimate=cost(price),
        name="weigh_rows",
    )(*flat, *grads, *extras, *after)


def add(values, others, heights, after, price=2, first=None):
    pairs = len(values)
    flat = [h for hs in heights for h in hs]
    words = [] if first is None else [first]

    def kernel(*refs):
        ins = refs[len(words) :]
        outs = refs[len(refs) - len(flat) - len(words) :]
        at_out = 0
        for at in range(pairs):
            top = 0
            for height in heights[at]:
                rows = slice(top, top + height)
                outs[at_out][...] = (
                    ins[at][rows].astype(jnp.float32) + ins[pairs + at][rows].astype(jnp.float32)
                ).astype(jnp.bfloat16)
                top += height
                at_out += 1
        for at in range(2 * len(words)):

            @pl.when(refs[0][0] == 1 - at)
            def _(at=at):
                outs[-1][: flat[at]] = outs[at][...]
                if flat[at] < max(flat):
                    outs[-1][flat[at] :] = jnp.zeros((max(flat) - flat[at], count), jnp.bfloat16)

    count = values[0].shape[1]
    whole = pl.BlockSpec(memory_space=pltpu.VMEM)
    shapes = [jax.ShapeDtypeStruct((h, count), jnp.bfloat16) for h in flat + [max(flat)] * len(words)]
    return pl.pallas_call(
        kernel,
        out_shape=shapes,
        in_specs=[pl.BlockSpec(memory_space=pltpu.SMEM)] * len(words)
        + [whole] * (2 * pairs)
        + [ANYWHERE] * len(after),
        out_specs=[whole] * len(shapes),
        compiler_params=pltpu.CompilerParams(vmem_limit_bytes=VMEM_BYTES),
        cost_estimate=cost(price),
        name="add_terms",
    )(*words, *values, *others, *after)


def assemble(words, count, features, part, near, far, chips, after, cuts):
    groups = lax.axis_size("groups")
    height = near[0][0].shape[0]
    tall = features // part
    arrays, index = [], {}

    def at_of(value):
        if id(value) not in index:
            index[id(value)] = len(arrays)
            arrays.append(value)
        return index[id(value)]

    near_at = [[at_of(v) for v in pair] for pair in near]
    far_at = {n: (row, [at_of(v) for v in pair], first) for n, (row, pair, first) in far.items()}
    edges = chunk_edges(part)
    height_out = features // cuts

    def kernel(words_ref, *refs):
        outs = refs[-cuts:]
        away, group, inside = words_ref[0], words_ref[1], words_ref[2]

        def total(pair, rows, cols):
            one, two = (refs[at][rows, cols].astype(jnp.float32) for at in pair)
            return (one + two).astype(jnp.bfloat16)

        for j in range(len(near)):

            @pl.when((away == 0) & (inside == j * height))
            def _(j=j):
                for at, out in enumerate(outs):
                    out[...] = total(
                        near_at[j], slice(at * height_out, (at + 1) * height_out), slice(0, count)
                    )

        for s in range(1, chips):
            for g in range(groups):
                for h in range(0, groups, tall):

                    @pl.when((away == s) & (group == g) & (inside == h * part))
                    def _(s=s, g=g, h=h):
                        for j in range(tall):
                            shift = (h + j - g) % groups
                            for k in range(len(CHUNKS)):
                                top = j * part + edges[k]
                                piece = edges[k + 1] - edges[k]
                                if (k, s, shift) in far_at:
                                    row, pair, first = far_at[k, s, shift]
                                    value = total(
                                        pair, slice(row, row + piece), slice(first, first + count)
                                    )
                                else:
                                    value = jnp.zeros((piece, count), jnp.bfloat16)
                                at = top % height_out
                                outs[top // height_out][at : at + piece] = value

    whole = pl.BlockSpec(memory_space=pltpu.VMEM)
    return pl.pallas_call(
        kernel,
        out_shape=[jax.ShapeDtypeStruct((height_out, count), jnp.bfloat16)] * cuts,
        in_specs=[pl.BlockSpec(memory_space=pltpu.SMEM)]
        + [whole] * len(arrays)
        + [ANYWHERE] * len(after),
        out_specs=[whole] * cuts,
        compiler_params=pltpu.CompilerParams(vmem_limit_bytes=VMEM_BYTES),
        cost_estimate=cost(1),
        name="assemble",
    )(words, *arrays, *after)


def finish(words, part, mine, theirs, late_mine, late_theirs, late, chips):
    count = mine[0].shape[1]
    features = sum(m.shape[0] for m in mine)
    groups = lax.axis_size("groups")
    tall = features // part
    edges = chunk_edges(part)

    def kernel(words_ref, *refs):
        mine_refs, theirs_refs = refs[: len(mine)], refs[len(mine) : len(mine) + len(theirs)]
        late_mine_ref, late_theirs_ref, out_ref, rows_ref = refs[-4:]
        away, group, inside = words_ref[0], words_ref[1], words_ref[2]
        for own, bases, extra in (
            (1, mine_refs, late_mine_ref),
            (0, theirs_refs, late_theirs_ref),
        ):

            @pl.when(words_ref[3] == own)
            def _(bases=bases, extra=extra):
                first = 0
                for base in bases:
                    rows_ref[first : first + base.shape[0]] = base[...]
                    first += base.shape[0]
                for g in range(groups):
                    for h in range(0, groups, tall):

                        @pl.when((away > 0) & (group == g) & (inside == h * part))
                        def _(g=g, h=h):
                            for j in range(tall):
                                row = 0
                                for k, r in late:
                                    top, piece = j * part + edges[k], edges[k + 1] - edges[k]
                                    if (h + j - g) % groups == r:
                                        rows_ref[top : top + piece] = extra[row : row + piece]
                                    row += piece

        out_ref[...] = rows_ref[...].T

    whole = pl.BlockSpec(memory_space=pltpu.VMEM)
    return pl.pallas_call(
        kernel,
        out_shape=jax.ShapeDtypeStruct((count, features), jnp.bfloat16),
        in_specs=[pl.BlockSpec(memory_space=pltpu.SMEM)] + [whole] * (len(mine) + len(theirs) + 2),
        out_specs=whole,
        scratch_shapes=[pltpu.VMEM((features, count), jnp.bfloat16)],
        compiler_params=pltpu.CompilerParams(vmem_limit_bytes=VMEM_BYTES),
        cost_estimate=cost(3),
        name="finish",
    )(words, *mine, *theirs, late_mine, late_theirs)


def exchange(value, bit):
    ranks = lax.axis_size("tensor")
    return lax.ppermute(value.astype(jnp.bfloat16), "tensor", [(i, i ^ bit) for i in range(ranks)])


def halve(value, bit):
    half = value.shape[0] // 2
    high = lax.axis_index("tensor") & bit != 0
    low_rows, high_rows = value[:half], value[half:]
    got = exchange(jnp.where(high, low_rows, high_rows), bit)
    return jnp.where(high, high_rows, low_rows), got


def hops(owner, bit):
    groups, ranks, blocks = (lax.axis_size(a) for a in ("groups", "tensor", "dp"))
    pairs = []
    for g in range(groups):
        for p in range(blocks):
            target = owner[g, p]
            for z in range(ranks):
                if z % bit == target % bit and (z ^ target) & bit:
                    pairs.append(((g * ranks + z) * blocks + p, (g * ranks + (z ^ bit)) * blocks + p))
    return pairs


def send(value, pairs):
    return lax.ppermute(value, ("groups", "tensor", "dp"), pairs)


def exchangeable(owners):
    if lax.axis_size("tensor") != 4 or len(owners) != 2:
        return False
    one, two = hops(owners[0], 2), hops(owners[1], 2)
    return all(not {x[i] for x in one} & {x[i] for x in two} for i in range(2))


def later_steps(values, owners):
    ranks = lax.axis_size("tensor")
    ends = []
    for value, owner in zip(values, owners):
        bit, got = 2, None
        while bit < ranks:
            if got is not None:
                (value,) = add([value], [got], [[value.shape[0]]], [])
            got = send(value, hops(owner, bit))
            bit *= 2
        ends.append((value, got))
    return ends


def per_device(
    layer_input,
    gate_act,
    up_act,
    out_grad,
    w_gate,
    w_up,
    w_down,
    proj_x,
    proj_u,
    proj_h,
    proj_g,
    doc_lengths,
):
    groups, ranks = lax.axis_size("groups"), lax.axis_size("tensor")
    blocks = lax.axis_size("dp")
    chips = blocks // CORES
    group, rank = lax.axis_index("groups"), lax.axis_index("tensor")
    place = lax.axis_index("dp")
    chip, core = place // CORES, place % CORES
    rows = w_gate.shape[0]
    count = layer_input.shape[0]
    features = out_grad.shape[1]
    part = rows // groups
    edges = chunk_edges(part)
    chunks = len(CHUNKS)
    split = max(1, ranks // blocks)
    group_word = jnp.full((1,), group, jnp.int32)
    rank_word = jnp.full((1,), rank, jnp.int32)

    below, above = spread_ranks(out_grad.T)
    spans = list(zip(edges, edges[1:]))
    _, shares = share_rows(w_gate, w_up, group_word, spans[:2], [], [])
    slopes, in_down_part = prepare(gate_act, up_act, proj_h.T, [shares[0]])
    early_part = jnp.concatenate([project(proj_x, layer_input), in_down_part], axis=0)
    out_down_part = project(proj_g, out_grad)
    fetched, ticks = {}, []

    def fetch(k):
        for s in range(1, chips):
            fetched[k, s, 0] = from_chip(shares[k], s)
            for r in range(1, groups):
                fetched[k, s, r] = from_group(fetched[k, s, 0], r)

    def forward(k, waits, after, held=()):
        names = [(k, 0)] + waits
        arrived = [fetched[n] for n in fetched if (n[0], n[2]) in names]
        arrived = [a for a in arrived if not any(a is h for h in held)]
        carried, fresh = share_rows(
            w_gate, w_up, group_word, spans[k + 2 : k + 3], list(held), arrived + list(after)
        )
        ticks.append(fresh[0])
        if k + 2 < chunks:
            shares.extend(fresh)
            fetch(k + 2)
        return carried

    def owner_of(s, first_of):
        table = np.zeros((groups, blocks), np.int64)
        for g in range(groups):
            for p in range(blocks):
                block = (p // CORES + s) % chips * CORES + p % CORES
                table[g, p] = (block * rows + first_of(g)) // features
        return table

    far_routes = []
    for s in range(1, chips):
        for r in range(groups):
            table = owner_of(s, lambda g: (g + r) % groups * part)
            for route in far_routes:
                if route[0] == s and (route[1] == table).all():
                    route[2].append(r)
                    break
            else:
                far_routes.append((s, table, [r]))
    height = rows // split
    near_tables = [owner_of(0, lambda g: j * height) for j in range(split)]
    near_routes = [
        [(w_gate[j * height : (j + 1) * height], w_up[j * height : (j + 1) * height])]
        for j in range(split)
    ]

    def terms(names, grads, after, price, near=False, extra=None):
        routes = list(zip(near_tables, near_routes, [None] * split)) if near else []
        for s, table, shifts in far_routes:
            units = [(k, s, q) for k, q in names if q in shifts]
            if units:
                routes.append((table, [(fetched[n],) for n in units], units))
        bundles = {}
        for route in routes:
            bundles.setdefault((route[0] % 2).tobytes(), []).append(route)
        bundles = list(bundles.values())
        joined = [[u for _, units, _ in b for u in units] for b in bundles]
        outs = list(weigh(joined, grads, after, price, extra))
        got = [send(out, hops(b[0][0], 1)) for out, b in zip(outs, bundles)]
        return outs, got, bundles

    def carry_on(works, after, price=2, at_once=False):
        outs, got, bundles = ([v for work in works for v in work[i]] for i in range(3))
        heights = [[sum(u[0].shape[-2] for u in units) for _, units, _ in b] for b in bundles]
        routes = [route for b in bundles for route in b]
        owners = [table for table, _, _ in routes]
        if at_once and exchangeable(owners):
            target = place * rows // features
            first = ((rank ^ target) & 2 != 0).astype(jnp.int32).reshape(1)
            *sums, sent = add(outs, got, heights, after, price, first)
            came = send(sent, sorted(hops(owners[0], 2) + hops(owners[1], 2)))
            ends = [(v, came) for v in sums]
        else:
            sums = list(add(outs, got, heights, after, price))
            ends = later_steps(sums, owners)
        return sums, [(names, *end) for (_, _, names), end in zip(routes, ends)]

    fetch(0)
    fetch(1)

    def hold_arrived(k, waits, after, held=()):
        names = [(k, s, 0) for s in range(1, chips)]
        values = forward(k, waits, after, [fetched[n] for n in names] + list(held))
        for n, value in zip(names, values):
            fetched[n] = value
            for r in range(1, groups):
                fetched[k, n[1], r] = from_group(value, r)
        return values[len(names) :]

    def chunks_of(numbers, shifts):
        return [(k, r) for r in shifts for k in numbers]

    others = range(1, groups)
    bits = [1 << i for i in range(ranks.bit_length() - 1)]
    hold_arrived(0, [], [slopes])
    so_far = hidden_part(rank_word, below, above, w_down, None, None, None, [ticks[0]])
    hold_arrived(1, chunks_of([0], others), [so_far])
    hold_arrived(2, chunks_of([1], others), [below[2], above[1], out_down_part, early_part])
    mine, up_out_part = hidden_part(
        rank_word, below, above, w_down, so_far, slopes, proj_u.T, [ticks[2]]
    )
    mine, early = forward(3, chunks_of([2], others) + [(4, 0)], [], [mine, early_part])
    theirs = swap_cores(mine)

    halvings = [bits[0], bits[-1]] + bits[1:-1]
    order = sorted(range(ranks), key=lambda r: [bool(r & b) for b in halvings])
    out_parts = jnp.stack([up_out_part, out_down_part]).reshape(2, ranks, -1, count)
    out_parts = jnp.concatenate([out_parts[:, r] for r in order], axis=0).reshape(-1, count)
    width = early.shape[0]

    def exchange_with(early, parts, bit):
        half = parts.shape[0] // 2
        high = rank & bit != 0
        got = exchange(
            jnp.concatenate([early, jnp.where(high, parts[:half], parts[half:])], axis=0), bit
        )
        return jnp.where(high, parts[half:], parts[:half]), got

    out_parts, got = exchange_with(early, out_parts, bits[0])
    first_names = chunks_of(range(5), [0]) + chunks_of(range(3), others)
    first_mine = terms(first_names, [mine], [ticks[3]], 24, near=True)
    early, out_parts, got = forward(
        4, chunks_of([3], others) + [(5, 0)], first_mine[0], [early, out_parts, got]
    )

    early, out_parts = early + got[:width], out_parts + got[width:]
    out_parts, got = exchange_with(early, out_parts, bits[-1])
    first_theirs = terms(first_names, [theirs], [ticks[4]], 24, near=True)
    got, *held = forward(
        5, chunks_of([4], others), first_theirs[0], [got] + [fetched[6, s, 0] for s in range(1, chips)]
    )
    for s, value in enumerate(held, 1):
        fetched[6, s, 0] = value
        for r in range(1, groups):
            fetched[6, s, r] = from_group(value, r)
    sums_mine, end_mine = carry_on([first_mine], first_theirs[0], at_once=True)
    second_names = chunks_of([5, 6], [0]) + chunks_of([3, 4, 5], others)
    last_names = chunks_of([7], [0]) + chunks_of([6, 7], others)
    second = terms(second_names, [mine, theirs], [ticks[5]] + sums_mine, 16)
    held = [fetched[7, s, 0] for s in range(1, chips)]
    got, *held = forward(6, chunks_of([5], others), second[0], [got] + held)
    for s, value in enumerate(held, 1):
        fetched[7, s, 0] = value
        for r in range(1, groups):
            fetched[7, s, r] = from_group(value, r)
    early, out_parts = early + got[:width], out_parts + got[width:]
    for bit in bits[1:-1]:
        early = early + exchange(early, bit)
        out_parts, got = halve(out_parts, bit)
        out_parts = out_parts + got
    received = [got for _, _, got in end_mine]
    received += [fetched[n] for n in fetched if n[0] == 6 and n[2] > 0]
    sums_theirs, end_theirs = carry_on([first_theirs], [ticks[6]] + received)
    sums_second, end_second = carry_on([second], sums_theirs)
    last = terms(last_names, [mine, theirs], sums_second, 60)
    received = [got for names, _, got in end_theirs + end_second if names is not None]
    sums_last, end_last = carry_on([last], received, 2)

    early = early.astype(jnp.bfloat16)
    width = in_down_part.shape[0]
    in_up, in_down = early[:width], early[width:]
    out_parts = out_parts.astype(jnp.bfloat16)
    slot = out_parts.shape[0] // 2
    up_out, out_down = out_parts[:slot], out_parts[slot:]
    member = pack_table(doc_lengths, count)
    doc_logs = jnp.stack(
        [doc_outer(member, up_out, in_up), doc_outer(member, out_down, in_down)], axis=1
    )

    first = rank * features
    away = (first // rows // CORES - chip) % chips
    owner = first // rows % CORES == core
    inside = first % rows
    def tops(names):
        sizes = [edges[n[0] + 1] - edges[n[0]] for n in names]
        return [(sum(sizes[:i]), n) for i, n in enumerate(names)]

    words = jnp.stack([away, group, inside, owner]).astype(jnp.int32)

    def assembled(end, first, after, cuts):
        near = [pair for names, *pair in end if names is None]
        far = {}
        for names, *pair in end:
            if names is not None:
                far.update((n, (row, pair, 0)) for row, n in tops(names))
        for names, *pair in end_second:
            far.update((n, (row, pair, first)) for row, n in tops(names))
        return assemble(words, count, features, part, near, far, chips, after, cuts)

    total_theirs = assembled(end_theirs, count, sums_last, 2)
    total_mine = assembled(end_mine, 0, total_theirs, 1)
    from_partner = [swap_cores(v) for v in total_theirs]

    def pick(index, options):
        value = options[0]
        for at, option in enumerate(options[1:], 1):
            value = jnp.where(index == at, option, value)
        return value

    tail = {}
    settled = add(
        [v for _, v, _ in end_last],
        [got for _, _, got in end_last],
        [[v.shape[0]] for _, v, _ in end_last],
        total_mine,
    )
    for (names, _, _), value in zip(end_last, settled):
        tail.update(
            (n, value[row : row + edges[n[0] + 1] - edges[n[0]]]) for row, n in tops(names)
        )
    late = sorted({(k, r) for k, _, r in tail})
    pieces = jnp.concatenate(
        [pick(away - 1, [tail[k, s, r] for s in range(1, chips)]) for k, r in late], axis=0
    )
    input_grad = finish(
        words,
        part,
        total_mine,
        from_partner,
        pieces[:, :count],
        swap_cores(pieces[:, count:]),
        late,
        chips,
    )
    return (input_grad, doc_logs)


def solution(mesh):
    placed = (
        P(("groups", "dp"), "tensor"),
        P(("groups", "dp"), "tensor"),
        P(("groups", "dp"), "tensor"),
        P(("groups", "dp"), "tensor"),
        P("dp", "tensor"),
        P("dp", "tensor"),
        P("tensor", None),
        P("tensor", None),
        P("tensor", None),
        P("tensor", None),
        P("tensor", None),
        P(("groups", "dp"), None),
    )
    return jax.shard_map(
        per_device,
        mesh=mesh,
        in_specs=placed,
        out_specs=(P(("groups", "dp"), "tensor"), P(("groups", "dp"), None, "tensor")),
        check_vma=False,
    )
```
